32 devices in a mesh: pipe: 2 (over core), dp: 16 (over z, y, x).
Axes of the slice: x: 2, y: 2, z: 4, core: 2. Of those that a mesh axis runs over, the one named last changes fastest.
Arguments:
- edge_slow: bfloat16 [2, 2, 16, 8, 8, 8, 1024], P('pipe', None, 'dp'), may hold values from -6 to 6
- edge_fast: bfloat16 [2, 2, 16, 32, 8, 8, 128], P('pipe', None, 'dp'), may hold values from -6 to 6
- slow_reduce: bfloat16 [2, 3, 1280, 256], P('pipe'), may hold values from -0.09375 to 0.09375
- slow_spatial: bfloat16 [2, 3, 3, 256, 256], P('pipe'), may hold values from -0.125 to 0.125
- slow_expand: bfloat16 [2, 256, 1024], P('pipe'), may hold values from -0.375 to 0.375
- fast_reduce: bfloat16 [2, 3, 128, 32], P('pipe'), may hold values from -0.3125 to 0.3125
- fast_spatial: bfloat16 [2, 3, 3, 32, 32], P('pipe'), may hold values from -0.375 to 0.375
- fast_expand: bfloat16 [2, 32, 128], P('pipe'), may hold values from -1 to 1
- lateral: bfloat16 [2, 5, 128, 256], P('pipe'), may hold values from -0.25 to 0.25
- norm_gain: float32 [2, 1984], P('pipe'), may hold values from 0.1 to 1.9
- norm_shift: float32 [2, 1984], P('pipe'), may hold values from -2 to 2
- present: int32 [2, 16], replicated, may hold values from 0 to 1, as said below
- crop_side: int32 [2, 16], replicated, may hold values from 5 to 8, as said below
Outputs:
- out_slow: bfloat16 [2, 2, 16, 8, 8, 8, 1024], P('pipe', None, 'dp')
- out_fast: bfloat16 [2, 2, 16, 32, 8, 8, 128], P('pipe', None, 'dp')
- grad_slow_reduce: float32 [2, 3, 1280, 256], P('pipe')
- grad_slow_spatial: float32 [2, 3, 3, 256, 256], P('pipe')
- grad_slow_expand: float32 [2, 256, 1024], P('pipe')
- grad_fast_reduce: float32 [2, 3, 128, 32], P('pipe')
- grad_fast_spatial: float32 [2, 3, 3, 32, 32], P('pipe')
- grad_fast_expand: float32 [2, 32, 128], P('pipe')
- grad_lateral: float32 [2, 5, 128, 256], P('pipe')
- grad_gain: float32 [2, 1984], P('pipe')
- grad_shift: float32 [2, 1984], P('pipe')
The draws below stay inside these ranges and needn't reach their ends.
Inputs may be any that keep to these rules, and one draw needn't show every extreme that they name: `present`: 1 where the group holds a sample in that micro-batch, 0 where it holds none; in every micro-batch some group holds one at crop_side 8. `crop_side`: one of 5, 7 and 8; the sample fills the first crop_side by crop_side cells of the canvas and the rest is outside it; in every micro-batch some present group has 8.
All inputs are finite; a program needn't handle non-finite values.
Results may differ from the reference program's by a relative error of at most 0.019.
Values may be sent and summed in bfloat16 or wider, within the bound.
No kernel may reach another device: no remote copies, remote signals or barrier semaphores. Data moves between devices by JAX's collectives and lax.ppermute only.
A program may use at most 256 MiB of HBM per device.

```python
import jax
import jax.numpy as jnp
from jax import lax

CS = 1024
CB = 256
CF = 128
FB = 32
CL = 256
TS = 8
TF = 32
KL = 5
CANVAS = 8
MICRO = 2
GROUPS = 16
CAT = 1280
NORMW = 1984


def forced_group(key):
    return jax.random.randint(key, (MICRO,), 0, GROUPS)


def draw_present(key, part):
    chosen = forced_group(key)
    key = jax.random.fold_in(key, 11)
    flags = (jax.random.randint(key, (MICRO, GROUPS), 0, 8) > 0).astype(jnp.int32)
    forced = jnp.arange(GROUPS)[None, :] == chosen[:, None]
    return jnp.where(forced, 1, flags).astype(jnp.int32)


def draw_crop_side(key, part):
    chosen = forced_group(key)
    key = jax.random.fold_in(key, 23)
    side_table = jnp.array([CANVAS * 5 // 8, CANVAS * 7 // 8, CANVAS], jnp.int32)
    picked = side_table[jax.random.randint(key, (MICRO, GROUPS), 0, 3)]
    forced = jnp.arange(GROUPS)[None, :] == chosen[:, None]
    return jnp.where(forced, CANVAS, picked).astype(jnp.int32)


def block_scale(stream_key, dims, shards, smallest, high):
    level, own = 1.0, jax.random.fold_in(stream_key, 6)
    for position, blocks in shards:
        steps = jnp.exp(jax.random.uniform(jax.random.fold_in(own, position), (blocks,), jnp.float32, smallest / len(shards), high / len(shards)))
        level = level * jnp.repeat(steps, dims[position] // blocks).reshape([-1 if axis == position else 1 for axis in range(len(dims))])
    return level


def normal_values(own_key, shape, width, reach, split=(), kind=jnp.bfloat16):
    values = width * jax.random.normal(own_key, shape, jnp.float32)
    if split:
        values = values * block_scale(own_key, shape, split, -0.22, 0.18)
    return jnp.clip(values, -reach, reach).astype(kind)


def setup_inputs(seed: int = 0) -> dict:
    key_list = jax.random.split(jax.random.key(seed), 14)
    return {
        "edge_slow": normal_values(key_list[0], (2, MICRO, GROUPS, TS, CANVAS, CANVAS, CS), 1.0, 6.0, ((0, 2), (2, 16))),
        "edge_fast": normal_values(key_list[1], (2, MICRO, GROUPS, TF, CANVAS, CANVAS, CF), 1.0, 6.0, ((0, 2), (2, 16))),
        "slow_reduce": normal_values(key_list[2], (2, 3, CAT, CB), (3 * CAT) ** -0.5, 0.09375, ((0, 2),)),
        "slow_spatial": normal_values(key_list[3], (2, 3, 3, CB, CB), (9 * CB) ** -0.5, 0.125, ((0, 2),)),
        "slow_expand": normal_values(key_list[4], (2, CB, CS), CB ** -0.5, 0.375, ((0, 2),)),
        "fast_reduce": normal_values(key_list[5], (2, 3, CF, FB), (3 * CF) ** -0.5, 0.3125, ((0, 2),)),
        "fast_spatial": normal_values(key_list[6], (2, 3, 3, FB, FB), (9 * FB) ** -0.5, 0.375, ((0, 2),)),
        "fast_expand": normal_values(key_list[7], (2, FB, CF), FB ** -0.5, 1.0, ((0, 2),)),
        "lateral": normal_values(key_list[8], (2, KL, CF, CL), (KL * CF) ** -0.5, 0.25, ((0, 2),)),
        "norm_gain": jnp.clip(1.0 + 0.18 * jax.random.normal(key_list[9], (2, NORMW), jnp.float32), 0.1, 1.9),
        "norm_shift": normal_values(key_list[10], (2, NORMW), 0.5, 2.0, ((0, 2),), jnp.float32),
        "present": draw_present(jax.random.fold_in(key_list[13], 71), 0),
        "crop_side": draw_crop_side(jax.random.fold_in(key_list[13], 71), 0),
    }


epsilon = 1e-05

@jax.custom_vjp
def low(v):
    return lax.optimization_barrier(v.astype(jnp.bfloat16)).astype(jnp.float32)

@jax.custom_vjp
def low_back(v):
    return v

def low_keep(v):
    return (low(v), None)

def low_pass(kept, grad):
    return (grad,)

def back_keep(v):
    return (v, None)

def back_low(kept, grad):
    return (low(grad),)
low.defvjp(low_keep, low_pass)
low_back.defvjp(back_keep, back_low)

def norm_spans(bottle_width, slow_width, fast_bottle, fast_width, side_width):
    extents = [bottle_width, bottle_width, slow_width, fast_bottle, fast_bottle, fast_width, side_width]
    span_list = []
    offset = 0
    for extent in extents:
        span_list.append((offset, extent))
        offset = offset + extent
    return span_list

def crop_masks(present, crop_side, canvas):
    cell_index = jnp.arange(canvas).astype(jnp.int32)
    side_limit = crop_side[:, :, None, None]
    inside = (cell_index[None, None, :, None] < side_limit) & (cell_index[None, None, None, :] < side_limit) & (present[:, :, None, None] > 0)
    crop_mask = inside.astype(jnp.float32)[:, :, None, :, :, None]
    return (crop_mask, lax.optimization_barrier(jnp.sum(crop_mask, axis=(1, 2, 3, 4, 5))))

def time_conv(field_in, weight, stride, padding):
    tap_count = weight.shape[0]
    out_frames = (field_in.shape[1] + 2 * padding - tap_count) // stride + 1
    padded = jnp.pad(field_in, ((0, 0), (padding, padding), (0, 0), (0, 0), (0, 0)))
    summed_terms = 0.0
    for tap_index in range(tap_count):
        window = padded[:, tap_index:tap_index + stride * (out_frames - 1) + 1:stride]
        summed_terms = summed_terms + jnp.einsum('bthwc,cd->bthwd', window, weight[tap_index], precision=lax.Precision.HIGHEST)
    return summed_terms

def space_conv(field_in, weight):
    height = field_in.shape[2]
    breadth = field_in.shape[3]
    padded = jnp.pad(field_in, ((0, 0), (0, 0), (1, 1), (1, 1), (0, 0)))
    summed_terms = 0.0
    for row_shift in range(3):
        for col_shift in range(3):
            window = padded[:, :, row_shift:row_shift + height, col_shift:col_shift + breadth]
            summed_terms = summed_terms + jnp.einsum('bthwc,cd->bthwd', window, weight[row_shift, col_shift], precision=lax.Precision.HIGHEST)
    return summed_terms

def layer_forward(slow_in, fast_in, params, mask_now, count_slow, count_fast):
    slow_reduce, slow_spatial, slow_expand, fast_reduce, fast_spatial, fast_expand, lateral, gain_all, shift_all = params
    span_list = norm_spans(slow_reduce.shape[2], slow_in.shape[-1], fast_reduce.shape[2], fast_in.shape[-1], lateral.shape[2])

    def normed(value_in, index_now, count_now):
        offset, extent = span_list[index_now]
        mean_now = lax.optimization_barrier(jnp.sum(value_in * mask_now, axis=(0, 1, 2, 3))) / count_now
        square_now = lax.optimization_barrier(jnp.sum(value_in * value_in * mask_now, axis=(0, 1, 2, 3))) / count_now
        scale_now = lax.rsqrt(square_now - mean_now * mean_now + epsilon)
        return (value_in - mean_now) * scale_now * gain_all[offset:offset + extent] + shift_all[offset:offset + extent]
    side_pre = low_back(time_conv(fast_in, lateral, 4, 2))
    side_act = low(jax.nn.silu(normed(side_pre, 6, count_slow)) * mask_now)
    slow_pre1 = low_back(time_conv(jnp.concatenate([slow_in, side_act], axis=-1), slow_reduce, 1, 1))
    slow_act1 = low(jax.nn.silu(normed(slow_pre1, 0, count_slow)) * mask_now)
    slow_pre2 = low_back(space_conv(slow_act1, slow_spatial))
    slow_act2 = low(jax.nn.silu(normed(slow_pre2, 1, count_slow)) * mask_now)
    slow_pre3 = low_back(jnp.einsum('bthwc,cd->bthwd', slow_act2, slow_expand, precision=lax.Precision.HIGHEST))
    slow_out = low_back(low(jax.nn.silu(slow_in + normed(slow_pre3, 2, count_slow)) * mask_now))
    fast_pre1 = low_back(time_conv(fast_in, fast_reduce, 1, 1))
    fast_act1 = low(jax.nn.silu(normed(fast_pre1, 3, count_fast)) * mask_now)
    fast_pre2 = low_back(space_conv(fast_act1, fast_spatial))
    fast_act2 = low(jax.nn.silu(normed(fast_pre2, 4, count_fast)) * mask_now)
    fast_pre3 = low_back(jnp.einsum('bthwc,cd->bthwd', fast_act2, fast_expand, precision=lax.Precision.HIGHEST))
    fast_out = low_back(low(jax.nn.silu(fast_in + normed(fast_pre3, 5, count_fast)) * mask_now))
    return (slow_out, fast_out)

def reference(edge_slow, edge_fast, slow_reduce, slow_spatial, slow_expand, fast_reduce, fast_spatial, fast_expand, lateral, norm_gain, norm_shift, present, crop_side):
    crop_mask, crop_area = crop_masks(present, crop_side, CANVAS)
    stepper = jax.checkpoint(layer_forward)
    floats = tuple((weight_now.astype(jnp.float32) for weight_now in (slow_reduce, slow_spatial, slow_expand, fast_reduce, fast_spatial, fast_expand, lateral))) + (norm_gain.astype(jnp.float32), norm_shift.astype(jnp.float32))

    def forward(params, slow_all, fast_all):
        slow_list = []
        fast_list = []
        for micro_now in range(MICRO):
            mask_now = crop_mask[micro_now]
            slow_now = slow_all[micro_now] * mask_now
            fast_now = fast_all[micro_now] * mask_now
            for layer_index in range(2):
                layer_params = tuple((param_now[layer_index] for param_now in params))
                slow_now, fast_now = stepper(slow_now, fast_now, layer_params, mask_now, crop_area[micro_now] * TS, crop_area[micro_now] * TF)
            slow_list.append(slow_now)
            fast_list.append(fast_now)
        return (jnp.stack(slow_list), jnp.stack(fast_list))
    (slow_result, fast_result), pullback = jax.vjp(forward, floats, edge_slow[0].astype(jnp.float32), edge_fast[0].astype(jnp.float32))
    weight_grads, slow_grad, fast_grad = pullback((edge_slow[1].astype(jnp.float32), edge_fast[1].astype(jnp.float32)))
    out_slow = jnp.stack([slow_grad, slow_result]).astype(jnp.bfloat16)
    out_fast = jnp.stack([fast_grad, fast_result]).astype(jnp.bfloat16)
    return (out_slow, out_fast, weight_grads[0], weight_grads[1], weight_grads[2], weight_grads[3], weight_grads[4], weight_grads[5], weight_grads[6], weight_grads[7], weight_grads[8])
```

```python
from types import SimpleNamespace

import jax
import jax.numpy as jnp
from jax import lax
from jax.experimental import pallas as pl
from jax.experimental.pallas import tpu as pltpu
from jax.sharding import PartitionSpec as P

epsilon = 1e-05
F32 = jnp.float32
BF = jnp.bfloat16
LANES = 128
SPAN = {
    "s1": (0, 2),
    "s2": (2, 2),
    "s3": (4, 8),
    "f1": (12, 1),
    "f2": (13, 1),
    "f3": (14, 1),
    "lp": (15, 2),
}
SHIFT_ROW = 24


SMEM_KEYS = ("ids", "present", "crop")


def space_of(key):
    if key in SMEM_KEYS:
        return pltpu.SMEM
    if key.startswith("hbm_"):
        return pltpu.HBM
    if key.startswith("any_"):
        return pl.ANY
    return pltpu.VMEM


def run(body, name, ins, outs, scratch=None, hold=(), far_hold=(), groups=1):
    scratch = dict(scratch or {})
    outs = dict(outs)
    ins = dict(ins, **{"any_hold%d" % i: value for i, value in enumerate(hold)})
    ins = dict(ins, **{"hbm_hold%d" % i: value for i, value in enumerate(far_hold)})
    shared = "part" in outs
    if shared:
        shape, kind = outs["part"]
        scratch["sums"] = (shape, kind)
        outs["part"] = ((groups,) + shape, kind)
    names = list(ins) + list(outs) + list(scratch)

    def kernel(*refs):
        r = SimpleNamespace(**dict(zip(names, refs)))
        if not shared:
            body(r)
            return
        spread = r.part
        r.part = r.sums
        r.sums[...] = jnp.zeros(r.sums.shape, F32)
        body(r)

        def copy(i, carry):
            spread[i] = r.sums[...]
            return carry

        lax.fori_loop(0, groups, copy, 0)

    result = pl.pallas_call(
        kernel,
        name=name,
        out_shape=[jax.ShapeDtypeStruct(shape, kind) for shape, kind in outs.values()],
        in_specs=[pl.BlockSpec(memory_space=space_of(key)) for key in ins],
        out_specs=[pl.BlockSpec(memory_space=space_of(key)) for key in outs],
        scratch_shapes=[
            pltpu.VMEM(*item) if isinstance(item, tuple) else item for item in scratch.values()
        ],
        compiler_params=pltpu.CompilerParams(vmem_limit_bytes=16 * 1024 * 1024),
        cost_estimate=pl.CostEstimate(flops=2_000_000_000, bytes_accessed=1000, transcendentals=0),
    )(*ins.values())
    return SimpleNamespace(**dict(zip(outs, result)))


def dot(a, b):
    return lax.dot_general(a, b, (((1,), (0,)), ((), ())), preferred_element_type=F32)


def dot_t(a, b):
    return lax.dot_general(a, b, (((1,), (1,)), ((), ())), preferred_element_type=F32)


def t_dot(a, b):
    return lax.dot_general(a, b, (((0,), (0,)), ((), ())), preferred_element_type=F32)


def sigm(v):
    return 0.5 * jnp.tanh(0.5 * v) + 0.5


def slope_of(v):
    s = sigm(v)
    return s * (1.0 + v * (1.0 - s))


def fold8(x):
    return jnp.sum(x.reshape(x.shape[0] // 8, 8, x.shape[1]), axis=0)


def wide(row, width):
    return row if row.shape[1] == width else jnp.concatenate([row] * (width // row.shape[1]), axis=1)


def lanes_of(block, start, count):
    if count == 1:
        return block[start : start + 1, :]
    return jnp.concatenate([block[start + i : start + i + 1, :] for i in range(count)], axis=1)


def put(part, row, acc8):
    total = jnp.sum(acc8, axis=0, keepdims=True)
    for i in range(total.shape[1] // LANES):
        part[row + i : row + i + 1, :] = total[:, i * LANES : (i + 1) * LANES]


def quarters(acc, width):
    count = acc.shape[1] // width
    total = acc[:, :width]
    for i in range(1, count):
        total = total + acc[:, i * width : (i + 1) * width]
    return total


def folded(tot, width):
    total = tot
    for i in range(1, LANES // width):
        total = total + pltpu.roll(tot, i * width, 1)
    return total


def gain(r, key):
    start, count = SPAN[key]
    return lanes_of(r.par[...], start, count)


def shift(r, key):
    start, count = SPAN[key]
    return lanes_of(r.par[...], SHIFT_ROW + start, count)


def moments(tot, row, key, inv, fast_bottle=32):
    count = SPAN[key][1]
    block = folded(tot, fast_bottle) if key in ("f1", "f2") else tot
    mean = lanes_of(block, row, count) * inv
    square = lanes_of(block, row + count, count) * inv
    return mean, lax.rsqrt(square - mean * mean + epsilon)


def pair_of(tot, row, key, fast_bottle=32):
    count = SPAN[key][1]
    block = folded(tot, fast_bottle) if key in ("f1", "f2") else tot
    return lanes_of(block, row, count), lanes_of(block, row + count, count)


def invs(r):
    return r.inv[0:1, :1], r.inv[1:2, :1]


def norm_of(r, tot, row, key, inv, width=None):
    mean, rs = moments(tot, row, key, inv)
    scale = rs * gain(r, key)
    offset = shift(r, key) - mean * scale
    if width is None:
        return mean, rs, scale, offset
    return tuple(wide(v, width) for v in (mean, rs, scale, offset))


def windows(x, side):
    rows, width = x.shape
    col = lax.broadcasted_iota(jnp.int32, (rows, width), 0) % side
    zero = jnp.zeros((side, width), x.dtype)
    out = {}
    for c in range(3):
        step = c - 1
        if step == 0:
            y = x
        else:
            y = pltpu.roll(x, (-step) % rows, 0)
            y = jnp.where((col + step >= 0) & (col + step < side), y, 0.0)
        out[0, c] = jnp.concatenate([zero, y[: rows - side]], axis=0)
        out[1, c] = y
        out[2, c] = jnp.concatenate([y[side:], zero], axis=0)
    return out


def put_windows(col, at, x, side, back):
    width = x.shape[1]
    for (i, j), y in windows(x, side).items():
        if back:
            i, j = 2 - i, 2 - j
        spot = (i * 3 + j) * width
        col[at, spot : spot + width] = y.astype(BF)


def loop(count, body, init=0):
    return lax.fori_loop(0, count, body, init)


def at_frame(t, cells, lead=0):
    return pl.ds(pl.multiple_of(t * cells, cells) + lead, cells)


def spans(total, step):
    return [(a, step) for a in range(0, total, step)]


def clear_ends(pad, cells):
    rows, width = pad.shape
    zero = jnp.zeros((cells, width), pad.dtype)
    pad[0:cells, :] = zero
    pad[rows - cells : rows, :] = zero


def chosen(r, layer, own, other):
    return jnp.where(r.ids[0] == layer, own, other)


def lane_group(shape, width):
    return lax.div(lax.broadcasted_iota(jnp.int32, shape, 1), width)


def placing(rows, group):
    lane = lax.broadcasted_iota(jnp.int32, (rows, LANES), 1)
    row = lax.broadcasted_iota(jnp.int32, (rows, LANES), 0)
    hit = lax.rem(lane, rows) == row if group is None else lane - group * rows == row
    return jnp.where(hit, 1.0, 0.0).astype(BF)


def first_mix(r, d, xpad, part, row):
    acc_s = acc_q = 0.0
    for a, n in spans(d.rows, d.step):
        got = (
            dot(xpad[a : a + n, 2 * d.cf : 4 * d.cf], r.wa[0 : 2 * d.cf, :])
            + dot(xpad[a + d.cells : a + d.cells + n, :], r.wa[2 * d.cf : 6 * d.cf, :])
            + dot(xpad[a + 2 * d.cells : a + 2 * d.cells + n, 0 : d.cf], r.wa[6 * d.cf : 7 * d.cf, :])
        )
        r.lp[a : a + n, :] = got[:, : d.cl]
        r.f1[a : a + n, :] = got[:, d.cl :]
        acc_s = acc_s + fold8(got)
        acc_q = acc_q + fold8(got * got)
    put(part, row, acc_s[:, : d.cl])
    put(part, row + 2, acc_q[:, : d.cl])
    put(part, row + 4, acc_s[:, d.cl :])
    put(part, row + 5, acc_q[:, d.cl :])


def stage_first(d):
    def body(r):
        sect, group = r.ids[0], r.ids[1]
        small = loading(
            r,
            [
                (r.hbm_lat_own, r.lat_own),
                (r.hbm_lat_other, r.lat_other),
                (r.hbm_fr_own, r.fr_own),
                (r.hbm_fr_other, r.fr_other),
            ],
        )
        large = loading(r, [(r.hbm_own.at[sect], r.own), (r.hbm_other.at[sect], r.other)], 4)

        def add(i, total):
            extent = r.crop[sect, i]
            return total + jnp.where(r.present[sect, i] > 0, extent * extent, 0)

        area = lax.fori_loop(0, d.groups, add, jnp.int32(0))
        area = jnp.full((1, LANES), area.astype(F32))
        r.inv[...] = jnp.zeros(r.inv.shape, F32)
        r.inv[0:1, :] = 1.0 / (area * d.frames)
        r.inv[1:2, :] = 1.0 / (area * (d.frames * d.quad))
        limit = jnp.where(r.present[sect, group] > 0, r.crop[sect, group], 0)
        cell = lax.broadcasted_iota(jnp.int32, (d.cells, LANES), 0)
        inside = (lax.div(cell, d.side) < limit) & (lax.rem(cell, d.side) < limit)
        mask = jnp.where(inside, 1.0, 0.0)
        r.mask[...] = mask
        small()
        for layer, wa in enumerate((r.wa, r.wa1)):
            for b in range(d.quad + 3):
                row = slice(b * d.cf, (b + 1) * d.cf)
                if b < d.taps:
                    wa[row, : d.cl] = chosen(r, layer, r.lat_own[b], r.lat_other[b])
                else:
                    wa[row, : d.cl] = jnp.zeros((d.cf, d.cl), BF)
                total = jnp.zeros((d.cf, LANES), F32)
                for q in range(d.quad):
                    k = b - 1 - q
                    if 0 <= k < 3:
                        tap = chosen(r, layer, r.fr_own[k], r.fr_other[k])
                        total = total + t_dot(tap, placing(d.fb, q))
                wa[row, d.cl :] = total.astype(BF)
        clear_ends(r.xpad, d.cells)
        large()

        def frame(t, carry):
            for q in range(d.quad):
                here = r.own[t, q].astype(F32)
                there = r.other[t, q].astype(F32)
                value = jnp.where(sect == 0, here, there)
                r.xpad[at_frame(t, d.cells, d.cells), q * d.cf : (q + 1) * d.cf] = (
                    value * mask
                ).astype(BF)
                r.cot[t, q] = jnp.where(sect == 0, there, here).astype(BF)
            return carry

        loop(d.frames, frame)
        first_mix(r, d, r.xpad, r.part, 0)

    return body


def stage_slow_in(d):
    pack = stage_pack(d)

    def body(r):
        sect = r.ids[0]
        names = ("fs", "fe", "gain", "shift")
        small = loading(
            r,
            [
                (getattr(r, "hbm_%s_%s" % (name, side)), getattr(r, "%s_%s" % (name, side)))
                for name in names
                for side in ("own", "other")
            ],
        )
        large = loading(r, [(r.hbm_own.at[sect], r.own), (r.hbm_other, r.other)], 8)
        fetch = fetching(r, [(r.hbm_red_own, r.hbm_red_other, r.wred_0, r.wred_1)])
        small()
        pack(r)
        large()
        clear_ends(r.spad, d.cells)
        mask = wide(r.mask[...], 256)

        def frame(t, carry):
            for c in range(0, d.cs, 256):
                lane = slice(c, c + 256)
                here = r.own[t, :, lane].astype(F32)
                there = r.other[t, :, lane].astype(F32)
                value = jnp.where(sect == 0, here, there)
                r.spad[at_frame(t, d.cells, d.cells), lane] = (value * mask).astype(BF)
                r.cot[t, :, lane] = jnp.where(sect == 0, there, here).astype(BF)
            return carry

        loop(d.frames, frame)
        fetch()
        for a, n in spans(d.rows, d.step):
            got = 0.0
            for k in range(3):
                b = a + k * d.cells
                got = got + dot(r.spad[b : b + n, :], r.wred_0[k, : d.cs, :])
            r.y[a : a + n, :] = got

    return body


def stage_pack(d):
    sizes = [d.cb, d.cb, d.cs, d.fb, d.fb, d.cf, d.cl]
    keys = ["s1", "s2", "s3", "f1", "f2", "f3", "lp"]

    def body(r):
        spread = placing(d.fb, None)
        for layer in range(2):
            w2, w2t, w3, par = (
                (r.w2_0, r.w2t_0, r.w3_0, r.par_0),
                (r.w2_1, r.w2t_1, r.w3_1, r.par_1),
            )[layer]
            where = lane_group((d.fb, LANES), d.fb)
            for j in range(9):
                tap = chosen(r, layer, r.fs_own[j], r.fs_other[j])
                for out, tiled in ((w2, dot(tap, spread)), (w2t, t_dot(tap, spread))):
                    for q in range(d.quad):
                        row = j * LANES + q * d.fb
                        out[row : row + d.fb, :] = jnp.where(where == q, tiled, 0.0).astype(BF)
            w3[...] = jnp.zeros(w3.shape, BF)
            tap = chosen(r, layer, r.fe_own[...], r.fe_other[...])
            for q in range(d.quad):
                w3[q * d.fb : (q + 1) * d.fb, q * d.cf : (q + 1) * d.cf] = tap
            par[...] = jnp.zeros(par.shape, F32)
            for base, own, other in (
                (0, r.gain_own, r.gain_other),
                (SHIFT_ROW, r.shift_own, r.shift_other),
            ):
                values = chosen(r, layer, own[...], other[...])
                offset = 0
                for key, size in zip(keys, sizes):
                    row = base + SPAN[key][0]
                    piece = values[:, offset : offset + size]
                    offset += size
                    if size < LANES:
                        par[row : row + 1, :] = wide(piece, LANES)
                    else:
                        for i in range(size // LANES):
                            par[row + i : row + i + 1, :] = piece[:, i * LANES : (i + 1) * LANES]

    return body


def fetching(r, weights):
    def copies(first):
        made = []
        for own, other, out_0, out_1 in weights:
            for source, target in ((own, out_0), (other, out_1)) if first else ((own, out_1), (other, out_0)):
                made.append(pltpu.make_async_copy(source, target, r.sems.at[len(made)]))
        return made

    def each(action):
        for first in (True, False):

            @pl.when(r.ids[0] == 0 if first else r.ids[0] != 0)
            def _():
                for copy in copies(first):
                    action(copy)

    each(lambda copy: copy.start())
    return lambda: each(lambda copy: copy.wait())


def loading(r, pairs, first=0):
    copies = [
        pltpu.make_async_copy(source, target, r.loads.at[first + i])
        for i, (source, target) in enumerate(pairs)
    ]
    for copy in copies:
        copy.start()

    def wait():
        for copy in copies:
            copy.wait()

    return wait


def gate(r):
    r.out[...] = r.part[...]


def stage_place(r):
    for i, (grad, value) in enumerate(((r.grad, r.value_got), (r.grad_got, r.value))):
        for t in range(grad.shape[0]):
            here, there = grad[t].astype(F32), value[t].astype(F32)
            r.both[i, t] = jnp.where(r.ids[0] == 0, here, there).astype(BF)
        pltpu.make_async_copy(r.both.at[i], r.hbm_out.at[i], r.sems.at[i]).start()
    for i in range(2):
        pltpu.make_async_copy(r.both.at[i], r.hbm_out.at[i], r.sems.at[i]).wait()


def stage_second(d, row, carried):
    def body(r):
        tot = jnp.sum(r.sync[...], axis=0)
        r.tot[...] = tot
        inv_s, inv_f = invs(r)
        _, _, lg, lb = norm_of(r, tot, row, "lp", inv_s)
        _, _, fg, fb = norm_of(r, tot, row + 4, "f1", inv_f)
        mask = r.mask[...]
        mask2 = wide(mask, d.cl)
        clear_ends(r.lapad, d.cells)
        if carried:
            clear_ends(r.spad, d.cells)
            _, _, sg, sb = norm_of(SimpleNamespace(par=r.par0), tot, 0, "s3", inv_s)

        def frame(t, carry):
            at = at_frame(t, d.cells)
            up = at_frame(t, d.cells, d.cells)
            v = r.lp[at, :] * lg + lb
            r.lapad[up, :] = (v * sigm(v) * mask2).astype(BF)
            v = r.f1[at, :] * fg + fb
            v = (v * sigm(v) * mask).astype(BF)
            r.k1[at, :] = v
            put_windows(r.colf, at, v.astype(F32), d.side, False)
            if carried:
                for c in range(0, d.cs, 256):
                    z = r.xpad[up, c : c + 256].astype(F32) + (
                        r.s3[at, c : c + 256] * sg[:, c : c + 256] + sb[:, c : c + 256]
                    )
                    r.spad[up, c : c + 256] = (z * sigm(z) * mask2).astype(BF)
            return carry

        loop(d.frames, frame)
        acc_s = acc_q = acc_fs = acc_fq = 0.0
        for a, n in spans(d.rows, d.step):
            got = 0.0 if carried else r.y[a : a + n, :]
            for k in range(3):
                b = a + k * d.cells
                if carried:
                    got = got + dot(r.spad[b : b + n, :], r.wred[k, : d.cs, :])
                got = got + dot(r.lapad[b : b + n, :], r.wred[k, d.cs :, :])
            r.s1[a : a + n, :] = got
            acc_s = acc_s + fold8(got)
            acc_q = acc_q + fold8(got * got)
            got = dot(r.colf[a : a + n, :], r.w2[...])
            r.f2[a : a + n, :] = got
            kept = (got.reshape(n // d.cells, d.cells, got.shape[1]) * mask[None]).reshape(got.shape)
            acc_fs = acc_fs + fold8(kept)
            acc_fq = acc_fq + fold8(kept * got)
        put(r.part, 0, acc_s)
        put(r.part, 2, acc_q)
        put(r.part, 4, acc_fs)
        put(r.part, 5, acc_fq)

    return body


def stage_third(d, fetched):
    def body(r):
        if fetched:
            fetch = fetching(
                r,
                [
                    (r.hbm_sp_own, r.hbm_sp_other, r.wsp_0, r.wsp_1),
                    (r.hbm_ex_own, r.hbm_ex_other, r.we_0, r.we_1),
                ],
            )
        tot = jnp.sum(r.sync[...], axis=0)
        r.tot[...] = tot
        inv_s, inv_f = invs(r)
        _, _, sg, sb = norm_of(r, tot, 0, "s1", inv_s)
        _, _, fg, fb = norm_of(r, tot, 4, "f2", inv_f)
        mask = r.mask[...]
        mask2 = wide(mask, d.cb)

        def frame(t, carry):
            at = at_frame(t, d.cells)
            v = r.s1[at, :] * sg + sb
            v = (v * sigm(v) * mask2).astype(BF)
            r.h1[at, :] = v
            put_windows(r.cols, at, v.astype(F32), d.side, False)
            v = r.f2[at, :] * fg + fb
            r.k2[at, :] = (v * sigm(v) * mask).astype(BF)
            return carry

        loop(d.frames, frame)
        if fetched:
            fetch()
        wsp = r.wsp_0 if fetched else r.wsp
        acc_s = acc_q = acc_fs = acc_fq = 0.0
        for a, n in spans(d.rows, d.step):
            got = dot(r.cols[a : a + n, :], wsp[...])
            r.s2[a : a + n, :] = got
            kept = (got.reshape(n // d.cells, d.cells, got.shape[1]) * mask2[None]).reshape(got.shape)
            acc_s = acc_s + fold8(kept)
            acc_q = acc_q + fold8(kept * got)
            got = dot(r.k2[a : a + n, :], r.w3[...])
            r.f3[a : a + n, :] = got
            acc_fs = acc_fs + fold8(got)
            acc_fq = acc_fq + fold8(got * got)
        put(r.part, 0, acc_s)
        put(r.part, 2, acc_q)
        put(r.part, 4, quarters(acc_fs, d.cf))
        put(r.part, 5, quarters(acc_fq, d.cf))

    return body


def expand_slow(r, d, sg, sb, mask2):
    def frame(t, carry):
        at = at_frame(t, d.cells)
        v = r.s2[at, :] * sg + sb
        r.h2[at, :] = (v * sigm(v) * mask2).astype(BF)
        return carry

    loop(d.frames, frame)
    for c in range(0, d.cs, 256):
        acc_s = acc_q = 0.0
        for a, n in spans(d.rows, d.step):
            got = dot(r.h2[a : a + n, :], r.we[:, c : c + 256])
            r.s3[a : a + n, c : c + 256] = got
            acc_s = acc_s + fold8(got)
            acc_q = acc_q + fold8(got * got)
        put(r.part, c // LANES, acc_s)
        put(r.part, (d.cs + c) // LANES, acc_q)


def stage_fourth(d, last):
    def body(r):
        tot = jnp.sum(r.sync[...], axis=0)
        r.tot[...] = tot
        inv_s, inv_f = invs(r)
        _, _, sg, sb = norm_of(r, tot, 0, "s2", inv_s)
        fm, fr, fg, fb = norm_of(r, tot, 4, "f3", inv_f)
        mask = r.mask[...]
        mask2 = wide(mask, d.cb)
        expand_slow(r, d, sg, sb, mask2)
        if not last:
            clear_ends(r.ypad, d.cells)

        def frame(t, carry):
            at = at_frame(t, d.cells)
            up = at_frame(t, d.cells, d.cells)
            for q in range(d.quad):
                lane = slice(q * d.cf, (q + 1) * d.cf)
                f3 = r.f3[at, lane]
                z = r.xpad[up, lane].astype(F32) + (f3 * fg + fb)
                s = sigm(z)
                y = (z * s * mask).astype(BF)
                if last:
                    r.yout[t, q] = y
                    grad = r.cot[t, q].astype(F32) * mask * (s * (1.0 + z * (1.0 - s)))
                    r.dzf[at, lane] = grad
                    u = (f3 - fm) * fr
                    carry = (carry[0] + fold8(grad), carry[1] + fold8(grad * u))
                else:
                    r.ypad[up, lane] = y
            return carry

        zero = jnp.zeros((8, d.cf), F32)
        done = loop(d.frames, frame, (zero, zero))
        if last:
            put(r.part, 16, done[0])
            put(r.part, 17, done[1])
        else:
            first_mix(r, d, r.ypad, r.part, 16)

    return body


def fast_back3(r, d, gs, gg, tot_f3, tot_f2, row):
    _, inv_f = invs(r)
    mask = r.mask[...]
    mean, rs = moments(tot_f3, 4, "f3", inv_f)
    factor = rs * gain(r, "f3")
    gs, gg = gs * inv_f, gg * inv_f
    m2, r2, g2, b2 = norm_of(r, tot_f2, 4, "f2", inv_f)

    def frame(t, carry):
        at = at_frame(t, d.cells)
        for q in range(d.quad):
            lane = slice(q * d.cf, (q + 1) * d.cf)
            u = (r.f3[at, lane] - mean) * rs
            r.df3[at, lane] = (factor * (r.dzf[at, lane] - mask * (gs + u * gg))).astype(BF)
        return carry

    loop(d.frames, frame)
    acc_s = acc_q = 0.0
    for a, n in spans(d.rows, d.step):
        got = dot_t(r.df3[a : a + n, :], r.w3[...])
        f2 = r.f2[a : a + n, :]
        kept = (got.reshape(n // d.cells, d.cells, got.shape[1]) * mask[None]).reshape(got.shape)
        kept = kept * slope_of(f2 * g2 + b2)
        r.d2f[a : a + n, :] = kept
        acc_s = acc_s + fold8(kept)
        acc_q = acc_q + fold8(kept * ((f2 - m2) * r2))
    put(r.part, row, acc_s)
    put(r.part, row + 1, acc_q)


def fast_back2(r, d, gs, gg, tot_f2, tot_f1, f1_row, row):
    _, inv_f = invs(r)
    mask = r.mask[...]
    mean, rs = moments(tot_f2, 4, "f2", inv_f)
    factor = rs * gain(r, "f2")
    gs, gg = gs * inv_f, gg * inv_f
    m1, r1, g1, b1 = norm_of(r, tot_f1, f1_row, "f1", inv_f)

    def frame(t, carry):
        at = at_frame(t, d.cells)
        u = (r.f2[at, :] - mean) * rs
        v = (factor * (r.d2f[at, :] - mask * (gs + u * gg))).astype(BF)
        r.df2[at, :] = v
        put_windows(r.colf, at, v.astype(F32), d.side, True)
        return carry

    loop(d.frames, frame)
    acc_s = acc_q = 0.0
    wide_row = d.quad * d.fb
    for a, n in spans(d.rows, d.step):
        got = dot(r.colf[a : a + n, :], r.w2t[...])
        f1 = r.f1[a : a + n, :]
        kept = (got.reshape(n // d.cells, d.cells, got.shape[1]) * mask[None]).reshape(got.shape)
        kept = kept * slope_of(f1 * g1 + b1)
        r.d1f[a : a + n, :] = kept
        acc_s = acc_s + fold8(kept)
        acc_q = acc_q + fold8(kept * ((f1 - m1) * r1))
    put(r.part, row, acc_s)
    put(r.part, row + 1, acc_q)


def fast_back1(r, d, gs, gg, tot_f1, f1_row):
    _, inv_f = invs(r)
    mask = r.mask[...]
    mean, rs = moments(tot_f1, f1_row, "f1", inv_f)
    factor = rs * gain(r, "f1")
    gs, gg = gs * inv_f, gg * inv_f

    def frame(t, carry):
        at = at_frame(t, d.cells)
        u = (r.f1[at, :] - mean) * rs
        r.gpad[at_frame(t, d.cells, d.cells), d.cl :] = (
            factor * (r.d1f[at, :] - mask * (gs + u * gg))
        ).astype(BF)
        return carry

    loop(d.frames, frame)


def lateral_back(r, d, gs, gg, tot_lp, lp_row):
    inv_s, _ = invs(r)
    mask2 = wide(r.mask[...], d.cl)
    mean, rs = moments(tot_lp, lp_row, "lp", inv_s)
    factor = rs * gain(r, "lp")
    gs, gg = gs * inv_s, gg * inv_s

    def frame(t, carry):
        at = at_frame(t, d.cells)
        u = (r.lp[at, :] - mean) * rs
        r.gpad[at_frame(t, d.cells, d.cells), : d.cl] = (
            factor * (r.dl[at, :] - mask2 * (gs + u * gg))
        ).astype(BF)
        return carry

    loop(d.frames, frame)


def fast_input_grad(r, d, a, n):
    c = d.cf
    mid = dot_t(r.gpad[a + d.cells : a + d.cells + n, :], r.wa[2 * c : 6 * c, :])
    late = dot_t(r.gpad[a + 2 * d.cells : a + 2 * d.cells + n, :], r.wa[0 : 2 * c, :])
    early = dot_t(r.gpad[a : a + n, :], r.wa[6 * c : 7 * c, :])
    return [
        mid[:, :c] + early,
        mid[:, c : 2 * c],
        mid[:, 2 * c : 3 * c] + late[:, :c],
        mid[:, 3 * c :] + late[:, c:],
    ]


def slow_back3(r, d, gs, gg, tot_s3, tot_s2, row):
    inv_s, _ = invs(r)
    mask2 = wide(r.mask[...], d.cb)
    mean, rs = moments(tot_s3, 0, "s3", inv_s)
    factor = rs * gain(r, "s3")
    gs, gg = gs * inv_s, gg * inv_s
    m2, r2, g2, b2 = norm_of(r, tot_s2, 0, "s2", inv_s)

    def frame(t, carry):
        at = at_frame(t, d.cells)
        for c in range(0, d.cs, 256):
            lane = slice(c, c + 256)
            u = (r.s3[at, lane] - mean[:, lane]) * rs[:, lane]
            r.ds3[at, lane] = (
                factor[:, lane] * (r.dzs[at, lane] - mask2 * (gs[:, lane] + u * gg[:, lane]))
            ).astype(BF)
        return carry

    loop(d.frames, frame)
    acc_s = acc_q = 0.0
    for a, n in spans(d.rows, d.step):
        got = dot_t(r.ds3[a : a + n, :], r.we[...])
        s2 = r.s2[a : a + n, :]
        kept = (got.reshape(n // d.cells, d.cells, got.shape[1]) * mask2[None]).reshape(got.shape)
        kept = kept * slope_of(s2 * g2 + b2)
        r.d2[a : a + n, :] = kept
        acc_s = acc_s + fold8(kept)
        acc_q = acc_q + fold8(kept * ((s2 - m2) * r2))
    put(r.part, row, acc_s)
    put(r.part, row + 2, acc_q)


def slow_back2(r, d, gs, gg, tot_s2, tot_s1, row):
    inv_s, _ = invs(r)
    mask2 = wide(r.mask[...], d.cb)
    mean, rs = moments(tot_s2, 0, "s2", inv_s)
    factor = rs * gain(r, "s2")
    gs, gg = gs * inv_s, gg * inv_s
    m1, r1, g1, b1 = norm_of(r, tot_s1, 0, "s1", inv_s)

    def frame(t, carry):
        at = at_frame(t, d.cells)
        u = (r.s2[at, :] - mean) * rs
        v = (factor * (r.d2[at, :] - mask2 * (gs + u * gg))).astype(BF)
        r.ds2[at, :] = v
        put_windows(r.cols, at, v.astype(F32), d.side, True)
        return carry

    loop(d.frames, frame)
    acc_s = acc_q = 0.0
    for a, n in spans(d.rows, d.step):
        got = 0.0
        for k in range(9):
            lane = slice(k * d.cb, (k + 1) * d.cb)
            got = got + dot_t(r.cols[a : a + n, lane], r.wsp[lane, :])
        s1 = r.s1[a : a + n, :]
        kept = (got.reshape(n // d.cells, d.cells, got.shape[1]) * mask2[None]).reshape(got.shape)
        kept = kept * slope_of(s1 * g1 + b1)
        r.d1[a : a + n, :] = kept
        acc_s = acc_s + fold8(kept)
        acc_q = acc_q + fold8(kept * ((s1 - m1) * r1))
    put(r.part, row, acc_s)
    put(r.part, row + 2, acc_q)


def slow_back1(r, d, gs, gg, tot_s1, tot_lp, lp_row, row):
    inv_s, _ = invs(r)
    mask2 = wide(r.mask[...], d.cb)
    mean, rs = moments(tot_s1, 0, "s1", inv_s)
    factor = rs * gain(r, "s1")
    gs, gg = gs * inv_s, gg * inv_s
    ml, rl, gl, bl = norm_of(r, tot_lp, lp_row, "lp", inv_s)
    clear_ends(r.dpad, d.cells)

    def frame(t, carry):
        at = at_frame(t, d.cells)
        u = (r.s1[at, :] - mean) * rs
        r.dpad[at_frame(t, d.cells, d.cells), :] = (
            factor * (r.d1[at, :] - mask2 * (gs + u * gg))
        ).astype(BF)
        return carry

    loop(d.frames, frame)
    acc_s = acc_q = 0.0
    for a, n in spans(d.rows, d.step):
        got = slow_input_grad(r, d, a, n, d.cs, d.cs + d.cl)
        lp = r.lp[a : a + n, :]
        kept = (got.reshape(n // d.cells, d.cells, got.shape[1]) * mask2[None]).reshape(got.shape)
        kept = kept * slope_of(lp * gl + bl)
        r.dl[a : a + n, :] = kept
        acc_s = acc_s + fold8(kept)
        acc_q = acc_q + fold8(kept * ((lp - ml) * rl))
    put(r.part, row, acc_s)
    put(r.part, row + 2, acc_q)


def slow_input_grad(r, d, a, n, first, last):
    got = 0.0
    for k in range(3):
        b = a + (2 - k) * d.cells
        got = got + dot_t(r.dpad[b : b + n, :], r.wred[k, first:last, :])
    return got


def masked(x, mask, d):
    return (x.reshape(x.shape[0] // d.cells, d.cells, x.shape[1]) * mask[None]).reshape(x.shape)


def stage_e(d):
    def body(r):
        tot = jnp.sum(r.sync[...], axis=0)
        r.tot[...] = tot
        inv_s, _ = invs(r)
        mean, rs, sg, sb = norm_of(r, tot, 0, "s3", inv_s)
        mask2 = wide(r.mask[...], 256)

        def frame(t, carry):
            at = at_frame(t, d.cells)
            up = at_frame(t, d.cells, d.cells)
            sums = []
            for i, c in enumerate(range(0, d.cs, 256)):
                lane = slice(c, c + 256)
                s3 = r.s3[at, lane]
                z = r.spad[up, lane].astype(F32) + (s3 * sg[:, lane] + sb[:, lane])
                s = sigm(z)
                r.yout[t, :, lane] = (z * s * mask2).astype(BF)
                grad = r.cot[t, :, lane].astype(F32) * mask2 * (s * (1.0 + z * (1.0 - s)))
                r.dzs[at, lane] = grad
                u = (s3 - mean[:, lane]) * rs[:, lane]
                sums.append((carry[i][0] + fold8(grad), carry[i][1] + fold8(grad * u)))
            return tuple(sums)

        zero = jnp.zeros((8, 256), F32)
        done = loop(d.frames, frame, tuple((zero, zero) for c in range(0, d.cs, 256)))
        for i, c in enumerate(range(0, d.cs, 256)):
            put(r.part, c // LANES, done[i][0])
            put(r.part, (d.cs + c) // LANES, done[i][1])
        gs, gg = pair_of(tot, 16, "f3")
        fast_back3(r, d, gs, gg, r.tot_c[...], r.tot_b[...], 16)

    return body


def stage_f(d):
    def body(r):
        tot = jnp.sum(r.sync[...], axis=0)
        r.tot[...] = tot
        gs, gg = pair_of(tot, 0, "s3")
        slow_back3(r, d, gs, gg, r.tot_d[...], r.tot_c[...], 0)
        gs, gg = pair_of(tot, 16, "f2")
        fast_back2(r, d, gs, gg, r.tot_b[...], r.tot_a[...], 20, 4)

    return body


def stage_g(d):
    def body(r):
        tot = jnp.sum(r.sync[...], axis=0)
        r.tot[...] = tot
        gs, gg = pair_of(tot, 0, "s2")
        slow_back2(r, d, gs, gg, r.tot_c[...], r.tot_b[...], 0)

    return body


def stage_h(d):
    def body(r):
        tot = jnp.sum(r.sync[...], axis=0)
        r.tot[...] = tot
        inv_s, _ = invs(r)
        gs, gg = pair_of(tot, 0, "s1")
        slow_back1(r, d, gs, gg, r.tot_b[...], r.tot_a[...], 16, 16)
        mask2 = wide(r.mask[...], 256)
        r.par = r.par0
        mean, rs, sg, sb = norm_of(r, r.tot_a[...], 0, "s3", inv_s)
        for c in range(0, d.cs, 256):
            lane = slice(c, c + 256)
            acc_s = acc_q = 0.0
            for a, n in spans(d.rows, d.step):
                got = slow_input_grad(r, d, a, n, c, c + 256)
                got = masked(r.dzs[a : a + n, lane] + got, mask2, d).astype(BF).astype(F32)
                s3 = r.s3[a : a + n, lane]
                z = r.spad[a + d.cells : a + d.cells + n, lane].astype(F32) + (
                    s3 * sg[:, lane] + sb[:, lane]
                )
                grad = got * slope_of(z)
                r.dzs0[a : a + n, lane] = grad
                u = (s3 - mean[:, lane]) * rs[:, lane]
                acc_s = acc_s + fold8(grad)
                acc_q = acc_q + fold8(grad * u)
            put(r.part, c // LANES, acc_s)
            put(r.part, (d.cs + c) // LANES, acc_q)

    return body


def stage_i(d):
    def body(r):
        tot = jnp.sum(r.sync[...], axis=0)
        r.tot[...] = tot
        _, inv_f = invs(r)
        clear_ends(r.gpad, d.cells)
        gs, gg = pair_of(r.tot_f[...], 4, "f1")
        fast_back1(r, d, gs, gg, r.tot_a[...], 20)
        gs, gg = pair_of(tot, 16, "lp")
        lateral_back(r, d, gs, gg, r.tot_a[...], 16)
        r.par = r.par0
        mask = r.mask[...]
        mean, rs, fg, fb = norm_of(r, r.tot_c0[...], 4, "f3", inv_f)
        acc_s = acc_q = 0.0
        for a, n in spans(d.rows, d.step):
            pieces = fast_input_grad(r, d, a, n)
            for q in range(d.quad):
                lane = slice(q * d.cf, (q + 1) * d.cf)
                got = masked(r.dzf[a : a + n, lane] + pieces[q], mask, d).astype(BF).astype(F32)
                f3 = r.f3[a : a + n, lane]
                z = r.xpad[a + d.cells : a + d.cells + n, lane].astype(F32) + (f3 * fg + fb)
                grad = got * slope_of(z)
                r.dzf0[a : a + n, lane] = grad
                acc_s = acc_s + fold8(grad)
                acc_q = acc_q + fold8(grad * ((f3 - mean) * rs))
        put(r.part, 4, acc_s)
        put(r.part, 5, acc_q)
        gs, gg = pair_of(tot, 0, "s3")
        r.dzs = r.dzs0
        slow_back3(r, d, gs, gg, r.tot_a[...], r.tot_c0[...], 0)

    return body


def stage_j(d):
    def body(r):
        tot = jnp.sum(r.sync[...], axis=0)
        r.tot[...] = tot
        gs, gg = pair_of(tot, 0, "s2")
        slow_back2(r, d, gs, gg, r.tot_c[...], r.tot_b[...], 0)
        gs, gg = pair_of(tot, 4, "f3")
        fast_back3(r, d, gs, gg, r.tot_c[...], r.tot_b[...], 4)

    return body


def stage_k(d):
    def body(r):
        tot = jnp.sum(r.sync[...], axis=0)
        r.tot[...] = tot
        gs, gg = pair_of(tot, 0, "s1")
        slow_back1(r, d, gs, gg, r.tot_b[...], r.tot_a[...], 0, 0)
        gs, gg = pair_of(tot, 4, "f2")
        fast_back2(r, d, gs, gg, r.tot_b[...], r.tot_a[...], 4, 4)

    return body


def stage_slow_out(d):
    def body(r):
        mask2 = wide(r.mask[...], 256)
        for c in range(0, d.cs, 256):
            lane = slice(c, c + 256)
            for a, n in spans(d.rows, d.step):
                got = slow_input_grad(r, d, a, n, c, c + 256)
                got = masked(r.dzs[a : a + n, lane] + got, mask2, d).astype(BF)
                for t in range(n // d.cells):
                    r.out[a // d.cells + t, :, lane] = got[t * d.cells : (t + 1) * d.cells, :]

    return body


def stage_l(d):
    def body(r):
        tot = jnp.sum(r.sync[...], axis=0)
        r.tot[...] = tot
        clear_ends(r.gpad, d.cells)
        gs, gg = pair_of(tot, 4, "f1")
        fast_back1(r, d, gs, gg, r.tot_a[...], 4)
        gs, gg = pair_of(tot, 0, "lp")
        lateral_back(r, d, gs, gg, r.tot_a[...], 0)
        mask = r.mask[...]
        for a, n in spans(d.rows, d.step):
            pieces = fast_input_grad(r, d, a, n)
            for q in range(d.quad):
                lane = slice(q * d.cf, (q + 1) * d.cf)
                got = masked(r.dzf[a : a + n, lane] + pieces[q], mask, d).astype(BF)
                for t in range(n // d.cells):
                    r.out[a // d.cells + t, q] = got[t * d.cells : (t + 1) * d.cells, :]

    return body


def small_block(r, row, value):
    for half in range(2):
        for i in range(2):
            at = 64 * half + 32 * i
            r.halves[half, row : row + 32, i * LANES : (i + 1) * LANES] = value[
                at : at + 32, :
            ].astype(BF)


def hand_over(r):
    r.keep[...] = r.halves[r.ids[0]]
    r.send[...] = r.halves[1 - r.ids[0]]


def grads_es(d):
    part = d.cb // 2

    def body(r):
        def frame(t, carry):
            at = at_frame(t, d.cells)
            put_windows(r.cols, at, r.ds2[at, :].astype(F32), d.side, True)
            put_windows(r.colf, at, r.df2[at, :].astype(F32), d.side, True)
            return carry

        loop(d.frames, frame)
        row = 0
        turned = r.h2[...].T
        for c in range(0, d.cs, 256):
            got = dot(turned, r.ds3[:, c : c + 256]).astype(BF)
            for half in range(2):
                r.halves[half, row : row + part, :] = got[half * part : (half + 1) * part, :]
            row += part
        turned = r.h1[...].T
        for k in range(9):
            got = dot(turned, r.cols[:, k * d.cb : (k + 1) * d.cb]).astype(BF)
            for half in range(2):
                r.halves[half, row : row + part, :] = got[half * part : (half + 1) * part, :]
            row += part
        r.g2[...] = t_dot(r.k1[...], r.colf[...])
        r.g3[...] = t_dot(r.k2[...], r.df3[...])
        where = lane_group((d.fb, LANES), d.fb)
        for i in range(3):
            total = jnp.zeros((d.fb, LANES), F32)
            for c in range(3):
                for q in range(d.quad):
                    tap = (3 * i + c) * LANES
                    piece = r.g2[q * d.fb : (q + 1) * d.fb, tap : tap + LANES]
                    if c != q:
                        piece = pltpu.roll(piece, ((c - q) * d.fb) % LANES, 1)
                    total = total + jnp.where(where == c, piece, 0.0)
            r.block[i * d.fb : (i + 1) * d.fb, :] = total
        total = jnp.zeros((d.fb, LANES), F32)
        for q in range(d.quad):
            total = total + r.g3[q * d.fb : (q + 1) * d.fb, q * d.cf : (q + 1) * d.cf]
        r.block[3 * d.fb :, :] = total
        small_block(r, row, r.block[...])
        hand_over(r)

    return body


def grads_reduce(d):
    split = (d.cs + d.cl) // 2

    def body(r):
        for c in range(0, d.cs + d.cl, 256):
            if c < d.cs:
                source = r.spad[d.cells : d.cells + d.rows, c : c + 256]
            else:
                source = r.lapad[d.cells : d.cells + d.rows, c - d.cs : c - d.cs + 256]
            turned = source.T
            cut = min(max(split - c, 0), 256)
            for k in range(3):
                b = (2 - k) * d.cells
                got = dot(turned, r.dpad[b : b + d.rows, :]).astype(BF)
                if cut > 0:
                    row = k * split + c
                    r.halves[0, row : row + cut, :] = got[:cut, :]
                if cut < 256:
                    row = k * split + c + cut - split
                    r.halves[1, row : row + 256 - cut, :] = got[cut:, :]
        hand_over(r)

    return body


def grads_first(d):
    def body(r):
        c = d.cf
        grad = r.gpad[d.cells : d.cells + d.rows, :]
        r.ga[0 : 2 * c, :] = t_dot(r.xpad[0 : d.rows, 2 * c : 4 * c], grad)
        r.ga[2 * c : 6 * c, :] = t_dot(r.xpad[d.cells : d.cells + d.rows, :], grad)
        r.ga[6 * c :, :] = t_dot(r.xpad[2 * d.cells : 2 * d.cells + d.rows, 0:c], grad)
        row = 0
        for b in range(d.taps):
            for half in range(2):
                at = b * c + half * (c // 2)
                r.halves[half, row : row + c // 2, :] = r.ga[at : at + c // 2, : d.cl].astype(BF)
            row += c // 2
        where = lane_group((c, LANES), d.fb)
        total = jnp.zeros((c, LANES), F32)
        for k in range(3):
            for q in range(d.quad):
                at = (q + k + 1) * c
                piece = r.ga[at : at + c, d.cl :]
                if k != q:
                    piece = pltpu.roll(piece, ((k - q) * d.fb) % LANES, 1)
                total = total + jnp.where(where == k, piece, 0.0)
        small_block(r, row, total)
        hand_over(r)

    return body


def gather_pieces(r, count):
    row = 0
    for i in range(count):
        keep, got = getattr(r, "keep_%d" % i), getattr(r, "got_%d" % i)
        r.mine[row : row + keep.shape[0], :] = (
            keep[...].astype(F32) + got[...].astype(F32)
        ).astype(BF)
        row += keep.shape[0]
    if row < r.mine.shape[0]:
        r.mine[row:, :] = jnp.zeros((r.mine.shape[0] - row, r.mine.shape[1]), BF)


def split_near(count):
    def body(r):
        gather_pieces(r, count)
        hand_shares(r, r.mine, r.ids[2])

    return body


def hand_shares(r, source, place):
    k = 0
    while hasattr(r, "to_%d" % k):
        target = getattr(r, "to_%d" % k)
        rows = target.shape[0]
        start = pl.multiple_of((place ^ k) * rows, 16)
        target[...] = source[pl.ds(start, rows), :]
        k += 1


def add_shares(r):
    total = r.from_0[...].astype(F32)
    k = 1
    while hasattr(r, "from_%d" % k):
        total = total + getattr(r, "from_%d" % k)[...].astype(F32)
        k += 1
    return total.astype(BF)


def sum_shares(r):
    r.out[...] = add_shares(r)


def halve(r, bit):
    rows = r.keep.shape[0]
    mine = jnp.where((r.ids[3] & bit) > 0, 1, 0)
    r.keep[...] = r.mine[pl.ds(pl.multiple_of(mine * rows, 16), rows), :]
    r.send[...] = r.mine[pl.ds(pl.multiple_of((1 - mine) * rows, 16), rows), :]


def split_far(bit):
    def body(r):
        rows = r.early.shape[0]
        r.mine[0:rows, :] = r.early[...]
        r.mine[rows:, :] = add_shares(r)
        halve(r, bit)

    return body


def next_far(bit):
    def body(r):
        total = (r.own[...].astype(F32) + r.got[...].astype(F32)).astype(BF)
        if bit:
            r.mine[...] = total
            halve(r, bit)
        else:
            r.keep[...] = total

    return body


def join_far(bit):
    def body(r):
        rows = r.own.shape[0]
        mine = jnp.where((r.ids[3] & bit) > 0, 1, 0)
        r.out[pl.ds(pl.multiple_of(mine * rows, 16), rows), :] = r.own[...]
        r.out[pl.ds(pl.multiple_of((1 - mine) * rows, 16), rows), :] = r.got[...]

    return body


def collect_near(r):
    k = 0
    while hasattr(r, "from_%d" % k):
        source = getattr(r, "from_%d" % k)
        place = r.ids[2] ^ k
        cut = 0
        for out in (r.es, r.red):
            rows = out.shape[0] // r.count.shape[0]
            start = pl.multiple_of(place * rows, 16)
            out[pl.ds(start, rows), :] = source[cut : cut + rows, :]
            cut += rows
        k += 1


def add_up(r):
    total = jnp.zeros(r.got.shape[1:], F32)
    for i in range(r.got.shape[0]):
        total = total + r.got[i].astype(F32)
    total = total.astype(BF)
    if len(r.out.shape) == len(total.shape):
        r.out[...] = total
    else:
        for i in range(r.out.shape[0]):
            r.out[i] = total


def spread_out(r):
    for i in range(r.out.shape[0]):
        r.out[i] = r.got[...]


def half_of(r, half, at_0, at_1, rows, lanes=slice(None), kind="1"):
    if half == 0:
        here, there = r.own_0, getattr(r, "got_" + kind)
    else:
        here, there = r.got_0, getattr(r, "own_" + kind)
    return jnp.where(
        r.ids[0] == 0,
        here[at_0 : at_0 + rows, lanes].astype(F32),
        there[at_1 : at_1 + rows, lanes].astype(F32),
    )


def small_rows(r, at_0, at_1, kind="1"):
    for half in range(2):
        for i in range(2):
            at = 64 * half + 32 * i
            r.block[at : at + 32, :] = half_of(
                r, half, at_0, at_1, 32, slice(i * LANES, (i + 1) * LANES), kind
            )


def finish_main(d, at_es, at_red):
    part = d.cb // 2
    split = (d.cs + d.cl) // 2

    def body(r):
        copies = []
        a, b = at_red
        for k in range(3):
            for half in range(2):
                r.reduce[k, half * split : (half + 1) * split, :] = half_of(r, half, a, b, split, kind="red")
            a, b = a + split, b + split
            copies.append(pltpu.make_async_copy(r.reduce.at[k], r.hbm_reduce.at[0, k], r.sems.at[k]))
            copies[-1].start()
        a, b = at_es
        for c in range(0, d.cs, 256):
            for half in range(2):
                r.expand[half * part : (half + 1) * part, c : c + 256] = half_of(r, half, a, b, part, kind="es")
            a, b = a + part, b + part
        copies.append(pltpu.make_async_copy(r.expand, r.hbm_expand.at[0], r.sems.at[3]))
        copies[-1].start()
        for k in range(9):
            for half in range(2):
                r.space[k, half * part : (half + 1) * part, :] = half_of(r, half, a, b, part, kind="es")
            a, b = a + part, b + part
        copies.append(pltpu.make_async_copy(r.space, r.hbm_space.at[0], r.sems.at[4]))
        copies[-1].start()
        small_rows(r, a, b, "es")
        for i in range(3):
            piece = r.block[i * d.fb : (i + 1) * d.fb, :]
            for c in range(3):
                moved = piece if c == 0 else pltpu.roll(piece, LANES - c * d.fb, 1)
                r.fspace[0, 3 * i + c] = moved[:, : d.fb]
        r.fexpand[0] = r.block[3 * d.fb :, :]
        for copy in copies:
            copy.wait()

    return body


def finish_first(d, at_first):
    part = d.cf // 2

    def body(r):
        a, b = at_first
        for tap in range(d.taps):
            for half in range(2):
                r.lateral[0, tap, half * part : (half + 1) * part, :] = half_of(r, half, a, b, part)
            a, b = a + part, b + part
        small_rows(r, a, b)
        turned = r.block[...].T
        for k in range(3):
            r.freduce[0, k] = turned[k * d.fb : (k + 1) * d.fb, :]

    return body


def norms_out(d, at):
    def body(r):
        made = []
        for layer in range(2):
            lines = []
            for which in (1, 0):
                pieces = []
                for key in ("s1", "s2", "s3", "f1", "f2", "f3", "lp"):
                    name, row = at[layer][key]
                    tot = getattr(r, name)[...]
                    count = SPAN[key][1]
                    if key in ("f1", "f2"):
                        tot = folded(tot, d.fb)
                    piece = lanes_of(tot, row + which * count, count)
                    pieces.append(piece[:, : d.fb] if key in ("f1", "f2") else piece)
                lines.append(jnp.concatenate(pieces, axis=1))
            made.append(lines)
        for i in range(2):
            r.keep[i : i + 1, :] = jnp.where(r.ids[0] == 0, made[0][i], made[1][i])
            r.send[i : i + 1, :] = jnp.where(r.ids[0] == 0, made[1][i], made[0][i])

    return body


def norms_add(r):
    total = r.keep[...] + r.got[...]
    r.gain[...] = total[0:1, :]
    r.shift[...] = total[1:2, :]


def on_device(
    edge_slow,
    edge_fast,
    slow_reduce,
    slow_spatial,
    slow_expand,
    fast_reduce,
    fast_spatial,
    fast_expand,
    lateral,
    norm_gain,
    norm_shift,
    present,
    crop_side,
):
    micro, _, frames, side, _, cs = edge_slow.shape[1:]
    cells = side * side
    fast_frames = edge_fast.shape[3]
    quad = fast_frames // frames
    d = SimpleNamespace(
        frames=frames,
        side=side,
        cells=cells,
        rows=frames * cells,
        step=min(256, frames * cells),
        quad=quad,
        cs=cs,
        cb=slow_expand.shape[1],
        cf=edge_fast.shape[-1],
        fb=fast_expand.shape[1],
        cl=lateral.shape[3],
    )
    d.taps = lateral.shape[1]
    d.groups = lax.axis_size("dp")
    groups = d.groups
    rows, pads = d.rows, d.rows + 2 * cells
    swap = [(0, 1), (1, 0)]
    own_slow = edge_slow.reshape(micro, frames, cells, cs)
    own_fast = edge_fast.reshape(micro, frames, quad, cells, d.cf)

    def across(value, pairs=swap):
        return lax.ppermute(value, "pipe", pairs)

    inner = 1
    while 4 * inner * inner <= groups:
        inner *= 2
    outer = groups // inner
    group = lax.axis_index("dp")
    ids = jnp.stack([lax.axis_index("pipe"), group, group % inner, group // inner]).astype(jnp.int32)
    lat_own, fr_own = lateral[0], jnp.swapaxes(fast_reduce[0], 1, 2)
    other_fast, lat_other, fr_other = across(own_fast), across(lat_own), across(fr_own)
    (
        own_slow,
        red_own,
        fs_own,
        fe_own,
        norm_gain,
        norm_shift,
        sp_own,
        ex_own,
        other_fast,
        lat_other,
        fr_other,
    ) = lax.optimization_barrier(
        (
            own_slow,
            slow_reduce[0],
            fast_spatial.reshape(9, d.fb, d.fb),
            fast_expand[0],
            norm_gain,
            norm_shift,
            slow_spatial.reshape(9 * d.cb, d.cb),
            slow_expand[0],
            other_fast,
            lat_other,
            fr_other,
        )
    )
    other_slow = across(lax.dynamic_index_in_dim(own_slow, 1 - lax.axis_index("pipe"), 0, keepdims=False))
    red_other = across(red_own)
    fs_other, fe_other = across(fs_own), across(fe_own)
    gain_other, shift_other = across(norm_gain), across(norm_shift)
    sems = pltpu.SemaphoreType.DMA

    def stage(*args, **others):
        return run(*args, groups=groups, **others)

    def exchange(part):
        return lax.all_to_all(part, "dp", 0, 0)

    slow_f = ((rows, cs), F32)
    mid_f = ((rows, d.cb), F32)
    fast_f = ((rows, quad * d.cf), F32)
    tiny_f = ((rows, quad * d.fb), F32)
    mid_b = ((rows, d.cb), BF)
    tiny_b = ((rows, quad * d.fb), BF)
    fast_b = ((rows, quad * d.cf), BF)
    small = ((8, LANES), F32)
    large = ((24, LANES), F32)
    xpad_s = ((pads, quad * d.cf), BF)
    spad_s = ((pads, cs), BF)
    mpad_s = ((pads, d.cb), BF)
    gpad_s = ((pads, d.cl + quad * d.fb), BF)
    cols_s = {"cols": ((rows, 9 * d.cb), BF)}
    colf_s = {"colf": ((rows, 9 * quad * d.fb), BF)}
    wa_s = (((quad + 3) * d.cf, d.cl + quad * d.fb), BF)

    out_fast = ((frames, quad, cells, d.cf), BF)
    out_slow = ((frames, cells, cs), BF)
    a0 = stage(
        stage_first(d),
        "stage_a0",
        dict(
            ids=ids,
            present=present,
            crop=crop_side,
            hbm_own=own_fast,
            hbm_other=other_fast,
            hbm_lat_own=lat_own,
            hbm_lat_other=lat_other,
            hbm_fr_own=fr_own,
            hbm_fr_other=fr_other,
        ),
        dict(
            mask=((cells, LANES), F32),
            inv=small,
            wa=wa_s,
            wa1=wa_s,
            xpad=xpad_s,
            cot=out_fast,
            lp=mid_f,
            f1=tiny_f,
            part=small,
        ),
        dict(
            own=out_fast,
            other=out_fast,
            lat_own=(lat_own.shape, BF),
            lat_other=(lat_own.shape, BF),
            fr_own=(fr_own.shape, BF),
            fr_other=(fr_own.shape, BF),
            loads=sems((6,)),
        ),
    )
    mask = a0.mask
    base = dict(mask=mask, inv=a0.inv)
    wa = (a0.wa, a0.wa1)
    rows_es = (cs // 256 + 9) * (d.cb // 2) + 32
    rows_red = 3 * (cs + d.cl) // 2
    rows_first = d.taps * (d.cf // 2) + 32

    def halves_of(body, name, rows_now, ins, scratch, hold):
        made = run(
            body,
            name,
            dict(ids=ids, **ins),
            dict(keep=((rows_now, 256), BF), send=((rows_now, 256), BF)),
            dict(scratch, halves=((2, rows_now, 256), BF)),
            hold=hold,
        )
        return made.keep, across(made.send)

    def halves_es(name, hold, **ins):
        scratch = dict(
            cols_s,
            **colf_s,
            g2=((quad * d.fb, 9 * quad * d.fb), F32),
            g3=((quad * d.fb, quad * d.cf), F32),
            block=((LANES, LANES), F32),
        )
        return halves_of(grads_es(d), "grads_es" + name, rows_es, ins, scratch, hold)

    def halves_red(name, hold, **ins):
        return halves_of(grads_reduce(d), "grads_red" + name, rows_red, ins, {}, hold)

    def halves_first(name, hold, **ins):
        scratch = dict(ga=(((quad + 3) * d.cf, d.cl + quad * d.fb), F32))
        return halves_of(grads_first(d), "grads_first" + name, rows_first, ins, scratch, hold)

    def padded(count):
        unit = 16 * groups
        return -(-count // unit) * unit

    es_all, red_all = padded(rows_es), padded(rows_red)
    near_1 = (es_all + red_all) // inner

    def shares(count, rows_now):
        return {"to_%d" % k: ((rows_now, 256), BF) for k in range(count)}

    def sent_near(made):
        pairs = lambda k: [(i, i ^ k) for i in range(groups)]
        return {
            "from_%d" % k: made[k] if k == 0 else lax.ppermute(made[k], "dp", pairs(k))
            for k in range(inner)
        }

    bits = []
    while (1 << len(bits)) < outer:
        bits.insert(0, 1 << len(bits))

    def over(value, bit):
        return lax.ppermute(value, "dp", [(i, i ^ (bit * inner)) for i in range(groups)])

    def targets(made, count):
        return [getattr(made, "to_%d" % k) for k in range(count)]

    def pieces_of(*pieces):
        return {
            "%s_%d" % (key, i): value
            for i, piece in enumerate(pieces)
            for key, value in zip(("keep", "got"), piece)
        }

    arrived = (other_slow, red_other, fs_other, fe_other, gain_other, shift_other)
    part = run(gate, "gate", dict(part=a0.part), dict(out=(a0.part.shape, F32)), far_hold=arrived).out
    sync = exchange(part)
    sp_own, ex_own, sync = lax.optimization_barrier((sp_own, ex_own, sync))
    sp_other, ex_other = across(sp_own), across(ex_own)
    packed_2 = ((9 * quad * d.fb, quad * d.fb), BF)
    packed_3 = ((quad * d.fb, quad * d.cf), BF)
    norm_s = ((2 * SHIFT_ROW, LANES), F32)
    red_s = (red_own.shape, BF)
    slow_in = pack = stage(
        stage_slow_in(d),
        "stage_slow_in",
        dict(
            ids=ids,
            mask=mask,
            hbm_own=own_slow,
            hbm_other=other_slow,
            hbm_red_own=red_own,
            hbm_red_other=red_other,
            hbm_fs_own=fs_own,
            hbm_fs_other=fs_other,
            hbm_fe_own=fe_own,
            hbm_fe_other=fe_other,
            hbm_gain_own=norm_gain,
            hbm_gain_other=gain_other,
            hbm_shift_own=norm_shift,
            hbm_shift_other=shift_other,
        ),
        dict(
            spad=spad_s,
            cot=out_slow,
            y=mid_f,
            wred_0=red_s,
            wred_1=red_s,
            w2_0=packed_2,
            w2_1=packed_2,
            w2t_0=packed_2,
            w2t_1=packed_2,
            w3_0=packed_3,
            w3_1=packed_3,
            par_0=norm_s,
            par_1=norm_s,
        ),
        dict(
            own=out_slow,
            other=out_slow,
            fs_own=(fs_own.shape, BF),
            fs_other=(fs_own.shape, BF),
            fe_own=(fe_own.shape, BF),
            fe_other=(fe_own.shape, BF),
            gain_own=(norm_gain.shape, F32),
            gain_other=(norm_gain.shape, F32),
            shift_own=(norm_gain.shape, F32),
            shift_other=(norm_gain.shape, F32),
            loads=sems((10,)),
            sems=sems((2,)),
        ),
        hold=(sync,),
    )
    wred = (slow_in.wred_0, slow_in.wred_1)
    w2, w2t = (pack.w2_0, pack.w2_1), (pack.w2t_0, pack.w2t_1)
    w3, par = (pack.w3_0, pack.w3_1), (pack.par_0, pack.par_1)

    def common(layer):
        return dict(base, par=par[layer])

    b0 = stage(
        stage_second(d, 0, False),
        "stage_b0",
        dict(
            common(0),
            ids=ids,
            sync=sync,
            lp=a0.lp,
            f1=a0.f1,
            y=slow_in.y,
            wred=wred[0],
            w2=w2[0],
        ),
        dict(
            lapad=mpad_s,
            k1=tiny_b,
            s1=mid_f,
            f2=tiny_f,
            tot=small,
            part=small,
        ),
        colf_s,
        far_hold=(sp_other, ex_other),
    )
    sync = exchange(b0.part)
    c0 = stage(
        stage_third(d, True),
        "stage_c0",
        dict(
            common(0),
            ids=ids,
            sync=sync,
            s1=b0.s1,
            f2=b0.f2,
            w3=w3[0],
            hbm_sp_own=sp_own,
            hbm_sp_other=sp_other,
            hbm_ex_own=ex_own,
            hbm_ex_other=ex_other,
        ),
        dict(
            h1=mid_b,
            k2=tiny_b,
            s2=mid_f,
            f3=fast_f,
            tot=small,
            wsp_0=(sp_own.shape, BF),
            wsp_1=(sp_own.shape, BF),
            we_0=(ex_own.shape, BF),
            we_1=(ex_own.shape, BF),
            part=small,
        ),
        dict(cols_s, sems=sems((4,))),
    )
    sync = exchange(c0.part)
    we, wsp = (c0.we_0, c0.we_1), (c0.wsp_0, c0.wsp_1)
    d0 = stage(
        stage_fourth(d, False),
        "stage_d0",
        dict(common(0), sync=sync, s2=c0.s2, f3=c0.f3, we=we[0], xpad=a0.xpad, wa=wa[1]),
        dict(h2=mid_b, s3=slow_f, ypad=xpad_s, lp=mid_f, f1=tiny_f, tot=small, part=large),
    )
    sync = exchange(d0.part)
    b1 = stage(
        stage_second(d, 16, True),
        "stage_b1",
        dict(
            base,
            par=par[1],
            par0=par[0],
            sync=sync,
            lp=d0.lp,
            f1=d0.f1,
            s3=d0.s3,
            xpad=slow_in.spad,
            wred=wred[1],
            w2=w2[1],
        ),
        dict(spad=spad_s, lapad=mpad_s, k1=tiny_b, s1=mid_f, f2=tiny_f, tot=large, part=small),
        colf_s,
    )
    sync = exchange(b1.part)
    c1 = stage(
        stage_third(d, False),
        "stage_c1",
        dict(common(1), sync=sync, s1=b1.s1, f2=b1.f2, wsp=wsp[1], w3=w3[1]),
        dict(h1=mid_b, k2=tiny_b, s2=mid_f, f3=fast_f, tot=small, part=small),
        cols_s,
    )
    sync = exchange(c1.part)
    d1 = stage(
        stage_fourth(d, True),
        "stage_d1",
        dict(
            common(1),
            sync=sync,
            s2=c1.s2,
            f3=c1.f3,
            we=we[1],
            xpad=d0.ypad,
            cot=a0.cot,
        ),
        dict(h2=mid_b, s3=slow_f, yout=out_fast, dzf=fast_f, tot=small, part=large),
    )
    sync = exchange(d1.part)
    e1 = stage(
        stage_e(d),
        "stage_e1",
        dict(
            common(1),
            sync=sync,
            s3=d1.s3,
            spad=b1.spad,
            cot=slow_in.cot,
            f3=c1.f3,
            dzf=d1.dzf,
            f2=b1.f2,
            w3=w3[1],
            tot_c=d1.tot,
            tot_b=c1.tot,
        ),
        dict(yout=out_slow, dzs=slow_f, df3=fast_b, d2f=tiny_f, tot=large, part=large),
    )
    sync = exchange(e1.part)
    f1 = stage(
        stage_f(d),
        "stage_f1",
        dict(
            common(1),
            sync=sync,
            s3=d1.s3,
            dzs=e1.dzs,
            s2=c1.s2,
            we=we[1],
            d2f=e1.d2f,
            f2=b1.f2,
            f1=d0.f1,
            w2t=w2t[1],
            tot_d=e1.tot,
            tot_c=d1.tot,
            tot_b=c1.tot,
            tot_a=b1.tot,
        ),
        dict(ds3=((rows, cs), BF), d2=mid_f, df2=tiny_b, d1f=tiny_f, tot=large, part=small),
        colf_s,
    )
    sync = exchange(f1.part)
    g1 = stage(
        stage_g(d),
        "stage_g1",
        dict(
            common(1), sync=sync, d2=f1.d2, s2=c1.s2, s1=b1.s1, wsp=wsp[1], tot_c=d1.tot, tot_b=c1.tot
        ),
        dict(ds2=mid_b, d1=mid_f, tot=small, part=small),
        cols_s,
    )
    sync = exchange(g1.part)
    es1 = halves_es(
        "1",
        (sync,),
        h2=d1.h2,
        k2=c1.k2,
        ds3=f1.ds3,
        df3=e1.df3,
        h1=c1.h1,
        k1=b1.k1,
        ds2=g1.ds2,
        df2=f1.df2,
    )
    h1 = stage(
        stage_h(d),
        "stage_h1",
        dict(
            base,
            par=par[1],
            par0=par[0],
            sync=sync,
            d1=g1.d1,
            s1=b1.s1,
            lp=d0.lp,
            wred=wred[1],
            dzs=e1.dzs,
            s3=d0.s3,
            spad=slow_in.spad,
            tot_b=c1.tot,
            tot_a=b1.tot,
        ),
        dict(dpad=mpad_s, dl=mid_f, dzs0=slow_f, tot=small, part=large),
        hold=(es1[0],),
    )
    sync = exchange(h1.part)
    red1 = halves_red("1", (sync,), spad=b1.spad, lapad=b1.lapad, dpad=h1.dpad)
    es_near = run(
        split_near(1),
        "es1_near",
        dict(ids=ids, **pieces_of(es1)),
        shares(inner, es_all // inner),
        dict(mine=((es_all, 256), BF)),
        hold=(sync,),
    )
    i0 = stage(
        stage_i(d),
        "stage_i0",
        dict(
            base,
            par=par[1],
            par0=par[0],
            sync=sync,
            lp=d0.lp,
            f1=d0.f1,
            d1f=f1.d1f,
            dl=h1.dl,
            wa=wa[1],
            dzf=d1.dzf,
            f3=c0.f3,
            xpad=a0.xpad,
            dzs0=h1.dzs0,
            s3=d0.s3,
            s2=c0.s2,
            we=we[0],
            tot_f=g1.tot,
            tot_a=b1.tot,
            tot_c0=d0.tot,
        ),
        dict(gpad=gpad_s, dzf0=fast_f, ds3=((rows, cs), BF), d2=mid_f, tot=large, part=small),
        hold=(red1[0], es_near.to_0),
    )
    sync = exchange(i0.part)
    red_near = run(
        split_near(1),
        "red1_near",
        dict(ids=ids, **pieces_of(red1)),
        shares(inner, red_all // inner),
        dict(mine=((red_all, 256), BF)),
        hold=(sync,),
    )
    es_sum = run(
        sum_shares,
        "es1_sum",
        sent_near(targets(es_near, inner)),
        dict(out=((es_all // inner, 256), BF)),
        hold=(sync,),
    ).out
    first1 = halves_first("1", (es_sum, red_near.to_0), xpad=d0.ypad, gpad=i0.gpad)
    j0 = stage(
        stage_j(d),
        "stage_j0",
        dict(
            common(0),
            sync=sync,
            d2=i0.d2,
            s2=c0.s2,
            s1=b0.s1,
            wsp=wsp[0],
            dzf=i0.dzf0,
            f3=c0.f3,
            f2=b0.f2,
            w3=w3[0],
            tot_c=d0.tot,
            tot_b=c0.tot,
        ),
        dict(ds2=mid_b, d1=mid_f, df3=fast_b, d2f=tiny_f, tot=small, part=small),
        cols_s,
        hold=(first1[0], red_near.to_0, es_sum),
    )
    sync = exchange(j0.part)
    sum_far = run(
        split_far(bits[0]),
        "sum1_far",
        dict(ids=ids, early=es_sum, **sent_near(targets(red_near, inner))),
        dict(keep=((near_1 // 2, 256), BF), send=((near_1 // 2, 256), BF)),
        dict(mine=((near_1, 256), BF)),
        hold=(sync,),
    )
    k0 = stage(
        stage_k(d),
        "stage_k0",
        dict(
            common(0),
            sync=sync,
            d1=j0.d1,
            s1=b0.s1,
            lp=a0.lp,
            wred=wred[0],
            d2f=j0.d2f,
            f2=b0.f2,
            f1=a0.f1,
            w2t=w2t[0],
            tot_b=c0.tot,
            tot_a=b0.tot,
        ),
        dict(dpad=mpad_s, dl=mid_f, df2=tiny_b, d1f=tiny_f, tot=small, part=small),
        colf_s,
        hold=(sum_far.keep,),
    )
    sync = exchange(k0.part)
    for i, bit in enumerate(bits):
        after = bits[i + 1] if i + 1 < len(bits) else 0
        extent = sum_far.keep.shape[0] // (2 if after else 1)
        outs = dict(keep=((extent, 256), BF))
        if after:
            outs.update(send=((extent, 256), BF))
        sum_far = run(
            next_far(after),
            "sum1_far_%d" % bit,
            dict(ids=ids, own=sum_far.keep, got=over(sum_far.send, bit)),
            outs,
            dict(mine=(sum_far.keep.shape, BF)),
            hold=(sync,),
        )
        if i == 0:
            far_sum1 = sum_far.keep
    all_far = [sum_far.keep]
    for bit in reversed(bits):
        own = all_far[-1]
        all_far.append(
            run(
                join_far(bit),
                "all1_far_%d" % bit,
                dict(ids=ids, own=own, got=over(own, bit)),
                dict(out=((2 * own.shape[0], 256), BF)),
            ).out
        )
    far_all1 = all_far[-1]
    es0 = halves_es(
        "0",
        (far_sum1,),
        h2=d0.h2,
        k2=c0.k2,
        ds3=i0.ds3,
        df3=j0.df3,
        h1=c0.h1,
        k1=b0.k1,
        ds2=j0.ds2,
        df2=k0.df2,
    )
    red0 = halves_red("0", (far_sum1,), spad=slow_in.spad, lapad=b0.lapad, dpad=k0.dpad)
    l0 = stage(
        stage_l(d),
        "stage_l0",
        dict(
            common(0),
            sync=sync,
            lp=a0.lp,
            f1=a0.f1,
            d1f=k0.d1f,
            dl=k0.dl,
            wa=wa[0],
            dzf=i0.dzf0,
            tot_a=b0.tot,
        ),
        dict(gpad=gpad_s, out=out_fast, tot=small),
        hold=(es0[0], red0[0], far_sum1),
    )
    slow_out = stage(
        stage_slow_out(d),
        "stage_slow_out",
        dict(mask=mask, dpad=k0.dpad, wred=wred[0], dzs=h1.dzs0),
        dict(out=out_slow),
    )

    first0 = halves_first("0", (), xpad=a0.xpad, gpad=l0.gpad)
    all1 = run(
        collect_near,
        "sum1_collect_near",
        dict(ids=ids, **sent_near([far_all1] * inner)),
        dict(es=((es_all, 256), BF), red=((red_all, 256), BF)),
        dict(count=((inner, LANES), F32)),
    )
    to_first, to_second = [(1, 0)], [(0, 1)]
    at_1 = dict(
        s1=("h1", 0), s2=("g1", 0), s3=("f1", 0), f1=("g1", 4), f2=("f1", 16), f3=("e1", 16), lp=("i0", 16)
    )
    at_0 = dict(
        s1=("k0", 0), s2=("j0", 0), s3=("i0", 0), f1=("l0", 4), f2=("k0", 4), f3=("j0", 4), lp=("l0", 0)
    )
    norms = run(
        norms_out(d, (at_0, at_1)),
        "norms_out",
        dict(
            ids=ids,
            e1=e1.tot,
            f1=f1.tot,
            g1=g1.tot,
            h1=h1.tot,
            i0=i0.tot,
            j0=j0.tot,
            k0=k0.tot,
            l0=l0.tot,
        ),
        dict(keep=((2, norm_gain.shape[1]), F32), send=((2, norm_gain.shape[1]), F32)),
    )
    norms = run(
        norms_add,
        "norms_add",
        dict(keep=norms.keep, got=across(norms.send)),
        dict(gain=(norm_gain.shape, F32), shift=(norm_shift.shape, F32)),
    )

    def placed(name, grad_now, value_now):
        whole = (micro,) + grad_now.shape
        return run(
            stage_place,
            "place_" + name,
            dict(
                ids=ids,
                grad=grad_now,
                grad_got=across(grad_now, to_first),
                value=value_now,
                value_got=across(value_now, to_second),
            ),
            dict(hbm_out=(whole, BF)),
            dict(both=(whole, BF), sems=sems((2,))),
        ).hbm_out

    placed_slow = placed("slow", slow_out.out, e1.yout)
    placed_fast = placed("fast", l0.out, d1.yout)

    near = [[b * inner + i for i in range(inner)] for b in range(outer)]
    far = [[b * inner + i for b in range(outer)] for i in range(inner)]

    def turn(x, where):
        return lax.all_to_all(x, "dp", 0, 0, axis_index_groups=where)

    rows_0 = padded(rows_es + rows_red + 2 * rows_first)
    near_0 = rows_0 // inner
    far_0 = near_0 // outer

    def gather_0(r):
        gather_pieces(r, 4)

    got = run(
        gather_0,
        "sum0_gather",
        pieces_of(es0, red0, first0, first1),
        dict(mine=((rows_0, 256), BF)),
        hold=(all_far[-2],),
    ).mine
    got = turn(got.reshape(inner, near_0, 256), near)
    got = run(
        add_up, "sum0_near", dict(got=got), dict(out=((near_0, 256), BF)), hold=(far_all1,)
    ).out
    got = turn(got.reshape(outer, far_0, 256), far)
    got = run(add_up, "sum0_far", dict(got=got), dict(out=((outer, far_0, 256), BF))).out
    got = turn(got, far).reshape(near_0, 256)
    got = run(
        spread_out,
        "sum0_spread",
        dict(got=got),
        dict(out=((inner, near_0, 256), BF)),
        hold=(all1.es, placed_slow, placed_fast, norms.gain),
    ).out
    all0 = turn(got, near).reshape(rows_0, 256)

    got0, got0s = across(all0, to_first), across(all0, to_second)
    got_es, got_red = across(all1.es, to_second), across(all1.red, to_second)
    done = run(
        finish_main(d, (0, 0), (rows_es, 0)),
        "finish_main",
        dict(
            ids=ids,
            own_0=all0,
            got_0=got0,
            own_es=all1.es,
            got_es=got_es,
            own_red=all1.red,
            got_red=got_red,
        ),
        dict(
            hbm_reduce=(slow_reduce.shape, F32),
            hbm_expand=(slow_expand.shape, F32),
            hbm_space=((1, 9, d.cb, d.cb), F32),
            fspace=((1, 9, d.fb, d.fb), F32),
            fexpand=(fast_expand.shape, F32),
        ),
        dict(
            reduce=((3, cs + d.cl, d.cb), F32),
            expand=((d.cb, cs), F32),
            space=((9, d.cb, d.cb), F32),
            block=((LANES, LANES), F32),
            sems=sems((5,)),
        ),
    )
    at_first = rows_es + rows_red
    done_first = run(
        finish_first(d, (at_first, at_first + rows_first)),
        "finish_first",
        dict(ids=ids, own_0=all0, got_0=got0, own_1=all0, got_1=got0s),
        dict(lateral=(lateral.shape, F32), freduce=((1, 3, d.fb, d.cf), F32)),
        dict(block=((LANES, LANES), F32)),
    )
    weights = (
        done.hbm_reduce,
        done.hbm_space.reshape(slow_spatial.shape),
        done.hbm_expand,
        jnp.swapaxes(done_first.freduce, 2, 3),
        done.fspace.reshape(fast_spatial.shape),
        done.fexpand,
        done_first.lateral,
    )

    return (
        placed_slow.reshape(edge_slow.shape),
        placed_fast.reshape(edge_fast.shape),
        *weights,
        norms.gain,
        norms.shift,
    )


def solution(mesh):
    edge = P("pipe", None, "dp", None, None, None, None)
    weights = (
        P("pipe", None, None, None),
        P("pipe", None, None, None, None),
        P("pipe", None, None),
        P("pipe", None, None, None),
        P("pipe", None, None, None, None),
        P("pipe", None, None),
        P("pipe", None, None, None),
    )
    norms = (P("pipe", None), P("pipe", None))
    return jax.shard_map(
        on_device,
        mesh=mesh,
        in_specs=(edge, edge, *weights, *norms, P(), P()),
        out_specs=(edge, edge, *weights, *norms),
        check_vma=False,
    )
```

```python
from types import SimpleNamespace

import jax
import jax.numpy as jnp
from jax import lax
from jax.experimental import pallas as pl
from jax.experimental.pallas import tpu as pltpu
from jax.sharding import PartitionSpec as P

epsilon = 1e-05
F32 = jnp.float32
BF = jnp.bfloat16
LANES = 128
SPAN = {
    "s1": (0, 2),
    "s2": (2, 2),
    "s3": (4, 8),
    "f1": (12, 1),
    "f2": (13, 1),
    "f3": (14, 1),
    "lp": (15, 2),
}
SHIFT_ROW = 24
TIMES = {
    "grads_es": 2.4,
    "stage_l": 1.8,
    "grads_first": 1.3,
    "stage_slow_out": 1.8,
    "r_split": 1.1,
    "b_split": 1.1,
    "place_fast": 1.7,
    "place_slow": 2.1,
    "finish_reduce": 2.6,
    "finish_rest": 3.4,
}
WEIGHT = 0.0


SMEM_KEYS = ("ids", "present", "crop")


def space_of(key):
    if key in SMEM_KEYS:
        return pltpu.SMEM
    if key.startswith("hbm_"):
        return pltpu.HBM
    if key.startswith("any_"):
        return pl.ANY
    return pltpu.VMEM


def run(body, name, ins, outs, scratch=None, hold=(), far_hold=(), groups=1, flops=2_000_000_000):
    scratch = dict(scratch or {})
    outs = dict(outs)
    ins = dict(ins, **{"any_hold%d" % i: value for i, value in enumerate(hold)})
    ins = dict(ins, **{"hbm_hold%d" % i: value for i, value in enumerate(far_hold)})
    shared = "part" in outs
    if shared:
        shape, kind = outs["part"]
        scratch["sums"] = (shape, kind)
        outs["part"] = ((groups,) + shape, kind)
    names = list(ins) + list(outs) + list(scratch)

    def kernel(*refs):
        r = SimpleNamespace(**dict(zip(names, refs)))
        if not shared:
            body(r)
            return
        spread = r.part
        r.part = r.sums
        r.sums[...] = jnp.zeros(r.sums.shape, F32)
        body(r)

        def copy(i, carry):
            spread[i] = r.sums[...]
            return carry

        lax.fori_loop(0, groups, copy, 0)

    result = pl.pallas_call(
        kernel,
        name=name,
        out_shape=[jax.ShapeDtypeStruct(shape, kind) for shape, kind in outs.values()],
        in_specs=[pl.BlockSpec(memory_space=space_of(key)) for key in ins],
        out_specs=[pl.BlockSpec(memory_space=space_of(key)) for key in outs],
        scratch_shapes=[
            pltpu.VMEM(*item) if isinstance(item, tuple) else item for item in scratch.values()
        ],
        compiler_params=pltpu.CompilerParams(vmem_limit_bytes=16 * 1024 * 1024),
        cost_estimate=pl.CostEstimate(flops=flops, bytes_accessed=1000, transcendentals=0),
    )(*ins.values())
    return SimpleNamespace(**dict(zip(outs, result)))


def dot(a, b):
    return lax.dot_general(a, b, (((1,), (0,)), ((), ())), preferred_element_type=F32)


def dot_t(a, b):
    return lax.dot_general(a, b, (((1,), (1,)), ((), ())), preferred_element_type=F32)


def t_dot(a, b):
    return lax.dot_general(a, b, (((0,), (0,)), ((), ())), preferred_element_type=F32)


def sigm(v):
    return 0.5 * jnp.tanh(0.5 * v) + 0.5


def slope_of(v):
    s = sigm(v)
    return s * (1.0 + v * (1.0 - s))


def fold8(x):
    return jnp.sum(x.reshape(x.shape[0] // 8, 8, x.shape[1]), axis=0)


def wide(row, width):
    return row if row.shape[1] == width else jnp.concatenate([row] * (width // row.shape[1]), axis=1)


def lanes_of(block, start, count):
    if count == 1:
        return block[start : start + 1, :]
    return jnp.concatenate([block[start + i : start + i + 1, :] for i in range(count)], axis=1)


def put(part, row, acc8):
    total = jnp.sum(acc8, axis=0, keepdims=True)
    for i in range(total.shape[1] // LANES):
        part[row + i : row + i + 1, :] = total[:, i * LANES : (i + 1) * LANES]


def quarters(acc, width):
    count = acc.shape[1] // width
    total = acc[:, :width]
    for i in range(1, count):
        total = total + acc[:, i * width : (i + 1) * width]
    return total


def folded(tot, width):
    total = tot
    for i in range(1, LANES // width):
        total = total + pltpu.roll(tot, i * width, 1)
    return total


def gain(r, key):
    start, count = SPAN[key]
    return lanes_of(r.par[...], start, count)


def shift(r, key):
    start, count = SPAN[key]
    return lanes_of(r.par[...], SHIFT_ROW + start, count)


def moments(tot, row, key, inv, fast_bottle=32):
    count = SPAN[key][1]
    block = folded(tot, fast_bottle) if key in ("f1", "f2") else tot
    mean = lanes_of(block, row, count) * inv
    square = lanes_of(block, row + count, count) * inv
    return mean, lax.rsqrt(square - mean * mean + epsilon)


def pair_of(tot, row, key, fast_bottle=32):
    count = SPAN[key][1]
    block = folded(tot, fast_bottle) if key in ("f1", "f2") else tot
    return lanes_of(block, row, count), lanes_of(block, row + count, count)


def invs(r):
    return r.inv[0:1, :1], r.inv[1:2, :1]


def norm_of(r, tot, row, key, inv, width=None):
    mean, rs = moments(tot, row, key, inv)
    scale = rs * gain(r, key)
    offset = shift(r, key) - mean * scale
    if width is None:
        return mean, rs, scale, offset
    return tuple(wide(v, width) for v in (mean, rs, scale, offset))


def windows(x, side):
    rows, width = x.shape
    col = lax.broadcasted_iota(jnp.int32, (rows, width), 0) % side
    zero = jnp.zeros((side, width), x.dtype)
    out = {}
    for c in range(3):
        step = c - 1
        if step == 0:
            y = x
        else:
            y = pltpu.roll(x, (-step) % rows, 0)
            y = jnp.where((col + step >= 0) & (col + step < side), y, 0.0)
        out[0, c] = jnp.concatenate([zero, y[: rows - side]], axis=0)
        out[1, c] = y
        out[2, c] = jnp.concatenate([y[side:], zero], axis=0)
    return out


def put_windows(col, at, x, side, back):
    width = x.shape[1]
    for (i, j), y in windows(x, side).items():
        if back:
            i, j = 2 - i, 2 - j
        spot = (i * 3 + j) * width
        col[at, spot : spot + width] = y.astype(BF)


def loop(count, body, init=0):
    return lax.fori_loop(0, count, body, init)


def at_frame(t, cells, lead=0):
    return pl.ds(pl.multiple_of(t * cells, cells) + lead, cells)


def spans(total, step):
    return [(a, step) for a in range(0, total, step)]


def clear_ends(pad, cells):
    rows, width = pad.shape
    zero = jnp.zeros((cells, width), pad.dtype)
    pad[0:cells, :] = zero
    pad[rows - cells : rows, :] = zero


def chosen(r, layer, own, other):
    return jnp.where(r.ids[0] == layer, own, other)


def lane_group(shape, width):
    return lax.div(lax.broadcasted_iota(jnp.int32, shape, 1), width)


def placing(rows, group):
    lane = lax.broadcasted_iota(jnp.int32, (rows, LANES), 1)
    row = lax.broadcasted_iota(jnp.int32, (rows, LANES), 0)
    hit = lax.rem(lane, rows) == row if group is None else lane - group * rows == row
    return jnp.where(hit, 1.0, 0.0).astype(BF)


def first_mix(r, d, xpad, part, row):
    acc_s = acc_q = 0.0
    for a, n in spans(d.rows, d.step):
        got = (
            dot(xpad[a : a + n, 2 * d.cf : 4 * d.cf], r.wa[0 : 2 * d.cf, :])
            + dot(xpad[a + d.cells : a + d.cells + n, :], r.wa[2 * d.cf : 6 * d.cf, :])
            + dot(xpad[a + 2 * d.cells : a + 2 * d.cells + n, 0 : d.cf], r.wa[6 * d.cf : 7 * d.cf, :])
        )
        r.lp[a : a + n, :] = got[:, : d.cl]
        r.f1[a : a + n, :] = got[:, d.cl :]
        acc_s = acc_s + fold8(got)
        acc_q = acc_q + fold8(got * got)
    put(part, row, acc_s[:, : d.cl])
    put(part, row + 2, acc_q[:, : d.cl])
    put(part, row + 4, acc_s[:, d.cl :])
    put(part, row + 5, acc_q[:, d.cl :])


def stage_first(d):
    def body(r):
        sect, group = r.ids[0], r.ids[1]
        small = loading(
            r,
            [
                (r.hbm_lat_own, r.lat_own),
                (r.hbm_lat_other, r.lat_other),
                (r.hbm_fr_own, r.fr_own),
                (r.hbm_fr_other, r.fr_other),
            ],
        )
        large = loading(r, [(r.hbm_own.at[sect], r.own), (r.hbm_other.at[sect], r.other)], 4)

        def add(i, total):
            extent = r.crop[sect, i]
            return total + jnp.where(r.present[sect, i] > 0, extent * extent, 0)

        area = lax.fori_loop(0, d.groups, add, jnp.int32(0))
        area = jnp.full((1, LANES), area.astype(F32))
        r.inv[...] = jnp.zeros(r.inv.shape, F32)
        r.inv[0:1, :] = 1.0 / (area * d.frames)
        r.inv[1:2, :] = 1.0 / (area * (d.frames * d.quad))
        limit = jnp.where(r.present[sect, group] > 0, r.crop[sect, group], 0)
        cell = lax.broadcasted_iota(jnp.int32, (d.cells, LANES), 0)
        inside = (lax.div(cell, d.side) < limit) & (lax.rem(cell, d.side) < limit)
        mask = jnp.where(inside, 1.0, 0.0)
        r.mask[...] = mask
        small()
        for layer, wa in enumerate((r.wa, r.wa1)):
            for b in range(d.quad + 3):
                row = slice(b * d.cf, (b + 1) * d.cf)
                if b < d.taps:
                    wa[row, : d.cl] = chosen(r, layer, r.lat_own[b], r.lat_other[b])
                else:
                    wa[row, : d.cl] = jnp.zeros((d.cf, d.cl), BF)
                total = jnp.zeros((d.cf, LANES), F32)
                for q in range(d.quad):
                    k = b - 1 - q
                    if 0 <= k < 3:
                        tap = chosen(r, layer, r.fr_own[k], r.fr_other[k])
                        total = total + t_dot(tap, placing(d.fb, q))
                wa[row, d.cl :] = total.astype(BF)
        clear_ends(r.xpad, d.cells)
        large()

        def frame(t, carry):
            for q in range(d.quad):
                here = r.own[t, q].astype(F32)
                there = r.other[t, q].astype(F32)
                value = jnp.where(sect == 0, here, there)
                r.xpad[at_frame(t, d.cells, d.cells), q * d.cf : (q + 1) * d.cf] = (
                    value * mask
                ).astype(BF)
                r.cot[t, q] = jnp.where(sect == 0, there, here).astype(BF)
            return carry

        loop(d.frames, frame)
        first_mix(r, d, r.xpad, r.part, 0)

    return body


def stage_slow_in(d):
    pack = stage_pack(d)

    def body(r):
        sect = r.ids[0]
        names = ("fs", "fe", "gain", "shift")
        small = loading(
            r,
            [
                (getattr(r, "hbm_%s_%s" % (name, side)), getattr(r, "%s_%s" % (name, side)))
                for name in names
                for side in ("own", "other")
            ],
        )
        large = loading(r, [(r.hbm_own.at[sect], r.own), (r.hbm_other, r.other)], 8)
        fetch = fetching(r, [(r.hbm_red_own, r.hbm_red_other, r.wred_0, r.wred_1)])
        small()
        pack(r)
        large()
        clear_ends(r.spad, d.cells)
        mask = wide(r.mask[...], 256)

        def frame(t, carry):
            for c in range(0, d.cs, 256):
                lane = slice(c, c + 256)
                here = r.own[t, :, lane].astype(F32)
                there = r.other[t, :, lane].astype(F32)
                value = jnp.where(sect == 0, here, there)
                r.spad[at_frame(t, d.cells, d.cells), lane] = (value * mask).astype(BF)
                r.cot[t, :, lane] = jnp.where(sect == 0, there, here).astype(BF)
            return carry

        loop(d.frames, frame)
        fetch()
        for a, n in spans(d.rows, d.step):
            got = 0.0
            for k in range(3):
                b = a + k * d.cells
                got = got + dot(r.spad[b : b + n, :], r.wred_0[k, : d.cs, :])
            r.y[a : a + n, :] = got

    return body


def stage_pack(d):
    sizes = [d.cb, d.cb, d.cs, d.fb, d.fb, d.cf, d.cl]
    keys = ["s1", "s2", "s3", "f1", "f2", "f3", "lp"]

    def body(r):
        spread = placing(d.fb, None)
        for layer in range(2):
            w2, w2t, w3, par = (
                (r.w2_0, r.w2t_0, r.w3_0, r.par_0),
                (r.w2_1, r.w2t_1, r.w3_1, r.par_1),
            )[layer]
            where = lane_group((d.fb, LANES), d.fb)
            for j in range(9):
                tap = chosen(r, layer, r.fs_own[j], r.fs_other[j])
                for out, tiled in ((w2, dot(tap, spread)), (w2t, t_dot(tap, spread))):
                    for q in range(d.quad):
                        row = j * LANES + q * d.fb
                        out[row : row + d.fb, :] = jnp.where(where == q, tiled, 0.0).astype(BF)
            w3[...] = jnp.zeros(w3.shape, BF)
            tap = chosen(r, layer, r.fe_own[...], r.fe_other[...])
            for q in range(d.quad):
                w3[q * d.fb : (q + 1) * d.fb, q * d.cf : (q + 1) * d.cf] = tap
            par[...] = jnp.zeros(par.shape, F32)
            for base, own, other in (
                (0, r.gain_own, r.gain_other),
                (SHIFT_ROW, r.shift_own, r.shift_other),
            ):
                values = chosen(r, layer, own[...], other[...])
                offset = 0
                for key, size in zip(keys, sizes):
                    row = base + SPAN[key][0]
                    piece = values[:, offset : offset + size]
                    offset += size
                    if size < LANES:
                        par[row : row + 1, :] = wide(piece, LANES)
                    else:
                        for i in range(size // LANES):
                            par[row + i : row + i + 1, :] = piece[:, i * LANES : (i + 1) * LANES]

    return body


def fetching(r, weights):
    def copies(first):
        made = []
        for own, other, out_0, out_1 in weights:
            for source, target in ((own, out_0), (other, out_1)) if first else ((own, out_1), (other, out_0)):
                made.append(pltpu.make_async_copy(source, target, r.sems.at[len(made)]))
        return made

    def each(action):
        for first in (True, False):

            @pl.when(r.ids[0] == 0 if first else r.ids[0] != 0)
            def _():
                for copy in copies(first):
                    action(copy)

    each(lambda copy: copy.start())
    return lambda: each(lambda copy: copy.wait())


def loading(r, pairs, first=0):
    copies = [
        pltpu.make_async_copy(source, target, r.loads.at[first + i])
        for i, (source, target) in enumerate(pairs)
    ]
    for copy in copies:
        copy.start()

    def wait():
        for copy in copies:
            copy.wait()

    return wait


def gate(r):
    r.out[...] = r.part[...]


def sort_out(r, grad, value, at):
    first = r.ids[0] == 0
    grad, value = grad.astype(F32), value.astype(F32)
    r.keep_out[at] = jnp.where(first, grad, value).astype(BF)
    r.send_out[at] = jnp.where(first, value, grad).astype(BF)


def stage_place(r):
    copies = []
    for i in range(2):
        for t in range(r.keep.shape[0]):
            keep, got = r.keep[t].astype(F32), r.got[t].astype(F32)
            r.both[i, t] = jnp.where(r.ids[0] == i, keep, got).astype(BF)
        copies.append(pltpu.make_async_copy(r.both.at[i], r.hbm_out.at[i], r.sems.at[i]))
        copies[-1].start()
    for copy in copies:
        copy.wait()


def stage_second(d, row, carried):
    def body(r):
        tot = jnp.sum(r.sync[...], axis=0)
        r.tot[...] = tot
        inv_s, inv_f = invs(r)
        _, _, lg, lb = norm_of(r, tot, row, "lp", inv_s)
        _, _, fg, fb = norm_of(r, tot, row + 4, "f1", inv_f)
        mask = r.mask[...]
        mask2 = wide(mask, d.cl)
        clear_ends(r.lapad, d.cells)
        if carried:
            clear_ends(r.spad, d.cells)
            _, _, sg, sb = norm_of(SimpleNamespace(par=r.par0), tot, 0, "s3", inv_s)

        def frame(t, carry):
            at = at_frame(t, d.cells)
            up = at_frame(t, d.cells, d.cells)
            v = r.lp[at, :] * lg + lb
            r.lapad[up, :] = (v * sigm(v) * mask2).astype(BF)
            v = r.f1[at, :] * fg + fb
            v = (v * sigm(v) * mask).astype(BF)
            r.k1[at, :] = v
            put_windows(r.colf, at, v.astype(F32), d.side, False)
            if carried:
                for c in range(0, d.cs, 256):
                    z = r.xpad[up, c : c + 256].astype(F32) + (
                        r.s3[at, c : c + 256] * sg[:, c : c + 256] + sb[:, c : c + 256]
                    )
                    r.spad[up, c : c + 256] = (z * sigm(z) * mask2).astype(BF)
            return carry

        loop(d.frames, frame)
        acc_s = acc_q = acc_fs = acc_fq = 0.0
        for a, n in spans(d.rows, d.step):
            got = 0.0 if carried else r.y[a : a + n, :]
            for k in range(3):
                b = a + k * d.cells
                if carried:
                    got = got + dot(r.spad[b : b + n, :], r.wred[k, : d.cs, :])
                got = got + dot(r.lapad[b : b + n, :], r.wred[k, d.cs :, :])
            r.s1[a : a + n, :] = got
            acc_s = acc_s + fold8(got)
            acc_q = acc_q + fold8(got * got)
            got = dot(r.colf[a : a + n, :], r.w2[...])
            r.f2[a : a + n, :] = got
            kept = (got.reshape(n // d.cells, d.cells, got.shape[1]) * mask[None]).reshape(got.shape)
            acc_fs = acc_fs + fold8(kept)
            acc_fq = acc_fq + fold8(kept * got)
        put(r.part, 0, acc_s)
        put(r.part, 2, acc_q)
        put(r.part, 4, acc_fs)
        put(r.part, 5, acc_fq)

    return body


def stage_third(d, fetched):
    def body(r):
        if fetched:
            fetch = fetching(
                r,
                [
                    (r.hbm_sp_own, r.hbm_sp_other, r.wsp_0, r.wsp_1),
                    (r.hbm_ex_own, r.hbm_ex_other, r.we_0, r.we_1),
                ],
            )
        tot = jnp.sum(r.sync[...], axis=0)
        r.tot[...] = tot
        inv_s, inv_f = invs(r)
        _, _, sg, sb = norm_of(r, tot, 0, "s1", inv_s)
        _, _, fg, fb = norm_of(r, tot, 4, "f2", inv_f)
        mask = r.mask[...]
        mask2 = wide(mask, d.cb)

        def frame(t, carry):
            at = at_frame(t, d.cells)
            v = r.s1[at, :] * sg + sb
            v = (v * sigm(v) * mask2).astype(BF)
            r.h1[at, :] = v
            put_windows(r.cols, at, v.astype(F32), d.side, False)
            v = r.f2[at, :] * fg + fb
            r.k2[at, :] = (v * sigm(v) * mask).astype(BF)
            return carry

        loop(d.frames, frame)
        if fetched:
            fetch()
        wsp = r.wsp_0 if fetched else r.wsp
        acc_s = acc_q = acc_fs = acc_fq = 0.0
        for a, n in spans(d.rows, d.step):
            got = dot(r.cols[a : a + n, :], wsp[...])
            r.s2[a : a + n, :] = got
            kept = (got.reshape(n // d.cells, d.cells, got.shape[1]) * mask2[None]).reshape(got.shape)
            acc_s = acc_s + fold8(kept)
            acc_q = acc_q + fold8(kept * got)
            got = dot(r.k2[a : a + n, :], r.w3[...])
            r.f3[a : a + n, :] = got
            acc_fs = acc_fs + fold8(got)
            acc_fq = acc_fq + fold8(got * got)
        put(r.part, 0, acc_s)
        put(r.part, 2, acc_q)
        put(r.part, 4, quarters(acc_fs, d.cf))
        put(r.part, 5, quarters(acc_fq, d.cf))

    return body


def expand_slow(r, d, sg, sb, mask2):
    def frame(t, carry):
        at = at_frame(t, d.cells)
        v = r.s2[at, :] * sg + sb
        r.h2[at, :] = (v * sigm(v) * mask2).astype(BF)
        return carry

    loop(d.frames, frame)
    for c in range(0, d.cs, 256):
        acc_s = acc_q = 0.0
        for a, n in spans(d.rows, d.step):
            got = dot(r.h2[a : a + n, :], r.we[:, c : c + 256])
            r.s3[a : a + n, c : c + 256] = got
            acc_s = acc_s + fold8(got)
            acc_q = acc_q + fold8(got * got)
        put(r.part, c // LANES, acc_s)
        put(r.part, (d.cs + c) // LANES, acc_q)


def stage_fourth(d, last):
    def body(r):
        tot = jnp.sum(r.sync[...], axis=0)
        r.tot[...] = tot
        inv_s, inv_f = invs(r)
        _, _, sg, sb = norm_of(r, tot, 0, "s2", inv_s)
        fm, fr, fg, fb = norm_of(r, tot, 4, "f3", inv_f)
        mask = r.mask[...]
        mask2 = wide(mask, d.cb)
        expand_slow(r, d, sg, sb, mask2)
        if not last:
            clear_ends(r.ypad, d.cells)

        def frame(t, carry):
            at = at_frame(t, d.cells)
            up = at_frame(t, d.cells, d.cells)
            for q in range(d.quad):
                lane = slice(q * d.cf, (q + 1) * d.cf)
                f3 = r.f3[at, lane]
                z = r.xpad[up, lane].astype(F32) + (f3 * fg + fb)
                s = sigm(z)
                y = (z * s * mask).astype(BF)
                if last:
                    r.yout[t, q] = y
                    grad = r.cot[t, q].astype(F32) * mask * (s * (1.0 + z * (1.0 - s)))
                    r.dzf[at, lane] = grad
                    u = (f3 - fm) * fr
                    carry = (carry[0] + fold8(grad), carry[1] + fold8(grad * u))
                else:
                    r.ypad[up, lane] = y
            return carry

        zero = jnp.zeros((8, d.cf), F32)
        done = loop(d.frames, frame, (zero, zero))
        if last:
            put(r.part, 16, done[0])
            put(r.part, 17, done[1])
        else:
            first_mix(r, d, r.ypad, r.part, 16)

    return body


def fast_back3(r, d, gs, gg, tot_f3, tot_f2, row):
    _, inv_f = invs(r)
    mask = r.mask[...]
    mean, rs = moments(tot_f3, 4, "f3", inv_f)
    factor = rs * gain(r, "f3")
    gs, gg = gs * inv_f, gg * inv_f
    m2, r2, g2, b2 = norm_of(r, tot_f2, 4, "f2", inv_f)

    def frame(t, carry):
        at = at_frame(t, d.cells)
        for q in range(d.quad):
            lane = slice(q * d.cf, (q + 1) * d.cf)
            u = (r.f3[at, lane] - mean) * rs
            r.df3[at, lane] = (factor * (r.dzf[at, lane] - mask * (gs + u * gg))).astype(BF)
        return carry

    loop(d.frames, frame)
    acc_s = acc_q = 0.0
    for a, n in spans(d.rows, d.step):
        got = dot_t(r.df3[a : a + n, :], r.w3[...])
        f2 = r.f2[a : a + n, :]
        kept = (got.reshape(n // d.cells, d.cells, got.shape[1]) * mask[None]).reshape(got.shape)
        kept = kept * slope_of(f2 * g2 + b2)
        r.d2f[a : a + n, :] = kept
        acc_s = acc_s + fold8(kept)
        acc_q = acc_q + fold8(kept * ((f2 - m2) * r2))
    put(r.part, row, acc_s)
    put(r.part, row + 1, acc_q)


def fast_back2(r, d, gs, gg, tot_f2, tot_f1, f1_row, row):
    _, inv_f = invs(r)
    mask = r.mask[...]
    mean, rs = moments(tot_f2, 4, "f2", inv_f)
    factor = rs * gain(r, "f2")
    gs, gg = gs * inv_f, gg * inv_f
    m1, r1, g1, b1 = norm_of(r, tot_f1, f1_row, "f1", inv_f)

    def frame(t, carry):
        at = at_frame(t, d.cells)
        u = (r.f2[at, :] - mean) * rs
        v = (factor * (r.d2f[at, :] - mask * (gs + u * gg))).astype(BF)
        r.df2[at, :] = v
        put_windows(r.colf, at, v.astype(F32), d.side, True)
        return carry

    loop(d.frames, frame)
    acc_s = acc_q = 0.0
    wide_row = d.quad * d.fb
    for a, n in spans(d.rows, d.step):
        got = dot(r.colf[a : a + n, :], r.w2t[...])
        f1 = r.f1[a : a + n, :]
        kept = (got.reshape(n // d.cells, d.cells, got.shape[1]) * mask[None]).reshape(got.shape)
        kept = kept * slope_of(f1 * g1 + b1)
        r.d1f[a : a + n, :] = kept
        acc_s = acc_s + fold8(kept)
        acc_q = acc_q + fold8(kept * ((f1 - m1) * r1))
    put(r.part, row, acc_s)
    put(r.part, row + 1, acc_q)


def fast_back1(r, d, gs, gg, tot_f1, f1_row):
    _, inv_f = invs(r)
    mask = r.mask[...]
    mean, rs = moments(tot_f1, f1_row, "f1", inv_f)
    factor = rs * gain(r, "f1")
    gs, gg = gs * inv_f, gg * inv_f

    def frame(t, carry):
        at = at_frame(t, d.cells)
        u = (r.f1[at, :] - mean) * rs
        r.gpad[at_frame(t, d.cells, d.cells), d.cl :] = (
            factor * (r.d1f[at, :] - mask * (gs + u * gg))
        ).astype(BF)
        return carry

    loop(d.frames, frame)


def lateral_back(r, d, gs, gg, tot_lp, lp_row):
    inv_s, _ = invs(r)
    mask2 = wide(r.mask[...], d.cl)
    mean, rs = moments(tot_lp, lp_row, "lp", inv_s)
    factor = rs * gain(r, "lp")
    gs, gg = gs * inv_s, gg * inv_s

    def frame(t, carry):
        at = at_frame(t, d.cells)
        u = (r.lp[at, :] - mean) * rs
        r.gpad[at_frame(t, d.cells, d.cells), : d.cl] = (
            factor * (r.dl[at, :] - mask2 * (gs + u * gg))
        ).astype(BF)
        return carry

    loop(d.frames, frame)


def fast_input_grad(r, d, a, n):
    c = d.cf
    mid = dot_t(r.gpad[a + d.cells : a + d.cells + n, :], r.wa[2 * c : 6 * c, :])
    late = dot_t(r.gpad[a + 2 * d.cells : a + 2 * d.cells + n, :], r.wa[0 : 2 * c, :])
    early = dot_t(r.gpad[a : a + n, :], r.wa[6 * c : 7 * c, :])
    return [
        mid[:, :c] + early,
        mid[:, c : 2 * c],
        mid[:, 2 * c : 3 * c] + late[:, :c],
        mid[:, 3 * c :] + late[:, c:],
    ]


def slow_back3(r, d, gs, gg, tot_s3, tot_s2, row):
    inv_s, _ = invs(r)
    mask2 = wide(r.mask[...], d.cb)
    mean, rs = moments(tot_s3, 0, "s3", inv_s)
    factor = rs * gain(r, "s3")
    gs, gg = gs * inv_s, gg * inv_s
    m2, r2, g2, b2 = norm_of(r, tot_s2, 0, "s2", inv_s)

    def frame(t, carry):
        at = at_frame(t, d.cells)
        for c in range(0, d.cs, 256):
            lane = slice(c, c + 256)
            u = (r.s3[at, lane] - mean[:, lane]) * rs[:, lane]
            r.ds3[at, lane] = (
                factor[:, lane] * (r.dzs[at, lane] - mask2 * (gs[:, lane] + u * gg[:, lane]))
            ).astype(BF)
        return carry

    loop(d.frames, frame)
    acc_s = acc_q = 0.0
    for a, n in spans(d.rows, d.step):
        got = dot_t(r.ds3[a : a + n, :], r.we[...])
        s2 = r.s2[a : a + n, :]
        kept = (got.reshape(n // d.cells, d.cells, got.shape[1]) * mask2[None]).reshape(got.shape)
        kept = kept * slope_of(s2 * g2 + b2)
        r.d2[a : a + n, :] = kept
        acc_s = acc_s + fold8(kept)
        acc_q = acc_q + fold8(kept * ((s2 - m2) * r2))
    put(r.part, row, acc_s)
    put(r.part, row + 2, acc_q)


def slow_back2(r, d, gs, gg, tot_s2, tot_s1, row):
    inv_s, _ = invs(r)
    mask2 = wide(r.mask[...], d.cb)
    mean, rs = moments(tot_s2, 0, "s2", inv_s)
    factor = rs * gain(r, "s2")
    gs, gg = gs * inv_s, gg * inv_s
    m1, r1, g1, b1 = norm_of(r, tot_s1, 0, "s1", inv_s)

    def frame(t, carry):
        at = at_frame(t, d.cells)
        u = (r.s2[at, :] - mean) * rs
        v = (factor * (r.d2[at, :] - mask2 * (gs + u * gg))).astype(BF)
        r.ds2[at, :] = v
        put_windows(r.cols, at, v.astype(F32), d.side, True)
        return carry

    loop(d.frames, frame)
    acc_s = acc_q = 0.0
    for a, n in spans(d.rows, d.step):
        got = 0.0
        for k in range(9):
            lane = slice(k * d.cb, (k + 1) * d.cb)
            got = got + dot_t(r.cols[a : a + n, lane], r.wsp[lane, :])
        s1 = r.s1[a : a + n, :]
        kept = (got.reshape(n // d.cells, d.cells, got.shape[1]) * mask2[None]).reshape(got.shape)
        kept = kept * slope_of(s1 * g1 + b1)
        r.d1[a : a + n, :] = kept
        acc_s = acc_s + fold8(kept)
        acc_q = acc_q + fold8(kept * ((s1 - m1) * r1))
    put(r.part, row, acc_s)
    put(r.part, row + 2, acc_q)


def slow_back1(r, d, gs, gg, tot_s1, tot_lp, lp_row, row):
    inv_s, _ = invs(r)
    mask2 = wide(r.mask[...], d.cb)
    mean, rs = moments(tot_s1, 0, "s1", inv_s)
    factor = rs * gain(r, "s1")
    gs, gg = gs * inv_s, gg * inv_s
    ml, rl, gl, bl = norm_of(r, tot_lp, lp_row, "lp", inv_s)
    clear_ends(r.dpad, d.cells)

    def frame(t, carry):
        at = at_frame(t, d.cells)
        u = (r.s1[at, :] - mean) * rs
        r.dpad[at_frame(t, d.cells, d.cells), :] = (
            factor * (r.d1[at, :] - mask2 * (gs + u * gg))
        ).astype(BF)
        return carry

    loop(d.frames, frame)
    acc_s = acc_q = 0.0
    for a, n in spans(d.rows, d.step):
        got = slow_input_grad(r, d, a, n, d.cs, d.cs + d.cl)
        lp = r.lp[a : a + n, :]
        kept = (got.reshape(n // d.cells, d.cells, got.shape[1]) * mask2[None]).reshape(got.shape)
        kept = kept * slope_of(lp * gl + bl)
        r.dl[a : a + n, :] = kept
        acc_s = acc_s + fold8(kept)
        acc_q = acc_q + fold8(kept * ((lp - ml) * rl))
    put(r.part, row, acc_s)
    put(r.part, row + 2, acc_q)


def slow_input_grad(r, d, a, n, first, last):
    got = 0.0
    for k in range(3):
        b = a + (2 - k) * d.cells
        got = got + dot_t(r.dpad[b : b + n, :], r.wred[k, first:last, :])
    return got


def masked(x, mask, d):
    return (x.reshape(x.shape[0] // d.cells, d.cells, x.shape[1]) * mask[None]).reshape(x.shape)


def stage_e(d):
    def body(r):
        tot = jnp.sum(r.sync[...], axis=0)
        r.tot[...] = tot
        inv_s, _ = invs(r)
        mean, rs, sg, sb = norm_of(r, tot, 0, "s3", inv_s)
        mask2 = wide(r.mask[...], 256)

        def frame(t, carry):
            at = at_frame(t, d.cells)
            up = at_frame(t, d.cells, d.cells)
            sums = []
            for i, c in enumerate(range(0, d.cs, 256)):
                lane = slice(c, c + 256)
                s3 = r.s3[at, lane]
                z = r.spad[up, lane].astype(F32) + (s3 * sg[:, lane] + sb[:, lane])
                s = sigm(z)
                r.yout[t, :, lane] = (z * s * mask2).astype(BF)
                grad = r.cot[t, :, lane].astype(F32) * mask2 * (s * (1.0 + z * (1.0 - s)))
                r.dzs[at, lane] = grad
                u = (s3 - mean[:, lane]) * rs[:, lane]
                sums.append((carry[i][0] + fold8(grad), carry[i][1] + fold8(grad * u)))
            return tuple(sums)

        zero = jnp.zeros((8, 256), F32)
        done = loop(d.frames, frame, tuple((zero, zero) for c in range(0, d.cs, 256)))
        for i, c in enumerate(range(0, d.cs, 256)):
            put(r.part, c // LANES, done[i][0])
            put(r.part, (d.cs + c) // LANES, done[i][1])
        gs, gg = pair_of(tot, 16, "f3")
        fast_back3(r, d, gs, gg, r.tot_c[...], r.tot_b[...], 16)

    return body


def stage_f(d):
    def body(r):
        tot = jnp.sum(r.sync[...], axis=0)
        r.tot[...] = tot
        gs, gg = pair_of(tot, 0, "s3")
        slow_back3(r, d, gs, gg, r.tot_d[...], r.tot_c[...], 0)
        gs, gg = pair_of(tot, 16, "f2")
        fast_back2(r, d, gs, gg, r.tot_b[...], r.tot_a[...], 20, 4)

    return body


def stage_g(d):
    def body(r):
        tot = jnp.sum(r.sync[...], axis=0)
        r.tot[...] = tot
        gs, gg = pair_of(tot, 0, "s2")
        slow_back2(r, d, gs, gg, r.tot_c[...], r.tot_b[...], 0)

    return body


def stage_h(d):
    def body(r):
        tot = jnp.sum(r.sync[...], axis=0)
        r.tot[...] = tot
        inv_s, _ = invs(r)
        gs, gg = pair_of(tot, 0, "s1")
        slow_back1(r, d, gs, gg, r.tot_b[...], r.tot_a[...], 16, 16)
        mask2 = wide(r.mask[...], 256)
        r.par = r.par0
        mean, rs, sg, sb = norm_of(r, r.tot_a[...], 0, "s3", inv_s)
        for c in range(0, d.cs, 256):
            lane = slice(c, c + 256)
            acc_s = acc_q = 0.0
            for a, n in spans(d.rows, d.step):
                got = slow_input_grad(r, d, a, n, c, c + 256)
                got = masked(r.dzs[a : a + n, lane] + got, mask2, d).astype(BF).astype(F32)
                s3 = r.s3[a : a + n, lane]
                z = r.spad[a + d.cells : a + d.cells + n, lane].astype(F32) + (
                    s3 * sg[:, lane] + sb[:, lane]
                )
                grad = got * slope_of(z)
                r.dzs0[a : a + n, lane] = grad
                u = (s3 - mean[:, lane]) * rs[:, lane]
                acc_s = acc_s + fold8(grad)
                acc_q = acc_q + fold8(grad * u)
            put(r.part, c // LANES, acc_s)
            put(r.part, (d.cs + c) // LANES, acc_q)

    return body


def stage_i(d):
    def body(r):
        tot = jnp.sum(r.sync[...], axis=0)
        r.tot[...] = tot
        _, inv_f = invs(r)
        clear_ends(r.gpad, d.cells)
        gs, gg = pair_of(r.tot_f[...], 4, "f1")
        fast_back1(r, d, gs, gg, r.tot_a[...], 20)
        gs, gg = pair_of(tot, 16, "lp")
        lateral_back(r, d, gs, gg, r.tot_a[...], 16)
        r.par = r.par0
        mask = r.mask[...]
        mean, rs, fg, fb = norm_of(r, r.tot_c0[...], 4, "f3", inv_f)
        acc_s = acc_q = 0.0
        for a, n in spans(d.rows, d.step):
            pieces = fast_input_grad(r, d, a, n)
            for q in range(d.quad):
                lane = slice(q * d.cf, (q + 1) * d.cf)
                got = masked(r.dzf[a : a + n, lane] + pieces[q], mask, d).astype(BF).astype(F32)
                f3 = r.f3[a : a + n, lane]
                z = r.xpad[a + d.cells : a + d.cells + n, lane].astype(F32) + (f3 * fg + fb)
                grad = got * slope_of(z)
                r.dzf0[a : a + n, lane] = grad
                acc_s = acc_s + fold8(grad)
                acc_q = acc_q + fold8(grad * ((f3 - mean) * rs))
        put(r.part, 4, acc_s)
        put(r.part, 5, acc_q)
        gs, gg = pair_of(tot, 0, "s3")
        r.dzs = r.dzs0
        slow_back3(r, d, gs, gg, r.tot_a[...], r.tot_c0[...], 0)

    return body


def stage_j(d):
    def body(r):
        tot = jnp.sum(r.sync[...], axis=0)
        r.tot[...] = tot
        gs, gg = pair_of(tot, 0, "s2")
        slow_back2(r, d, gs, gg, r.tot_c[...], r.tot_b[...], 0)
        gs, gg = pair_of(tot, 4, "f3")
        fast_back3(r, d, gs, gg, r.tot_c[...], r.tot_b[...], 4)

    return body


def stage_k(d):
    def body(r):
        tot = jnp.sum(r.sync[...], axis=0)
        r.tot[...] = tot
        gs, gg = pair_of(tot, 0, "s1")
        slow_back1(r, d, gs, gg, r.tot_b[...], r.tot_a[...], 0, 0)
        gs, gg = pair_of(tot, 4, "f2")
        fast_back2(r, d, gs, gg, r.tot_b[...], r.tot_a[...], 4, 4)

    return body


def stage_slow_out(d):
    def body(r):
        mask2 = wide(r.mask[...], 256)
        for c in range(0, d.cs, 256):
            lane = slice(c, c + 256)
            for a, n in spans(d.rows, d.step):
                got = slow_input_grad(r, d, a, n, c, c + 256)
                got = masked(r.dzs[a : a + n, lane] + got, mask2, d)
                for t in range(n // d.cells):
                    at = (a // d.cells + t, slice(None), lane)
                    sort_out(r, got[t * d.cells : (t + 1) * d.cells, :], r.value[at], at)

    return body


def stage_l(d):
    def body(r):
        tot = jnp.sum(r.sync[...], axis=0)
        r.tot[...] = tot
        clear_ends(r.gpad, d.cells)
        gs, gg = pair_of(tot, 4, "f1")
        fast_back1(r, d, gs, gg, r.tot_a[...], 4)
        gs, gg = pair_of(tot, 0, "lp")
        lateral_back(r, d, gs, gg, r.tot_a[...], 0)
        mask = r.mask[...]
        for a, n in spans(d.rows, d.step):
            pieces = fast_input_grad(r, d, a, n)
            for q in range(d.quad):
                lane = slice(q * d.cf, (q + 1) * d.cf)
                got = masked(r.dzf[a : a + n, lane] + pieces[q], mask, d)
                for t in range(n // d.cells):
                    at = (a // d.cells + t, q)
                    sort_out(r, got[t * d.cells : (t + 1) * d.cells, :], r.value[at], at)

    return body


def small_block(r, row, value):
    for half in range(2):
        for i in range(2):
            at = 64 * half + 32 * i
            r.halves[half, row : row + 32, i * LANES : (i + 1) * LANES] = value[
                at : at + 32, :
            ].astype(BF)


def hand_over(r):
    r.keep[...] = r.halves[r.ids[0]]
    r.send[...] = r.halves[1 - r.ids[0]]


def grads_es(d):
    part = d.cb // 2

    def body(r):
        def frame(t, carry):
            at = at_frame(t, d.cells)
            put_windows(r.cols, at, r.ds2[at, :].astype(F32), d.side, True)
            put_windows(r.colf, at, r.df2[at, :].astype(F32), d.side, True)
            return carry

        loop(d.frames, frame)
        row = 0
        turned = r.h2[...].T
        for c in range(0, d.cs, 256):
            got = dot(turned, r.ds3[:, c : c + 256]).astype(BF)
            for half in range(2):
                r.halves[half, row : row + part, :] = got[half * part : (half + 1) * part, :]
            row += part
        turned = r.h1[...].T
        for k in range(9):
            got = dot(turned, r.cols[:, k * d.cb : (k + 1) * d.cb]).astype(BF)
            for half in range(2):
                r.halves[half, row : row + part, :] = got[half * part : (half + 1) * part, :]
            row += part
        r.g2[...] = t_dot(r.k1[...], r.colf[...])
        r.g3[...] = t_dot(r.k2[...], r.df3[...])
        where = lane_group((d.fb, LANES), d.fb)
        for i in range(3):
            total = jnp.zeros((d.fb, LANES), F32)
            for c in range(3):
                for q in range(d.quad):
                    tap = (3 * i + c) * LANES
                    piece = r.g2[q * d.fb : (q + 1) * d.fb, tap : tap + LANES]
                    if c != q:
                        piece = pltpu.roll(piece, ((c - q) * d.fb) % LANES, 1)
                    total = total + jnp.where(where == c, piece, 0.0)
            r.block[i * d.fb : (i + 1) * d.fb, :] = total
        total = jnp.zeros((d.fb, LANES), F32)
        for q in range(d.quad):
            total = total + r.g3[q * d.fb : (q + 1) * d.fb, q * d.cf : (q + 1) * d.cf]
        r.block[3 * d.fb :, :] = total
        small_block(r, row, r.block[...])
        hand_over(r)

    return body


def with_grads(stage_body, grads_body, names):
    def body(r):
        stage_body(r)
        for target, source in names.items():
            setattr(r, target, getattr(r, source))
        grads_body(r)

    return body


def grads_reduce(d):
    split = (d.cs + d.cl) // 2

    def body(r):
        for c in range(0, d.cs + d.cl, 256):
            if c < d.cs:
                source = r.spad[d.cells : d.cells + d.rows, c : c + 256]
            else:
                source = r.lapad[d.cells : d.cells + d.rows, c - d.cs : c - d.cs + 256]
            turned = source.T
            cut = min(max(split - c, 0), 256)
            for k in range(3):
                b = (2 - k) * d.cells
                got = dot(turned, r.dpad[b : b + d.rows, :]).astype(BF)
                if cut > 0:
                    row = k * split + c
                    r.halves[0, row : row + cut, :] = got[:cut, :]
                if cut < 256:
                    row = k * split + c + cut - split
                    r.halves[1, row : row + 256 - cut, :] = got[cut:, :]
        hand_over(r)

    return body


def grads_first(d):
    def body(r):
        c = d.cf
        grad = r.gpad[d.cells : d.cells + d.rows, :]
        r.ga[0 : 2 * c, :] = t_dot(r.xpad[0 : d.rows, 2 * c : 4 * c], grad)
        r.ga[2 * c : 6 * c, :] = t_dot(r.xpad[d.cells : d.cells + d.rows, :], grad)
        r.ga[6 * c :, :] = t_dot(r.xpad[2 * d.cells : 2 * d.cells + d.rows, 0:c], grad)
        row = 0
        for b in range(d.taps):
            for half in range(2):
                at = b * c + half * (c // 2)
                r.halves[half, row : row + c // 2, :] = r.ga[at : at + c // 2, : d.cl].astype(BF)
            row += c // 2
        where = lane_group((c, LANES), d.fb)
        total = jnp.zeros((c, LANES), F32)
        for k in range(3):
            for q in range(d.quad):
                at = (q + k + 1) * c
                piece = r.ga[at : at + c, d.cl :]
                if k != q:
                    piece = pltpu.roll(piece, ((k - q) * d.fb) % LANES, 1)
                total = total + jnp.where(where == k, piece, 0.0)
        small_block(r, row, total)
        hand_over(r)

    return body


def gather_pieces(r, count):
    row = 0
    for i in range(count):
        keep, got = getattr(r, "keep_%d" % i), getattr(r, "got_%d" % i)
        r.mine[row : row + keep.shape[0], :] = (
            keep[...].astype(F32) + got[...].astype(F32)
        ).astype(BF)
        row += keep.shape[0]
    if row < r.mine.shape[0]:
        r.mine[row:, :] = jnp.zeros((r.mine.shape[0] - row, r.mine.shape[1]), BF)


def split_near(count, turned=None):
    def body(r):
        gather_pieces(r, count)
        hand_shares(r, r.mine, r.ids[2 if turned is None else 4], turned)

    return body


def split_half(count, bit):
    def body(r):
        gather_pieces(r, count)
        halve(r, bit)

    return body


def hand_shares(r, source, place, turned=None):
    k = 0
    while hasattr(r, "to_%d" % k):
        target = getattr(r, "to_%d" % k)
        rows = target.shape[0]
        start = pl.multiple_of((place ^ (k if turned is None else turned[k])) * rows, 16)
        target[...] = source[pl.ds(start, rows), :]
        k += 1


def add_shares(r):
    total = r.from_0[...].astype(F32)
    k = 1
    while hasattr(r, "from_%d" % k):
        total = total + getattr(r, "from_%d" % k)[...].astype(F32)
        k += 1
    return total.astype(BF)


def sum_shares(r):
    r.out[...] = add_shares(r)


def sum_and_share(r):
    r.mine[...] = add_shares(r)
    hand_shares(r, r.mine, r.ids[3])


def collect(which):
    def body(r):
        rows = r.from_0.shape[0]
        k = 0
        while hasattr(r, "from_%d" % k):
            start = pl.multiple_of((r.ids[which] ^ k) * rows, 16)
            r.out[pl.ds(start, rows), :] = getattr(r, "from_%d" % k)[...]
            k += 1

    return body


def halve(r, bit):
    rows = r.keep.shape[0]
    mine = jnp.where((r.ids[1] & bit) > 0, 1, 0)
    r.keep[...] = r.mine[pl.ds(pl.multiple_of(mine * rows, 16), rows), :]
    r.send[...] = r.mine[pl.ds(pl.multiple_of((1 - mine) * rows, 16), rows), :]


def split_far(bit):
    def body(r):
        rows = r.early.shape[0]
        r.mine[0:rows, :] = r.early[...]
        r.mine[rows:, :] = add_shares(r)
        halve(r, bit)

    return body


def next_far(bit):
    def body(r):
        total = (r.own[...].astype(F32) + r.got[...].astype(F32)).astype(BF)
        if bit:
            r.mine[...] = total
            halve(r, bit)
        else:
            r.keep[...] = total

    return body


def join_far(bit):
    def body(r):
        rows = r.own.shape[0]
        mine = jnp.where((r.ids[1] & bit) > 0, 1, 0)
        r.out[pl.ds(pl.multiple_of(mine * rows, 16), rows), :] = r.own[...]
        r.out[pl.ds(pl.multiple_of((1 - mine) * rows, 16), rows), :] = r.got[...]

    return body


def join_last(bit):
    def body(r):
        rows = r.own.shape[0]
        mine = jnp.where((r.ids[1] & bit) > 0, 1, 0)
        r.all[pl.ds(pl.multiple_of(mine * rows, 16), rows), :] = r.own[...]
        r.all[pl.ds(pl.multiple_of((1 - mine) * rows, 16), rows), :] = r.got[...]
        cut = r.es.shape[0]
        r.es[...] = r.all[0:cut, :]
        r.red[...] = r.all[cut:, :]

    return body


def halve_parts(r, sizes, bit):
    mine = jnp.where((r.ids[1] & bit) > 0, 1, 0)
    start = done = 0
    for size in sizes:
        half = size // 2
        at = slice(done, done + half)
        r.keep[at, :] = r.mine[pl.ds(pl.multiple_of(start + mine * half, 16), half), :]
        r.send[at, :] = r.mine[pl.ds(pl.multiple_of(start + (1 - mine) * half, 16), half), :]
        start += size
        done += half


def join_parts(sizes, bit):
    def body(r):
        start = 0
        for i, size in enumerate(sizes):
            own, got = getattr(r, "own_%d" % i), getattr(r, "got_%d" % i)
            r.mine[start : start + size, :] = (own[...].astype(F32) + got[...].astype(F32)).astype(BF)
            start += size
        halve_parts(r, sizes, bit)

    return body


def next_parts(sizes, bit):
    def body(r):
        r.mine[...] = (r.own[...].astype(F32) + r.got[...].astype(F32)).astype(BF)
        halve_parts(r, sizes, bit)

    return body


def merge_far(bit):
    def body(r):
        rows = r.early.shape[0]
        r.mine[0:rows, :] = r.early[...]
        if hasattr(r, "own"):
            late = (r.own[...].astype(F32) + r.got[...].astype(F32)).astype(BF)
        else:
            late = r.late[...]
        r.mine[rows:, :] = late
        halve(r, bit)

    return body


def part_far(bit):
    def body(r):
        rows = r.own.shape[0]
        mine = jnp.where((r.ids[1] & bit) > 0, 1, 0)
        r.all[pl.ds(pl.multiple_of(mine * rows, 16), rows), :] = r.own[...]
        r.all[pl.ds(pl.multiple_of((1 - mine) * rows, 16), rows), :] = r.got[...]
        cut = r.early.shape[0]
        r.early[...] = r.all[0:cut, :]
        r.late[...] = r.all[cut:, :]

    return body


def join_send(bit):
    def body(r):
        join_far(bit)(r)

        @pl.when(r.ids[0] == 0)
        def _():
            r.send[0 : r.second.shape[0], :] = r.second[...]

        @pl.when(r.ids[0] != 0)
        def _():
            r.send[0 : r.out.shape[0], :] = r.out[...]

    return body


def add_near(r):
    rows = r.got.shape[1]
    total = r.got[0].astype(F32)
    for i in range(1, r.got.shape[0]):
        total = total + r.got[i].astype(F32)
    r.out[0:rows, :] = total.astype(BF)
    r.out[rows:, :] = add_shares(r)


def add_up(r):
    total = jnp.zeros(r.got.shape[1:], F32)
    for i in range(r.got.shape[0]):
        total = total + r.got[i].astype(F32)
    total = total.astype(BF)
    if len(r.out.shape) == len(total.shape):
        r.out[...] = total
    else:
        for i in range(r.out.shape[0]):
            r.out[i] = total


def spread_out(r):
    for i in range(r.out.shape[0]):
        r.out[i] = r.got[...]


def store_half(r, spots, half, out, here_at, there_at, count, lanes=slice(None)):
    done = 0
    while done < count:
        step = count - done
        found = []
        for (kind, row), mine in ((here_at, half == 0), (there_at, half == 1)):
            own, got, piece, stride, offset = spots[kind]
            i, rest = divmod(row + done, piece)
            step = min(step, piece - rest)
            found.append((getattr(r, own if mine else got), i * stride + offset + rest))
        (first, at_0), (second, at_1) = found
        out[done : done + step, :] = jnp.where(
            r.ids[0] == 0,
            first[at_0 : at_0 + step, lanes].astype(F32),
            second[at_1 : at_1 + step, lanes].astype(F32),
        )
        done += step


def finish_reduce(d, spots):
    split = (d.cs + d.cl) // 2

    def body(r):
        copies = []
        for k in range(3):
            for half in range(2):
                out = r.reduce.at[k, half * split : (half + 1) * split, :]
                store_half(r, spots, half, out, ("r", k * split), ("red", k * split), split)
            copies.append(
                pltpu.make_async_copy(r.reduce.at[k], r.hbm_reduce.at[0, k], r.sems.at[k])
            )
            copies[-1].start()
        for copy in copies:
            copy.wait()

    return body


def finish_rest(d, spots, rows_red):
    part = d.cb // 2
    side = d.cf // 2

    def body(r):
        row = 0
        for c in range(0, d.cs, 256):
            for half in range(2):
                out = r.expand.at[half * part : (half + 1) * part, c : c + 256]
                store_half(r, spots, half, out, ("b", row), ("es", row), part)
            row += part
        copies = [pltpu.make_async_copy(r.expand, r.hbm_expand.at[0], r.sems.at[0])]
        copies[-1].start()
        for k in range(9):
            for half in range(2):
                out = r.space.at[k, half * part : (half + 1) * part, :]
                store_half(r, spots, half, out, ("b", row), ("es", row), part)
            row += part
        copies.append(pltpu.make_async_copy(r.space, r.hbm_space.at[0], r.sems.at[1]))
        copies[-1].start()

        def small(here_at, there_at):
            for half in range(2):
                for i in range(2):
                    at = 64 * half + 32 * i
                    lanes = slice(i * LANES, (i + 1) * LANES)
                    store_half(r, spots, half, r.block.at[at : at + 32, :], here_at, there_at, 32, lanes)

        small(("b", row), ("es", row))
        for i in range(3):
            piece = r.block[i * d.fb : (i + 1) * d.fb, :]
            for c in range(3):
                moved = piece if c == 0 else pltpu.roll(piece, LANES - c * d.fb, 1)
                r.fspace[0, 3 * i + c] = moved[:, : d.fb]
        r.fexpand[0] = r.block[3 * d.fb :, :]
        row, row_1 = 0, rows_red
        for tap in range(d.taps):
            for half in range(2):
                out = r.lateral.at[0, tap, half * side : (half + 1) * side, :]
                store_half(r, spots, half, out, ("f", row), ("red", row_1), side)
            row, row_1 = row + side, row_1 + side
        small(("f", row), ("red", row_1))
        turned = r.block[...].T
        for k in range(3):
            r.freduce[0, k] = turned[k * d.fb : (k + 1) * d.fb, :]
        for copy in copies:
            copy.wait()

    return body


def norms_out(d, at):
    def body(r):
        made = []
        for layer in range(2):
            lines = []
            for which in (1, 0):
                pieces = []
                for key in ("s1", "s2", "s3", "f1", "f2", "f3", "lp"):
                    name, row = at[layer][key]
                    tot = getattr(r, name)[...]
                    count = SPAN[key][1]
                    if key in ("f1", "f2"):
                        tot = folded(tot, d.fb)
                    piece = lanes_of(tot, row + which * count, count)
                    pieces.append(piece[:, : d.fb] if key in ("f1", "f2") else piece)
                lines.append(jnp.concatenate(pieces, axis=1))
            made.append(lines)
        for i in range(2):
            r.keep[i : i + 1, :] = jnp.where(r.ids[0] == 0, made[0][i], made[1][i])
            r.send[i : i + 1, :] = jnp.where(r.ids[0] == 0, made[1][i], made[0][i])

    return body


def norms_add(r):
    total = r.keep[...] + r.got[...]
    r.gain[...] = total[0:1, :]
    r.shift[...] = total[1:2, :]


def on_device(
    edge_slow,
    edge_fast,
    slow_reduce,
    slow_spatial,
    slow_expand,
    fast_reduce,
    fast_spatial,
    fast_expand,
    lateral,
    norm_gain,
    norm_shift,
    present,
    crop_side,
):
    micro, _, frames, side, _, cs = edge_slow.shape[1:]
    cells = side * side
    fast_frames = edge_fast.shape[3]
    quad = fast_frames // frames
    d = SimpleNamespace(
        frames=frames,
        side=side,
        cells=cells,
        rows=frames * cells,
        step=min(256, frames * cells),
        quad=quad,
        cs=cs,
        cb=slow_expand.shape[1],
        cf=edge_fast.shape[-1],
        fb=fast_expand.shape[1],
        cl=lateral.shape[3],
    )
    d.taps = lateral.shape[1]
    d.groups = lax.axis_size("dp")
    groups = d.groups
    rows, pads = d.rows, d.rows + 2 * cells
    swap = [(0, 1), (1, 0)]
    own_slow = edge_slow.reshape(micro, frames, cells, cs)
    own_fast = edge_fast.reshape(micro, frames, quad, cells, d.cf)

    def across(value, pairs=swap):
        return lax.ppermute(value, "pipe", pairs)

    inner = 1
    while 4 * inner * inner <= groups:
        inner *= 2
    outer = groups // inner
    group = lax.axis_index("dp")
    sect = lax.axis_index("pipe")
    shift_by = inner.bit_length() - 1
    turned = [
        sum(((i >> b) & 1) << (shift_by - 1 - b) for b in range(shift_by)) for i in range(inner)
    ]
    turned_place = jnp.int32(0)
    for b in range(shift_by):
        turned_place += (lax.shift_right_logical(group, jnp.int32(b)) & 1) << (shift_by - 1 - b)
    far_place = lax.shift_right_logical(group, jnp.int32(shift_by))
    ids = jnp.stack([sect, group, group & (inner - 1), far_place, turned_place]).astype(jnp.int32)
    own_fast, lat_own, fr_own, ids, sect = lax.optimization_barrier(
        (own_fast, lateral[0], jnp.swapaxes(fast_reduce[0], 1, 2), ids, sect)
    )
    other_fast, lat_other, fr_other = across(own_fast), across(lat_own), across(fr_own)
    red_own, other_fast, lat_other, fr_other = lax.optimization_barrier(
        (slow_reduce[0], other_fast, lat_other, fr_other)
    )
    red_other = across(red_own)
    sems = pltpu.SemaphoreType.DMA

    def stage(*args, **others):
        return run(*args, groups=groups, **others)

    def exchange(part):
        return lax.all_to_all(part, "dp", 0, 0)

    slow_f = ((rows, cs), F32)
    mid_f = ((rows, d.cb), F32)
    fast_f = ((rows, quad * d.cf), F32)
    tiny_f = ((rows, quad * d.fb), F32)
    mid_b = ((rows, d.cb), BF)
    tiny_b = ((rows, quad * d.fb), BF)
    fast_b = ((rows, quad * d.cf), BF)
    small = ((8, LANES), F32)
    large = ((24, LANES), F32)
    xpad_s = ((pads, quad * d.cf), BF)
    spad_s = ((pads, cs), BF)
    mpad_s = ((pads, d.cb), BF)
    gpad_s = ((pads, d.cl + quad * d.fb), BF)
    cols_s = {"cols": ((rows, 9 * d.cb), BF)}
    colf_s = {"colf": ((rows, 9 * quad * d.fb), BF)}
    wa_s = (((quad + 3) * d.cf, d.cl + quad * d.fb), BF)

    out_fast = ((frames, quad, cells, d.cf), BF)
    out_slow = ((frames, cells, cs), BF)
    a0 = stage(
        stage_first(d),
        "stage_a0",
        dict(
            ids=ids,
            present=present,
            crop=crop_side,
            hbm_own=own_fast,
            hbm_other=other_fast,
            hbm_lat_own=lat_own,
            hbm_lat_other=lat_other,
            hbm_fr_own=fr_own,
            hbm_fr_other=fr_other,
        ),
        dict(
            mask=((cells, LANES), F32),
            inv=small,
            wa=wa_s,
            wa1=wa_s,
            xpad=xpad_s,
            cot=out_fast,
            lp=mid_f,
            f1=tiny_f,
            part=small,
        ),
        dict(
            own=out_fast,
            other=out_fast,
            lat_own=(lat_own.shape, BF),
            lat_other=(lat_own.shape, BF),
            fr_own=(fr_own.shape, BF),
            fr_other=(fr_own.shape, BF),
            loads=sems((6,)),
        ),
    )
    own_slow, fs_own, fe_own, norm_gain, norm_shift, a0_inv = lax.optimization_barrier(
        (own_slow, fast_spatial.reshape(9, d.fb, d.fb), fast_expand[0], norm_gain, norm_shift, a0.inv)
    )
    other_slow = across(lax.dynamic_index_in_dim(own_slow, 1 - sect, 0, keepdims=False))
    fs_other, fe_other = across(fs_own), across(fe_own)
    gain_other, shift_other = across(norm_gain), across(norm_shift)
    mask = a0.mask
    base = dict(mask=mask, inv=a0_inv)
    wa = (a0.wa, a0.wa1)
    rows_es = (cs // 256 + 9) * (d.cb // 2) + 32
    rows_red = 3 * (cs + d.cl) // 2
    rows_first = d.taps * (d.cf // 2) + 32

    def halves_of(body, name, rows_now, ins, scratch, hold):
        made = run(
            body,
            name,
            dict(ids=ids, **ins),
            dict(keep=((rows_now, 256), BF), send=((rows_now, 256), BF)),
            dict(scratch, halves=((2, rows_now, 256), BF)),
            hold=hold,
        )
        return made.keep, across(made.send)

    def halves_es(name, hold, **ins):
        scratch = dict(
            cols_s,
            **colf_s,
            g2=((quad * d.fb, 9 * quad * d.fb), F32),
            g3=((quad * d.fb, quad * d.cf), F32),
            block=((LANES, LANES), F32),
        )
        return halves_of(grads_es(d), "grads_es" + name, rows_es, ins, scratch, hold)

    def halves_red(name, hold, **ins):
        return halves_of(grads_reduce(d), "grads_red" + name, rows_red, ins, {}, hold)

    def halves_first(name, hold, **ins):
        scratch = dict(ga=(((quad + 3) * d.cf, d.cl + quad * d.fb), F32))
        return halves_of(grads_first(d), "grads_first" + name, rows_first, ins, scratch, hold)

    def padded(count):
        unit = 16 * groups
        return -(-count // unit) * unit

    es_all, red_all = padded(rows_es), padded(rows_red + rows_first)
    ga_s = (((quad + 3) * d.cf, d.cl + quad * d.fb), F32)

    def kept(count):
        return dict(keep=((count, 256), BF), send=((count, 256), BF))

    near_1 = (es_all + red_all) // inner

    def shares(count, rows_now):
        return {"to_%d" % k: ((rows_now, 256), BF) for k in range(count)}

    def sent_near(made):
        pairs = lambda k: [(i, i ^ k) for i in range(groups)]
        return {
            "from_%d" % k: made[k] if k == 0 else lax.ppermute(made[k], "dp", pairs(k))
            for k in range(inner)
        }

    bits = [inner << i for i in range(outer.bit_length() - 1)][::-1]
    near_bits = [1 << i for i in range(shift_by)]

    def over(value, bit):
        return lax.ppermute(value, "dp", [(i, i ^ bit) for i in range(groups)])

    def targets(made, count):
        return [getattr(made, "to_%d" % k) for k in range(count)]

    def pieces_of(*pieces):
        return {
            "%s_%d" % (key, i): value
            for i, piece in enumerate(pieces)
            for key, value in zip(("keep", "got"), piece)
        }

    arrived = (other_slow, red_other, fs_other, fe_other, gain_other, shift_other)
    part = run(gate, "gate", dict(part=a0.part), dict(out=(a0.part.shape, F32)), far_hold=arrived).out
    sync = exchange(part)
    sp_own, ex_own, sync = lax.optimization_barrier(
        (slow_spatial.reshape(9 * d.cb, d.cb), slow_expand[0], sync)
    )
    sp_other, ex_other = across(sp_own), across(ex_own)
    packed_2 = ((9 * quad * d.fb, quad * d.fb), BF)
    packed_3 = ((quad * d.fb, quad * d.cf), BF)
    norm_s = ((2 * SHIFT_ROW, LANES), F32)
    red_s = (red_own.shape, BF)
    slow_in = pack = stage(
        stage_slow_in(d),
        "stage_slow_in",
        dict(
            ids=ids,
            mask=mask,
            hbm_own=own_slow,
            hbm_other=other_slow,
            hbm_red_own=red_own,
            hbm_red_other=red_other,
            hbm_fs_own=fs_own,
            hbm_fs_other=fs_other,
            hbm_fe_own=fe_own,
            hbm_fe_other=fe_other,
            hbm_gain_own=norm_gain,
            hbm_gain_other=gain_other,
            hbm_shift_own=norm_shift,
            hbm_shift_other=shift_other,
        ),
        dict(
            spad=spad_s,
            cot=out_slow,
            y=mid_f,
            wred_0=red_s,
            wred_1=red_s,
            w2_0=packed_2,
            w2_1=packed_2,
            w2t_0=packed_2,
            w2t_1=packed_2,
            w3_0=packed_3,
            w3_1=packed_3,
            par_0=norm_s,
            par_1=norm_s,
        ),
        dict(
            own=out_slow,
            other=out_slow,
            fs_own=(fs_own.shape, BF),
            fs_other=(fs_own.shape, BF),
            fe_own=(fe_own.shape, BF),
            fe_other=(fe_own.shape, BF),
            gain_own=(norm_gain.shape, F32),
            gain_other=(norm_gain.shape, F32),
            shift_own=(norm_gain.shape, F32),
            shift_other=(norm_gain.shape, F32),
            loads=sems((10,)),
            sems=sems((2,)),
        ),
        hold=(sync,),
    )
    wred = (slow_in.wred_0, slow_in.wred_1)
    w2, w2t = (pack.w2_0, pack.w2_1), (pack.w2t_0, pack.w2t_1)
    w3, par = (pack.w3_0, pack.w3_1), (pack.par_0, pack.par_1)

    def common(layer):
        return dict(base, par=par[layer])

    b0 = stage(
        stage_second(d, 0, False),
        "stage_b0",
        dict(
            common(0),
            ids=ids,
            sync=sync,
            lp=a0.lp,
            f1=a0.f1,
            y=slow_in.y,
            wred=wred[0],
            w2=w2[0],
        ),
        dict(
            lapad=mpad_s,
            k1=tiny_b,
            s1=mid_f,
            f2=tiny_f,
            tot=small,
            part=small,
        ),
        colf_s,
        far_hold=(sp_other, ex_other),
    )
    sync = exchange(b0.part)
    c0 = stage(
        stage_third(d, True),
        "stage_c0",
        dict(
            common(0),
            ids=ids,
            sync=sync,
            s1=b0.s1,
            f2=b0.f2,
            w3=w3[0],
            hbm_sp_own=sp_own,
            hbm_sp_other=sp_other,
            hbm_ex_own=ex_own,
            hbm_ex_other=ex_other,
        ),
        dict(
            h1=mid_b,
            k2=tiny_b,
            s2=mid_f,
            f3=fast_f,
            tot=small,
            wsp_0=(sp_own.shape, BF),
            wsp_1=(sp_own.shape, BF),
            we_0=(ex_own.shape, BF),
            we_1=(ex_own.shape, BF),
            part=small,
        ),
        dict(cols_s, sems=sems((4,))),
    )
    sync = exchange(c0.part)
    we, wsp = (c0.we_0, c0.we_1), (c0.wsp_0, c0.wsp_1)
    d0 = stage(
        stage_fourth(d, False),
        "stage_d0",
        dict(common(0), sync=sync, s2=c0.s2, f3=c0.f3, we=we[0], xpad=a0.xpad, wa=wa[1]),
        dict(h2=mid_b, s3=slow_f, ypad=xpad_s, lp=mid_f, f1=tiny_f, tot=small, part=large),
    )
    sync = exchange(d0.part)
    b1 = stage(
        stage_second(d, 16, True),
        "stage_b1",
        dict(
            base,
            par=par[1],
            par0=par[0],
            sync=sync,
            lp=d0.lp,
            f1=d0.f1,
            s3=d0.s3,
            xpad=slow_in.spad,
            wred=wred[1],
            w2=w2[1],
        ),
        dict(spad=spad_s, lapad=mpad_s, k1=tiny_b, s1=mid_f, f2=tiny_f, tot=large, part=small),
        colf_s,
    )
    sync = exchange(b1.part)
    c1 = stage(
        stage_third(d, False),
        "stage_c1",
        dict(common(1), sync=sync, s1=b1.s1, f2=b1.f2, wsp=wsp[1], w3=w3[1]),
        dict(h1=mid_b, k2=tiny_b, s2=mid_f, f3=fast_f, tot=small, part=small),
        cols_s,
    )
    sync = exchange(c1.part)
    d1 = stage(
        stage_fourth(d, True),
        "stage_d1",
        dict(
            common(1),
            sync=sync,
            s2=c1.s2,
            f3=c1.f3,
            we=we[1],
            xpad=d0.ypad,
            cot=a0.cot,
        ),
        dict(h2=mid_b, s3=slow_f, yout=out_fast, dzf=fast_f, tot=small, part=large),
    )
    sync = exchange(d1.part)
    e1 = stage(
        stage_e(d),
        "stage_e1",
        dict(
            common(1),
            sync=sync,
            s3=d1.s3,
            spad=b1.spad,
            cot=slow_in.cot,
            f3=c1.f3,
            dzf=d1.dzf,
            f2=b1.f2,
            w3=w3[1],
            tot_c=d1.tot,
            tot_b=c1.tot,
        ),
        dict(yout=out_slow, dzs=slow_f, df3=fast_b, d2f=tiny_f, tot=large, part=large),
    )
    sync = exchange(e1.part)
    f1 = stage(
        stage_f(d),
        "stage_f1",
        dict(
            common(1),
            sync=sync,
            s3=d1.s3,
            dzs=e1.dzs,
            s2=c1.s2,
            we=we[1],
            d2f=e1.d2f,
            f2=b1.f2,
            f1=d0.f1,
            w2t=w2t[1],
            tot_d=e1.tot,
            tot_c=d1.tot,
            tot_b=c1.tot,
            tot_a=b1.tot,
        ),
        dict(ds3=((rows, cs), BF), d2=mid_f, df2=tiny_b, d1f=tiny_f, tot=large, part=small),
        colf_s,
    )
    sync = exchange(f1.part)
    g1 = stage(
        stage_g(d),
        "stage_g1",
        dict(
            common(1), sync=sync, d2=f1.d2, s2=c1.s2, s1=b1.s1, wsp=wsp[1], tot_c=d1.tot, tot_b=c1.tot
        ),
        dict(ds2=mid_b, d1=mid_f, tot=small, part=small),
        cols_s,
    )
    sync = exchange(g1.part)
    es1 = halves_es(
        "1",
        (sync,),
        h2=d1.h2,
        k2=c1.k2,
        ds3=f1.ds3,
        df3=e1.df3,
        h1=c1.h1,
        k1=b1.k1,
        ds2=g1.ds2,
        df2=f1.df2,
    )
    h1 = stage(
        stage_h(d),
        "stage_h1",
        dict(
            base,
            par=par[1],
            par0=par[0],
            sync=sync,
            d1=g1.d1,
            s1=b1.s1,
            lp=d0.lp,
            wred=wred[1],
            dzs=e1.dzs,
            s3=d0.s3,
            spad=slow_in.spad,
            tot_b=c1.tot,
            tot_a=b1.tot,
        ),
        dict(dpad=mpad_s, dl=mid_f, dzs0=slow_f, tot=small, part=large),
        hold=(es1[0],),
    )
    sync = exchange(h1.part)
    red1 = halves_red("1", (sync,), spad=b1.spad, lapad=b1.lapad, dpad=h1.dpad)
    es_near = run(
        split_near(1),
        "es1_near",
        dict(ids=ids, **pieces_of(es1)),
        shares(inner, es_all // inner),
        dict(mine=((es_all, 256), BF)),
        hold=(sync,),
    )
    i0 = stage(
        stage_i(d),
        "stage_i0",
        dict(
            base,
            par=par[1],
            par0=par[0],
            sync=sync,
            lp=d0.lp,
            f1=d0.f1,
            d1f=f1.d1f,
            dl=h1.dl,
            wa=wa[1],
            dzf=d1.dzf,
            f3=c0.f3,
            xpad=a0.xpad,
            dzs0=h1.dzs0,
            s3=d0.s3,
            s2=c0.s2,
            we=we[0],
            tot_f=g1.tot,
            tot_a=b1.tot,
            tot_c0=d0.tot,
        ),
        dict(gpad=gpad_s, dzf0=fast_f, ds3=((rows, cs), BF), d2=mid_f, tot=large, part=small),
        hold=(red1[0], es_near.to_0),
    )
    sync = exchange(i0.part)
    es_shares = sent_near(targets(es_near, inner))
    first1 = halves_first("1", (sync, *list(es_shares.values())[1:]), xpad=d0.ypad, gpad=i0.gpad)
    es_sum = run(
        sum_shares,
        "es1_sum",
        es_shares,
        dict(out=((es_all // inner, 256), BF)),
        hold=(first1[0],),
    ).out
    red_near = run(
        split_near(2, turned),
        "red1_near",
        dict(ids=ids, **pieces_of(red1, first1)),
        shares(inner, red_all // inner),
        dict(mine=((red_all, 256), BF)),
        hold=(es_sum,),
    )
    j0 = stage(
        stage_j(d),
        "stage_j0",
        dict(
            common(0),
            sync=sync,
            d2=i0.d2,
            s2=c0.s2,
            s1=b0.s1,
            wsp=wsp[0],
            dzf=i0.dzf0,
            f3=c0.f3,
            f2=b0.f2,
            w3=w3[0],
            tot_c=d0.tot,
            tot_b=c0.tot,
        ),
        dict(ds2=mid_b, d1=mid_f, df3=fast_b, d2f=tiny_f, tot=small, part=small),
        cols_s,
        hold=(red_near.to_0, es_sum),
    )
    sync = exchange(j0.part)
    red_sum = run(
        sum_shares,
        "red1_sum",
        sent_near(targets(red_near, inner)),
        dict(out=((red_all // inner, 256), BF)),
        hold=(sync,),
    ).out
    k0 = stage(
        with_grads(
            with_grads(stage_k(d), grads_reduce(d), {}),
            grads_es(d),
            dict(keep="keep_es", send="send_es", halves="halves_es"),
        ),
        "stage_k0",
        dict(
            common(0),
            ids=ids,
            spad=slow_in.spad,
            lapad=b0.lapad,
            h2=d0.h2,
            k2=c0.k2,
            ds3=i0.ds3,
            df3=j0.df3,
            h1=c0.h1,
            k1=b0.k1,
            ds2=j0.ds2,
            sync=sync,
            d1=j0.d1,
            s1=b0.s1,
            lp=a0.lp,
            wred=wred[0],
            d2f=j0.d2f,
            f2=b0.f2,
            f1=a0.f1,
            w2t=w2t[0],
            tot_b=c0.tot,
            tot_a=b0.tot,
        ),
        dict(
            kept(rows_red),
            keep_es=((rows_es, 256), BF),
            send_es=((rows_es, 256), BF),
            dpad=mpad_s,
            dl=mid_f,
            df2=tiny_b,
            d1f=tiny_f,
            tot=small,
            part=small,
        ),
        dict(
            colf_s,
            **cols_s,
            halves=((2, rows_red, 256), BF),
            halves_es=((2, rows_es, 256), BF),
            g2=((quad * d.fb, 9 * quad * d.fb), F32),
            g3=((quad * d.fb, quad * d.cf), F32),
            block=((LANES, LANES), F32),
        ),
        hold=(red_sum,),
    )
    red0, es0 = (k0.keep, across(k0.send)), (k0.keep_es, across(k0.send_es))
    sync = exchange(k0.part)

    order = [sync]

    def step(body, name, ins, outs, scratch=None):
        key = name.rstrip("01")
        made = run(
            body,
            name,
            ins,
            outs,
            scratch,
            hold=(order[-1],),
            groups=groups,
            flops=int(WEIGHT * TIMES.get(key, 0.6)),
        )
        order.append(getattr(made, next(iter(outs))))
        return made

    def block(count):
        return ((count, 256), BF)

    b_all, r_all, f_all = padded(rows_es), padded(rows_red), padded(rows_first)
    b_near, r_near, f_near = b_all // inner, r_all // inner, f_all // inner
    es_near, red_near = es_all // inner, red_all // inner

    def down(name, made, bit, after):
        rows_now = made.keep.shape[0]
        extent = rows_now // 2 if after else rows_now
        outs = dict(keep=block(extent))
        if after:
            outs.update(send=block(extent))
        return step(
            next_far(after),
            "%s_down_%d" % (name, bit),
            dict(ids=ids, own=made.keep, got=over(made.send, bit)),
            outs,
            dict(mine=block(rows_now)),
        )

    def up(name, own, bit):
        return step(
            join_far(bit),
            "%s_up_%d" % (name, bit),
            dict(ids=ids, own=own, got=over(own, bit)),
            dict(out=block(2 * own.shape[0])),
        ).out

    def halved(name, pieces, count, bit):
        return step(
            split_half(len(pieces), bit),
            name + "_split",
            dict(ids=ids, **pieces_of(*pieces)),
            dict(keep=block(count // 2), send=block(count // 2)),
            dict(mine=block(count)),
        )

    far_bits = bits[::-1]
    down_way, turned_way = list(near_bits), near_bits[::-1]

    def merge(name, count, **ins):
        return step(
            merge_far(far_bits[0]),
            name + "_merge",
            dict(ids=ids, **ins),
            dict(keep=block(count // 2), send=block(count // 2)),
            dict(mine=block(count)),
        )

    def apart(name, own, early, late):
        made = step(
            part_far(far_bits[0]),
            name + "_part",
            dict(ids=ids, own=own, got=over(own, far_bits[0])),
            dict(early=block(early), late=block(late)),
            dict(all=block(early + late)),
        )
        return made.early, made.late

    l1 = merge("l1", es_near + red_near, early=es_sum, late=red_sum)
    r_made = halved("r", (red0,), r_all, down_way[0])
    b_made = halved("b", (es0,), b_all, turned_way[0])
    l0 = step(
        stage_l(d),
        "stage_l0",
        dict(
            common(0),
            sync=sync,
            lp=a0.lp,
            f1=a0.f1,
            d1f=k0.d1f,
            dl=k0.dl,
            wa=wa[0],
            dzf=i0.dzf0,
            tot_a=b0.tot,
            ids=ids,
            value=d1.yout,
        ),
        dict(gpad=gpad_s, keep_out=out_fast, send_out=out_fast, tot=small),
    )
    first0 = step(
        grads_first(d),
        "grads_first0",
        dict(ids=ids, xpad=a0.xpad, gpad=l0.gpad),
        kept(rows_first),
        dict(ga=ga_s, halves=((2, rows_first, 256), BF)),
    )
    first0 = (first0.keep, across(first0.send))
    for i, bit in enumerate(far_bits[:-1]):
        l1 = down("l1", l1, bit, far_bits[i + 1])
    slow_out = step(
        stage_slow_out(d),
        "stage_slow_out",
        dict(ids=ids, mask=mask, dpad=k0.dpad, wred=wred[0], dzs=h1.dzs0, value=e1.yout),
        dict(keep_out=out_slow, send_out=out_slow),
    )
    f_made = halved("f", (first0,), f_all, turned_way[0])
    l1 = down("l1", l1, far_bits[-1], 0).keep
    at_1 = dict(
        s1=("h1", 0), s2=("g1", 0), s3=("f1", 0), f1=("g1", 4), f2=("f1", 16), f3=("e1", 16), lp=("i0", 16)
    )
    at_0 = dict(
        s1=("k0", 0), s2=("j0", 0), s3=("i0", 0), f1=("l0", 4), f2=("k0", 4), f3=("j0", 4), lp=("l0", 0)
    )
    norms = step(
        norms_out(d, (at_0, at_1)),
        "norms_out",
        dict(
            ids=ids,
            e1=e1.tot,
            f1=f1.tot,
            g1=g1.tot,
            h1=h1.tot,
            i0=i0.tot,
            j0=j0.tot,
            k0=k0.tot,
            l0=l0.tot,
        ),
        dict(keep=((2, norm_gain.shape[1]), F32), send=((2, norm_gain.shape[1]), F32)),
    )
    r_made = down("r", r_made, down_way[0], (down_way + [0])[1])
    for bit in far_bits[:0:-1]:
        l1 = up("l1", l1, bit)
    b_part, f_part = b_all // 2, f_all // 2
    bf_ins = dict(
        own_0=b_made.keep,
        got_0=over(b_made.send, turned_way[0]),
        own_1=f_made.keep,
        got_1=over(f_made.send, turned_way[0]),
    )
    bf_made = step(
        join_parts((b_part, f_part), (turned_way + [0])[1]),
        "bf_down",
        dict(ids=ids, **bf_ins),
        dict(keep=block((b_part + f_part) // 2), send=block((b_part + f_part) // 2)),
        dict(mine=block(b_part + f_part)),
    )
    for i, bit in enumerate(turned_way[1:-1]):
        b_part, f_part = b_part // 2, f_part // 2
        bf_made = step(
            next_parts((b_part, f_part), turned_way[i + 2]),
            "bf_down_%d" % bit,
            dict(ids=ids, own=bf_made.keep, got=over(bf_made.send, bit)),
            dict(keep=block((b_part + f_part) // 2), send=block((b_part + f_part) // 2)),
            dict(mine=block(b_part + f_part)),
        )
    for i, bit in enumerate(down_way[1:]):
        r_made = down("r", r_made, bit, (down_way + [0])[i + 2])
    es1_all, red1_all = apart("l1", l1, es_near, red_near)
    bf_near = b_near + f_near
    t = merge(
        "t",
        r_near + bf_near,
        early=r_made.keep,
        own=bf_made.keep,
        got=over(bf_made.send, turned_way[-1]),
    )
    for i in range(shift_by - 1):
        es1_all = up("es1", es1_all, down_way[i])
        red1_all = up("red1", red1_all, turned_way[i])
    for i, bit in enumerate(far_bits):
        t = down("t", t, bit, (far_bits + [0])[i + 1])
    t = t.keep
    for bit in far_bits[:0:-1]:
        t = up("t", t, bit)
    r_up, bf_up = apart("t", t, r_near, bf_near)
    es1_all = up("es1", es1_all, down_way[-1])
    red1_all = up("red1", red1_all, turned_way[-1])
    for i in range(shift_by - 1):
        r_up = up("r", r_up, turned_way[i])
        bf_up = up("bf", bf_up, down_way[i])
    def placed(name, made):
        whole = (micro,) + made.keep_out.shape
        return step(
            stage_place,
            "place_" + name,
            dict(ids=ids, keep=made.keep_out, got=across(made.send_out)),
            dict(hbm_out=(whole, BF)),
            dict(both=(whole, BF), sems=sems((2,))),
        ).hbm_out

    placed_fast, placed_slow = placed("fast", l0), placed("slow", slow_out)
    norms = step(
        norms_add,
        "norms_add",
        dict(keep=norms.keep, got=across(norms.send)),
        dict(gain=(norm_gain.shape, F32), shift=(norm_shift.shape, F32)),
    )

    def last(name, own, second, bit):
        made = step(
            join_send(bit),
            name + "_last",
            dict(ids=ids, own=own, got=over(own, bit), second=second),
            dict(out=block(2 * own.shape[0]), send=block(max(2 * own.shape[0], second.shape[0]))),
        )
        return made, across(made.send)

    r_all_up, got_a = last("r", r_up, red1_all, turned_way[-1])
    b_all_up, got_b = last("bf", bf_up, es1_all, down_way[-1])
    spots = dict(
        r=("own_r", "got_a", r_all, r_all, 0),
        red=("own_red", "got_a", red_all, red_all, 0),
        b=("own_b", "got_b", b_near, bf_near, 0),
        f=("own_b", "got_b", f_near, bf_near, b_near),
        es=("own_es", "got_b", es_all, es_all, 0),
    )
    done_red = step(
        finish_reduce(d, spots),
        "finish_reduce",
        dict(ids=ids, own_r=r_all_up.out, own_red=red1_all, got_a=got_a),
        dict(hbm_reduce=(slow_reduce.shape, F32)),
        dict(reduce=((3, cs + d.cl, d.cb), F32), sems=sems((3,))),
    )
    done = step(
        finish_rest(d, spots, rows_red),
        "finish_rest",
        dict(
            ids=ids,
            own_red=red1_all,
            got_a=got_a,
            own_b=b_all_up.out,
            own_es=es1_all,
            got_b=got_b,
        ),
        dict(
            fspace=((1, 9, d.fb, d.fb), F32),
            hbm_expand=(slow_expand.shape, F32),
            hbm_space=((1, 9, d.cb, d.cb), F32),
            fexpand=(fast_expand.shape, F32),
            lateral=(lateral.shape, F32),
            freduce=((1, 3, d.fb, d.cf), F32),
        ),
        dict(
            expand=((d.cb, cs), F32),
            space=((9, d.cb, d.cb), F32),
            block=((LANES, LANES), F32),
            sems=sems((2,)),
        ),
    )
    weights = (
        done_red.hbm_reduce,
        done.hbm_space.reshape(slow_spatial.shape),
        done.hbm_expand,
        jnp.swapaxes(done.freduce, 2, 3),
        done.fspace.reshape(fast_spatial.shape),
        done.fexpand,
        done.lateral,
    )

    return (
        placed_slow.reshape(edge_slow.shape),
        placed_fast.reshape(edge_fast.shape),
        *weights,
        norms.gain,
        norms.shift,
    )


def solution(mesh):
    edge = P("pipe", None, "dp", None, None, None, None)
    weights = (
        P("pipe", None, None, None),
        P("pipe", None, None, None, None),
        P("pipe", None, None),
        P("pipe", None, None, None),
        P("pipe", None, None, None, None),
        P("pipe", None, None),
        P("pipe", None, None, None),
    )
    norms = (P("pipe", None), P("pipe", None))
    return jax.shard_map(
        on_device,
        mesh=mesh,
        in_specs=(edge, edge, *weights, *norms, P(), P()),
        out_specs=(edge, edge, *weights, *norms),
        check_vma=False,
    )
```

```python
from types import SimpleNamespace

import jax
import jax.numpy as jnp
from jax import lax
from jax.experimental import pallas as pl
from jax.experimental.pallas import tpu as pltpu
from jax.sharding import PartitionSpec as P

epsilon = 1e-05
F32 = jnp.float32
BF = jnp.bfloat16
LANES = 128
SPAN = {
    "s1": (0, 2),
    "s2": (2, 2),
    "s3": (4, 8),
    "f1": (12, 1),
    "f2": (13, 1),
    "f3": (14, 1),
    "lp": (15, 2),
}
SHIFT_ROW = 24
TIMES = {
    "grads_es": 2.4,
    "stage_l": 1.8,
    "grads_first": 1.3,
    "stage_slow_out": 1.8,
    "r_split": 1.1,
    "b_split": 1.1,
    "place_fast": 1.7,
    "place_slow": 2.1,
    "finish_reduce": 2.6,
    "finish_rest": 3.4,
}
WEIGHT = 0.0


SMEM_KEYS = ("ids",)


def space_of(key):
    if key in SMEM_KEYS:
        return pltpu.SMEM
    if key.startswith("hbm_"):
        return pltpu.HBM
    if key.startswith("any_"):
        return pl.ANY
    return pltpu.VMEM


def run(body, name, ins, outs, scratch=None, hold=(), far_hold=(), groups=1, flops=2_000_000_000, grant=16):
    scratch = dict(scratch or {})
    outs = dict(outs)
    ins = dict(ins, **{"any_hold%d" % i: value for i, value in enumerate(hold)})
    ins = dict(ins, **{"hbm_hold%d" % i: value for i, value in enumerate(far_hold)})
    shared = "part" in outs
    if shared:
        shape, kind = outs["part"]
        scratch["sums"] = (shape, kind)
        outs["part"] = ((groups,) + shape, kind)
    names = list(ins) + list(outs) + list(scratch)

    def kernel(*refs):
        r = SimpleNamespace(**dict(zip(names, refs)))
        if not shared:
            body(r)
            return
        spread = r.part
        r.part = r.sums
        r.sums[...] = jnp.zeros(r.sums.shape, F32)
        body(r)

        def copy(i, carry):
            spread[i] = r.sums[...]
            return carry

        lax.fori_loop(0, groups, copy, 0)

    result = pl.pallas_call(
        kernel,
        name=name,
        out_shape=[jax.ShapeDtypeStruct(shape, kind) for shape, kind in outs.values()],
        in_specs=[pl.BlockSpec(memory_space=space_of(key)) for key in ins],
        out_specs=[pl.BlockSpec(memory_space=space_of(key)) for key in outs],
        scratch_shapes=[
            pltpu.VMEM(*item) if isinstance(item, tuple) else item for item in scratch.values()
        ],
        compiler_params=pltpu.CompilerParams(vmem_limit_bytes=grant * 1024 * 1024),
        cost_estimate=pl.CostEstimate(flops=flops, bytes_accessed=1000, transcendentals=0),
    )(*ins.values())
    return SimpleNamespace(**dict(zip(outs, result)))


def dot(a, b):
    return lax.dot_general(a, b, (((1,), (0,)), ((), ())), preferred_element_type=F32)


def dot_t(a, b):
    return lax.dot_general(a, b, (((1,), (1,)), ((), ())), preferred_element_type=F32)


def t_dot(a, b):
    return lax.dot_general(a, b, (((0,), (0,)), ((), ())), preferred_element_type=F32)


def sigm(v):
    return 0.5 * jnp.tanh(0.5 * v) + 0.5


def slope_of(v):
    s = sigm(v)
    return s * (1.0 + v * (1.0 - s))


def fold8(x):
    return jnp.sum(x.reshape(x.shape[0] // 8, 8, x.shape[1]), axis=0)


def wide(row, width):
    return row if row.shape[1] == width else jnp.concatenate([row] * (width // row.shape[1]), axis=1)


def lanes_of(block, start, count):
    if count == 1:
        return block[start : start + 1, :]
    return jnp.concatenate([block[start + i : start + i + 1, :] for i in range(count)], axis=1)


def put(part, row, acc8):
    total = jnp.sum(acc8, axis=0, keepdims=True)
    for i in range(total.shape[1] // LANES):
        part[row + i : row + i + 1, :] = total[:, i * LANES : (i + 1) * LANES]


def quarters(acc, width):
    count = acc.shape[1] // width
    total = acc[:, :width]
    for i in range(1, count):
        total = total + acc[:, i * width : (i + 1) * width]
    return total


def folded(tot, width):
    total = tot
    for i in range(1, LANES // width):
        total = total + pltpu.roll(tot, i * width, 1)
    return total


def gain(r, key):
    start, count = SPAN[key]
    return lanes_of(r.par[...], start, count)


def shift(r, key):
    start, count = SPAN[key]
    return lanes_of(r.par[...], SHIFT_ROW + start, count)


def moments(tot, row, key, inv, fast_bottle=32):
    count = SPAN[key][1]
    block = folded(tot, fast_bottle) if key in ("f1", "f2") else tot
    mean = lanes_of(block, row, count) * inv
    square = lanes_of(block, row + count, count) * inv
    return mean, lax.rsqrt(square - mean * mean + epsilon)


def pair_of(tot, row, key, fast_bottle=32):
    count = SPAN[key][1]
    block = folded(tot, fast_bottle) if key in ("f1", "f2") else tot
    return lanes_of(block, row, count), lanes_of(block, row + count, count)


def invs(r):
    return r.inv[0:1, :1], r.inv[1:2, :1]


def norm_of(r, tot, row, key, inv, width=None):
    mean, rs = moments(tot, row, key, inv)
    scale = rs * gain(r, key)
    offset = shift(r, key) - mean * scale
    if width is None:
        return mean, rs, scale, offset
    return tuple(wide(v, width) for v in (mean, rs, scale, offset))


def windows(x, side):
    rows, width = x.shape
    col = lax.broadcasted_iota(jnp.int32, (rows, width), 0) % side
    zero = jnp.zeros((side, width), x.dtype)
    out = {}
    for c in range(3):
        step = c - 1
        if step == 0:
            y = x
        else:
            y = pltpu.roll(x, (-step) % rows, 0)
            y = jnp.where((col + step >= 0) & (col + step < side), y, 0.0)
        out[0, c] = jnp.concatenate([zero, y[: rows - side]], axis=0)
        out[1, c] = y
        out[2, c] = jnp.concatenate([y[side:], zero], axis=0)
    return out


def put_windows(col, at, x, side, back):
    width = x.shape[1]
    for (i, j), y in windows(x, side).items():
        if back:
            i, j = 2 - i, 2 - j
        spot = (i * 3 + j) * width
        col[at, spot : spot + width] = y.astype(BF)


def loop(count, body, init=0):
    return lax.fori_loop(0, count, body, init, unroll=True)


def at_frame(t, cells, lead=0):
    return pl.ds(pl.multiple_of(t * cells, cells) + lead, cells)


def spans(total, step):
    return [(a, step) for a in range(0, total, step)]


def clear_ends(pad, cells):
    rows, width = pad.shape
    zero = jnp.zeros((cells, width), pad.dtype)
    pad[0:cells, :] = zero
    pad[rows - cells : rows, :] = zero


def chosen(r, layer, own, other):
    return jnp.where(r.ids[0] == layer, own, other)


def lane_group(shape, width):
    return lax.div(lax.broadcasted_iota(jnp.int32, shape, 1), width)


def placing(rows, group):
    lane = lax.broadcasted_iota(jnp.int32, (rows, LANES), 1)
    row = lax.broadcasted_iota(jnp.int32, (rows, LANES), 0)
    hit = lax.rem(lane, rows) == row if group is None else lane - group * rows == row
    return jnp.where(hit, 1.0, 0.0).astype(BF)


def first_mix(r, d, xpad, part, row):
    acc_s = acc_q = 0.0
    for a, n in spans(d.rows, d.step):
        got = (
            dot(xpad[a : a + n, 2 * d.cf : 4 * d.cf], r.wa[0 : 2 * d.cf, :])
            + dot(xpad[a + d.cells : a + d.cells + n, :], r.wa[2 * d.cf : 6 * d.cf, :])
            + dot(xpad[a + 2 * d.cells : a + 2 * d.cells + n, 0 : d.cf], r.wa[6 * d.cf : 7 * d.cf, :])
        )
        r.lp[a : a + n, :] = got[:, : d.cl]
        r.f1[a : a + n, :] = got[:, d.cl :]
        acc_s = acc_s + fold8(got)
        acc_q = acc_q + fold8(got * got)
    put(part, row, acc_s[:, : d.cl])
    put(part, row + 2, acc_q[:, : d.cl])
    put(part, row + 4, acc_s[:, d.cl :])
    put(part, row + 5, acc_q[:, d.cl :])


def stage_first(d):
    def body(r):
        sect, group = r.ids[0], r.ids[1]
        small = loading(
            r,
            [
                (r.hbm_lat_own, r.lat_own),
                (r.hbm_lat_other, r.lat_other),
                (r.hbm_fr_own, r.fr_own),
                (r.hbm_fr_other, r.fr_other),
            ],
        )
        large = loading(r, [(r.hbm_own.at[sect], r.own), (r.hbm_other.at[sect], r.other)], 4)

        def present_at(i):
            return 5 + sect * d.groups + i

        def crop_at(i):
            return 5 + (d.micro + sect) * d.groups + i

        def add(i, total):
            extent = r.ids[crop_at(i)]
            return total + jnp.where(r.ids[present_at(i)] > 0, extent * extent, 0)

        area = lax.fori_loop(0, d.groups, add, jnp.int32(0))
        area = jnp.full((1, LANES), area.astype(F32))
        r.inv[...] = jnp.zeros(r.inv.shape, F32)
        r.inv[0:1, :] = 1.0 / (area * d.frames)
        r.inv[1:2, :] = 1.0 / (area * (d.frames * d.quad))
        limit = jnp.where(r.ids[present_at(group)] > 0, r.ids[crop_at(group)], 0)
        cell = lax.broadcasted_iota(jnp.int32, (d.cells, LANES), 0)
        inside = (lax.div(cell, d.side) < limit) & (lax.rem(cell, d.side) < limit)
        mask = jnp.where(inside, 1.0, 0.0)
        r.mask[...] = mask
        small()
        for layer, wa in enumerate((r.wa, r.wa1)):
            for b in range(d.quad + 3):
                row = slice(b * d.cf, (b + 1) * d.cf)
                if b < d.taps:
                    wa[row, : d.cl] = chosen(r, layer, r.lat_own[b], r.lat_other[b])
                else:
                    wa[row, : d.cl] = jnp.zeros((d.cf, d.cl), BF)
                total = jnp.zeros((d.cf, LANES), F32)
                for q in range(d.quad):
                    k = b - 1 - q
                    if 0 <= k < 3:
                        tap = chosen(r, layer, r.fr_own[k], r.fr_other[k])
                        total = total + t_dot(tap, placing(d.fb, q))
                wa[row, d.cl :] = total.astype(BF)
        clear_ends(r.xpad, d.cells)
        large()

        def frame(t, carry):
            for q in range(d.quad):
                here = r.own[t, q].astype(F32)
                there = r.other[t, q].astype(F32)
                value = jnp.where(sect == 0, here, there)
                r.xpad[at_frame(t, d.cells, d.cells), q * d.cf : (q + 1) * d.cf] = (
                    value * mask
                ).astype(BF)
                r.cot[t, q] = jnp.where(sect == 0, there, here).astype(BF)
            return carry

        loop(d.frames, frame)
        first_mix(r, d, r.xpad, r.part, 0)

    return body


def stage_slow_in(d):
    pack = stage_pack(d)

    def body(r):
        sect = r.ids[0]
        names = ("fs", "fe", "gain", "shift")
        small = loading(
            r,
            [
                (getattr(r, "hbm_%s_%s" % (name, side)), getattr(r, "%s_%s" % (name, side)))
                for name in names
                for side in ("own", "other")
            ],
        )
        large = loading(r, [(r.hbm_own.at[sect], r.own), (r.hbm_other.at[sect], r.other)], 8)
        fetch = fetching(r, 0, [(r.hbm_red_own, r.hbm_red_other, r.wred_0)])
        small()
        pack(r)
        large()
        clear_ends(r.spad, d.cells)
        mask = wide(r.mask[...], 256)

        def frame(t, carry):
            for c in range(0, d.cs, 256):
                lane = slice(c, c + 256)
                here = r.own[t, :, lane].astype(F32)
                there = r.other[t, :, lane].astype(F32)
                value = jnp.where(sect == 0, here, there)
                r.spad[at_frame(t, d.cells, d.cells), lane] = (value * mask).astype(BF)
                r.cot[t, :, lane] = jnp.where(sect == 0, there, here).astype(BF)
            return carry

        loop(d.frames, frame)
        fetch()
        for a, n in spans(d.rows, d.step):
            got = 0.0
            for k in range(3):
                b = a + k * d.cells
                got = got + dot(r.spad[b : b + n, :], r.wred_0[k, : d.cs, :])
            r.y[a : a + n, :] = got

    return body


def stage_pack(d):
    sizes = [d.cb, d.cb, d.cs, d.fb, d.fb, d.cf, d.cl]
    keys = ["s1", "s2", "s3", "f1", "f2", "f3", "lp"]

    def body(r):
        spread = placing(d.fb, None)
        for layer in range(2):
            w2, w2t, w3, par = (
                (r.w2_0, r.w2t_0, r.w3_0, r.par_0),
                (r.w2_1, r.w2t_1, r.w3_1, r.par_1),
            )[layer]
            where = lane_group((d.fb, LANES), d.fb)
            for j in range(9):
                tap = chosen(r, layer, r.fs_own[j], r.fs_other[j])
                for out, tiled in ((w2, dot(tap, spread)), (w2t, t_dot(tap, spread))):
                    for q in range(d.quad):
                        row = j * LANES + q * d.fb
                        out[row : row + d.fb, :] = jnp.where(where == q, tiled, 0.0).astype(BF)
            w3[...] = jnp.zeros(w3.shape, BF)
            tap = chosen(r, layer, r.fe_own[...], r.fe_other[...])
            for q in range(d.quad):
                w3[q * d.fb : (q + 1) * d.fb, q * d.cf : (q + 1) * d.cf] = tap
            par[...] = jnp.zeros(par.shape, F32)
            for base, own, other in (
                (0, r.gain_own, r.gain_other),
                (SHIFT_ROW, r.shift_own, r.shift_other),
            ):
                values = chosen(r, layer, own[...], other[...])
                offset = 0
                for key, size in zip(keys, sizes):
                    row = base + SPAN[key][0]
                    piece = values[:, offset : offset + size]
                    offset += size
                    if size < LANES:
                        par[row : row + 1, :] = wide(piece, LANES)
                    else:
                        for i in range(size // LANES):
                            par[row + i : row + i + 1, :] = piece[:, i * LANES : (i + 1) * LANES]

    return body


def fetching(r, layer, weights):
    def copies(first):
        return [
            pltpu.make_async_copy(own if first == (layer == 0) else other, out, r.sems.at[i])
            for i, (own, other, out) in enumerate(weights)
        ]

    def each(action):
        for first in (True, False):

            @pl.when(r.ids[0] == 0 if first else r.ids[0] != 0)
            def _():
                for copy in copies(first):
                    action(copy)

    each(lambda copy: copy.start())
    return lambda: each(lambda copy: copy.wait())


def loading(r, pairs, first=0):
    copies = [
        pltpu.make_async_copy(source, target, r.loads.at[first + i])
        for i, (source, target) in enumerate(pairs)
    ]
    for copy in copies:
        copy.start()

    def wait():
        for copy in copies:
            copy.wait()

    return wait


def gate(r):
    r.out[...] = r.part[...]


def sort_out(r, grad, value, at):
    first = r.ids[0] == 0
    grad, value = grad.astype(F32), value.astype(F32)
    r.keep_out[at] = jnp.where(first, grad, value).astype(BF)
    r.send_out[at] = jnp.where(first, value, grad).astype(BF)


def stage_place(r):
    r.mark[...] = jnp.zeros(r.mark.shape, F32)
    copies = []
    for i in range(2):
        for t in range(r.keep.shape[0]):
            keep, got = r.keep[t].astype(F32), r.got[t].astype(F32)
            r.both[i, t] = jnp.where(r.ids[0] == i, keep, got).astype(BF)
        copies.append(pltpu.make_async_copy(r.both.at[i], r.hbm_out.at[i], r.sems.at[i]))
        copies[-1].start()
    for copy in copies:
        copy.wait()


def stage_second(d, row, carried):
    def body(r):
        if not carried:
            fetch = fetching(r, 1, [(r.hbm_red_own, r.hbm_red_other, r.wred_1)])
        tot = jnp.sum(r.sync[...], axis=0)
        r.tot[...] = tot
        inv_s, inv_f = invs(r)
        _, _, lg, lb = norm_of(r, tot, row, "lp", inv_s)
        _, _, fg, fb = norm_of(r, tot, row + 4, "f1", inv_f)
        mask = r.mask[...]
        mask2 = wide(mask, d.cl)
        clear_ends(r.lapad, d.cells)
        if carried:
            clear_ends(r.spad, d.cells)
            _, _, sg, sb = norm_of(SimpleNamespace(par=r.par0), tot, 0, "s3", inv_s)

        def frame(t, carry):
            at = at_frame(t, d.cells)
            up = at_frame(t, d.cells, d.cells)
            v = r.lp[at, :] * lg + lb
            r.lapad[up, :] = (v * sigm(v) * mask2).astype(BF)
            v = r.f1[at, :] * fg + fb
            v = (v * sigm(v) * mask).astype(BF)
            r.k1[at, :] = v
            put_windows(r.colf, at, v.astype(F32), d.side, False)
            if carried:
                for c in range(0, d.cs, 256):
                    z = r.xpad[up, c : c + 256].astype(F32) + (
                        r.s3[at, c : c + 256] * sg[:, c : c + 256] + sb[:, c : c + 256]
                    )
                    r.spad[up, c : c + 256] = (z * sigm(z) * mask2).astype(BF)
            return carry

        loop(d.frames, frame)
        acc_s = acc_q = acc_fs = acc_fq = 0.0
        for a, n in spans(d.rows, d.step):
            got = 0.0 if carried else r.y[a : a + n, :]
            for k in range(3):
                b = a + k * d.cells
                if carried:
                    got = got + dot(r.spad[b : b + n, :], r.wred[k, : d.cs, :])
                got = got + dot(r.lapad[b : b + n, :], r.wred[k, d.cs :, :])
            r.s1[a : a + n, :] = got
            acc_s = acc_s + fold8(got)
            acc_q = acc_q + fold8(got * got)
            got = dot(r.colf[a : a + n, :], r.w2[...])
            r.f2[a : a + n, :] = got
            kept = (got.reshape(n // d.cells, d.cells, got.shape[1]) * mask[None]).reshape(got.shape)
            acc_fs = acc_fs + fold8(kept)
            acc_fq = acc_fq + fold8(kept * got)
        put(r.part, 0, acc_s)
        put(r.part, 2, acc_q)
        put(r.part, 4, acc_fs)
        put(r.part, 5, acc_fq)
        if not carried:
            fetch()

    return body


def stage_third(d, fetched):
    def body(r):
        if fetched:
            fetch = fetching(
                r,
                0,
                [
                    (r.hbm_sp_own, r.hbm_sp_other, r.wsp_0),
                    (r.hbm_ex_own, r.hbm_ex_other, r.we_0),
                ],
            )
        tot = jnp.sum(r.sync[...], axis=0)
        r.tot[...] = tot
        inv_s, inv_f = invs(r)
        _, _, sg, sb = norm_of(r, tot, 0, "s1", inv_s)
        _, _, fg, fb = norm_of(r, tot, 4, "f2", inv_f)
        mask = r.mask[...]
        mask2 = wide(mask, d.cb)

        def frame(t, carry):
            at = at_frame(t, d.cells)
            v = r.s1[at, :] * sg + sb
            v = (v * sigm(v) * mask2).astype(BF)
            r.h1[at, :] = v
            put_windows(r.cols, at, v.astype(F32), d.side, False)
            v = r.f2[at, :] * fg + fb
            r.k2[at, :] = (v * sigm(v) * mask).astype(BF)
            return carry

        loop(d.frames, frame)
        if fetched:
            fetch()
        wsp = r.wsp_0 if fetched else r.wsp
        acc_s = acc_q = acc_fs = acc_fq = 0.0
        for a, n in spans(d.rows, d.step):
            got = dot(r.cols[a : a + n, :], wsp[...])
            r.s2[a : a + n, :] = got
            kept = (got.reshape(n // d.cells, d.cells, got.shape[1]) * mask2[None]).reshape(got.shape)
            acc_s = acc_s + fold8(kept)
            acc_q = acc_q + fold8(kept * got)
            got = dot(r.k2[a : a + n, :], r.w3[...])
            r.f3[a : a + n, :] = got
            acc_fs = acc_fs + fold8(got)
            acc_fq = acc_fq + fold8(got * got)
        put(r.part, 0, acc_s)
        put(r.part, 2, acc_q)
        put(r.part, 4, quarters(acc_fs, d.cf))
        put(r.part, 5, quarters(acc_fq, d.cf))

    return body


def expand_slow(r, d, sg, sb, mask2):
    def frame(t, carry):
        at = at_frame(t, d.cells)
        v = r.s2[at, :] * sg + sb
        r.h2[at, :] = (v * sigm(v) * mask2).astype(BF)
        return carry

    loop(d.frames, frame)
    for c in range(0, d.cs, 256):
        acc_s = acc_q = 0.0
        for a, n in spans(d.rows, d.step):
            got = dot(r.h2[a : a + n, :], r.we[:, c : c + 256])
            r.s3[a : a + n, c : c + 256] = got
            acc_s = acc_s + fold8(got)
            acc_q = acc_q + fold8(got * got)
        put(r.part, c // LANES, acc_s)
        put(r.part, (d.cs + c) // LANES, acc_q)


def stage_fourth(d, last):
    def body(r):
        if not last:
            fetch = fetching(
                r,
                1,
                [
                    (r.hbm_sp_own, r.hbm_sp_other, r.wsp_1),
                    (r.hbm_ex_own, r.hbm_ex_other, r.we_1),
                ],
            )
        tot = jnp.sum(r.sync[...], axis=0)
        r.tot[...] = tot
        inv_s, inv_f = invs(r)
        _, _, sg, sb = norm_of(r, tot, 0, "s2", inv_s)
        fm, fr, fg, fb = norm_of(r, tot, 4, "f3", inv_f)
        mask = r.mask[...]
        mask2 = wide(mask, d.cb)
        expand_slow(r, d, sg, sb, mask2)
        if not last:
            clear_ends(r.ypad, d.cells)

        def frame(t, carry):
            at = at_frame(t, d.cells)
            up = at_frame(t, d.cells, d.cells)
            for q in range(d.quad):
                lane = slice(q * d.cf, (q + 1) * d.cf)
                f3 = r.f3[at, lane]
                z = r.xpad[up, lane].astype(F32) + (f3 * fg + fb)
                s = sigm(z)
                y = (z * s * mask).astype(BF)
                if last:
                    r.yout[t, q] = y
                    grad = r.cot[t, q].astype(F32) * mask * (s * (1.0 + z * (1.0 - s)))
                    r.dzf[at, lane] = grad
                    u = (f3 - fm) * fr
                    carry = (carry[0] + fold8(grad), carry[1] + fold8(grad * u))
                else:
                    r.ypad[up, lane] = y
            return carry

        zero = jnp.zeros((8, d.cf), F32)
        done = loop(d.frames, frame, (zero, zero))
        if last:
            put(r.part, 16, done[0])
            put(r.part, 17, done[1])
        else:
            first_mix(r, d, r.ypad, r.part, 16)
            fetch()

    return body


def fast_back3(r, d, gs, gg, tot_f3, tot_f2, row):
    _, inv_f = invs(r)
    mask = r.mask[...]
    mean, rs = moments(tot_f3, 4, "f3", inv_f)
    factor = rs * gain(r, "f3")
    gs, gg = gs * inv_f, gg * inv_f
    m2, r2, g2, b2 = norm_of(r, tot_f2, 4, "f2", inv_f)

    def frame(t, carry):
        at = at_frame(t, d.cells)
        for q in range(d.quad):
            lane = slice(q * d.cf, (q + 1) * d.cf)
            u = (r.f3[at, lane] - mean) * rs
            r.df3[at, lane] = (factor * (r.dzf[at, lane] - mask * (gs + u * gg))).astype(BF)
        return carry

    loop(d.frames, frame)
    acc_s = acc_q = 0.0
    for a, n in spans(d.rows, d.step):
        got = dot_t(r.df3[a : a + n, :], r.w3[...])
        f2 = r.f2[a : a + n, :]
        kept = (got.reshape(n // d.cells, d.cells, got.shape[1]) * mask[None]).reshape(got.shape)
        kept = kept * slope_of(f2 * g2 + b2)
        r.d2f[a : a + n, :] = kept
        acc_s = acc_s + fold8(kept)
        acc_q = acc_q + fold8(kept * ((f2 - m2) * r2))
    put(r.part, row, acc_s)
    put(r.part, row + 1, acc_q)


def fast_back2(r, d, gs, gg, tot_f2, tot_f1, f1_row, row):
    _, inv_f = invs(r)
    mask = r.mask[...]
    mean, rs = moments(tot_f2, 4, "f2", inv_f)
    factor = rs * gain(r, "f2")
    gs, gg = gs * inv_f, gg * inv_f
    m1, r1, g1, b1 = norm_of(r, tot_f1, f1_row, "f1", inv_f)

    def frame(t, carry):
        at = at_frame(t, d.cells)
        u = (r.f2[at, :] - mean) * rs
        v = (factor * (r.d2f[at, :] - mask * (gs + u * gg))).astype(BF)
        r.df2[at, :] = v
        put_windows(r.colf, at, v.astype(F32), d.side, True)
        return carry

    loop(d.frames, frame)
    acc_s = acc_q = 0.0
    wide_row = d.quad * d.fb
    for a, n in spans(d.rows, d.step):
        got = dot(r.colf[a : a + n, :], r.w2t[...])
        f1 = r.f1[a : a + n, :]
        kept = (got.reshape(n // d.cells, d.cells, got.shape[1]) * mask[None]).reshape(got.shape)
        kept = kept * slope_of(f1 * g1 + b1)
        r.d1f[a : a + n, :] = kept
        acc_s = acc_s + fold8(kept)
        acc_q = acc_q + fold8(kept * ((f1 - m1) * r1))
    put(r.part, row, acc_s)
    put(r.part, row + 1, acc_q)


def fast_back1(r, d, gs, gg, tot_f1, f1_row):
    _, inv_f = invs(r)
    mask = r.mask[...]
    mean, rs = moments(tot_f1, f1_row, "f1", inv_f)
    factor = rs * gain(r, "f1")
    gs, gg = gs * inv_f, gg * inv_f

    def frame(t, carry):
        at = at_frame(t, d.cells)
        u = (r.f1[at, :] - mean) * rs
        r.gpad[at_frame(t, d.cells, d.cells), d.cl :] = (
            factor * (r.d1f[at, :] - mask * (gs + u * gg))
        ).astype(BF)
        return carry

    loop(d.frames, frame)


def lateral_back(r, d, gs, gg, tot_lp, lp_row):
    inv_s, _ = invs(r)
    mask2 = wide(r.mask[...], d.cl)
    mean, rs = moments(tot_lp, lp_row, "lp", inv_s)
    factor = rs * gain(r, "lp")
    gs, gg = gs * inv_s, gg * inv_s

    def frame(t, carry):
        at = at_frame(t, d.cells)
        u = (r.lp[at, :] - mean) * rs
        r.gpad[at_frame(t, d.cells, d.cells), : d.cl] = (
            factor * (r.dl[at, :] - mask2 * (gs + u * gg))
        ).astype(BF)
        return carry

    loop(d.frames, frame)


def fast_input_grad(r, d, a, n):
    c = d.cf
    mid = dot_t(r.gpad[a + d.cells : a + d.cells + n, :], r.wa[2 * c : 6 * c, :])
    late = dot_t(r.gpad[a + 2 * d.cells : a + 2 * d.cells + n, :], r.wa[0 : 2 * c, :])
    early = dot_t(r.gpad[a : a + n, :], r.wa[6 * c : 7 * c, :])
    return [
        mid[:, :c] + early,
        mid[:, c : 2 * c],
        mid[:, 2 * c : 3 * c] + late[:, :c],
        mid[:, 3 * c :] + late[:, c:],
    ]


def slow_back3(r, d, gs, gg, tot_s3, tot_s2, row):
    inv_s, _ = invs(r)
    mask2 = wide(r.mask[...], d.cb)
    mean, rs = moments(tot_s3, 0, "s3", inv_s)
    factor = rs * gain(r, "s3")
    gs, gg = gs * inv_s, gg * inv_s
    m2, r2, g2, b2 = norm_of(r, tot_s2, 0, "s2", inv_s)

    def frame(t, carry):
        at = at_frame(t, d.cells)
        for c in range(0, d.cs, 256):
            lane = slice(c, c + 256)
            u = (r.s3[at, lane] - mean[:, lane]) * rs[:, lane]
            r.ds3[at, lane] = (
                factor[:, lane] * (r.dzs[at, lane] - mask2 * (gs[:, lane] + u * gg[:, lane]))
            ).astype(BF)
        return carry

    loop(d.frames, frame)
    acc_s = acc_q = 0.0
    for a, n in spans(d.rows, d.step):
        got = dot_t(r.ds3[a : a + n, :], r.we[...])
        s2 = r.s2[a : a + n, :]
        kept = (got.reshape(n // d.cells, d.cells, got.shape[1]) * mask2[None]).reshape(got.shape)
        kept = kept * slope_of(s2 * g2 + b2)
        r.d2[a : a + n, :] = kept
        acc_s = acc_s + fold8(kept)
        acc_q = acc_q + fold8(kept * ((s2 - m2) * r2))
    put(r.part, row, acc_s)
    put(r.part, row + 2, acc_q)


def slow_back2(r, d, gs, gg, tot_s2, tot_s1, row):
    inv_s, _ = invs(r)
    mask2 = wide(r.mask[...], d.cb)
    mean, rs = moments(tot_s2, 0, "s2", inv_s)
    factor = rs * gain(r, "s2")
    gs, gg = gs * inv_s, gg * inv_s
    m1, r1, g1, b1 = norm_of(r, tot_s1, 0, "s1", inv_s)

    def frame(t, carry):
        at = at_frame(t, d.cells)
        u = (r.s2[at, :] - mean) * rs
        v = (factor * (r.d2[at, :] - mask2 * (gs + u * gg))).astype(BF)
        r.ds2[at, :] = v
        put_windows(r.cols, at, v.astype(F32), d.side, True)
        return carry

    loop(d.frames, frame)
    acc_s = acc_q = 0.0
    for a, n in spans(d.rows, d.step):
        got = 0.0
        for k in range(9):
            lane = slice(k * d.cb, (k + 1) * d.cb)
            got = got + dot_t(r.cols[a : a + n, lane], r.wsp[lane, :])
        s1 = r.s1[a : a + n, :]
        kept = (got.reshape(n // d.cells, d.cells, got.shape[1]) * mask2[None]).reshape(got.shape)
        kept = kept * slope_of(s1 * g1 + b1)
        r.d1[a : a + n, :] = kept
        acc_s = acc_s + fold8(kept)
        acc_q = acc_q + fold8(kept * ((s1 - m1) * r1))
    put(r.part, row, acc_s)
    put(r.part, row + 2, acc_q)


def slow_back1(r, d, gs, gg, tot_s1, tot_lp, lp_row, row):
    inv_s, _ = invs(r)
    mask2 = wide(r.mask[...], d.cb)
    mean, rs = moments(tot_s1, 0, "s1", inv_s)
    factor = rs * gain(r, "s1")
    gs, gg = gs * inv_s, gg * inv_s
    ml, rl, gl, bl = norm_of(r, tot_lp, lp_row, "lp", inv_s)
    clear_ends(r.dpad, d.cells)

    def frame(t, carry):
        at = at_frame(t, d.cells)
        u = (r.s1[at, :] - mean) * rs
        r.dpad[at_frame(t, d.cells, d.cells), :] = (
            factor * (r.d1[at, :] - mask2 * (gs + u * gg))
        ).astype(BF)
        return carry

    loop(d.frames, frame)
    acc_s = acc_q = 0.0
    for a, n in spans(d.rows, d.step):
        got = slow_input_grad(r, d, a, n, d.cs, d.cs + d.cl)
        lp = r.lp[a : a + n, :]
        kept = (got.reshape(n // d.cells, d.cells, got.shape[1]) * mask2[None]).reshape(got.shape)
        kept = kept * slope_of(lp * gl + bl)
        r.dl[a : a + n, :] = kept
        acc_s = acc_s + fold8(kept)
        acc_q = acc_q + fold8(kept * ((lp - ml) * rl))
    put(r.part, row, acc_s)
    put(r.part, row + 2, acc_q)


def slow_input_grad(r, d, a, n, first, last):
    got = 0.0
    for k in range(3):
        b = a + (2 - k) * d.cells
        got = got + dot_t(r.dpad[b : b + n, :], r.wred[k, first:last, :])
    return got


def masked(x, mask, d):
    return (x.reshape(x.shape[0] // d.cells, d.cells, x.shape[1]) * mask[None]).reshape(x.shape)


def stage_e(d):
    def body(r):
        tot = jnp.sum(r.sync[...], axis=0)
        r.tot[...] = tot
        inv_s, _ = invs(r)
        mean, rs, sg, sb = norm_of(r, tot, 0, "s3", inv_s)
        mask2 = wide(r.mask[...], 256)

        def frame(t, carry):
            at = at_frame(t, d.cells)
            up = at_frame(t, d.cells, d.cells)
            sums = []
            for i, c in enumerate(range(0, d.cs, 256)):
                lane = slice(c, c + 256)
                s3 = r.s3[at, lane]
                z = r.spad[up, lane].astype(F32) + (s3 * sg[:, lane] + sb[:, lane])
                s = sigm(z)
                r.yout[t, :, lane] = (z * s * mask2).astype(BF)
                grad = r.cot[t, :, lane].astype(F32) * mask2 * (s * (1.0 + z * (1.0 - s)))
                r.dzs[at, lane] = grad
                u = (s3 - mean[:, lane]) * rs[:, lane]
                sums.append((carry[i][0] + fold8(grad), carry[i][1] + fold8(grad * u)))
            return tuple(sums)

        zero = jnp.zeros((8, 256), F32)
        done = loop(d.frames, frame, tuple((zero, zero) for c in range(0, d.cs, 256)))
        for i, c in enumerate(range(0, d.cs, 256)):
            put(r.part, c // LANES, done[i][0])
            put(r.part, (d.cs + c) // LANES, done[i][1])
        gs, gg = pair_of(tot, 16, "f3")
        fast_back3(r, d, gs, gg, r.tot_c[...], r.tot_b[...], 16)

    return body


def stage_f(d):
    def body(r):
        tot = jnp.sum(r.sync[...], axis=0)
        r.tot[...] = tot
        gs, gg = pair_of(tot, 0, "s3")
        slow_back3(r, d, gs, gg, r.tot_d[...], r.tot_c[...], 0)
        gs, gg = pair_of(tot, 16, "f2")
        fast_back2(r, d, gs, gg, r.tot_b[...], r.tot_a[...], 20, 4)

    return body


def stage_g(d):
    def body(r):
        tot = jnp.sum(r.sync[...], axis=0)
        r.tot[...] = tot
        gs, gg = pair_of(tot, 0, "s2")
        slow_back2(r, d, gs, gg, r.tot_c[...], r.tot_b[...], 0)

    return body


def stage_h(d):
    def body(r):
        tot = jnp.sum(r.sync[...], axis=0)
        r.tot[...] = tot
        inv_s, _ = invs(r)
        gs, gg = pair_of(tot, 0, "s1")
        slow_back1(r, d, gs, gg, r.tot_b[...], r.tot_a[...], 16, 16)
        mask2 = wide(r.mask[...], 256)
        r.par = r.par0
        mean, rs, sg, sb = norm_of(r, r.tot_a[...], 0, "s3", inv_s)
        for c in range(0, d.cs, 256):
            lane = slice(c, c + 256)
            acc_s = acc_q = 0.0
            for a, n in spans(d.rows, d.step):
                got = slow_input_grad(r, d, a, n, c, c + 256)
                got = masked(r.dzs[a : a + n, lane] + got, mask2, d).astype(BF).astype(F32)
                s3 = r.s3[a : a + n, lane]
                z = r.spad[a + d.cells : a + d.cells + n, lane].astype(F32) + (
                    s3 * sg[:, lane] + sb[:, lane]
                )
                grad = got * slope_of(z)
                r.dzs0[a : a + n, lane] = grad
                u = (s3 - mean[:, lane]) * rs[:, lane]
                acc_s = acc_s + fold8(grad)
                acc_q = acc_q + fold8(grad * u)
            put(r.part, c // LANES, acc_s)
            put(r.part, (d.cs + c) // LANES, acc_q)

    return body


def stage_i(d):
    def body(r):
        tot = jnp.sum(r.sync[...], axis=0)
        r.tot[...] = tot
        _, inv_f = invs(r)
        clear_ends(r.gpad, d.cells)
        gs, gg = pair_of(r.tot_f[...], 4, "f1")
        fast_back1(r, d, gs, gg, r.tot_a[...], 20)
        gs, gg = pair_of(tot, 16, "lp")
        lateral_back(r, d, gs, gg, r.tot_a[...], 16)
        r.par = r.par0
        mask = r.mask[...]
        mean, rs, fg, fb = norm_of(r, r.tot_c0[...], 4, "f3", inv_f)
        acc_s = acc_q = 0.0
        for a, n in spans(d.rows, d.step):
            pieces = fast_input_grad(r, d, a, n)
            for q in range(d.quad):
                lane = slice(q * d.cf, (q + 1) * d.cf)
                got = masked(r.dzf[a : a + n, lane] + pieces[q], mask, d).astype(BF).astype(F32)
                f3 = r.f3[a : a + n, lane]
                z = r.xpad[a + d.cells : a + d.cells + n, lane].astype(F32) + (f3 * fg + fb)
                grad = got * slope_of(z)
                r.dzf0[a : a + n, lane] = grad
                acc_s = acc_s + fold8(grad)
                acc_q = acc_q + fold8(grad * ((f3 - mean) * rs))
        put(r.part, 4, acc_s)
        put(r.part, 5, acc_q)
        gs, gg = pair_of(tot, 0, "s3")
        r.dzs = r.dzs0
        slow_back3(r, d, gs, gg, r.tot_a[...], r.tot_c0[...], 0)

    return body


def stage_j(d):
    def body(r):
        tot = jnp.sum(r.sync[...], axis=0)
        r.tot[...] = tot
        gs, gg = pair_of(tot, 0, "s2")
        slow_back2(r, d, gs, gg, r.tot_c[...], r.tot_b[...], 0)
        gs, gg = pair_of(tot, 4, "f3")
        fast_back3(r, d, gs, gg, r.tot_c[...], r.tot_b[...], 4)

    return body


def stage_k(d):
    def body(r):
        tot = jnp.sum(r.sync[...], axis=0)
        r.tot[...] = tot
        gs, gg = pair_of(tot, 0, "s1")
        slow_back1(r, d, gs, gg, r.tot_b[...], r.tot_a[...], 0, 0)
        gs, gg = pair_of(tot, 4, "f2")
        fast_back2(r, d, gs, gg, r.tot_b[...], r.tot_a[...], 4, 4)

    return body


def stage_slow_out(d):
    def body(r):
        mask2 = wide(r.mask[...], 256)
        for c in range(0, d.cs, 256):
            lane = slice(c, c + 256)
            for a, n in spans(d.rows, d.step):
                got = slow_input_grad(r, d, a, n, c, c + 256)
                got = masked(r.dzs[a : a + n, lane] + got, mask2, d)
                for t in range(n // d.cells):
                    at = (a // d.cells + t, slice(None), lane)
                    sort_out(r, got[t * d.cells : (t + 1) * d.cells, :], r.value[at], at)

    return body


def stage_l(d):
    def body(r):
        tot = jnp.sum(r.sync[...], axis=0)
        r.tot[...] = tot
        clear_ends(r.gpad, d.cells)
        gs, gg = pair_of(tot, 4, "f1")
        fast_back1(r, d, gs, gg, r.tot_a[...], 4)
        gs, gg = pair_of(tot, 0, "lp")
        lateral_back(r, d, gs, gg, r.tot_a[...], 0)
        mask = r.mask[...]
        for a, n in spans(d.rows, d.step):
            pieces = fast_input_grad(r, d, a, n)
            for q in range(d.quad):
                lane = slice(q * d.cf, (q + 1) * d.cf)
                got = masked(r.dzf[a : a + n, lane] + pieces[q], mask, d)
                for t in range(n // d.cells):
                    at = (a // d.cells + t, q)
                    sort_out(r, got[t * d.cells : (t + 1) * d.cells, :], r.value[at], at)

    return body


def small_block(r, row, value):
    for half in range(2):
        for i in range(2):
            at = 64 * half + 32 * i
            r.halves[half, row : row + 32, i * LANES : (i + 1) * LANES] = value[
                at : at + 32, :
            ].astype(BF)


def hand_over(r):
    r.keep[...] = r.halves[r.ids[0]]
    r.send[...] = r.halves[1 - r.ids[0]]


def grads_es(d):
    part = d.cb // 2

    def body(r):
        def frame(t, carry):
            at = at_frame(t, d.cells)
            put_windows(r.cols, at, r.ds2[at, :].astype(F32), d.side, True)
            put_windows(r.colf, at, r.df2[at, :].astype(F32), d.side, True)
            return carry

        loop(d.frames, frame)
        row = 0
        turned = r.h2[...].T
        for c in range(0, d.cs, 256):
            got = dot(turned, r.ds3[:, c : c + 256]).astype(BF)
            for half in range(2):
                r.halves[half, row : row + part, :] = got[half * part : (half + 1) * part, :]
            row += part
        turned = r.h1[...].T
        for k in range(9):
            got = dot(turned, r.cols[:, k * d.cb : (k + 1) * d.cb]).astype(BF)
            for half in range(2):
                r.halves[half, row : row + part, :] = got[half * part : (half + 1) * part, :]
            row += part
        r.g2[...] = t_dot(r.k1[...], r.colf[...])
        r.g3[...] = t_dot(r.k2[...], r.df3[...])
        where = lane_group((d.fb, LANES), d.fb)
        for i in range(3):
            total = jnp.zeros((d.fb, LANES), F32)
            for c in range(3):
                for q in range(d.quad):
                    tap = (3 * i + c) * LANES
                    piece = r.g2[q * d.fb : (q + 1) * d.fb, tap : tap + LANES]
                    if c != q:
                        piece = pltpu.roll(piece, ((c - q) * d.fb) % LANES, 1)
                    total = total + jnp.where(where == c, piece, 0.0)
            r.block[i * d.fb : (i + 1) * d.fb, :] = total
        total = jnp.zeros((d.fb, LANES), F32)
        for q in range(d.quad):
            total = total + r.g3[q * d.fb : (q + 1) * d.fb, q * d.cf : (q + 1) * d.cf]
        r.block[3 * d.fb :, :] = total
        small_block(r, row, r.block[...])
        hand_over(r)

    return body


def with_grads(stage_body, grads_body, names):
    def body(r):
        stage_body(r)
        for target, source in names.items():
            setattr(r, target, getattr(r, source))
        grads_body(r)

    return body


def grads_reduce(d):
    split = (d.cs + d.cl) // 2

    def body(r):
        for c in range(0, d.cs + d.cl, 256):
            if c < d.cs:
                source = r.spad[d.cells : d.cells + d.rows, c : c + 256]
            else:
                source = r.lapad[d.cells : d.cells + d.rows, c - d.cs : c - d.cs + 256]
            turned = source.T
            cut = min(max(split - c, 0), 256)
            for k in range(3):
                b = (2 - k) * d.cells
                got = dot(turned, r.dpad[b : b + d.rows, :]).astype(BF)
                if cut > 0:
                    row = k * split + c
                    r.halves[0, row : row + cut, :] = got[:cut, :]
                if cut < 256:
                    row = k * split + c + cut - split
                    r.halves[1, row : row + 256 - cut, :] = got[cut:, :]
        hand_over(r)

    return body


def grads_first(d):
    def body(r):
        c = d.cf
        grad = r.gpad[d.cells : d.cells + d.rows, :]
        r.ga[0 : 2 * c, :] = t_dot(r.xpad[0 : d.rows, 2 * c : 4 * c], grad)
        r.ga[2 * c : 6 * c, :] = t_dot(r.xpad[d.cells : d.cells + d.rows, :], grad)
        r.ga[6 * c :, :] = t_dot(r.xpad[2 * d.cells : 2 * d.cells + d.rows, 0:c], grad)
        row = 0
        for b in range(d.taps):
            for half in range(2):
                at = b * c + half * (c // 2)
                r.halves[half, row : row + c // 2, :] = r.ga[at : at + c // 2, : d.cl].astype(BF)
            row += c // 2
        where = lane_group((c, LANES), d.fb)
        total = jnp.zeros((c, LANES), F32)
        for k in range(3):
            for q in range(d.quad):
                at = (q + k + 1) * c
                piece = r.ga[at : at + c, d.cl :]
                if k != q:
                    piece = pltpu.roll(piece, ((k - q) * d.fb) % LANES, 1)
                total = total + jnp.where(where == k, piece, 0.0)
        small_block(r, row, total)
        hand_over(r)

    return body


def gather_pieces(r, count):
    row = 0
    for i in range(count):
        keep, got = getattr(r, "keep_%d" % i), getattr(r, "got_%d" % i)
        r.mine[row : row + keep.shape[0], :] = (
            keep[...].astype(F32) + got[...].astype(F32)
        ).astype(BF)
        row += keep.shape[0]
    if row < r.mine.shape[0]:
        r.mine[row:, :] = jnp.zeros((r.mine.shape[0] - row, r.mine.shape[1]), BF)


def split_near(count, turned=None):
    def body(r):
        gather_pieces(r, count)
        hand_shares(r, r.mine, r.ids[2 if turned is None else 4], turned)

    return body


def split_half(count, bit):
    def body(r):
        gather_pieces(r, count)
        halve(r, bit)

    return body


def hand_shares(r, source, place, turned=None):
    k = 0
    while hasattr(r, "to_%d" % k):
        target = getattr(r, "to_%d" % k)
        rows = target.shape[0]
        start = pl.multiple_of((place ^ (k if turned is None else turned[k])) * rows, 16)
        target[...] = source[pl.ds(start, rows), :]
        k += 1


def add_shares(r):
    total = r.from_0[...].astype(F32)
    k = 1
    while hasattr(r, "from_%d" % k):
        total = total + getattr(r, "from_%d" % k)[...].astype(F32)
        k += 1
    return total.astype(BF)


def sum_shares(r):
    r.out[...] = add_shares(r)


def sum_and_share(r):
    r.mine[...] = add_shares(r)
    hand_shares(r, r.mine, r.ids[3])


def collect(which):
    def body(r):
        rows = r.from_0.shape[0]
        k = 0
        while hasattr(r, "from_%d" % k):
            start = pl.multiple_of((r.ids[which] ^ k) * rows, 16)
            r.out[pl.ds(start, rows), :] = getattr(r, "from_%d" % k)[...]
            k += 1

    return body


def halve(r, bit):
    rows = r.keep.shape[0]
    mine = jnp.where((r.ids[1] & bit) > 0, 1, 0)
    r.keep[...] = r.mine[pl.ds(pl.multiple_of(mine * rows, 16), rows), :]
    r.send[...] = r.mine[pl.ds(pl.multiple_of((1 - mine) * rows, 16), rows), :]


def split_far(bit):
    def body(r):
        rows = r.early.shape[0]
        r.mine[0:rows, :] = r.early[...]
        r.mine[rows:, :] = add_shares(r)
        halve(r, bit)

    return body


def next_far(bit):
    def body(r):
        total = (r.own[...].astype(F32) + r.got[...].astype(F32)).astype(BF)
        if bit:
            r.mine[...] = total
            halve(r, bit)
        else:
            r.keep[...] = total

    return body


def join_far(bit):
    def body(r):
        rows = r.own.shape[0]
        mine = jnp.where((r.ids[1] & bit) > 0, 1, 0)
        r.out[pl.ds(pl.multiple_of(mine * rows, 16), rows), :] = r.own[...]
        r.out[pl.ds(pl.multiple_of((1 - mine) * rows, 16), rows), :] = r.got[...]

    return body


def join_last(bit):
    def body(r):
        rows = r.own.shape[0]
        mine = jnp.where((r.ids[1] & bit) > 0, 1, 0)
        r.all[pl.ds(pl.multiple_of(mine * rows, 16), rows), :] = r.own[...]
        r.all[pl.ds(pl.multiple_of((1 - mine) * rows, 16), rows), :] = r.got[...]
        cut = r.es.shape[0]
        r.es[...] = r.all[0:cut, :]
        r.red[...] = r.all[cut:, :]

    return body


def halve_parts(r, sizes, bit):
    mine = jnp.where((r.ids[1] & bit) > 0, 1, 0)
    start = done = 0
    for size in sizes:
        half = size // 2
        at = slice(done, done + half)
        r.keep[at, :] = r.mine[pl.ds(pl.multiple_of(start + mine * half, 16), half), :]
        r.send[at, :] = r.mine[pl.ds(pl.multiple_of(start + (1 - mine) * half, 16), half), :]
        start += size
        done += half


def join_parts(sizes, bit):
    def body(r):
        start = 0
        for i, size in enumerate(sizes):
            own, got = getattr(r, "own_%d" % i), getattr(r, "got_%d" % i)
            r.mine[start : start + size, :] = (own[...].astype(F32) + got[...].astype(F32)).astype(BF)
            start += size
        halve_parts(r, sizes, bit)

    return body


def next_parts(sizes, bit):
    def body(r):
        r.mine[...] = (r.own[...].astype(F32) + r.got[...].astype(F32)).astype(BF)
        halve_parts(r, sizes, bit)

    return body


def merge_far(bit):
    def body(r):
        rows = r.early.shape[0]
        r.mine[0:rows, :] = r.early[...]
        if hasattr(r, "own"):
            late = (r.own[...].astype(F32) + r.got[...].astype(F32)).astype(BF)
        else:
            late = r.late[...]
        r.mine[rows:, :] = late
        halve(r, bit)

    return body


def part_far(bit):
    def body(r):
        rows = r.own.shape[0]
        mine = jnp.where((r.ids[1] & bit) > 0, 1, 0)
        r.all[pl.ds(pl.multiple_of(mine * rows, 16), rows), :] = r.own[...]
        r.all[pl.ds(pl.multiple_of((1 - mine) * rows, 16), rows), :] = r.got[...]
        cut = r.early.shape[0]
        r.early[...] = r.all[0:cut, :]
        r.late[...] = r.all[cut:, :]

    return body


def join_send(bit):
    def body(r):
        join_far(bit)(r)

        @pl.when(r.ids[0] == 0)
        def _():
            r.send[0 : r.second.shape[0], :] = r.second[...]

        @pl.when(r.ids[0] != 0)
        def _():
            r.send[0 : r.out.shape[0], :] = r.out[...]

    return body


def add_near(r):
    rows = r.got.shape[1]
    total = r.got[0].astype(F32)
    for i in range(1, r.got.shape[0]):
        total = total + r.got[i].astype(F32)
    r.out[0:rows, :] = total.astype(BF)
    r.out[rows:, :] = add_shares(r)


def add_up(r):
    total = jnp.zeros(r.got.shape[1:], F32)
    for i in range(r.got.shape[0]):
        total = total + r.got[i].astype(F32)
    total = total.astype(BF)
    if len(r.out.shape) == len(total.shape):
        r.out[...] = total
    else:
        for i in range(r.out.shape[0]):
            r.out[i] = total


def spread_out(r):
    for i in range(r.out.shape[0]):
        r.out[i] = r.got[...]


def store_half(r, spots, half, out, here_at, there_at, count, lanes=slice(None)):
    done = 0
    while done < count:
        step = count - done
        found = []
        for (kind, row), mine in ((here_at, half == 0), (there_at, half == 1)):
            own, got, piece, stride, offset = spots[kind]
            i, rest = divmod(row + done, piece)
            step = min(step, piece - rest)
            found.append((getattr(r, own if mine else got), i * stride + offset + rest))
        (first, at_0), (second, at_1) = found
        out[done : done + step, :] = jnp.where(
            r.ids[0] == 0,
            first[at_0 : at_0 + step, lanes].astype(F32),
            second[at_1 : at_1 + step, lanes].astype(F32),
        )
        done += step


def finish_reduce(d, spots):
    split = (d.cs + d.cl) // 2

    def body(r):
        r.mark[...] = jnp.zeros(r.mark.shape, F32)
        copies = []
        for k in range(3):
            for half in range(2):
                out = r.reduce.at[k, half * split : (half + 1) * split, :]
                store_half(r, spots, half, out, ("r", k * split), ("red", k * split), split)
            copies.append(
                pltpu.make_async_copy(r.reduce.at[k], r.hbm_reduce.at[0, k], r.sems.at[k])
            )
            copies[-1].start()
        for copy in copies:
            copy.wait()

    return body


def finish_rest(d, spots, rows_red):
    part = d.cb // 2
    side = d.cf // 2

    def body(r):
        row = 0
        for c in range(0, d.cs, 256):
            for half in range(2):
                out = r.expand.at[half * part : (half + 1) * part, c : c + 256]
                store_half(r, spots, half, out, ("b", row), ("es", row), part)
            row += part
        copies = [pltpu.make_async_copy(r.expand, r.hbm_expand.at[0], r.sems.at[0])]
        copies[-1].start()
        for k in range(9):
            for half in range(2):
                out = r.space.at[k, half * part : (half + 1) * part, :]
                store_half(r, spots, half, out, ("b", row), ("es", row), part)
            row += part
        copies.append(pltpu.make_async_copy(r.space, r.hbm_space.at[0], r.sems.at[1]))
        copies[-1].start()

        def small(here_at, there_at):
            for half in range(2):
                for i in range(2):
                    at = 64 * half + 32 * i
                    lanes = slice(i * LANES, (i + 1) * LANES)
                    store_half(r, spots, half, r.block.at[at : at + 32, :], here_at, there_at, 32, lanes)

        small(("b", row), ("es", row))
        for i in range(3):
            piece = r.block[i * d.fb : (i + 1) * d.fb, :]
            for c in range(3):
                moved = piece if c == 0 else pltpu.roll(piece, LANES - c * d.fb, 1)
                r.fspace[0, 3 * i + c] = moved[:, : d.fb]
        r.fexpand[0] = r.block[3 * d.fb :, :]
        row, row_1 = 0, rows_red
        for tap in range(d.taps):
            for half in range(2):
                out = r.lateral.at[0, tap, half * side : (half + 1) * side, :]
                store_half(r, spots, half, out, ("f", row), ("red", row_1), side)
            row, row_1 = row + side, row_1 + side
        small(("f", row), ("red", row_1))
        turned = r.block[...].T
        for k in range(3):
            r.freduce[0, k] = turned[k * d.fb : (k + 1) * d.fb, :]
        for copy in copies:
            copy.wait()

    return body


def norms_out(d, at):
    def body(r):
        made = []
        for layer in range(2):
            lines = []
            for which in (1, 0):
                pieces = []
                for key in ("s1", "s2", "s3", "f1", "f2", "f3", "lp"):
                    name, row = at[layer][key]
                    tot = getattr(r, name)[...]
                    count = SPAN[key][1]
                    if key in ("f1", "f2"):
                        tot = folded(tot, d.fb)
                    piece = lanes_of(tot, row + which * count, count)
                    pieces.append(piece[:, : d.fb] if key in ("f1", "f2") else piece)
                lines.append(jnp.concatenate(pieces, axis=1))
            made.append(lines)
        for i in range(2):
            r.keep[i : i + 1, :] = jnp.where(r.ids[0] == 0, made[0][i], made[1][i])
            r.send[i : i + 1, :] = jnp.where(r.ids[0] == 0, made[1][i], made[0][i])

    return body


def norms_add(r):
    total = r.keep[...] + r.got[...]
    r.gain[...] = total[0:1, :]
    r.shift[...] = total[1:2, :]


def on_device(
    edge_slow,
    edge_fast,
    slow_reduce,
    slow_spatial,
    slow_expand,
    fast_reduce,
    fast_spatial,
    fast_expand,
    lateral,
    norm_gain,
    norm_shift,
    present,
    crop_side,
):
    micro, _, frames, side, _, cs = edge_slow.shape[1:]
    cells = side * side
    fast_frames = edge_fast.shape[3]
    quad = fast_frames // frames
    d = SimpleNamespace(
        frames=frames,
        side=side,
        cells=cells,
        rows=frames * cells,
        step=min(256, frames * cells),
        quad=quad,
        cs=cs,
        cb=slow_expand.shape[1],
        cf=edge_fast.shape[-1],
        fb=fast_expand.shape[1],
        cl=lateral.shape[3],
    )
    d.taps = lateral.shape[1]
    d.micro = micro
    d.groups = lax.axis_size("dp")
    groups = d.groups
    rows, pads = d.rows, d.rows + 2 * cells
    swap = [(0, 1), (1, 0)]
    own_slow = edge_slow.reshape(micro, frames, cells, cs)
    own_fast = edge_fast.reshape(micro, frames, quad, cells, d.cf)

    def across(value, pairs=swap):
        return lax.ppermute(value, "pipe", pairs)

    inner = 1
    while 4 * inner * inner <= groups:
        inner *= 2
    outer = groups // inner
    group = lax.axis_index("dp")
    sect = lax.axis_index("pipe")
    shift_by = inner.bit_length() - 1
    turned = [
        sum(((i >> b) & 1) << (shift_by - 1 - b) for b in range(shift_by)) for i in range(inner)
    ]
    turned_place = jnp.int32(0)
    for b in range(shift_by):
        turned_place += (lax.shift_right_logical(group, jnp.int32(b)) & 1) << (shift_by - 1 - b)
    far_place = lax.shift_right_logical(group, jnp.int32(shift_by))
    ids = jnp.stack([sect, group, group & (inner - 1), far_place, turned_place]).astype(jnp.int32)
    meta = jnp.concatenate([ids, present.reshape(-1), crop_side.reshape(-1)])
    own_fast, lat_own, fr_own, ids = lax.optimization_barrier(
        (own_fast, lateral[0], jnp.swapaxes(fast_reduce[0], 1, 2), ids)
    )
    other_fast, lat_other, fr_other = across(own_fast), across(lat_own), across(fr_own)
    red_own, own_slow, fr_other, lat_other, other_fast, meta = lax.optimization_barrier(
        (slow_reduce[0], own_slow, fr_other, lat_other, other_fast, meta)
    )
    other_slow, red_other = across(own_slow), across(red_own)
    sems = pltpu.SemaphoreType.DMA

    def stage(*args, **others):
        return run(*args, groups=groups, **others)

    def exchange(part):
        return lax.all_to_all(part, "dp", 0, 0)

    slow_f = ((rows, cs), F32)
    mid_f = ((rows, d.cb), F32)
    fast_f = ((rows, quad * d.cf), F32)
    tiny_f = ((rows, quad * d.fb), F32)
    mid_b = ((rows, d.cb), BF)
    tiny_b = ((rows, quad * d.fb), BF)
    fast_b = ((rows, quad * d.cf), BF)
    small = ((8, LANES), F32)
    large = ((24, LANES), F32)
    xpad_s = ((pads, quad * d.cf), BF)
    spad_s = ((pads, cs), BF)
    mpad_s = ((pads, d.cb), BF)
    gpad_s = ((pads, d.cl + quad * d.fb), BF)
    cols_s = {"cols": ((rows, 9 * d.cb), BF)}
    colf_s = {"colf": ((rows, 9 * quad * d.fb), BF)}
    wa_s = (((quad + 3) * d.cf, d.cl + quad * d.fb), BF)

    out_fast = ((frames, quad, cells, d.cf), BF)
    out_slow = ((frames, cells, cs), BF)
    a0 = stage(
        stage_first(d),
        "stage_a0",
        dict(
            ids=meta,
            hbm_own=own_fast,
            hbm_other=other_fast,
            hbm_lat_own=lat_own,
            hbm_lat_other=lat_other,
            hbm_fr_own=fr_own,
            hbm_fr_other=fr_other,
        ),
        dict(
            mask=((cells, LANES), F32),
            inv=small,
            wa=wa_s,
            wa1=wa_s,
            xpad=xpad_s,
            cot=out_fast,
            lp=mid_f,
            f1=tiny_f,
            part=small,
        ),
        dict(
            own=out_fast,
            other=out_fast,
            lat_own=(lat_own.shape, BF),
            lat_other=(lat_own.shape, BF),
            fr_own=(fr_own.shape, BF),
            fr_other=(fr_own.shape, BF),
            loads=sems((6,)),
        ),
    )
    fs_own, fe_own, norm_gain, norm_shift, a0_inv = lax.optimization_barrier(
        (fast_spatial.reshape(9, d.fb, d.fb), fast_expand[0], norm_gain, norm_shift, a0.inv)
    )
    fs_other, fe_other = across(fs_own), across(fe_own)
    gain_other, shift_other = across(norm_gain), across(norm_shift)
    mask = a0.mask
    base = dict(mask=mask, inv=a0_inv)
    wa = (a0.wa, a0.wa1)
    rows_es = (cs // 256 + 9) * (d.cb // 2) + 32
    rows_red = 3 * (cs + d.cl) // 2
    rows_first = d.taps * (d.cf // 2) + 32

    def halves_of(body, name, rows_now, ins, scratch, hold):
        made = run(
            body,
            name,
            dict(ids=ids, **ins),
            dict(keep=((rows_now, 256), BF), send=((rows_now, 256), BF)),
            dict(scratch, halves=((2, rows_now, 256), BF)),
            hold=hold,
        )
        return made.keep, across(made.send)

    def halves_es(name, hold, **ins):
        scratch = dict(
            cols_s,
            **colf_s,
            g2=((quad * d.fb, 9 * quad * d.fb), F32),
            g3=((quad * d.fb, quad * d.cf), F32),
            block=((LANES, LANES), F32),
        )
        return halves_of(grads_es(d), "grads_es" + name, rows_es, ins, scratch, hold)

    def halves_red(name, hold, **ins):
        return halves_of(grads_reduce(d), "grads_red" + name, rows_red, ins, {}, hold)

    def halves_first(name, hold, **ins):
        scratch = dict(ga=(((quad + 3) * d.cf, d.cl + quad * d.fb), F32))
        return halves_of(grads_first(d), "grads_first" + name, rows_first, ins, scratch, hold)

    def padded(count):
        unit = 16 * groups
        return -(-count // unit) * unit

    es_all, red_all = padded(rows_es), padded(rows_red + rows_first)
    ga_s = (((quad + 3) * d.cf, d.cl + quad * d.fb), F32)

    def kept(count):
        return dict(keep=((count, 256), BF), send=((count, 256), BF))

    near_1 = (es_all + red_all) // inner

    def shares(count, rows_now):
        return {"to_%d" % k: ((rows_now, 256), BF) for k in range(count)}

    def sent_near(made):
        pairs = lambda k: [(i, i ^ k) for i in range(groups)]
        return {
            "from_%d" % k: made[k] if k == 0 else lax.ppermute(made[k], "dp", pairs(k))
            for k in range(inner)
        }

    bits = [inner << i for i in range(outer.bit_length() - 1)][::-1]
    near_bits = [1 << i for i in range(shift_by)]

    def over(value, bit):
        return lax.ppermute(value, "dp", [(i, i ^ bit) for i in range(groups)])

    def targets(made, count):
        return [getattr(made, "to_%d" % k) for k in range(count)]

    def pieces_of(*pieces):
        return {
            "%s_%d" % (key, i): value
            for i, piece in enumerate(pieces)
            for key, value in zip(("keep", "got"), piece)
        }

    arrived = (other_slow, red_other, fs_other, fe_other, gain_other, shift_other)
    part = run(gate, "gate", dict(part=a0.part), dict(out=(a0.part.shape, F32)), far_hold=arrived).out
    sync = exchange(part)
    sp_own, ex_own, sync = lax.optimization_barrier(
        (slow_spatial.reshape(9 * d.cb, d.cb), slow_expand[0], sync)
    )
    sp_other, ex_other = across(sp_own), across(ex_own)
    packed_2 = ((9 * quad * d.fb, quad * d.fb), BF)
    packed_3 = ((quad * d.fb, quad * d.cf), BF)
    norm_s = ((2 * SHIFT_ROW, LANES), F32)
    red_s = (red_own.shape, BF)
    slow_in = pack = stage(
        stage_slow_in(d),
        "stage_slow_in",
        dict(
            ids=ids,
            mask=mask,
            hbm_own=own_slow,
            hbm_other=other_slow,
            hbm_red_own=red_own,
            hbm_red_other=red_other,
            hbm_fs_own=fs_own,
            hbm_fs_other=fs_other,
            hbm_fe_own=fe_own,
            hbm_fe_other=fe_other,
            hbm_gain_own=norm_gain,
            hbm_gain_other=gain_other,
            hbm_shift_own=norm_shift,
            hbm_shift_other=shift_other,
        ),
        dict(
            spad=spad_s,
            cot=out_slow,
            y=mid_f,
            wred_0=red_s,
            w2_0=packed_2,
            w2_1=packed_2,
            w2t_0=packed_2,
            w2t_1=packed_2,
            w3_0=packed_3,
            w3_1=packed_3,
            par_0=norm_s,
            par_1=norm_s,
        ),
        dict(
            own=out_slow,
            other=out_slow,
            fs_own=(fs_own.shape, BF),
            fs_other=(fs_own.shape, BF),
            fe_own=(fe_own.shape, BF),
            fe_other=(fe_own.shape, BF),
            gain_own=(norm_gain.shape, F32),
            gain_other=(norm_gain.shape, F32),
            shift_own=(norm_gain.shape, F32),
            shift_other=(norm_gain.shape, F32),
            loads=sems((10,)),
            sems=sems((1,)),
        ),
        hold=(sync,),
    )
    w2, w2t = (pack.w2_0, pack.w2_1), (pack.w2t_0, pack.w2t_1)
    w3, par = (pack.w3_0, pack.w3_1), (pack.par_0, pack.par_1)

    def common(layer):
        return dict(base, par=par[layer])

    b0 = stage(
        stage_second(d, 0, False),
        "stage_b0",
        dict(
            common(0),
            sync=sync,
            lp=a0.lp,
            f1=a0.f1,
            y=slow_in.y,
            wred=slow_in.wred_0,
            w2=w2[0],
            ids=ids,
            hbm_red_own=red_own,
            hbm_red_other=red_other,
        ),
        dict(
            lapad=mpad_s,
            k1=tiny_b,
            s1=mid_f,
            f2=tiny_f,
            tot=small,
            wred_1=red_s,
            part=small,
        ),
        dict(colf_s, sems=sems((1,))),
        far_hold=(sp_other, ex_other),
    )
    sync = exchange(b0.part)
    wred = (slow_in.wred_0, b0.wred_1)
    c0 = stage(
        stage_third(d, True),
        "stage_c0",
        dict(
            common(0),
            ids=ids,
            sync=sync,
            s1=b0.s1,
            f2=b0.f2,
            w3=w3[0],
            hbm_sp_own=sp_own,
            hbm_sp_other=sp_other,
            hbm_ex_own=ex_own,
            hbm_ex_other=ex_other,
        ),
        dict(
            h1=mid_b,
            k2=tiny_b,
            s2=mid_f,
            f3=fast_f,
            tot=small,
            wsp_0=(sp_own.shape, BF),
            we_0=(ex_own.shape, BF),
            part=small,
        ),
        dict(cols_s, sems=sems((2,))),
    )
    sync = exchange(c0.part)
    d0 = stage(
        stage_fourth(d, False),
        "stage_d0",
        dict(common(0), sync=sync, s2=c0.s2, f3=c0.f3, we=c0.we_0,
            ids=ids,
            hbm_sp_own=sp_own,
            hbm_sp_other=sp_other,
            hbm_ex_own=ex_own,
            hbm_ex_other=ex_other, xpad=a0.xpad, wa=wa[1]),
        dict(h2=mid_b, s3=slow_f, ypad=xpad_s, lp=mid_f, f1=tiny_f, tot=small, wsp_1=(sp_own.shape, BF), we_1=(ex_own.shape, BF), part=large),
        dict(sems=sems((2,))),
    )
    sync = exchange(d0.part)
    we, wsp = (c0.we_0, d0.we_1), (c0.wsp_0, d0.wsp_1)
    b1 = stage(
        stage_second(d, 16, True),
        "stage_b1",
        dict(
            base,
            par=par[1],
            par0=par[0],
            sync=sync,
            lp=d0.lp,
            f1=d0.f1,
            s3=d0.s3,
            xpad=slow_in.spad,
            wred=wred[1],
            w2=w2[1],
        ),
        dict(spad=spad_s, lapad=mpad_s, k1=tiny_b, s1=mid_f, f2=tiny_f, tot=large, part=small),
        colf_s,
    )
    sync = exchange(b1.part)
    c1 = stage(
        stage_third(d, False),
        "stage_c1",
        dict(common(1), sync=sync, s1=b1.s1, f2=b1.f2, wsp=wsp[1], w3=w3[1]),
        dict(h1=mid_b, k2=tiny_b, s2=mid_f, f3=fast_f, tot=small, part=small),
        cols_s,
    )
    sync = exchange(c1.part)
    d1 = stage(
        stage_fourth(d, True),
        "stage_d1",
        dict(
            common(1),
            sync=sync,
            s2=c1.s2,
            f3=c1.f3,
            we=we[1],
            xpad=d0.ypad,
            cot=a0.cot,
        ),
        dict(h2=mid_b, s3=slow_f, yout=out_fast, dzf=fast_f, tot=small, part=large),
    )
    sync = exchange(d1.part)
    e1 = stage(
        stage_e(d),
        "stage_e1",
        dict(
            common(1),
            sync=sync,
            s3=d1.s3,
            spad=b1.spad,
            cot=slow_in.cot,
            f3=c1.f3,
            dzf=d1.dzf,
            f2=b1.f2,
            w3=w3[1],
            tot_c=d1.tot,
            tot_b=c1.tot,
        ),
        dict(yout=out_slow, dzs=slow_f, df3=fast_b, d2f=tiny_f, tot=large, part=large),
    )
    sync = exchange(e1.part)
    f1 = stage(
        stage_f(d),
        "stage_f1",
        dict(
            common(1),
            sync=sync,
            s3=d1.s3,
            dzs=e1.dzs,
            s2=c1.s2,
            we=we[1],
            d2f=e1.d2f,
            f2=b1.f2,
            f1=d0.f1,
            w2t=w2t[1],
            tot_d=e1.tot,
            tot_c=d1.tot,
            tot_b=c1.tot,
            tot_a=b1.tot,
        ),
        dict(ds3=((rows, cs), BF), d2=mid_f, df2=tiny_b, d1f=tiny_f, tot=large, part=small),
        colf_s,
    )
    sync = exchange(f1.part)
    g1 = stage(
        stage_g(d),
        "stage_g1",
        dict(
            common(1), sync=sync, d2=f1.d2, s2=c1.s2, s1=b1.s1, wsp=wsp[1], tot_c=d1.tot, tot_b=c1.tot
        ),
        dict(ds2=mid_b, d1=mid_f, tot=small, part=small),
        cols_s,
    )
    sync = exchange(g1.part)
    es1 = halves_es(
        "1",
        (sync,),
        h2=d1.h2,
        k2=c1.k2,
        ds3=f1.ds3,
        df3=e1.df3,
        h1=c1.h1,
        k1=b1.k1,
        ds2=g1.ds2,
        df2=f1.df2,
    )
    h1 = stage(
        stage_h(d),
        "stage_h1",
        dict(
            base,
            par=par[1],
            par0=par[0],
            sync=sync,
            d1=g1.d1,
            s1=b1.s1,
            lp=d0.lp,
            wred=wred[1],
            dzs=e1.dzs,
            s3=d0.s3,
            spad=slow_in.spad,
            tot_b=c1.tot,
            tot_a=b1.tot,
        ),
        dict(dpad=mpad_s, dl=mid_f, dzs0=slow_f, tot=small, part=large),
        hold=(es1[0],),
    )
    sync = exchange(h1.part)
    red1 = halves_red("1", (sync,), spad=b1.spad, lapad=b1.lapad, dpad=h1.dpad)
    es_near = run(
        split_near(1),
        "es1_near",
        dict(ids=ids, **pieces_of(es1)),
        shares(inner, es_all // inner),
        dict(mine=((es_all, 256), BF)),
        hold=(sync,),
    )
    i0 = stage(
        stage_i(d),
        "stage_i0",
        dict(
            base,
            par=par[1],
            par0=par[0],
            sync=sync,
            lp=d0.lp,
            f1=d0.f1,
            d1f=f1.d1f,
            dl=h1.dl,
            wa=wa[1],
            dzf=d1.dzf,
            f3=c0.f3,
            xpad=a0.xpad,
            dzs0=h1.dzs0,
            s3=d0.s3,
            s2=c0.s2,
            we=we[0],
            tot_f=g1.tot,
            tot_a=b1.tot,
            tot_c0=d0.tot,
        ),
        dict(gpad=gpad_s, dzf0=fast_f, ds3=((rows, cs), BF), d2=mid_f, tot=large, part=small),
        hold=(red1[0], es_near.to_0),
    )
    sync = exchange(i0.part)
    es_shares = sent_near(targets(es_near, inner))
    first1 = halves_first("1", (sync, *list(es_shares.values())[1:]), xpad=d0.ypad, gpad=i0.gpad)
    es_sum = run(
        sum_shares,
        "es1_sum",
        es_shares,
        dict(out=((es_all // inner, 256), BF)),
        hold=(first1[0],),
    ).out
    red_near = run(
        split_near(2, turned),
        "red1_near",
        dict(ids=ids, **pieces_of(red1, first1)),
        shares(inner, red_all // inner),
        dict(mine=((red_all, 256), BF)),
        hold=(es_sum,),
    )
    j0 = stage(
        stage_j(d),
        "stage_j0",
        dict(
            common(0),
            sync=sync,
            d2=i0.d2,
            s2=c0.s2,
            s1=b0.s1,
            wsp=wsp[0],
            dzf=i0.dzf0,
            f3=c0.f3,
            f2=b0.f2,
            w3=w3[0],
            tot_c=d0.tot,
            tot_b=c0.tot,
        ),
        dict(ds2=mid_b, d1=mid_f, df3=fast_b, d2f=tiny_f, tot=small, part=small),
        cols_s,
        hold=(red_near.to_0, es_sum),
    )
    sync = exchange(j0.part)
    red_sum = run(
        sum_shares,
        "red1_sum",
        sent_near(targets(red_near, inner)),
        dict(out=((red_all // inner, 256), BF)),
        hold=(sync,),
    ).out
    k0 = stage(
        with_grads(
            with_grads(stage_k(d), grads_reduce(d), {}),
            grads_es(d),
            dict(keep="keep_es", send="send_es", halves="halves_es"),
        ),
        "stage_k0",
        dict(
            common(0),
            ids=ids,
            spad=slow_in.spad,
            lapad=b0.lapad,
            h2=d0.h2,
            k2=c0.k2,
            ds3=i0.ds3,
            df3=j0.df3,
            h1=c0.h1,
            k1=b0.k1,
            ds2=j0.ds2,
            sync=sync,
            d1=j0.d1,
            s1=b0.s1,
            lp=a0.lp,
            wred=wred[0],
            d2f=j0.d2f,
            f2=b0.f2,
            f1=a0.f1,
            w2t=w2t[0],
            tot_b=c0.tot,
            tot_a=b0.tot,
        ),
        dict(
            kept(rows_red),
            keep_es=((rows_es, 256), BF),
            send_es=((rows_es, 256), BF),
            dpad=mpad_s,
            dl=mid_f,
            df2=tiny_b,
            d1f=tiny_f,
            tot=small,
            part=small,
        ),
        dict(
            colf_s,
            **cols_s,
            halves=((2, rows_red, 256), BF),
            halves_es=((2, rows_es, 256), BF),
            g2=((quad * d.fb, 9 * quad * d.fb), F32),
            g3=((quad * d.fb, quad * d.cf), F32),
            block=((LANES, LANES), F32),
        ),
        hold=(red_sum,),
    )
    red0, es0 = (k0.keep, across(k0.send)), (k0.keep_es, across(k0.send_es))
    sync = exchange(k0.part)

    order = [sync]

    def step(body, name, ins, outs, scratch=None, grant=16):
        key = name.rstrip("01")
        made = run(
            body,
            name,
            ins,
            outs,
            scratch,
            hold=(order[-1],),
            groups=groups,
            flops=int(WEIGHT * TIMES.get(key, 0.6)),
            grant=grant,
        )
        order.append(getattr(made, next(iter(outs))))
        return made

    def block(count):
        return ((count, 256), BF)

    b_all, r_all, f_all = padded(rows_es), padded(rows_red), padded(rows_first)
    b_near, r_near, f_near = b_all // inner, r_all // inner, f_all // inner
    es_near, red_near = es_all // inner, red_all // inner

    def down(name, made, bit, after):
        rows_now = made.keep.shape[0]
        extent = rows_now // 2 if after else rows_now
        outs = dict(keep=block(extent))
        if after:
            outs.update(send=block(extent))
        return step(
            next_far(after),
            "%s_down_%d" % (name, bit),
            dict(ids=ids, own=made.keep, got=over(made.send, bit)),
            outs,
            dict(mine=block(rows_now)),
        )

    def up(name, own, bit):
        return step(
            join_far(bit),
            "%s_up_%d" % (name, bit),
            dict(ids=ids, own=own, got=over(own, bit)),
            dict(out=block(2 * own.shape[0])),
        ).out

    def halved(name, pieces, count, bit):
        return step(
            split_half(len(pieces), bit),
            name + "_split",
            dict(ids=ids, **pieces_of(*pieces)),
            dict(keep=block(count // 2), send=block(count // 2)),
            dict(mine=block(count)),
        )

    far_bits = bits[::-1]
    down_way, turned_way = list(near_bits), near_bits[::-1]

    def merge(name, count, **ins):
        return step(
            merge_far(far_bits[0]),
            name + "_merge",
            dict(ids=ids, **ins),
            dict(keep=block(count // 2), send=block(count // 2)),
            dict(mine=block(count)),
        )

    def apart(name, own, early, late):
        made = step(
            part_far(far_bits[0]),
            name + "_part",
            dict(ids=ids, own=own, got=over(own, far_bits[0])),
            dict(early=block(early), late=block(late)),
            dict(all=block(early + late)),
        )
        return made.early, made.late

    l1 = merge("l1", es_near + red_near, early=es_sum, late=red_sum)
    r_made = halved("r", (red0,), r_all, down_way[0])
    b_made = halved("b", (es0,), b_all, turned_way[0])
    l0 = step(
        stage_l(d),
        "stage_l0",
        dict(
            common(0),
            sync=sync,
            lp=a0.lp,
            f1=a0.f1,
            d1f=k0.d1f,
            dl=k0.dl,
            wa=wa[0],
            dzf=i0.dzf0,
            tot_a=b0.tot,
            ids=ids,
            value=d1.yout,
        ),
        dict(gpad=gpad_s, keep_out=out_fast, send_out=out_fast, tot=small),
    )
    first0 = step(
        grads_first(d),
        "grads_first0",
        dict(ids=ids, xpad=a0.xpad, gpad=l0.gpad),
        kept(rows_first),
        dict(ga=ga_s, halves=((2, rows_first, 256), BF)),
    )
    first0 = (first0.keep, across(first0.send))
    for i, bit in enumerate(far_bits[:-1]):
        l1 = down("l1", l1, bit, far_bits[i + 1])
    slow_out = step(
        stage_slow_out(d),
        "stage_slow_out",
        dict(ids=ids, mask=mask, dpad=k0.dpad, wred=wred[0], dzs=h1.dzs0, value=e1.yout),
        dict(keep_out=out_slow, send_out=out_slow),
    )
    f_made = halved("f", (first0,), f_all, turned_way[0])
    r_made = down("r", r_made, down_way[0], (down_way + [0])[1])
    b_part, f_part = b_all // 2, f_all // 2
    bf_ins = dict(
        own_0=b_made.keep,
        got_0=over(b_made.send, turned_way[0]),
        own_1=f_made.keep,
        got_1=over(f_made.send, turned_way[0]),
    )
    bf_made = step(
        join_parts((b_part, f_part), (turned_way + [0])[1]),
        "bf_down",
        dict(ids=ids, **bf_ins),
        dict(keep=block((b_part + f_part) // 2), send=block((b_part + f_part) // 2)),
        dict(mine=block(b_part + f_part)),
    )
    for i, bit in enumerate(turned_way[1:-1]):
        b_part, f_part = b_part // 2, f_part // 2
        bf_made = step(
            next_parts((b_part, f_part), turned_way[i + 2]),
            "bf_down_%d" % bit,
            dict(ids=ids, own=bf_made.keep, got=over(bf_made.send, bit)),
            dict(keep=block((b_part + f_part) // 2), send=block((b_part + f_part) // 2)),
            dict(mine=block(b_part + f_part)),
        )
    l1 = down("l1", l1, far_bits[-1], 0).keep
    at_1 = dict(
        s1=("h1", 0), s2=("g1", 0), s3=("f1", 0), f1=("g1", 4), f2=("f1", 16), f3=("e1", 16), lp=("i0", 16)
    )
    at_0 = dict(
        s1=("k0", 0), s2=("j0", 0), s3=("i0", 0), f1=("l0", 4), f2=("k0", 4), f3=("j0", 4), lp=("l0", 0)
    )
    norms = step(
        norms_out(d, (at_0, at_1)),
        "norms_out",
        dict(
            ids=ids,
            e1=e1.tot,
            f1=f1.tot,
            g1=g1.tot,
            h1=h1.tot,
            i0=i0.tot,
            j0=j0.tot,
            k0=k0.tot,
            l0=l0.tot,
        ),
        dict(keep=((2, norm_gain.shape[1]), F32), send=((2, norm_gain.shape[1]), F32)),
    )
    for bit in far_bits[:0:-1]:
        l1 = up("l1", l1, bit)
    for i, bit in enumerate(down_way[1:]):
        r_made = down("r", r_made, bit, (down_way + [0])[i + 2])
    bf_near = b_near + f_near
    t = merge(
        "t",
        r_near + bf_near,
        early=r_made.keep,
        own=bf_made.keep,
        got=over(bf_made.send, turned_way[-1]),
    )
    es1_all, red1_all = apart("l1", l1, es_near, red_near)
    def placed(name, made):
        whole = (micro,) + made.keep_out.shape
        return step(
            stage_place,
            "place_" + name,
            dict(ids=ids, keep=made.keep_out, got=across(made.send_out)),
            dict(mark=small, hbm_out=(whole, BF)),
            dict(both=(whole, BF), sems=sems((2,))),
        ).hbm_out

    placed_fast = placed("fast", l0)
    for i in range(shift_by - 1):
        es1_all = up("es1", es1_all, down_way[i])
        red1_all = up("red1", red1_all, turned_way[i])
    for i, bit in enumerate(far_bits):
        t = down("t", t, bit, (far_bits + [0])[i + 1])
        if i == 0:
            placed_slow = placed("slow", slow_out)
    t = t.keep
    for bit in far_bits[:0:-1]:
        t = up("t", t, bit)
    r_up, bf_up = apart("t", t, r_near, bf_near)
    es1_all = up("es1", es1_all, down_way[-1])
    red1_all = up("red1", red1_all, turned_way[-1])
    for i in range(shift_by - 1):
        r_up = up("r", r_up, turned_way[i])
        bf_up = up("bf", bf_up, down_way[i])
    norms = step(
        norms_add,
        "norms_add",
        dict(keep=norms.keep, got=across(norms.send)),
        dict(gain=(norm_gain.shape, F32), shift=(norm_shift.shape, F32)),
    )

    def last(name, own, second, bit):
        made = step(
            join_send(bit),
            name + "_last",
            dict(ids=ids, own=own, got=over(own, bit), second=second),
            dict(out=block(2 * own.shape[0]), send=block(max(2 * own.shape[0], second.shape[0]))),
        )
        return made, across(made.send)

    r_all_up, got_a = last("r", r_up, red1_all, turned_way[-1])
    b_all_up, got_b = last("bf", bf_up, es1_all, down_way[-1])
    spots = dict(
        r=("own_r", "got_a", r_all, r_all, 0),
        red=("own_red", "got_a", red_all, red_all, 0),
        b=("own_b", "got_b", b_near, bf_near, 0),
        f=("own_b", "got_b", f_near, bf_near, b_near),
        es=("own_es", "got_b", es_all, es_all, 0),
    )
    done_red = step(
        finish_reduce(d, spots),
        "finish_reduce",
        dict(ids=ids, own_r=r_all_up.out, own_red=red1_all, got_a=got_a),
        dict(mark=small, hbm_reduce=(slow_reduce.shape, F32)),
        dict(reduce=((3, cs + d.cl, d.cb), F32), sems=sems((3,))),
    )
    done = step(
        finish_rest(d, spots, rows_red),
        "finish_rest",
        dict(
            ids=ids,
            own_red=red1_all,
            got_a=got_a,
            own_b=b_all_up.out,
            own_es=es1_all,
            got_b=got_b,
        ),
        dict(
            fspace=((1, 9, d.fb, d.fb), F32),
            hbm_expand=(slow_expand.shape, F32),
            hbm_space=((1, 9, d.cb, d.cb), F32),
            fexpand=(fast_expand.shape, F32),
            lateral=(lateral.shape, F32),
            freduce=((1, 3, d.fb, d.cf), F32),
        ),
        dict(
            expand=((d.cb, cs), F32),
            space=((9, d.cb, d.cb), F32),
            block=((LANES, LANES), F32),
            sems=sems((2,)),
        ),
    )
    weights = (
        done_red.hbm_reduce,
        done.hbm_space.reshape(slow_spatial.shape),
        done.hbm_expand,
        jnp.swapaxes(done.freduce, 2, 3),
        done.fspace.reshape(fast_spatial.shape),
        done.fexpand,
        done.lateral,
    )

    return (
        placed_slow.reshape(edge_slow.shape),
        placed_fast.reshape(edge_fast.shape),
        *weights,
        norms.gain,
        norms.shift,
    )


def solution(mesh):
    edge = P("pipe", None, "dp", None, None, None, None)
    weights = (
        P("pipe", None, None, None),
        P("pipe", None, None, None, None),
        P("pipe", None, None),
        P("pipe", None, None, None),
        P("pipe", None, None, None, None),
        P("pipe", None, None),
        P("pipe", None, None, None),
    )
    norms = (P("pipe", None), P("pipe", None))
    return jax.shard_map(
        on_device,
        mesh=mesh,
        in_specs=(edge, edge, *weights, *norms, P(), P()),
        out_specs=(edge, edge, *weights, *norms),
        check_vma=False,
    )
```

```python
from types import SimpleNamespace

import jax
import jax.numpy as jnp
from jax import lax
from jax.experimental import pallas as pl
from jax.experimental.pallas import tpu as pltpu
from jax.sharding import PartitionSpec as P

epsilon = 1e-05
F32 = jnp.float32
BF = jnp.bfloat16
LANES = 128
SPAN = {
    "s1": (0, 2),
    "s2": (2, 2),
    "s3": (4, 8),
    "f1": (12, 1),
    "f2": (13, 1),
    "f3": (14, 1),
    "lp": (15, 2),
}
SHIFT_ROW = 24
TIMES = {
    "grads_es": 2.4,
    "stage_l": 1.8,
    "grads_first": 1.3,
    "stage_slow_out": 1.8,
    "r_split": 1.1,
    "b_split": 1.1,
    "place_fast": 1.7,
    "place_slow": 2.1,
    "finish_reduce": 2.6,
    "finish_rest": 3.4,
}
WEIGHT = 0.0


SMEM_KEYS = ("ids",)


def space_of(key):
    if key in SMEM_KEYS:
        return pltpu.SMEM
    if key.startswith("hbm_"):
        return pltpu.HBM
    if key.startswith("any_"):
        return pl.ANY
    return pltpu.VMEM


def run(body, name, ins, outs, scratch=None, hold=(), far_hold=(), groups=1, flops=2_000_000_000, grant=16):
    scratch = dict(scratch or {})
    outs = dict(outs)
    ins = dict(ins, **{"any_hold%d" % i: value for i, value in enumerate(hold)})
    ins = dict(ins, **{"hbm_hold%d" % i: value for i, value in enumerate(far_hold)})
    shared = "part" in outs
    if shared:
        shape, kind = outs["part"]
        scratch["sums"] = (shape, kind)
        outs["part"] = ((groups,) + shape, kind)
    names = list(ins) + list(outs) + list(scratch)

    def kernel(*refs):
        r = SimpleNamespace(**dict(zip(names, refs)))
        if not shared:
            body(r)
            return
        spread = r.part
        r.part = r.sums
        r.sums[...] = jnp.zeros(r.sums.shape, F32)
        body(r)

        def copy(i, carry):
            spread[i] = r.sums[...]
            return carry

        lax.fori_loop(0, groups, copy, 0)

    result = pl.pallas_call(
        kernel,
        name=name,
        out_shape=[jax.ShapeDtypeStruct(shape, kind) for shape, kind in outs.values()],
        in_specs=[pl.BlockSpec(memory_space=space_of(key)) for key in ins],
        out_specs=[pl.BlockSpec(memory_space=space_of(key)) for key in outs],
        scratch_shapes=[
            pltpu.VMEM(*item) if isinstance(item, tuple) else item for item in scratch.values()
        ],
        compiler_params=pltpu.CompilerParams(vmem_limit_bytes=grant * 1024 * 1024),
        cost_estimate=pl.CostEstimate(flops=flops, bytes_accessed=1000, transcendentals=0),
    )(*ins.values())
    return SimpleNamespace(**dict(zip(outs, result)))


def dot(a, b):
    return lax.dot_general(a, b, (((1,), (0,)), ((), ())), preferred_element_type=F32)


def dot_t(a, b):
    return lax.dot_general(a, b, (((1,), (1,)), ((), ())), preferred_element_type=F32)


def t_dot(a, b):
    return lax.dot_general(a, b, (((0,), (0,)), ((), ())), preferred_element_type=F32)


def sigm(v):
    return 0.5 * jnp.tanh(0.5 * v) + 0.5


def slope_of(v):
    s = sigm(v)
    return s * (1.0 + v * (1.0 - s))


def fold8(x):
    return jnp.sum(x.reshape(x.shape[0] // 8, 8, x.shape[1]), axis=0)


def wide(row, width):
    return row if row.shape[1] == width else jnp.concatenate([row] * (width // row.shape[1]), axis=1)


def lanes_of(block, start, count):
    if count == 1:
        return block[start : start + 1, :]
    return jnp.concatenate([block[start + i : start + i + 1, :] for i in range(count)], axis=1)


def put(part, row, acc8):
    total = jnp.sum(acc8, axis=0, keepdims=True)
    for i in range(total.shape[1] // LANES):
        part[row + i : row + i + 1, :] = total[:, i * LANES : (i + 1) * LANES]


def quarters(acc, width):
    count = acc.shape[1] // width
    total = acc[:, :width]
    for i in range(1, count):
        total = total + acc[:, i * width : (i + 1) * width]
    return total


def folded(tot, width):
    total = tot
    for i in range(1, LANES // width):
        total = total + pltpu.roll(tot, i * width, 1)
    return total


def gain(r, key):
    start, count = SPAN[key]
    return lanes_of(r.par[...], start, count)


def shift(r, key):
    start, count = SPAN[key]
    return lanes_of(r.par[...], SHIFT_ROW + start, count)


def moments(tot, row, key, inv, fast_bottle=32):
    count = SPAN[key][1]
    block = folded(tot, fast_bottle) if key in ("f1", "f2") else tot
    mean = lanes_of(block, row, count) * inv
    square = lanes_of(block, row + count, count) * inv
    return mean, lax.rsqrt(square - mean * mean + epsilon)


def pair_of(tot, row, key, fast_bottle=32):
    count = SPAN[key][1]
    block = folded(tot, fast_bottle) if key in ("f1", "f2") else tot
    return lanes_of(block, row, count), lanes_of(block, row + count, count)


def invs(r):
    return r.inv[0:1, :1], r.inv[1:2, :1]


def norm_of(r, tot, row, key, inv, width=None):
    mean, rs = moments(tot, row, key, inv)
    scale = rs * gain(r, key)
    offset = shift(r, key) - mean * scale
    if width is None:
        return mean, rs, scale, offset
    return tuple(wide(v, width) for v in (mean, rs, scale, offset))


def windows(x, side):
    rows, width = x.shape
    col = lax.broadcasted_iota(jnp.int32, (rows, width), 0) % side
    zero = jnp.zeros((side, width), x.dtype)
    out = {}
    for c in range(3):
        step = c - 1
        if step == 0:
            y = x
        else:
            y = pltpu.roll(x, (-step) % rows, 0)
            y = jnp.where((col + step >= 0) & (col + step < side), y, 0.0)
        out[0, c] = jnp.concatenate([zero, y[: rows - side]], axis=0)
        out[1, c] = y
        out[2, c] = jnp.concatenate([y[side:], zero], axis=0)
    return out


def put_windows(col, at, x, side, back):
    width = x.shape[1]
    for (i, j), y in windows(x, side).items():
        if back:
            i, j = 2 - i, 2 - j
        spot = (i * 3 + j) * width
        col[at, spot : spot + width] = y.astype(BF)


def loop(count, body, init=0):
    return lax.fori_loop(0, count, body, init, unroll=True)


def at_frame(t, cells, lead=0):
    return pl.ds(pl.multiple_of(t * cells, cells) + lead, cells)


def spans(total, step):
    return [(a, step) for a in range(0, total, step)]


def clear_ends(pad, cells):
    rows, width = pad.shape
    zero = jnp.zeros((cells, width), pad.dtype)
    pad[0:cells, :] = zero
    pad[rows - cells : rows, :] = zero


def chosen(r, layer, own, other):
    return jnp.where(r.ids[0] == layer, own, other)


def lane_group(shape, width):
    return lax.div(lax.broadcasted_iota(jnp.int32, shape, 1), width)


def placing(rows, group):
    lane = lax.broadcasted_iota(jnp.int32, (rows, LANES), 1)
    row = lax.broadcasted_iota(jnp.int32, (rows, LANES), 0)
    hit = lax.rem(lane, rows) == row if group is None else lane - group * rows == row
    return jnp.where(hit, 1.0, 0.0).astype(BF)


def first_mix(r, d, xpad, part, row):
    acc_s = acc_q = 0.0
    for a, n in spans(d.rows, d.step):
        got = (
            dot(xpad[a : a + n, 2 * d.cf : 4 * d.cf], r.wa[0 : 2 * d.cf, :])
            + dot(xpad[a + d.cells : a + d.cells + n, :], r.wa[2 * d.cf : 6 * d.cf, :])
            + dot(xpad[a + 2 * d.cells : a + 2 * d.cells + n, 0 : d.cf], r.wa[6 * d.cf : 7 * d.cf, :])
        )
        r.lp[a : a + n, :] = got[:, : d.cl]
        r.f1[a : a + n, :] = got[:, d.cl :]
        acc_s = acc_s + fold8(got)
        acc_q = acc_q + fold8(got * got)
    put(part, row, acc_s[:, : d.cl])
    put(part, row + 2, acc_q[:, : d.cl])
    put(part, row + 4, acc_s[:, d.cl :])
    put(part, row + 5, acc_q[:, d.cl :])


def stage_first(d):
    def body(r):
        sect, group = r.ids[0], r.ids[1]
        small = loading(
            r,
            [
                (r.hbm_lat_own, r.lat_own),
                (r.hbm_lat_other, r.lat_other),
                (r.hbm_fr_own, r.fr_own),
                (r.hbm_fr_other, r.fr_other),
            ],
        )

        def present_at(i):
            return 5 + sect * d.groups + i

        def crop_at(i):
            return 5 + (d.micro + sect) * d.groups + i

        def add(i, total):
            extent = r.ids[crop_at(i)]
            return total + jnp.where(r.ids[present_at(i)] > 0, extent * extent, 0)

        area = lax.fori_loop(0, d.groups, add, jnp.int32(0))
        area = jnp.full((1, LANES), area.astype(F32))
        r.inv[...] = jnp.zeros(r.inv.shape, F32)
        r.inv[0:1, :] = 1.0 / (area * d.frames)
        r.inv[1:2, :] = 1.0 / (area * (d.frames * d.quad))
        limit = jnp.where(r.ids[present_at(group)] > 0, r.ids[crop_at(group)], 0)
        cell = lax.broadcasted_iota(jnp.int32, (d.cells, LANES), 0)
        inside = (lax.div(cell, d.side) < limit) & (lax.rem(cell, d.side) < limit)
        mask = jnp.where(inside, 1.0, 0.0)
        r.mask[...] = mask
        small()
        for layer, wa in enumerate((r.wa, r.wa1)):
            for b in range(d.quad + 3):
                row = slice(b * d.cf, (b + 1) * d.cf)
                if b < d.taps:
                    wa[row, : d.cl] = chosen(r, layer, r.lat_own[b], r.lat_other[b])
                else:
                    wa[row, : d.cl] = jnp.zeros((d.cf, d.cl), BF)
                total = jnp.zeros((d.cf, LANES), F32)
                for q in range(d.quad):
                    k = b - 1 - q
                    if 0 <= k < 3:
                        tap = chosen(r, layer, r.fr_own[k], r.fr_other[k])
                        total = total + t_dot(tap, placing(d.fb, q))
                wa[row, d.cl :] = total.astype(BF)
        clear_ends(r.xpad, d.cells)

        def frame(t, carry):
            for q in range(d.quad):
                here = r.own[sect, t, q].astype(F32)
                there = r.other[sect, t, q].astype(F32)
                value = jnp.where(sect == 0, here, there)
                r.xpad[at_frame(t, d.cells, d.cells), q * d.cf : (q + 1) * d.cf] = (
                    value * mask
                ).astype(BF)
                r.cot[t, q] = jnp.where(sect == 0, there, here).astype(BF)
            return carry

        loop(d.frames, frame)
        first_mix(r, d, r.xpad, r.part, 0)

    return body


def stage_slow_in(d):
    pack = stage_pack(d)

    def body(r):
        sect = r.ids[0]
        names = ("fs", "fe", "gain", "shift")
        small = loading(
            r,
            [
                (getattr(r, "hbm_%s_%s" % (name, side)), getattr(r, "%s_%s" % (name, side)))
                for name in names
                for side in ("own", "other")
            ],
        )
        fetch = fetching(r, 0, [(r.hbm_red_own, r.hbm_red_other, r.wred_0)])
        small()
        pack(r)
        clear_ends(r.spad, d.cells)
        mask = wide(r.mask[...], 256)

        def frame(t, carry):
            for c in range(0, d.cs, 256):
                lane = slice(c, c + 256)
                here = r.own[sect, t, :, lane].astype(F32)
                there = r.other[sect, t, :, lane].astype(F32)
                value = jnp.where(sect == 0, here, there)
                r.spad[at_frame(t, d.cells, d.cells), lane] = (value * mask).astype(BF)
                r.cot[t, :, lane] = jnp.where(sect == 0, there, here).astype(BF)
            return carry

        loop(d.frames, frame)
        fetch()
        for a, n in spans(d.rows, d.step):
            got = 0.0
            for k in range(3):
                b = a + k * d.cells
                got = got + dot(r.spad[b : b + n, :], r.wred_0[k, : d.cs, :])
            r.y[a : a + n, :] = got

    return body


def stage_pack(d):
    sizes = [d.cb, d.cb, d.cs, d.fb, d.fb, d.cf, d.cl]
    keys = ["s1", "s2", "s3", "f1", "f2", "f3", "lp"]

    def body(r):
        spread = placing(d.fb, None)
        for layer in range(2):
            w2, w2t, w3, par = (
                (r.w2_0, r.w2t_0, r.w3_0, r.par_0),
                (r.w2_1, r.w2t_1, r.w3_1, r.par_1),
            )[layer]
            where = lane_group((d.fb, LANES), d.fb)
            for j in range(9):
                tap = chosen(r, layer, r.fs_own[j], r.fs_other[j])
                for out, tiled in ((w2, dot(tap, spread)), (w2t, t_dot(tap, spread))):
                    for q in range(d.quad):
                        row = j * LANES + q * d.fb
                        out[row : row + d.fb, :] = jnp.where(where == q, tiled, 0.0).astype(BF)
            w3[...] = jnp.zeros(w3.shape, BF)
            tap = chosen(r, layer, r.fe_own[...], r.fe_other[...])
            for q in range(d.quad):
                w3[q * d.fb : (q + 1) * d.fb, q * d.cf : (q + 1) * d.cf] = tap
            par[...] = jnp.zeros(par.shape, F32)
            for base, own, other in (
                (0, r.gain_own, r.gain_other),
                (SHIFT_ROW, r.shift_own, r.shift_other),
            ):
                values = chosen(r, layer, own[...], other[...])
                offset = 0
                for key, size in zip(keys, sizes):
                    row = base + SPAN[key][0]
                    piece = values[:, offset : offset + size]
                    offset += size
                    if size < LANES:
                        par[row : row + 1, :] = wide(piece, LANES)
                    else:
                        for i in range(size // LANES):
                            par[row + i : row + i + 1, :] = piece[:, i * LANES : (i + 1) * LANES]

    return body


def fetching(r, layer, weights):
    def copies(first):
        return [
            pltpu.make_async_copy(own if first == (layer == 0) else other, out, r.sems.at[i])
            for i, (own, other, out) in enumerate(weights)
        ]

    def each(action):
        for first in (True, False):

            @pl.when(r.ids[0] == 0 if first else r.ids[0] != 0)
            def _():
                for copy in copies(first):
                    action(copy)

    each(lambda copy: copy.start())
    return lambda: each(lambda copy: copy.wait())


def loading(r, pairs, first=0):
    copies = [
        pltpu.make_async_copy(source, target, r.loads.at[first + i])
        for i, (source, target) in enumerate(pairs)
    ]
    for copy in copies:
        copy.start()

    def wait():
        for copy in copies:
            copy.wait()

    return wait


def gate(r):
    r.out[...] = r.part[...]


def sort_out(r, grad, value, at):
    first = r.ids[0] == 0
    grad, value = grad.astype(F32), value.astype(F32)
    r.keep_out[at] = jnp.where(first, grad, value).astype(BF)
    r.send_out[at] = jnp.where(first, value, grad).astype(BF)


def stage_place(r):
    r.mark[...] = jnp.zeros(r.mark.shape, F32)
    copies = []
    for i in range(2):
        for t in range(r.keep.shape[0]):
            keep, got = r.keep[t].astype(F32), r.got[t].astype(F32)
            r.both[i, t] = jnp.where(r.ids[0] == i, keep, got).astype(BF)
        copies.append(pltpu.make_async_copy(r.both.at[i], r.hbm_out.at[i], r.sems.at[i]))
        copies[-1].start()
    for copy in copies:
        copy.wait()


def stage_second(d, row, carried):
    def body(r):
        if not carried:
            fetch = fetching(r, 1, [(r.hbm_red_own, r.hbm_red_other, r.wred_1)])
        tot = jnp.sum(r.sync[...], axis=0)
        r.tot[...] = tot
        inv_s, inv_f = invs(r)
        _, _, lg, lb = norm_of(r, tot, row, "lp", inv_s)
        _, _, fg, fb = norm_of(r, tot, row + 4, "f1", inv_f)
        mask = r.mask[...]
        mask2 = wide(mask, d.cl)
        clear_ends(r.lapad, d.cells)
        if carried:
            clear_ends(r.spad, d.cells)
            _, _, sg, sb = norm_of(SimpleNamespace(par=r.par0), tot, 0, "s3", inv_s)

        def frame(t, carry):
            at = at_frame(t, d.cells)
            up = at_frame(t, d.cells, d.cells)
            v = r.lp[at, :] * lg + lb
            r.lapad[up, :] = (v * sigm(v) * mask2).astype(BF)
            v = r.f1[at, :] * fg + fb
            v = (v * sigm(v) * mask).astype(BF)
            r.k1[at, :] = v
            put_windows(r.colf, at, v.astype(F32), d.side, False)
            if carried:
                for c in range(0, d.cs, 256):
                    z = r.xpad[up, c : c + 256].astype(F32) + (
                        r.s3[at, c : c + 256] * sg[:, c : c + 256] + sb[:, c : c + 256]
                    )
                    r.spad[up, c : c + 256] = (z * sigm(z) * mask2).astype(BF)
            return carry

        loop(d.frames, frame)
        acc_s = acc_q = acc_fs = acc_fq = 0.0
        for a, n in spans(d.rows, d.step):
            got = 0.0 if carried else r.y[a : a + n, :]
            for k in range(3):
                b = a + k * d.cells
                if carried:
                    got = got + dot(r.spad[b : b + n, :], r.wred[k, : d.cs, :])
                got = got + dot(r.lapad[b : b + n, :], r.wred[k, d.cs :, :])
            r.s1[a : a + n, :] = got
            acc_s = acc_s + fold8(got)
            acc_q = acc_q + fold8(got * got)
            got = dot(r.colf[a : a + n, :], r.w2[...])
            r.f2[a : a + n, :] = got
            kept = (got.reshape(n // d.cells, d.cells, got.shape[1]) * mask[None]).reshape(got.shape)
            acc_fs = acc_fs + fold8(kept)
            acc_fq = acc_fq + fold8(kept * got)
        put(r.part, 0, acc_s)
        put(r.part, 2, acc_q)
        put(r.part, 4, acc_fs)
        put(r.part, 5, acc_fq)
        if not carried:
            fetch()

    return body


def stage_third(d, fetched):
    def body(r):
        if fetched:
            fetch = fetching(
                r,
                0,
                [
                    (r.hbm_sp_own, r.hbm_sp_other, r.wsp_0),
                    (r.hbm_ex_own, r.hbm_ex_other, r.we_0),
                ],
            )
        tot = jnp.sum(r.sync[...], axis=0)
        r.tot[...] = tot
        inv_s, inv_f = invs(r)
        _, _, sg, sb = norm_of(r, tot, 0, "s1", inv_s)
        _, _, fg, fb = norm_of(r, tot, 4, "f2", inv_f)
        mask = r.mask[...]
        mask2 = wide(mask, d.cb)

        def frame(t, carry):
            at = at_frame(t, d.cells)
            v = r.s1[at, :] * sg + sb
            v = (v * sigm(v) * mask2).astype(BF)
            r.h1[at, :] = v
            put_windows(r.cols, at, v.astype(F32), d.side, False)
            v = r.f2[at, :] * fg + fb
            r.k2[at, :] = (v * sigm(v) * mask).astype(BF)
            return carry

        loop(d.frames, frame)
        if fetched:
            fetch()
        wsp = r.wsp_0 if fetched else r.wsp
        acc_s = acc_q = acc_fs = acc_fq = 0.0
        for a, n in spans(d.rows, d.step):
            got = dot(r.cols[a : a + n, :], wsp[...])
            r.s2[a : a + n, :] = got
            kept = (got.reshape(n // d.cells, d.cells, got.shape[1]) * mask2[None]).reshape(got.shape)
            acc_s = acc_s + fold8(kept)
            acc_q = acc_q + fold8(kept * got)
            got = dot(r.k2[a : a + n, :], r.w3[...])
            r.f3[a : a + n, :] = got
            acc_fs = acc_fs + fold8(got)
            acc_fq = acc_fq + fold8(got * got)
        put(r.part, 0, acc_s)
        put(r.part, 2, acc_q)
        put(r.part, 4, quarters(acc_fs, d.cf))
        put(r.part, 5, quarters(acc_fq, d.cf))

    return body


def expand_slow(r, d, sg, sb, mask2):
    def frame(t, carry):
        at = at_frame(t, d.cells)
        v = r.s2[at, :] * sg + sb
        r.h2[at, :] = (v * sigm(v) * mask2).astype(BF)
        return carry

    loop(d.frames, frame)
    for c in range(0, d.cs, 256):
        acc_s = acc_q = 0.0
        for a, n in spans(d.rows, d.step):
            got = dot(r.h2[a : a + n, :], r.we[:, c : c + 256])
            r.s3[a : a + n, c : c + 256] = got
            acc_s = acc_s + fold8(got)
            acc_q = acc_q + fold8(got * got)
        put(r.part, c // LANES, acc_s)
        put(r.part, (d.cs + c) // LANES, acc_q)


def stage_fourth(d, last):
    def body(r):
        if not last:
            fetch = fetching(
                r,
                1,
                [
                    (r.hbm_sp_own, r.hbm_sp_other, r.wsp_1),
                    (r.hbm_ex_own, r.hbm_ex_other, r.we_1),
                ],
            )
        tot = jnp.sum(r.sync[...], axis=0)
        r.tot[...] = tot
        inv_s, inv_f = invs(r)
        _, _, sg, sb = norm_of(r, tot, 0, "s2", inv_s)
        fm, fr, fg, fb = norm_of(r, tot, 4, "f3", inv_f)
        mask = r.mask[...]
        mask2 = wide(mask, d.cb)
        expand_slow(r, d, sg, sb, mask2)
        if not last:
            clear_ends(r.ypad, d.cells)

        def frame(t, carry):
            at = at_frame(t, d.cells)
            up = at_frame(t, d.cells, d.cells)
            for q in range(d.quad):
                lane = slice(q * d.cf, (q + 1) * d.cf)
                f3 = r.f3[at, lane]
                z = r.xpad[up, lane].astype(F32) + (f3 * fg + fb)
                s = sigm(z)
                y = (z * s * mask).astype(BF)
                if last:
                    r.yout[t, q] = y
                    grad = r.cot[t, q].astype(F32) * mask * (s * (1.0 + z * (1.0 - s)))
                    r.dzf[at, lane] = grad
                    u = (f3 - fm) * fr
                    carry = (carry[0] + fold8(grad), carry[1] + fold8(grad * u))
                else:
                    r.ypad[up, lane] = y
            return carry

        zero = jnp.zeros((8, d.cf), F32)
        done = loop(d.frames, frame, (zero, zero))
        if last:
            put(r.part, 16, done[0])
            put(r.part, 17, done[1])
        else:
            first_mix(r, d, r.ypad, r.part, 16)
            fetch()

    return body


def fast_back3(r, d, gs, gg, tot_f3, tot_f2, row):
    _, inv_f = invs(r)
    mask = r.mask[...]
    mean, rs = moments(tot_f3, 4, "f3", inv_f)
    factor = rs * gain(r, "f3")
    gs, gg = gs * inv_f, gg * inv_f
    m2, r2, g2, b2 = norm_of(r, tot_f2, 4, "f2", inv_f)

    def frame(t, carry):
        at = at_frame(t, d.cells)
        for q in range(d.quad):
            lane = slice(q * d.cf, (q + 1) * d.cf)
            u = (r.f3[at, lane] - mean) * rs
            r.df3[at, lane] = (factor * (r.dzf[at, lane] - mask * (gs + u * gg))).astype(BF)
        return carry

    loop(d.frames, frame)
    acc_s = acc_q = 0.0
    for a, n in spans(d.rows, d.step):
        got = dot_t(r.df3[a : a + n, :], r.w3[...])
        f2 = r.f2[a : a + n, :]
        kept = (got.reshape(n // d.cells, d.cells, got.shape[1]) * mask[None]).reshape(got.shape)
        kept = kept * slope_of(f2 * g2 + b2)
        r.d2f[a : a + n, :] = kept
        acc_s = acc_s + fold8(kept)
        acc_q = acc_q + fold8(kept * ((f2 - m2) * r2))
    put(r.part, row, acc_s)
    put(r.part, row + 1, acc_q)


def fast_back2(r, d, gs, gg, tot_f2, tot_f1, f1_row, row):
    _, inv_f = invs(r)
    mask = r.mask[...]
    mean, rs = moments(tot_f2, 4, "f2", inv_f)
    factor = rs * gain(r, "f2")
    gs, gg = gs * inv_f, gg * inv_f
    m1, r1, g1, b1 = norm_of(r, tot_f1, f1_row, "f1", inv_f)

    def frame(t, carry):
        at = at_frame(t, d.cells)
        u = (r.f2[at, :] - mean) * rs
        v = (factor * (r.d2f[at, :] - mask * (gs + u * gg))).astype(BF)
        r.df2[at, :] = v
        put_windows(r.colf, at, v.astype(F32), d.side, True)
        return carry

    loop(d.frames, frame)
    acc_s = acc_q = 0.0
    wide_row = d.quad * d.fb
    for a, n in spans(d.rows, d.step):
        got = dot(r.colf[a : a + n, :], r.w2t[...])
        f1 = r.f1[a : a + n, :]
        kept = (got.reshape(n // d.cells, d.cells, got.shape[1]) * mask[None]).reshape(got.shape)
        kept = kept * slope_of(f1 * g1 + b1)
        r.d1f[a : a + n, :] = kept
        acc_s = acc_s + fold8(kept)
        acc_q = acc_q + fold8(kept * ((f1 - m1) * r1))
    put(r.part, row, acc_s)
    put(r.part, row + 1, acc_q)


def fast_back1(r, d, gs, gg, tot_f1, f1_row):
    _, inv_f = invs(r)
    mask = r.mask[...]
    mean, rs = moments(tot_f1, f1_row, "f1", inv_f)
    factor = rs * gain(r, "f1")
    gs, gg = gs * inv_f, gg * inv_f

    def frame(t, carry):
        at = at_frame(t, d.cells)
        u = (r.f1[at, :] - mean) * rs
        r.gpad[at_frame(t, d.cells, d.cells), d.cl :] = (
            factor * (r.d1f[at, :] - mask * (gs + u * gg))
        ).astype(BF)
        return carry

    loop(d.frames, frame)


def lateral_back(r, d, gs, gg, tot_lp, lp_row):
    inv_s, _ = invs(r)
    mask2 = wide(r.mask[...], d.cl)
    mean, rs = moments(tot_lp, lp_row, "lp", inv_s)
    factor = rs * gain(r, "lp")
    gs, gg = gs * inv_s, gg * inv_s

    def frame(t, carry):
        at = at_frame(t, d.cells)
        u = (r.lp[at, :] - mean) * rs
        r.gpad[at_frame(t, d.cells, d.cells), : d.cl] = (
            factor * (r.dl[at, :] - mask2 * (gs + u * gg))
        ).astype(BF)
        return carry

    loop(d.frames, frame)


def fast_input_grad(r, d, a, n):
    c = d.cf
    mid = dot_t(r.gpad[a + d.cells : a + d.cells + n, :], r.wa[2 * c : 6 * c, :])
    late = dot_t(r.gpad[a + 2 * d.cells : a + 2 * d.cells + n, :], r.wa[0 : 2 * c, :])
    early = dot_t(r.gpad[a : a + n, :], r.wa[6 * c : 7 * c, :])
    return [
        mid[:, :c] + early,
        mid[:, c : 2 * c],
        mid[:, 2 * c : 3 * c] + late[:, :c],
        mid[:, 3 * c :] + late[:, c:],
    ]


def slow_back3(r, d, gs, gg, tot_s3, tot_s2, row):
    inv_s, _ = invs(r)
    mask2 = wide(r.mask[...], d.cb)
    mean, rs = moments(tot_s3, 0, "s3", inv_s)
    factor = rs * gain(r, "s3")
    gs, gg = gs * inv_s, gg * inv_s
    m2, r2, g2, b2 = norm_of(r, tot_s2, 0, "s2", inv_s)

    def frame(t, carry):
        at = at_frame(t, d.cells)
        for c in range(0, d.cs, 256):
            lane = slice(c, c + 256)
            u = (r.s3[at, lane] - mean[:, lane]) * rs[:, lane]
            r.ds3[at, lane] = (
                factor[:, lane] * (r.dzs[at, lane] - mask2 * (gs[:, lane] + u * gg[:, lane]))
            ).astype(BF)
        return carry

    loop(d.frames, frame)
    acc_s = acc_q = 0.0
    for a, n in spans(d.rows, d.step):
        got = dot_t(r.ds3[a : a + n, :], r.we[...])
        s2 = r.s2[a : a + n, :]
        kept = (got.reshape(n // d.cells, d.cells, got.shape[1]) * mask2[None]).reshape(got.shape)
        kept = kept * slope_of(s2 * g2 + b2)
        r.d2[a : a + n, :] = kept
        acc_s = acc_s + fold8(kept)
        acc_q = acc_q + fold8(kept * ((s2 - m2) * r2))
    put(r.part, row, acc_s)
    put(r.part, row + 2, acc_q)


def slow_back2(r, d, gs, gg, tot_s2, tot_s1, row):
    inv_s, _ = invs(r)
    mask2 = wide(r.mask[...], d.cb)
    mean, rs = moments(tot_s2, 0, "s2", inv_s)
    factor = rs * gain(r, "s2")
    gs, gg = gs * inv_s, gg * inv_s
    m1, r1, g1, b1 = norm_of(r, tot_s1, 0, "s1", inv_s)

    def frame(t, carry):
        at = at_frame(t, d.cells)
        u = (r.s2[at, :] - mean) * rs
        v = (factor * (r.d2[at, :] - mask2 * (gs + u * gg))).astype(BF)
        r.ds2[at, :] = v
        put_windows(r.cols, at, v.astype(F32), d.side, True)
        return carry

    loop(d.frames, frame)
    acc_s = acc_q = 0.0
    for a, n in spans(d.rows, d.step):
        got = 0.0
        for k in range(9):
            lane = slice(k * d.cb, (k + 1) * d.cb)
            got = got + dot_t(r.cols[a : a + n, lane], r.wsp[lane, :])
        s1 = r.s1[a : a + n, :]
        kept = (got.reshape(n // d.cells, d.cells, got.shape[1]) * mask2[None]).reshape(got.shape)
        kept = kept * slope_of(s1 * g1 + b1)
        r.d1[a : a + n, :] = kept
        acc_s = acc_s + fold8(kept)
        acc_q = acc_q + fold8(kept * ((s1 - m1) * r1))
    put(r.part, row, acc_s)
    put(r.part, row + 2, acc_q)


def slow_back1(r, d, gs, gg, tot_s1, tot_lp, lp_row, row):
    inv_s, _ = invs(r)
    mask2 = wide(r.mask[...], d.cb)
    mean, rs = moments(tot_s1, 0, "s1", inv_s)
    factor = rs * gain(r, "s1")
    gs, gg = gs * inv_s, gg * inv_s
    ml, rl, gl, bl = norm_of(r, tot_lp, lp_row, "lp", inv_s)
    clear_ends(r.dpad, d.cells)

    def frame(t, carry):
        at = at_frame(t, d.cells)
        u = (r.s1[at, :] - mean) * rs
        r.dpad[at_frame(t, d.cells, d.cells), :] = (
            factor * (r.d1[at, :] - mask2 * (gs + u * gg))
        ).astype(BF)
        return carry

    loop(d.frames, frame)
    acc_s = acc_q = 0.0
    for a, n in spans(d.rows, d.step):
        got = slow_input_grad(r, d, a, n, d.cs, d.cs + d.cl)
        lp = r.lp[a : a + n, :]
        kept = (got.reshape(n // d.cells, d.cells, got.shape[1]) * mask2[None]).reshape(got.shape)
        kept = kept * slope_of(lp * gl + bl)
        r.dl[a : a + n, :] = kept
        acc_s = acc_s + fold8(kept)
        acc_q = acc_q + fold8(kept * ((lp - ml) * rl))
    put(r.part, row, acc_s)
    put(r.part, row + 2, acc_q)


def slow_input_grad(r, d, a, n, first, last):
    got = 0.0
    for k in range(3):
        b = a + (2 - k) * d.cells
        got = got + dot_t(r.dpad[b : b + n, :], r.wred[k, first:last, :])
    return got


def masked(x, mask, d):
    return (x.reshape(x.shape[0] // d.cells, d.cells, x.shape[1]) * mask[None]).reshape(x.shape)


def stage_e(d):
    def body(r):
        tot = jnp.sum(r.sync[...], axis=0)
        r.tot[...] = tot
        inv_s, _ = invs(r)
        mean, rs, sg, sb = norm_of(r, tot, 0, "s3", inv_s)
        mask2 = wide(r.mask[...], 256)

        def frame(t, carry):
            at = at_frame(t, d.cells)
            up = at_frame(t, d.cells, d.cells)
            sums = []
            for i, c in enumerate(range(0, d.cs, 256)):
                lane = slice(c, c + 256)
                s3 = r.s3[at, lane]
                z = r.spad[up, lane].astype(F32) + (s3 * sg[:, lane] + sb[:, lane])
                s = sigm(z)
                r.yout[t, :, lane] = (z * s * mask2).astype(BF)
                grad = r.cot[t, :, lane].astype(F32) * mask2 * (s * (1.0 + z * (1.0 - s)))
                r.dzs[at, lane] = grad
                u = (s3 - mean[:, lane]) * rs[:, lane]
                sums.append((carry[i][0] + fold8(grad), carry[i][1] + fold8(grad * u)))
            return tuple(sums)

        zero = jnp.zeros((8, 256), F32)
        done = loop(d.frames, frame, tuple((zero, zero) for c in range(0, d.cs, 256)))
        for i, c in enumerate(range(0, d.cs, 256)):
            put(r.part, c // LANES, done[i][0])
            put(r.part, (d.cs + c) // LANES, done[i][1])
        gs, gg = pair_of(tot, 16, "f3")
        fast_back3(r, d, gs, gg, r.tot_c[...], r.tot_b[...], 16)

    return body


def stage_f(d):
    def body(r):
        tot = jnp.sum(r.sync[...], axis=0)
        r.tot[...] = tot
        gs, gg = pair_of(tot, 0, "s3")
        slow_back3(r, d, gs, gg, r.tot_d[...], r.tot_c[...], 0)
        gs, gg = pair_of(tot, 16, "f2")
        fast_back2(r, d, gs, gg, r.tot_b[...], r.tot_a[...], 20, 4)

    return body


def stage_g(d):
    def body(r):
        tot = jnp.sum(r.sync[...], axis=0)
        r.tot[...] = tot
        gs, gg = pair_of(tot, 0, "s2")
        slow_back2(r, d, gs, gg, r.tot_c[...], r.tot_b[...], 0)

    return body


def stage_h(d):
    def body(r):
        tot = jnp.sum(r.sync[...], axis=0)
        r.tot[...] = tot
        inv_s, _ = invs(r)
        gs, gg = pair_of(tot, 0, "s1")
        slow_back1(r, d, gs, gg, r.tot_b[...], r.tot_a[...], 16, 16)
        mask2 = wide(r.mask[...], 256)
        r.par = r.par0
        mean, rs, sg, sb = norm_of(r, r.tot_a[...], 0, "s3", inv_s)
        for c in range(0, d.cs, 256):
            lane = slice(c, c + 256)
            acc_s = acc_q = 0.0
            for a, n in spans(d.rows, d.step):
                got = slow_input_grad(r, d, a, n, c, c + 256)
                got = masked(r.dzs[a : a + n, lane] + got, mask2, d).astype(BF).astype(F32)
                s3 = r.s3[a : a + n, lane]
                z = r.spad[a + d.cells : a + d.cells + n, lane].astype(F32) + (
                    s3 * sg[:, lane] + sb[:, lane]
                )
                grad = got * slope_of(z)
                r.dzs0[a : a + n, lane] = grad
                u = (s3 - mean[:, lane]) * rs[:, lane]
                acc_s = acc_s + fold8(grad)
                acc_q = acc_q + fold8(grad * u)
            put(r.part, c // LANES, acc_s)
            put(r.part, (d.cs + c) // LANES, acc_q)

    return body


def stage_i(d):
    def body(r):
        tot = jnp.sum(r.sync[...], axis=0)
        r.tot[...] = tot
        _, inv_f = invs(r)
        clear_ends(r.gpad, d.cells)
        gs, gg = pair_of(r.tot_f[...], 4, "f1")
        fast_back1(r, d, gs, gg, r.tot_a[...], 20)
        gs, gg = pair_of(tot, 16, "lp")
        lateral_back(r, d, gs, gg, r.tot_a[...], 16)
        r.par = r.par0
        mask = r.mask[...]
        mean, rs, fg, fb = norm_of(r, r.tot_c0[...], 4, "f3", inv_f)
        acc_s = acc_q = 0.0
        for a, n in spans(d.rows, d.step):
            pieces = fast_input_grad(r, d, a, n)
            for q in range(d.quad):
                lane = slice(q * d.cf, (q + 1) * d.cf)
                got = masked(r.dzf[a : a + n, lane] + pieces[q], mask, d).astype(BF).astype(F32)
                f3 = r.f3[a : a + n, lane]
                z = r.xpad[a + d.cells : a + d.cells + n, lane].astype(F32) + (f3 * fg + fb)
                grad = got * slope_of(z)
                r.dzf0[a : a + n, lane] = grad
                acc_s = acc_s + fold8(grad)
                acc_q = acc_q + fold8(grad * ((f3 - mean) * rs))
        put(r.part, 4, acc_s)
        put(r.part, 5, acc_q)
        gs, gg = pair_of(tot, 0, "s3")
        r.dzs = r.dzs0
        slow_back3(r, d, gs, gg, r.tot_a[...], r.tot_c0[...], 0)

    return body


def stage_j(d):
    def body(r):
        tot = jnp.sum(r.sync[...], axis=0)
        r.tot[...] = tot
        gs, gg = pair_of(tot, 0, "s2")
        slow_back2(r, d, gs, gg, r.tot_c[...], r.tot_b[...], 0)
        gs, gg = pair_of(tot, 4, "f3")
        fast_back3(r, d, gs, gg, r.tot_c[...], r.tot_b[...], 4)

    return body


def stage_k(d):
    def body(r):
        tot = jnp.sum(r.sync[...], axis=0)
        r.tot[...] = tot
        gs, gg = pair_of(tot, 0, "s1")
        slow_back1(r, d, gs, gg, r.tot_b[...], r.tot_a[...], 0, 0)
        gs, gg = pair_of(tot, 4, "f2")
        fast_back2(r, d, gs, gg, r.tot_b[...], r.tot_a[...], 4, 4)

    return body


def stage_slow_out(d):
    def body(r):
        mask2 = wide(r.mask[...], 256)
        for c in range(0, d.cs, 256):
            lane = slice(c, c + 256)
            for a, n in spans(d.rows, d.step):
                got = slow_input_grad(r, d, a, n, c, c + 256)
                got = masked(r.dzs[a : a + n, lane] + got, mask2, d)
                for t in range(n // d.cells):
                    at = (a // d.cells + t, slice(None), lane)
                    sort_out(r, got[t * d.cells : (t + 1) * d.cells, :], r.value[at], at)

    return body


def stage_l(d):
    def body(r):
        tot = jnp.sum(r.sync[...], axis=0)
        r.tot[...] = tot
        clear_ends(r.gpad, d.cells)
        gs, gg = pair_of(tot, 4, "f1")
        fast_back1(r, d, gs, gg, r.tot_a[...], 4)
        gs, gg = pair_of(tot, 0, "lp")
        lateral_back(r, d, gs, gg, r.tot_a[...], 0)
        mask = r.mask[...]
        for a, n in spans(d.rows, d.step):
            pieces = fast_input_grad(r, d, a, n)
            for q in range(d.quad):
                lane = slice(q * d.cf, (q + 1) * d.cf)
                got = masked(r.dzf[a : a + n, lane] + pieces[q], mask, d)
                for t in range(n // d.cells):
                    at = (a // d.cells + t, q)
                    sort_out(r, got[t * d.cells : (t + 1) * d.cells, :], r.value[at], at)

    return body


def small_block(r, row, value):
    for half in range(2):
        for i in range(2):
            at = 64 * half + 32 * i
            r.halves[half, row : row + 32, i * LANES : (i + 1) * LANES] = value[
                at : at + 32, :
            ].astype(BF)


def hand_over(r):
    r.keep[...] = r.halves[r.ids[0]]
    r.send[...] = r.halves[1 - r.ids[0]]


def grads_es(d):
    part = d.cb // 2

    def body(r):
        def frame(t, carry):
            at = at_frame(t, d.cells)
            put_windows(r.cols, at, r.ds2[at, :].astype(F32), d.side, True)
            put_windows(r.colf, at, r.df2[at, :].astype(F32), d.side, True)
            return carry

        loop(d.frames, frame)
        row = 0
        turned = r.h2[...].T
        for c in range(0, d.cs, 256):
            got = dot(turned, r.ds3[:, c : c + 256]).astype(BF)
            for half in range(2):
                r.halves[half, row : row + part, :] = got[half * part : (half + 1) * part, :]
            row += part
        turned = r.h1[...].T
        for k in range(9):
            got = dot(turned, r.cols[:, k * d.cb : (k + 1) * d.cb]).astype(BF)
            for half in range(2):
                r.halves[half, row : row + part, :] = got[half * part : (half + 1) * part, :]
            row += part
        r.g2[...] = t_dot(r.k1[...], r.colf[...])
        r.g3[...] = t_dot(r.k2[...], r.df3[...])
        where = lane_group((d.fb, LANES), d.fb)
        for i in range(3):
            total = jnp.zeros((d.fb, LANES), F32)
            for c in range(3):
                for q in range(d.quad):
                    tap = (3 * i + c) * LANES
                    piece = r.g2[q * d.fb : (q + 1) * d.fb, tap : tap + LANES]
                    if c != q:
                        piece = pltpu.roll(piece, ((c - q) * d.fb) % LANES, 1)
                    total = total + jnp.where(where == c, piece, 0.0)
            r.block[i * d.fb : (i + 1) * d.fb, :] = total
        total = jnp.zeros((d.fb, LANES), F32)
        for q in range(d.quad):
            total = total + r.g3[q * d.fb : (q + 1) * d.fb, q * d.cf : (q + 1) * d.cf]
        r.block[3 * d.fb :, :] = total
        small_block(r, row, r.block[...])
        hand_over(r)

    return body


def with_grads(stage_body, grads_body, names):
    def body(r):
        stage_body(r)
        for target, source in names.items():
            setattr(r, target, getattr(r, source))
        grads_body(r)

    return body


def grads_reduce(d):
    split = (d.cs + d.cl) // 2

    def body(r):
        for c in range(0, d.cs + d.cl, 256):
            if c < d.cs:
                source = r.spad[d.cells : d.cells + d.rows, c : c + 256]
            else:
                source = r.lapad[d.cells : d.cells + d.rows, c - d.cs : c - d.cs + 256]
            turned = source.T
            cut = min(max(split - c, 0), 256)
            for k in range(3):
                b = (2 - k) * d.cells
                got = dot(turned, r.dpad[b : b + d.rows, :]).astype(BF)
                if cut > 0:
                    row = k * split + c
                    r.halves[0, row : row + cut, :] = got[:cut, :]
                if cut < 256:
                    row = k * split + c + cut - split
                    r.halves[1, row : row + 256 - cut, :] = got[cut:, :]
        hand_over(r)

    return body


def grads_first(d):
    def body(r):
        c = d.cf
        grad = r.gpad[d.cells : d.cells + d.rows, :]
        r.ga[0 : 2 * c, :] = t_dot(r.xpad[0 : d.rows, 2 * c : 4 * c], grad)
        r.ga[2 * c : 6 * c, :] = t_dot(r.xpad[d.cells : d.cells + d.rows, :], grad)
        r.ga[6 * c :, :] = t_dot(r.xpad[2 * d.cells : 2 * d.cells + d.rows, 0:c], grad)
        row = 0
        for b in range(d.taps):
            for half in range(2):
                at = b * c + half * (c // 2)
                r.halves[half, row : row + c // 2, :] = r.ga[at : at + c // 2, : d.cl].astype(BF)
            row += c // 2
        where = lane_group((c, LANES), d.fb)
        total = jnp.zeros((c, LANES), F32)
        for k in range(3):
            for q in range(d.quad):
                at = (q + k + 1) * c
                piece = r.ga[at : at + c, d.cl :]
                if k != q:
                    piece = pltpu.roll(piece, ((k - q) * d.fb) % LANES, 1)
                total = total + jnp.where(where == k, piece, 0.0)
        small_block(r, row, total)
        hand_over(r)

    return body


def gather_pieces(r, count):
    row = 0
    for i in range(count):
        keep, got = getattr(r, "keep_%d" % i), getattr(r, "got_%d" % i)
        r.mine[row : row + keep.shape[0], :] = (
            keep[...].astype(F32) + got[...].astype(F32)
        ).astype(BF)
        row += keep.shape[0]
    if row < r.mine.shape[0]:
        r.mine[row:, :] = jnp.zeros((r.mine.shape[0] - row, r.mine.shape[1]), BF)


def split_near(count, turned=None):
    def body(r):
        gather_pieces(r, count)
        hand_shares(r, r.mine, r.ids[2 if turned is None else 4], turned)

    return body


def split_half(count, bit):
    def body(r):
        gather_pieces(r, count)
        halve(r, bit)

    return body


def hand_shares(r, source, place, turned=None):
    k = 0
    while hasattr(r, "to_%d" % k):
        target = getattr(r, "to_%d" % k)
        rows = target.shape[0]
        start = pl.multiple_of((place ^ (k if turned is None else turned[k])) * rows, 16)
        target[...] = source[pl.ds(start, rows), :]
        k += 1


def add_shares(r):
    total = r.from_0[...].astype(F32)
    k = 1
    while hasattr(r, "from_%d" % k):
        total = total + getattr(r, "from_%d" % k)[...].astype(F32)
        k += 1
    return total.astype(BF)


def sum_shares(r):
    r.out[...] = add_shares(r)


def sum_and_share(r):
    r.mine[...] = add_shares(r)
    hand_shares(r, r.mine, r.ids[3])


def collect(which):
    def body(r):
        rows = r.from_0.shape[0]
        k = 0
        while hasattr(r, "from_%d" % k):
            start = pl.multiple_of((r.ids[which] ^ k) * rows, 16)
            r.out[pl.ds(start, rows), :] = getattr(r, "from_%d" % k)[...]
            k += 1

    return body


def halve(r, bit):
    rows = r.keep.shape[0]
    mine = jnp.where((r.ids[1] & bit) > 0, 1, 0)
    r.keep[...] = r.mine[pl.ds(pl.multiple_of(mine * rows, 16), rows), :]
    r.send[...] = r.mine[pl.ds(pl.multiple_of((1 - mine) * rows, 16), rows), :]


def split_far(bit):
    def body(r):
        rows = r.early.shape[0]
        r.mine[0:rows, :] = r.early[...]
        r.mine[rows:, :] = add_shares(r)
        halve(r, bit)

    return body


def next_far(bit):
    def body(r):
        total = (r.own[...].astype(F32) + r.got[...].astype(F32)).astype(BF)
        if bit:
            r.mine[...] = total
            halve(r, bit)
        else:
            r.keep[...] = total

    return body


def join_far(bit):
    def body(r):
        rows = r.own.shape[0]
        mine = jnp.where((r.ids[1] & bit) > 0, 1, 0)
        r.out[pl.ds(pl.multiple_of(mine * rows, 16), rows), :] = r.own[...]
        r.out[pl.ds(pl.multiple_of((1 - mine) * rows, 16), rows), :] = r.got[...]

    return body


def join_last(bit):
    def body(r):
        rows = r.own.shape[0]
        mine = jnp.where((r.ids[1] & bit) > 0, 1, 0)
        r.all[pl.ds(pl.multiple_of(mine * rows, 16), rows), :] = r.own[...]
        r.all[pl.ds(pl.multiple_of((1 - mine) * rows, 16), rows), :] = r.got[...]
        cut = r.es.shape[0]
        r.es[...] = r.all[0:cut, :]
        r.red[...] = r.all[cut:, :]

    return body


def halve_parts(r, sizes, bit):
    mine = jnp.where((r.ids[1] & bit) > 0, 1, 0)
    start = done = 0
    for size in sizes:
        half = size // 2
        at = slice(done, done + half)
        r.keep[at, :] = r.mine[pl.ds(pl.multiple_of(start + mine * half, 16), half), :]
        r.send[at, :] = r.mine[pl.ds(pl.multiple_of(start + (1 - mine) * half, 16), half), :]
        start += size
        done += half


def join_parts(sizes, bit):
    def body(r):
        start = 0
        for i, size in enumerate(sizes):
            own, got = getattr(r, "own_%d" % i), getattr(r, "got_%d" % i)
            r.mine[start : start + size, :] = (own[...].astype(F32) + got[...].astype(F32)).astype(BF)
            start += size
        halve_parts(r, sizes, bit)

    return body


def next_parts(sizes, bit):
    def body(r):
        r.mine[...] = (r.own[...].astype(F32) + r.got[...].astype(F32)).astype(BF)
        halve_parts(r, sizes, bit)

    return body


def merge_far(bit):
    def body(r):
        rows = r.early.shape[0]
        r.mine[0:rows, :] = r.early[...]
        if hasattr(r, "own"):
            late = (r.own[...].astype(F32) + r.got[...].astype(F32)).astype(BF)
        else:
            late = r.late[...]
        r.mine[rows:, :] = late
        halve(r, bit)

    return body


def part_far(bit):
    def body(r):
        rows = r.own.shape[0]
        mine = jnp.where((r.ids[1] & bit) > 0, 1, 0)
        r.all[pl.ds(pl.multiple_of(mine * rows, 16), rows), :] = r.own[...]
        r.all[pl.ds(pl.multiple_of((1 - mine) * rows, 16), rows), :] = r.got[...]
        cut = r.early.shape[0]
        r.early[...] = r.all[0:cut, :]
        r.late[...] = r.all[cut:, :]

    return body


def join_pair(bits):
    def body(r):
        for i, bit in enumerate(bits):
            own, got, out = (getattr(r, name + str(i)) for name in ("own_", "got_", "out_"))
            rows = own.shape[0]
            mine = jnp.where((r.ids[1] & bit) > 0, 1, 0)
            out[pl.ds(pl.multiple_of(mine * rows, 16), rows), :] = own[...]
            out[pl.ds(pl.multiple_of((1 - mine) * rows, 16), rows), :] = got[...]

    return body


def join_send(bit):
    def body(r):
        join_far(bit)(r)

        @pl.when(r.ids[0] == 0)
        def _():
            r.send[0 : r.second.shape[0], :] = r.second[...]

        @pl.when(r.ids[0] != 0)
        def _():
            r.send[0 : r.out.shape[0], :] = r.out[...]

    return body


def add_near(r):
    rows = r.got.shape[1]
    total = r.got[0].astype(F32)
    for i in range(1, r.got.shape[0]):
        total = total + r.got[i].astype(F32)
    r.out[0:rows, :] = total.astype(BF)
    r.out[rows:, :] = add_shares(r)


def add_up(r):
    total = jnp.zeros(r.got.shape[1:], F32)
    for i in range(r.got.shape[0]):
        total = total + r.got[i].astype(F32)
    total = total.astype(BF)
    if len(r.out.shape) == len(total.shape):
        r.out[...] = total
    else:
        for i in range(r.out.shape[0]):
            r.out[i] = total


def spread_out(r):
    for i in range(r.out.shape[0]):
        r.out[i] = r.got[...]


def store_all(r, todo):
    @pl.when(r.ids[0] == 0)
    def _():
        for out, done, step, first, at, _, _, lanes in todo:
            out[done : done + step, :] = first[at : at + step, lanes].astype(F32)

    @pl.when(r.ids[0] != 0)
    def _():
        for out, done, step, _, _, second, at, lanes in todo:
            out[done : done + step, :] = second[at : at + step, lanes].astype(F32)


def store_half(r, todo, spots, half, out, here_at, there_at, count, lanes=slice(None)):
    done = 0
    while done < count:
        step = count - done
        found = []
        for (kind, row), mine in ((here_at, half == 0), (there_at, half == 1)):
            own, got, piece, stride, offset = spots[kind]
            i, rest = divmod(row + done, piece)
            step = min(step, piece - rest)
            found.append((getattr(r, own if mine else got), i * stride + offset + rest))
        (first, at_0), (second, at_1) = found
        todo.append((out, done, step, first, at_0, second, at_1, lanes))
        done += step


def finish_reduce(d, spots):
    split = (d.cs + d.cl) // 2

    def body(r):
        r.mark[...] = jnp.zeros(r.mark.shape, F32)
        copies = []
        for k in range(3):
            todo = []
            for half in range(2):
                out = r.reduce.at[k, half * split : (half + 1) * split, :]
                store_half(r, todo, spots, half, out, ("r", k * split), ("red", k * split), split)
            store_all(r, todo)
            copies.append(
                pltpu.make_async_copy(r.reduce.at[k], r.hbm_reduce.at[0, k], r.sems.at[k])
            )
            copies[-1].start()
        for copy in copies:
            copy.wait()

    return body


def finish_rest(d, spots, rows_red):
    part = d.cb // 2
    side = d.cf // 2

    def body(r):
        row = 0
        todo = []
        for c in range(0, d.cs, 256):
            for half in range(2):
                out = r.expand.at[half * part : (half + 1) * part, c : c + 256]
                store_half(r, todo, spots, half, out, ("b", row), ("es", row), part)
            row += part
        store_all(r, todo)
        copies = [pltpu.make_async_copy(r.expand, r.hbm_expand.at[0], r.sems.at[0])]
        copies[-1].start()
        todo = []
        for k in range(9):
            for half in range(2):
                out = r.space.at[k, half * part : (half + 1) * part, :]
                store_half(r, todo, spots, half, out, ("b", row), ("es", row), part)
            row += part
        store_all(r, todo)
        copies.append(pltpu.make_async_copy(r.space, r.hbm_space.at[0], r.sems.at[1]))
        copies[-1].start()

        def small(here_at, there_at):
            todo = []
            for half in range(2):
                for i in range(2):
                    at = 64 * half + 32 * i
                    lanes = slice(i * LANES, (i + 1) * LANES)
                    store_half(
                        r, todo, spots, half, r.block.at[at : at + 32, :], here_at, there_at, 32, lanes
                    )
            store_all(r, todo)

        small(("b", row), ("es", row))
        for i in range(3):
            piece = r.block[i * d.fb : (i + 1) * d.fb, :]
            for c in range(3):
                moved = piece if c == 0 else pltpu.roll(piece, LANES - c * d.fb, 1)
                r.fspace[0, 3 * i + c] = moved[:, : d.fb]
        r.fexpand[0] = r.block[3 * d.fb :, :]
        row, row_1 = 0, rows_red
        todo = []
        for tap in range(d.taps):
            for half in range(2):
                out = r.lateral.at[0, tap, half * side : (half + 1) * side, :]
                store_half(r, todo, spots, half, out, ("f", row), ("red", row_1), side)
            row, row_1 = row + side, row_1 + side
        store_all(r, todo)
        small(("f", row), ("red", row_1))
        turned = r.block[...].T
        for k in range(3):
            r.freduce[0, k] = turned[k * d.fb : (k + 1) * d.fb, :]
        for copy in copies:
            copy.wait()

    return body


def norms_out(d, at):
    def body(r):
        made = []
        for layer in range(2):
            lines = []
            for which in (1, 0):
                pieces = []
                for key in ("s1", "s2", "s3", "f1", "f2", "f3", "lp"):
                    name, row = at[layer][key]
                    tot = getattr(r, name)[...]
                    count = SPAN[key][1]
                    if key in ("f1", "f2"):
                        tot = folded(tot, d.fb)
                    piece = lanes_of(tot, row + which * count, count)
                    pieces.append(piece[:, : d.fb] if key in ("f1", "f2") else piece)
                lines.append(jnp.concatenate(pieces, axis=1))
            made.append(lines)
        for i in range(2):
            r.keep[i : i + 1, :] = jnp.where(r.ids[0] == 0, made[0][i], made[1][i])
            r.send[i : i + 1, :] = jnp.where(r.ids[0] == 0, made[1][i], made[0][i])

    return body


def norms_add(r):
    total = r.keep[...] + r.got[...]
    r.gain[...] = total[0:1, :]
    r.shift[...] = total[1:2, :]


def on_device(
    edge_slow,
    edge_fast,
    slow_reduce,
    slow_spatial,
    slow_expand,
    fast_reduce,
    fast_spatial,
    fast_expand,
    lateral,
    norm_gain,
    norm_shift,
    present,
    crop_side,
):
    micro, _, frames, side, _, cs = edge_slow.shape[1:]
    cells = side * side
    fast_frames = edge_fast.shape[3]
    quad = fast_frames // frames
    d = SimpleNamespace(
        frames=frames,
        side=side,
        cells=cells,
        rows=frames * cells,
        step=min(512, frames * cells),
        quad=quad,
        cs=cs,
        cb=slow_expand.shape[1],
        cf=edge_fast.shape[-1],
        fb=fast_expand.shape[1],
        cl=lateral.shape[3],
    )
    d.taps = lateral.shape[1]
    d.micro = micro
    d.groups = lax.axis_size("dp")
    groups = d.groups
    rows, pads = d.rows, d.rows + 2 * cells
    swap = [(0, 1), (1, 0)]
    own_slow = edge_slow.reshape(micro, frames, cells, cs)
    own_fast = edge_fast.reshape(micro, frames, quad, cells, d.cf)

    def across(value, pairs=swap):
        return lax.ppermute(value, "pipe", pairs)

    inner = 1
    while 4 * inner * inner <= groups:
        inner *= 2
    outer = groups // inner
    group = lax.axis_index("dp")
    sect = lax.axis_index("pipe")
    shift_by = inner.bit_length() - 1
    turned = [
        sum(((i >> b) & 1) << (shift_by - 1 - b) for b in range(shift_by)) for i in range(inner)
    ]
    turned_place = jnp.int32(0)
    for b in range(shift_by):
        turned_place += (lax.shift_right_logical(group, jnp.int32(b)) & 1) << (shift_by - 1 - b)
    far_place = lax.shift_right_logical(group, jnp.int32(shift_by))
    ids = jnp.stack([sect, group, group & (inner - 1), far_place, turned_place]).astype(jnp.int32)
    meta = jnp.concatenate([ids, present.reshape(-1), crop_side.reshape(-1)])
    own_fast, lat_own, fr_own, ids = lax.optimization_barrier(
        (own_fast, lateral[0], jnp.swapaxes(fast_reduce[0], 1, 2), ids)
    )
    other_fast, lat_other, fr_other = across(own_fast), across(lat_own), across(fr_own)
    red_own, own_slow, fr_other, lat_other, other_fast, meta = lax.optimization_barrier(
        (slow_reduce[0], own_slow, fr_other, lat_other, other_fast, meta)
    )
    other_slow, red_other = across(own_slow), across(red_own)
    sems = pltpu.SemaphoreType.DMA

    def stage(*args, **others):
        return run(*args, groups=groups, **others)

    def exchange(part):
        return lax.all_to_all(part, "dp", 0, 0)

    slow_f = ((rows, cs), F32)
    mid_f = ((rows, d.cb), F32)
    fast_f = ((rows, quad * d.cf), F32)
    tiny_f = ((rows, quad * d.fb), F32)
    mid_b = ((rows, d.cb), BF)
    tiny_b = ((rows, quad * d.fb), BF)
    fast_b = ((rows, quad * d.cf), BF)
    small = ((8, LANES), F32)
    large = ((24, LANES), F32)
    xpad_s = ((pads, quad * d.cf), BF)
    spad_s = ((pads, cs), BF)
    mpad_s = ((pads, d.cb), BF)
    gpad_s = ((pads, d.cl + quad * d.fb), BF)
    cols_s = {"cols": ((rows, 9 * d.cb), BF)}
    colf_s = {"colf": ((rows, 9 * quad * d.fb), BF)}
    wa_s = (((quad + 3) * d.cf, d.cl + quad * d.fb), BF)

    out_fast = ((frames, quad, cells, d.cf), BF)
    out_slow = ((frames, cells, cs), BF)
    a0 = stage(
        stage_first(d),
        "stage_a0",
        dict(
            ids=meta,
            own=own_fast,
            other=other_fast,
            hbm_lat_own=lat_own,
            hbm_lat_other=lat_other,
            hbm_fr_own=fr_own,
            hbm_fr_other=fr_other,
        ),
        dict(
            mask=((cells, LANES), F32),
            inv=small,
            wa=wa_s,
            wa1=wa_s,
            xpad=xpad_s,
            cot=out_fast,
            lp=mid_f,
            f1=tiny_f,
            part=small,
        ),
        dict(
            lat_own=(lat_own.shape, BF),
            lat_other=(lat_own.shape, BF),
            fr_own=(fr_own.shape, BF),
            fr_other=(fr_own.shape, BF),
            loads=sems((6,)),
        ),
    )
    fs_own, fe_own, norm_gain, norm_shift, a0_inv = lax.optimization_barrier(
        (fast_spatial.reshape(9, d.fb, d.fb), fast_expand[0], norm_gain, norm_shift, a0.inv)
    )
    fs_other, fe_other = across(fs_own), across(fe_own)
    gain_other, shift_other = across(norm_gain), across(norm_shift)
    mask = a0.mask
    base = dict(mask=mask, inv=a0_inv)
    wa = (a0.wa, a0.wa1)
    rows_es = (cs // 256 + 9) * (d.cb // 2) + 32
    rows_red = 3 * (cs + d.cl) // 2
    rows_first = d.taps * (d.cf // 2) + 32

    def halves_of(body, name, rows_now, ins, scratch, hold):
        made = run(
            body,
            name,
            dict(ids=ids, **ins),
            dict(keep=((rows_now, 256), BF), send=((rows_now, 256), BF)),
            dict(scratch, halves=((2, rows_now, 256), BF)),
            hold=hold,
        )
        return made.keep, across(made.send)

    def halves_es(name, hold, **ins):
        scratch = dict(
            cols_s,
            **colf_s,
            g2=((quad * d.fb, 9 * quad * d.fb), F32),
            g3=((quad * d.fb, quad * d.cf), F32),
            block=((LANES, LANES), F32),
        )
        return halves_of(grads_es(d), "grads_es" + name, rows_es, ins, scratch, hold)

    def halves_red(name, hold, **ins):
        return halves_of(grads_reduce(d), "grads_red" + name, rows_red, ins, {}, hold)

    def halves_first(name, hold, **ins):
        scratch = dict(ga=(((quad + 3) * d.cf, d.cl + quad * d.fb), F32))
        return halves_of(grads_first(d), "grads_first" + name, rows_first, ins, scratch, hold)

    def padded(count):
        unit = 16 * groups
        return -(-count // unit) * unit

    es_all, red_all = padded(rows_es), padded(rows_red + rows_first)
    ga_s = (((quad + 3) * d.cf, d.cl + quad * d.fb), F32)

    def kept(count):
        return dict(keep=((count, 256), BF), send=((count, 256), BF))

    near_1 = (es_all + red_all) // inner

    def shares(count, rows_now):
        return {"to_%d" % k: ((rows_now, 256), BF) for k in range(count)}

    def sent_near(made):
        pairs = lambda k: [(i, i ^ k) for i in range(groups)]
        return {
            "from_%d" % k: made[k] if k == 0 else lax.ppermute(made[k], "dp", pairs(k))
            for k in range(inner)
        }

    bits = [inner << i for i in range(outer.bit_length() - 1)][::-1]
    near_bits = [1 << i for i in range(shift_by)]

    def over(value, bit):
        return lax.ppermute(value, "dp", [(i, i ^ bit) for i in range(groups)])

    def targets(made, count):
        return [getattr(made, "to_%d" % k) for k in range(count)]

    def pieces_of(*pieces):
        return {
            "%s_%d" % (key, i): value
            for i, piece in enumerate(pieces)
            for key, value in zip(("keep", "got"), piece)
        }

    arrived = (other_slow, red_other, fs_other, fe_other, gain_other, shift_other)
    part = run(gate, "gate", dict(part=a0.part), dict(out=(a0.part.shape, F32)), far_hold=arrived).out
    sync = exchange(part)
    sp_own, ex_own, sync = lax.optimization_barrier(
        (slow_spatial.reshape(9 * d.cb, d.cb), slow_expand[0], sync)
    )
    sp_other, ex_other = across(sp_own), across(ex_own)
    packed_2 = ((9 * quad * d.fb, quad * d.fb), BF)
    packed_3 = ((quad * d.fb, quad * d.cf), BF)
    norm_s = ((2 * SHIFT_ROW, LANES), F32)
    red_s = (red_own.shape, BF)
    slow_in = pack = stage(
        stage_slow_in(d),
        "stage_slow_in",
        dict(
            ids=ids,
            mask=mask,
            own=own_slow,
            other=other_slow,
            hbm_red_own=red_own,
            hbm_red_other=red_other,
            hbm_fs_own=fs_own,
            hbm_fs_other=fs_other,
            hbm_fe_own=fe_own,
            hbm_fe_other=fe_other,
            hbm_gain_own=norm_gain,
            hbm_gain_other=gain_other,
            hbm_shift_own=norm_shift,
            hbm_shift_other=shift_other,
        ),
        dict(
            spad=spad_s,
            cot=out_slow,
            y=mid_f,
            wred_0=red_s,
            w2_0=packed_2,
            w2_1=packed_2,
            w2t_0=packed_2,
            w2t_1=packed_2,
            w3_0=packed_3,
            w3_1=packed_3,
            par_0=norm_s,
            par_1=norm_s,
        ),
        dict(
            fs_own=(fs_own.shape, BF),
            fs_other=(fs_own.shape, BF),
            fe_own=(fe_own.shape, BF),
            fe_other=(fe_own.shape, BF),
            gain_own=(norm_gain.shape, F32),
            gain_other=(norm_gain.shape, F32),
            shift_own=(norm_gain.shape, F32),
            shift_other=(norm_gain.shape, F32),
            loads=sems((10,)),
            sems=sems((1,)),
        ),
        hold=(sync,),
    )
    w2, w2t = (pack.w2_0, pack.w2_1), (pack.w2t_0, pack.w2t_1)
    w3, par = (pack.w3_0, pack.w3_1), (pack.par_0, pack.par_1)

    def common(layer):
        return dict(base, par=par[layer])

    b0 = stage(
        stage_second(d, 0, False),
        "stage_b0",
        dict(
            common(0),
            sync=sync,
            lp=a0.lp,
            f1=a0.f1,
            y=slow_in.y,
            wred=slow_in.wred_0,
            w2=w2[0],
            ids=ids,
            hbm_red_own=red_own,
            hbm_red_other=red_other,
        ),
        dict(
            lapad=mpad_s,
            k1=tiny_b,
            s1=mid_f,
            f2=tiny_f,
            tot=small,
            wred_1=red_s,
            part=small,
        ),
        dict(colf_s, sems=sems((1,))),
        far_hold=(sp_other, ex_other),
    )
    sync = exchange(b0.part)
    wred = (slow_in.wred_0, b0.wred_1)
    c0 = stage(
        stage_third(d, True),
        "stage_c0",
        dict(
            common(0),
            ids=ids,
            sync=sync,
            s1=b0.s1,
            f2=b0.f2,
            w3=w3[0],
            hbm_sp_own=sp_own,
            hbm_sp_other=sp_other,
            hbm_ex_own=ex_own,
            hbm_ex_other=ex_other,
        ),
        dict(
            h1=mid_b,
            k2=tiny_b,
            s2=mid_f,
            f3=fast_f,
            tot=small,
            wsp_0=(sp_own.shape, BF),
            we_0=(ex_own.shape, BF),
            part=small,
        ),
        dict(cols_s, sems=sems((2,))),
    )
    sync = exchange(c0.part)
    d0 = stage(
        stage_fourth(d, False),
        "stage_d0",
        dict(common(0), sync=sync, s2=c0.s2, f3=c0.f3, we=c0.we_0,
            ids=ids,
            hbm_sp_own=sp_own,
            hbm_sp_other=sp_other,
            hbm_ex_own=ex_own,
            hbm_ex_other=ex_other, xpad=a0.xpad, wa=wa[1]),
        dict(h2=mid_b, s3=slow_f, ypad=xpad_s, lp=mid_f, f1=tiny_f, tot=small, wsp_1=(sp_own.shape, BF), we_1=(ex_own.shape, BF), part=large),
        dict(sems=sems((2,))),
    )
    sync = exchange(d0.part)
    we, wsp = (c0.we_0, d0.we_1), (c0.wsp_0, d0.wsp_1)
    b1 = stage(
        stage_second(d, 16, True),
        "stage_b1",
        dict(
            base,
            par=par[1],
            par0=par[0],
            sync=sync,
            lp=d0.lp,
            f1=d0.f1,
            s3=d0.s3,
            xpad=slow_in.spad,
            wred=wred[1],
            w2=w2[1],
        ),
        dict(spad=spad_s, lapad=mpad_s, k1=tiny_b, s1=mid_f, f2=tiny_f, tot=large, part=small),
        colf_s,
    )
    sync = exchange(b1.part)
    c1 = stage(
        stage_third(d, False),
        "stage_c1",
        dict(common(1), sync=sync, s1=b1.s1, f2=b1.f2, wsp=wsp[1], w3=w3[1]),
        dict(h1=mid_b, k2=tiny_b, s2=mid_f, f3=fast_f, tot=small, part=small),
        cols_s,
    )
    sync = exchange(c1.part)
    d1 = stage(
        stage_fourth(d, True),
        "stage_d1",
        dict(
            common(1),
            sync=sync,
            s2=c1.s2,
            f3=c1.f3,
            we=we[1],
            xpad=d0.ypad,
            cot=a0.cot,
        ),
        dict(h2=mid_b, s3=slow_f, yout=out_fast, dzf=fast_f, tot=small, part=large),
    )
    sync = exchange(d1.part)
    e1 = stage(
        stage_e(d),
        "stage_e1",
        dict(
            common(1),
            sync=sync,
            s3=d1.s3,
            spad=b1.spad,
            cot=slow_in.cot,
            f3=c1.f3,
            dzf=d1.dzf,
            f2=b1.f2,
            w3=w3[1],
            tot_c=d1.tot,
            tot_b=c1.tot,
        ),
        dict(yout=out_slow, dzs=slow_f, df3=fast_b, d2f=tiny_f, tot=large, part=large),
    )
    sync = exchange(e1.part)
    f1 = stage(
        stage_f(d),
        "stage_f1",
        dict(
            common(1),
            sync=sync,
            s3=d1.s3,
            dzs=e1.dzs,
            s2=c1.s2,
            we=we[1],
            d2f=e1.d2f,
            f2=b1.f2,
            f1=d0.f1,
            w2t=w2t[1],
            tot_d=e1.tot,
            tot_c=d1.tot,
            tot_b=c1.tot,
            tot_a=b1.tot,
        ),
        dict(ds3=((rows, cs), BF), d2=mid_f, df2=tiny_b, d1f=tiny_f, tot=large, part=small),
        colf_s,
    )
    sync = exchange(f1.part)
    g1 = stage(
        stage_g(d),
        "stage_g1",
        dict(
            common(1), sync=sync, d2=f1.d2, s2=c1.s2, s1=b1.s1, wsp=wsp[1], tot_c=d1.tot, tot_b=c1.tot
        ),
        dict(ds2=mid_b, d1=mid_f, tot=small, part=small),
        cols_s,
    )
    sync = exchange(g1.part)
    es1 = halves_es(
        "1",
        (sync,),
        h2=d1.h2,
        k2=c1.k2,
        ds3=f1.ds3,
        df3=e1.df3,
        h1=c1.h1,
        k1=b1.k1,
        ds2=g1.ds2,
        df2=f1.df2,
    )
    h1 = stage(
        stage_h(d),
        "stage_h1",
        dict(
            base,
            par=par[1],
            par0=par[0],
            sync=sync,
            d1=g1.d1,
            s1=b1.s1,
            lp=d0.lp,
            wred=wred[1],
            dzs=e1.dzs,
            s3=d0.s3,
            spad=slow_in.spad,
            tot_b=c1.tot,
            tot_a=b1.tot,
        ),
        dict(dpad=mpad_s, dl=mid_f, dzs0=slow_f, tot=small, part=large),
        hold=(es1[0],),
    )
    sync = exchange(h1.part)
    red1 = halves_red("1", (sync,), spad=b1.spad, lapad=b1.lapad, dpad=h1.dpad)
    es_near = run(
        split_near(1),
        "es1_near",
        dict(ids=ids, **pieces_of(es1)),
        shares(inner, es_all // inner),
        dict(mine=((es_all, 256), BF)),
        hold=(sync,),
    )
    i0 = stage(
        stage_i(d),
        "stage_i0",
        dict(
            base,
            par=par[1],
            par0=par[0],
            sync=sync,
            lp=d0.lp,
            f1=d0.f1,
            d1f=f1.d1f,
            dl=h1.dl,
            wa=wa[1],
            dzf=d1.dzf,
            f3=c0.f3,
            xpad=a0.xpad,
            dzs0=h1.dzs0,
            s3=d0.s3,
            s2=c0.s2,
            we=we[0],
            tot_f=g1.tot,
            tot_a=b1.tot,
            tot_c0=d0.tot,
        ),
        dict(gpad=gpad_s, dzf0=fast_f, ds3=((rows, cs), BF), d2=mid_f, tot=large, part=small),
        hold=(red1[0], es_near.to_0),
    )
    sync = exchange(i0.part)
    es_shares = sent_near(targets(es_near, inner))
    first1 = halves_first("1", (sync, *list(es_shares.values())[1:]), xpad=d0.ypad, gpad=i0.gpad)
    es_sum = run(
        sum_shares,
        "es1_sum",
        es_shares,
        dict(out=((es_all // inner, 256), BF)),
        hold=(first1[0],),
    ).out
    red_near = run(
        split_near(2, turned),
        "red1_near",
        dict(ids=ids, **pieces_of(red1, first1)),
        shares(inner, red_all // inner),
        dict(mine=((red_all, 256), BF)),
        hold=(es_sum,),
    )
    j0 = stage(
        stage_j(d),
        "stage_j0",
        dict(
            common(0),
            sync=sync,
            d2=i0.d2,
            s2=c0.s2,
            s1=b0.s1,
            wsp=wsp[0],
            dzf=i0.dzf0,
            f3=c0.f3,
            f2=b0.f2,
            w3=w3[0],
            tot_c=d0.tot,
            tot_b=c0.tot,
        ),
        dict(ds2=mid_b, d1=mid_f, df3=fast_b, d2f=tiny_f, tot=small, part=small),
        cols_s,
        hold=(red_near.to_0, es_sum),
    )
    sync = exchange(j0.part)
    red_sum = run(
        sum_shares,
        "red1_sum",
        sent_near(targets(red_near, inner)),
        dict(out=((red_all // inner, 256), BF)),
        hold=(sync,),
    ).out
    k0 = stage(
        with_grads(
            with_grads(stage_k(d), grads_reduce(d), {}),
            grads_es(d),
            dict(keep="keep_es", send="send_es", halves="halves_es"),
        ),
        "stage_k0",
        dict(
            common(0),
            ids=ids,
            spad=slow_in.spad,
            lapad=b0.lapad,
            h2=d0.h2,
            k2=c0.k2,
            ds3=i0.ds3,
            df3=j0.df3,
            h1=c0.h1,
            k1=b0.k1,
            ds2=j0.ds2,
            sync=sync,
            d1=j0.d1,
            s1=b0.s1,
            lp=a0.lp,
            wred=wred[0],
            d2f=j0.d2f,
            f2=b0.f2,
            f1=a0.f1,
            w2t=w2t[0],
            tot_b=c0.tot,
            tot_a=b0.tot,
        ),
        dict(
            kept(rows_red),
            keep_es=((rows_es, 256), BF),
            send_es=((rows_es, 256), BF),
            dpad=mpad_s,
            dl=mid_f,
            df2=tiny_b,
            d1f=tiny_f,
            tot=small,
            part=small,
        ),
        dict(
            colf_s,
            **cols_s,
            halves=((2, rows_red, 256), BF),
            halves_es=((2, rows_es, 256), BF),
            g2=((quad * d.fb, 9 * quad * d.fb), F32),
            g3=((quad * d.fb, quad * d.cf), F32),
            block=((LANES, LANES), F32),
        ),
        hold=(red_sum,),
    )
    red0, es0 = (k0.keep, across(k0.send)), (k0.keep_es, across(k0.send_es))
    sync = exchange(k0.part)

    order = [sync]

    def step(body, name, ins, outs, scratch=None, grant=16):
        key = name.rstrip("01")
        made = run(
            body,
            name,
            ins,
            outs,
            scratch,
            hold=(order[-1],),
            groups=groups,
            flops=int(WEIGHT * TIMES.get(key, 0.6)),
            grant=grant,
        )
        order.append(getattr(made, next(iter(outs))))
        return made

    def block(count):
        return ((count, 256), BF)

    b_all, r_all, f_all = padded(rows_es), padded(rows_red), padded(rows_first)
    b_near, r_near, f_near = b_all // inner, r_all // inner, f_all // inner
    es_near, red_near = es_all // inner, red_all // inner

    def down(name, made, bit, after):
        rows_now = made.keep.shape[0]
        extent = rows_now // 2 if after else rows_now
        outs = dict(keep=block(extent))
        if after:
            outs.update(send=block(extent))
        return step(
            next_far(after),
            "%s_down_%d" % (name, bit),
            dict(ids=ids, own=made.keep, got=over(made.send, bit)),
            outs,
            dict(mine=block(rows_now)),
        )

    def up(name, own, bit):
        return step(
            join_far(bit),
            "%s_up_%d" % (name, bit),
            dict(ids=ids, own=own, got=over(own, bit)),
            dict(out=block(2 * own.shape[0])),
        ).out

    def up_pair(name, first, second, bits):
        made = step(
            join_pair(bits),
            "%s_up_%d" % (name, bits[0]),
            dict(
                ids=ids,
                own_0=first,
                got_0=over(first, bits[0]),
                own_1=second,
                got_1=over(second, bits[1]),
            ),
            dict(out_0=block(2 * first.shape[0]), out_1=block(2 * second.shape[0])),
        )
        return made.out_0, made.out_1

    def halved(name, pieces, count, bit):
        return step(
            split_half(len(pieces), bit),
            name + "_split",
            dict(ids=ids, **pieces_of(*pieces)),
            dict(keep=block(count // 2), send=block(count // 2)),
            dict(mine=block(count)),
        )

    far_bits = bits[::-1]
    down_way, turned_way = list(near_bits), near_bits[::-1]

    def merge(name, count, **ins):
        return step(
            merge_far(far_bits[0]),
            name + "_merge",
            dict(ids=ids, **ins),
            dict(keep=block(count // 2), send=block(count // 2)),
            dict(mine=block(count)),
        )

    def apart(name, own, early, late):
        made = step(
            part_far(far_bits[0]),
            name + "_part",
            dict(ids=ids, own=own, got=over(own, far_bits[0])),
            dict(early=block(early), late=block(late)),
            dict(all=block(early + late)),
        )
        return made.early, made.late

    l1 = merge("l1", es_near + red_near, early=es_sum, late=red_sum)
    r_made = halved("r", (red0,), r_all, down_way[0])
    b_made = halved("b", (es0,), b_all, turned_way[0])
    l0 = step(
        stage_l(d),
        "stage_l0",
        dict(
            common(0),
            sync=sync,
            lp=a0.lp,
            f1=a0.f1,
            d1f=k0.d1f,
            dl=k0.dl,
            wa=wa[0],
            dzf=i0.dzf0,
            tot_a=b0.tot,
            ids=ids,
            value=d1.yout,
        ),
        dict(gpad=gpad_s, keep_out=out_fast, send_out=out_fast, tot=small),
    )
    first0 = step(
        grads_first(d),
        "grads_first0",
        dict(ids=ids, xpad=a0.xpad, gpad=l0.gpad),
        kept(rows_first),
        dict(ga=ga_s, halves=((2, rows_first, 256), BF)),
    )
    first0 = (first0.keep, across(first0.send))
    for i, bit in enumerate(far_bits[:-1]):
        l1 = down("l1", l1, bit, far_bits[i + 1])
    slow_out = step(
        stage_slow_out(d),
        "stage_slow_out",
        dict(ids=ids, mask=mask, dpad=k0.dpad, wred=wred[0], dzs=h1.dzs0, value=e1.yout),
        dict(keep_out=out_slow, send_out=out_slow),
    )
    f_made = halved("f", (first0,), f_all, turned_way[0])
    r_made = down("r", r_made, down_way[0], (down_way + [0])[1])
    b_part, f_part = b_all // 2, f_all // 2
    bf_ins = dict(
        own_0=b_made.keep,
        got_0=over(b_made.send, turned_way[0]),
        own_1=f_made.keep,
        got_1=over(f_made.send, turned_way[0]),
    )
    bf_made = step(
        join_parts((b_part, f_part), (turned_way + [0])[1]),
        "bf_down",
        dict(ids=ids, **bf_ins),
        dict(keep=block((b_part + f_part) // 2), send=block((b_part + f_part) // 2)),
        dict(mine=block(b_part + f_part)),
    )
    for i, bit in enumerate(turned_way[1:-1]):
        b_part, f_part = b_part // 2, f_part // 2
        bf_made = step(
            next_parts((b_part, f_part), turned_way[i + 2]),
            "bf_down_%d" % bit,
            dict(ids=ids, own=bf_made.keep, got=over(bf_made.send, bit)),
            dict(keep=block((b_part + f_part) // 2), send=block((b_part + f_part) // 2)),
            dict(mine=block(b_part + f_part)),
        )
    l1 = down("l1", l1, far_bits[-1], 0).keep
    at_1 = dict(
        s1=("h1", 0), s2=("g1", 0), s3=("f1", 0), f1=("g1", 4), f2=("f1", 16), f3=("e1", 16), lp=("i0", 16)
    )
    at_0 = dict(
        s1=("k0", 0), s2=("j0", 0), s3=("i0", 0), f1=("l0", 4), f2=("k0", 4), f3=("j0", 4), lp=("l0", 0)
    )
    norms = step(
        norms_out(d, (at_0, at_1)),
        "norms_out",
        dict(
            ids=ids,
            e1=e1.tot,
            f1=f1.tot,
            g1=g1.tot,
            h1=h1.tot,
            i0=i0.tot,
            j0=j0.tot,
            k0=k0.tot,
            l0=l0.tot,
        ),
        dict(keep=((2, norm_gain.shape[1]), F32), send=((2, norm_gain.shape[1]), F32)),
    )
    for bit in far_bits[:0:-1]:
        l1 = up("l1", l1, bit)
    for i, bit in enumerate(down_way[1:]):
        r_made = down("r", r_made, bit, (down_way + [0])[i + 2])
    bf_near = b_near + f_near
    t = merge(
        "t",
        r_near + bf_near,
        early=r_made.keep,
        own=bf_made.keep,
        got=over(bf_made.send, turned_way[-1]),
    )
    def placed(name, made):
        whole = (micro,) + made.keep_out.shape
        return step(
            stage_place,
            "place_" + name,
            dict(ids=ids, keep=made.keep_out, got=across(made.send_out)),
            dict(mark=small, hbm_out=(whole, BF)),
            dict(both=(whole, BF), sems=sems((2,))),
        ).hbm_out

    placed_fast = placed("fast", l0)
    es1_all, red1_all = apart("l1", l1, es_near, red_near)
    for i in range(shift_by - 1):
        es1_all, red1_all = up_pair("l1", es1_all, red1_all, (down_way[i], turned_way[i]))
    for i, bit in enumerate(far_bits):
        t = down("t", t, bit, (far_bits + [0])[i + 1])
        if i == 0:
            placed_slow = placed("slow", slow_out)
    t = t.keep
    for bit in far_bits[:0:-1]:
        t = up("t", t, bit)
    r_up, bf_up = apart("t", t, r_near, bf_near)
    es1_all, red1_all = up_pair("l1", es1_all, red1_all, (down_way[-1], turned_way[-1]))
    for i in range(shift_by - 1):
        r_up, bf_up = up_pair("r_bf", r_up, bf_up, (turned_way[i], down_way[i]))
    norms = step(
        norms_add,
        "norms_add",
        dict(keep=norms.keep, got=across(norms.send)),
        dict(gain=(norm_gain.shape, F32), shift=(norm_shift.shape, F32)),
    )

    def last(name, own, second, bit):
        made = step(
            join_send(bit),
            name + "_last",
            dict(ids=ids, own=own, got=over(own, bit), second=second),
            dict(out=block(2 * own.shape[0]), send=block(max(2 * own.shape[0], second.shape[0]))),
        )
        return made, across(made.send)

    r_all_up, got_a = last("r", r_up, red1_all, turned_way[-1])
    b_all_up, got_b = last("bf", bf_up, es1_all, down_way[-1])
    spots = dict(
        r=("own_r", "got_a", r_all, r_all, 0),
        red=("own_red", "got_a", red_all, red_all, 0),
        b=("own_b", "got_b", b_near, bf_near, 0),
        f=("own_b", "got_b", f_near, bf_near, b_near),
        es=("own_es", "got_b", es_all, es_all, 0),
    )
    done_red = step(
        finish_reduce(d, spots),
        "finish_reduce",
        dict(ids=ids, own_r=r_all_up.out, own_red=red1_all, got_a=got_a),
        dict(mark=small, hbm_reduce=(slow_reduce.shape, F32)),
        dict(reduce=((3, cs + d.cl, d.cb), F32), sems=sems((3,))),
    )
    done = step(
        finish_rest(d, spots, rows_red),
        "finish_rest",
        dict(
            ids=ids,
            own_red=red1_all,
            got_a=got_a,
            own_b=b_all_up.out,
            own_es=es1_all,
            got_b=got_b,
        ),
        dict(
            fspace=((1, 9, d.fb, d.fb), F32),
            hbm_expand=(slow_expand.shape, F32),
            hbm_space=((1, 9, d.cb, d.cb), F32),
            fexpand=(fast_expand.shape, F32),
            lateral=(lateral.shape, F32),
            freduce=((1, 3, d.fb, d.cf), F32),
        ),
        dict(
            expand=((d.cb, cs), F32),
            space=((9, d.cb, d.cb), F32),
            block=((LANES, LANES), F32),
            sems=sems((2,)),
        ),
    )
    weights = (
        done_red.hbm_reduce,
        done.hbm_space.reshape(slow_spatial.shape),
        done.hbm_expand,
        jnp.swapaxes(done.freduce, 2, 3),
        done.fspace.reshape(fast_spatial.shape),
        done.fexpand,
        done.lateral,
    )

    return (
        placed_slow.reshape(edge_slow.shape),
        placed_fast.reshape(edge_fast.shape),
        *weights,
        norms.gain,
        norms.shift,
    )


def solution(mesh):
    edge = P("pipe", None, "dp", None, None, None, None)
    weights = (
        P("pipe", None, None, None),
        P("pipe", None, None, None, None),
        P("pipe", None, None),
        P("pipe", None, None, None),
        P("pipe", None, None, None, None),
        P("pipe", None, None),
        P("pipe", None, None, None),
    )
    norms = (P("pipe", None), P("pipe", None))
    return jax.shard_map(
        on_device,
        mesh=mesh,
        in_specs=(edge, edge, *weights, *norms, P(), P()),
        out_specs=(edge, edge, *weights, *norms),
        check_vma=False,
    )
```

```python
from types import SimpleNamespace

import jax
import jax.numpy as jnp
from jax import lax
from jax.experimental import pallas as pl
from jax.experimental.pallas import tpu as pltpu
from jax.sharding import PartitionSpec as P

epsilon = 1e-05
F32 = jnp.float32
BF = jnp.bfloat16
LANES = 128
SPAN = {
    "s1": (0, 2),
    "s2": (2, 2),
    "s3": (4, 8),
    "f1": (12, 1),
    "f2": (13, 1),
    "f3": (14, 1),
    "lp": (15, 2),
}
SHIFT_ROW = 24
TIMES = {
    "grads_es": 2.4,
    "stage_l": 1.8,
    "grads_first": 1.3,
    "stage_slow_out": 1.8,
    "r_split": 1.1,
    "b_split": 1.1,
    "place_fast": 1.7,
    "place_slow": 2.1,
    "finish_reduce": 2.6,
    "finish_rest": 3.4,
}
WEIGHT = 0.0


SMEM_KEYS = ("ids",)


def space_of(key):
    if key in SMEM_KEYS:
        return pltpu.SMEM
    if key.startswith("hbm_"):
        return pltpu.HBM
    if key.startswith("any_"):
        return pl.ANY
    return pltpu.VMEM


def run(body, name, ins, outs, scratch=None, hold=(), far_hold=(), groups=1, flops=2_000_000_000, grant=16):
    scratch = dict(scratch or {})
    outs = dict(outs)
    ins = dict(ins, **{"any_hold%d" % i: value for i, value in enumerate(hold)})
    ins = dict(ins, **{"hbm_hold%d" % i: value for i, value in enumerate(far_hold)})
    shared = "part" in outs
    if shared:
        shape, kind = outs["part"]
        scratch["sums"] = (shape, kind)
        outs["part"] = ((groups,) + shape, kind)
    names = list(ins) + list(outs) + list(scratch)

    def kernel(*refs):
        r = SimpleNamespace(**dict(zip(names, refs)))
        if not shared:
            body(r)
            return
        spread = r.part
        r.part = r.sums
        r.sums[...] = jnp.zeros(r.sums.shape, F32)
        body(r)

        def copy(i, carry):
            spread[i] = r.sums[...]
            return carry

        lax.fori_loop(0, groups, copy, 0)

    result = pl.pallas_call(
        kernel,
        name=name,
        out_shape=[jax.ShapeDtypeStruct(shape, kind) for shape, kind in outs.values()],
        in_specs=[pl.BlockSpec(memory_space=space_of(key)) for key in ins],
        out_specs=[pl.BlockSpec(memory_space=space_of(key)) for key in outs],
        scratch_shapes=[
            pltpu.VMEM(*item) if isinstance(item, tuple) else item for item in scratch.values()
        ],
        compiler_params=pltpu.CompilerParams(vmem_limit_bytes=grant * 1024 * 1024),
        cost_estimate=pl.CostEstimate(flops=flops, bytes_accessed=1000, transcendentals=0),
    )(*ins.values())
    return SimpleNamespace(**dict(zip(outs, result)))


def dot(a, b):
    return lax.dot_general(a, b, (((1,), (0,)), ((), ())), preferred_element_type=F32)


def dot_t(a, b):
    return lax.dot_general(a, b, (((1,), (1,)), ((), ())), preferred_element_type=F32)


def t_dot(a, b):
    return lax.dot_general(a, b, (((0,), (0,)), ((), ())), preferred_element_type=F32)


def sigm(v):
    return 0.5 * jnp.tanh(0.5 * v) + 0.5


def slope_of(v):
    s = sigm(v)
    return s * (1.0 + v * (1.0 - s))


def fold8(x):
    return jnp.sum(x.reshape(x.shape[0] // 8, 8, x.shape[1]), axis=0)


def wide(row, width):
    return row if row.shape[1] == width else jnp.concatenate([row] * (width // row.shape[1]), axis=1)


def lanes_of(block, start, count):
    if count == 1:
        return block[start : start + 1, :]
    return jnp.concatenate([block[start + i : start + i + 1, :] for i in range(count)], axis=1)


def put(part, row, acc8):
    total = jnp.sum(acc8, axis=0, keepdims=True)
    for i in range(total.shape[1] // LANES):
        part[row + i : row + i + 1, :] = total[:, i * LANES : (i + 1) * LANES]


def quarters(acc, width):
    count = acc.shape[1] // width
    total = acc[:, :width]
    for i in range(1, count):
        total = total + acc[:, i * width : (i + 1) * width]
    return total


def folded(tot, width):
    total = tot
    for i in range(1, LANES // width):
        total = total + pltpu.roll(tot, i * width, 1)
    return total


def gain(r, key):
    start, count = SPAN[key]
    return lanes_of(r.par[...], start, count)


def shift(r, key):
    start, count = SPAN[key]
    return lanes_of(r.par[...], SHIFT_ROW + start, count)


def moments(tot, row, key, inv, fast_bottle=32):
    count = SPAN[key][1]
    block = folded(tot, fast_bottle) if key in ("f1", "f2") else tot
    mean = lanes_of(block, row, count) * inv
    square = lanes_of(block, row + count, count) * inv
    return mean, lax.rsqrt(square - mean * mean + epsilon)


def pair_of(tot, row, key, fast_bottle=32):
    count = SPAN[key][1]
    block = folded(tot, fast_bottle) if key in ("f1", "f2") else tot
    return lanes_of(block, row, count), lanes_of(block, row + count, count)


def invs(r):
    return r.inv[0:1, :1], r.inv[1:2, :1]


def norm_of(r, tot, row, key, inv, width=None):
    mean, rs = moments(tot, row, key, inv)
    scale = rs * gain(r, key)
    offset = shift(r, key) - mean * scale
    if width is None:
        return mean, rs, scale, offset
    return tuple(wide(v, width) for v in (mean, rs, scale, offset))


def windows(x, side):
    rows, width = x.shape
    col = lax.broadcasted_iota(jnp.int32, (rows, width), 0) % side
    zero = jnp.zeros((side, width), x.dtype)
    out = {}
    for c in range(3):
        step = c - 1
        if step == 0:
            y = x
        else:
            y = pltpu.roll(x, (-step) % rows, 0)
            y = jnp.where((col + step >= 0) & (col + step < side), y, 0.0)
        out[0, c] = jnp.concatenate([zero, y[: rows - side]], axis=0)
        out[1, c] = y
        out[2, c] = jnp.concatenate([y[side:], zero], axis=0)
    return out


def put_windows(col, at, x, side, back):
    width = x.shape[1]
    for (i, j), y in windows(x, side).items():
        if back:
            i, j = 2 - i, 2 - j
        spot = (i * 3 + j) * width
        col[at, spot : spot + width] = y.astype(BF)


def loop(count, body, init=0):
    return lax.fori_loop(0, count, body, init, unroll=True)


def at_frame(t, cells, lead=0):
    return pl.ds(pl.multiple_of(t * cells, cells) + lead, cells)


def spans(total, step):
    return [(a, step) for a in range(0, total, step)]


def clear_ends(pad, cells):
    rows, width = pad.shape
    zero = jnp.zeros((cells, width), pad.dtype)
    pad[0:cells, :] = zero
    pad[rows - cells : rows, :] = zero


def chosen(r, layer, own, other):
    return jnp.where(r.ids[0] == layer, own, other)


def lane_group(shape, width):
    return lax.div(lax.broadcasted_iota(jnp.int32, shape, 1), width)


def placing(rows, group):
    lane = lax.broadcasted_iota(jnp.int32, (rows, LANES), 1)
    row = lax.broadcasted_iota(jnp.int32, (rows, LANES), 0)
    hit = lax.rem(lane, rows) == row if group is None else lane - group * rows == row
    return jnp.where(hit, 1.0, 0.0).astype(BF)


def first_mix(r, d, xpad, part, row):
    acc_s = acc_q = 0.0
    for a, n in spans(d.rows, d.step):
        got = (
            dot(xpad[a : a + n, 2 * d.cf : 4 * d.cf], r.wa[0 : 2 * d.cf, :])
            + dot(xpad[a + d.cells : a + d.cells + n, :], r.wa[2 * d.cf : 6 * d.cf, :])
            + dot(xpad[a + 2 * d.cells : a + 2 * d.cells + n, 0 : d.cf], r.wa[6 * d.cf : 7 * d.cf, :])
        )
        r.lp[a : a + n, :] = got[:, : d.cl]
        r.f1[a : a + n, :] = got[:, d.cl :]
        acc_s = acc_s + fold8(got)
        acc_q = acc_q + fold8(got * got)
    put(part, row, acc_s[:, : d.cl])
    put(part, row + 2, acc_q[:, : d.cl])
    put(part, row + 4, acc_s[:, d.cl :])
    put(part, row + 5, acc_q[:, d.cl :])


def stage_first(d):
    def body(r):
        sect, group = r.ids[0], r.ids[1]
        small = loading(
            r,
            [
                (r.hbm_lat_own, r.lat_own),
                (r.hbm_lat_other, r.lat_other),
                (r.hbm_fr_own, r.fr_own),
                (r.hbm_fr_other, r.fr_other),
            ],
        )

        def present_at(i):
            return 5 + sect * d.groups + i

        def crop_at(i):
            return 5 + (d.micro + sect) * d.groups + i

        def add(i, total):
            extent = r.ids[crop_at(i)]
            return total + jnp.where(r.ids[present_at(i)] > 0, extent * extent, 0)

        area = lax.fori_loop(0, d.groups, add, jnp.int32(0))
        area = jnp.full((1, LANES), area.astype(F32))
        r.inv[...] = jnp.zeros(r.inv.shape, F32)
        r.inv[0:1, :] = 1.0 / (area * d.frames)
        r.inv[1:2, :] = 1.0 / (area * (d.frames * d.quad))
        limit = jnp.where(r.ids[present_at(group)] > 0, r.ids[crop_at(group)], 0)
        cell = lax.broadcasted_iota(jnp.int32, (d.cells, LANES), 0)
        inside = (lax.div(cell, d.side) < limit) & (lax.rem(cell, d.side) < limit)
        mask = jnp.where(inside, 1.0, 0.0)
        r.mask[...] = mask
        small()
        for layer, wa in enumerate((r.wa, r.wa1)):
            for b in range(d.quad + 3):
                row = slice(b * d.cf, (b + 1) * d.cf)
                if b < d.taps:
                    wa[row, : d.cl] = chosen(r, layer, r.lat_own[b], r.lat_other[b])
                else:
                    wa[row, : d.cl] = jnp.zeros((d.cf, d.cl), BF)
                total = jnp.zeros((d.cf, LANES), F32)
                for q in range(d.quad):
                    k = b - 1 - q
                    if 0 <= k < 3:
                        tap = chosen(r, layer, r.fr_own[k], r.fr_other[k])
                        total = total + t_dot(tap, placing(d.fb, q))
                wa[row, d.cl :] = total.astype(BF)
        clear_ends(r.xpad, d.cells)

        def frame(t, carry):
            for q in range(d.quad):
                here = r.own[sect, t, q].astype(F32)
                there = r.other[sect, t, q].astype(F32)
                value = jnp.where(sect == 0, here, there)
                r.xpad[at_frame(t, d.cells, d.cells), q * d.cf : (q + 1) * d.cf] = (
                    value * mask
                ).astype(BF)
                r.cot[t, q] = jnp.where(sect == 0, there, here).astype(BF)
            return carry

        loop(d.frames, frame)
        first_mix(r, d, r.xpad, r.part, 0)

    return body


def stage_slow_in(d):
    pack = stage_pack(d)

    def body(r):
        sect = r.ids[0]
        names = ("fs", "fe", "gain", "shift")
        small = loading(
            r,
            [
                (getattr(r, "hbm_%s_%s" % (name, side)), getattr(r, "%s_%s" % (name, side)))
                for name in names
                for side in ("own", "other")
            ],
        )
        fetch = fetching(r, 0, [(r.hbm_red_own, r.hbm_red_other, r.wred_0)])
        small()
        pack(r)
        clear_ends(r.spad, d.cells)
        mask = wide(r.mask[...], 256)

        def frame(t, carry):
            for c in range(0, d.cs, 256):
                lane = slice(c, c + 256)
                here = r.own[sect, t, :, lane].astype(F32)
                there = r.other[sect, t, :, lane].astype(F32)
                value = jnp.where(sect == 0, here, there)
                r.spad[at_frame(t, d.cells, d.cells), lane] = (value * mask).astype(BF)
                r.cot[t, :, lane] = jnp.where(sect == 0, there, here).astype(BF)
            return carry

        loop(d.frames, frame)
        fetch()
        for a, n in spans(d.rows, d.step):
            got = 0.0
            for k in range(3):
                b = a + k * d.cells
                got = got + dot(r.spad[b : b + n, :], r.wred_0[k, : d.cs, :])
            r.y[a : a + n, :] = got

    return body


def stage_pack(d):
    sizes = [d.cb, d.cb, d.cs, d.fb, d.fb, d.cf, d.cl]
    keys = ["s1", "s2", "s3", "f1", "f2", "f3", "lp"]

    def body(r):
        spread = placing(d.fb, None)
        for layer in range(2):
            w2, w2t, w3, par = (
                (r.w2_0, r.w2t_0, r.w3_0, r.par_0),
                (r.w2_1, r.w2t_1, r.w3_1, r.par_1),
            )[layer]
            where = lane_group((d.fb, LANES), d.fb)
            for j in range(9):
                tap = chosen(r, layer, r.fs_own[j], r.fs_other[j])
                for out, tiled in ((w2, dot(tap, spread)), (w2t, t_dot(tap, spread))):
                    for q in range(d.quad):
                        row = j * LANES + q * d.fb
                        out[row : row + d.fb, :] = jnp.where(where == q, tiled, 0.0).astype(BF)
            w3[...] = jnp.zeros(w3.shape, BF)
            tap = chosen(r, layer, r.fe_own[...], r.fe_other[...])
            for q in range(d.quad):
                w3[q * d.fb : (q + 1) * d.fb, q * d.cf : (q + 1) * d.cf] = tap
            par[...] = jnp.zeros(par.shape, F32)
            for base, own, other in (
                (0, r.gain_own, r.gain_other),
                (SHIFT_ROW, r.shift_own, r.shift_other),
            ):
                values = chosen(r, layer, own[...], other[...])
                offset = 0
                for key, size in zip(keys, sizes):
                    row = base + SPAN[key][0]
                    piece = values[:, offset : offset + size]
                    offset += size
                    if size < LANES:
                        par[row : row + 1, :] = wide(piece, LANES)
                    else:
                        for i in range(size // LANES):
                            par[row + i : row + i + 1, :] = piece[:, i * LANES : (i + 1) * LANES]

    return body


def fetching(r, layer, weights, sem=0):
    def copies(first):
        return [
            pltpu.make_async_copy(own if first == (layer == 0) else other, out, r.sems.at[sem + i])
            for i, (own, other, out) in enumerate(weights)
        ]

    def each(action):
        for first in (True, False):

            @pl.when(r.ids[0] == 0 if first else r.ids[0] != 0)
            def _():
                for copy in copies(first):
                    action(copy)

    each(lambda copy: copy.start())
    return lambda: each(lambda copy: copy.wait())


def loading(r, pairs, first=0):
    copies = [
        pltpu.make_async_copy(source, target, r.loads.at[first + i])
        for i, (source, target) in enumerate(pairs)
    ]
    for copy in copies:
        copy.start()

    def wait():
        for copy in copies:
            copy.wait()

    return wait


def gate(r):
    r.out[...] = r.part[...]


def sort_out(r, grad, value, at):
    first = r.ids[0] == 0
    grad, value = grad.astype(F32), value.astype(F32)
    r.keep_out[at] = jnp.where(first, grad, value).astype(BF)
    r.send_out[at] = jnp.where(first, value, grad).astype(BF)


def stage_place(r):
    r.mark[...] = jnp.zeros(r.mark.shape, F32)
    copies = []
    for i in range(2):
        for t in range(r.keep.shape[0]):
            keep, got = r.keep[t].astype(F32), r.got[t].astype(F32)
            r.both[i, t] = jnp.where(r.ids[0] == i, keep, got).astype(BF)
        copies.append(pltpu.make_async_copy(r.both.at[i], r.hbm_out.at[i], r.sems.at[i]))
        copies[-1].start()
    for copy in copies:
        copy.wait()


def stage_second(d, row, carried):
    def body(r):
        if not carried:
            fetch = fetching(r, 0, [(r.hbm_sp_own, r.hbm_sp_other, r.wsp_0)])
        tot = jnp.sum(r.sync[...], axis=0)
        r.tot[...] = tot
        inv_s, inv_f = invs(r)
        _, _, lg, lb = norm_of(r, tot, row, "lp", inv_s)
        _, _, fg, fb = norm_of(r, tot, row + 4, "f1", inv_f)
        mask = r.mask[...]
        mask2 = wide(mask, d.cl)
        clear_ends(r.lapad, d.cells)
        if carried:
            clear_ends(r.spad, d.cells)
            _, _, sg, sb = norm_of(SimpleNamespace(par=r.par0), tot, 0, "s3", inv_s)

        def frame(t, carry):
            at = at_frame(t, d.cells)
            up = at_frame(t, d.cells, d.cells)
            v = r.lp[at, :] * lg + lb
            r.lapad[up, :] = (v * sigm(v) * mask2).astype(BF)
            v = r.f1[at, :] * fg + fb
            v = (v * sigm(v) * mask).astype(BF)
            r.k1[at, :] = v
            put_windows(r.colf, at, v.astype(F32), d.side, False)
            if carried:
                for c in range(0, d.cs, 256):
                    z = r.xpad[up, c : c + 256].astype(F32) + (
                        r.s3[at, c : c + 256] * sg[:, c : c + 256] + sb[:, c : c + 256]
                    )
                    r.spad[up, c : c + 256] = (z * sigm(z) * mask2).astype(BF)
            return carry

        loop(d.frames, frame)
        acc_s = acc_q = acc_fs = acc_fq = 0.0
        for a, n in spans(d.rows, d.step):
            got = 0.0 if carried else r.y[a : a + n, :]
            for k in range(3):
                b = a + k * d.cells
                if carried:
                    got = got + dot(r.spad[b : b + n, :], r.wred[k, : d.cs, :])
                got = got + dot(r.lapad[b : b + n, :], r.wred[k, d.cs :, :])
            r.s1[a : a + n, :] = got
            acc_s = acc_s + fold8(got)
            acc_q = acc_q + fold8(got * got)
            got = dot(r.colf[a : a + n, :], r.w2[...])
            r.f2[a : a + n, :] = got
            kept = (got.reshape(n // d.cells, d.cells, got.shape[1]) * mask[None]).reshape(got.shape)
            acc_fs = acc_fs + fold8(kept)
            acc_fq = acc_fq + fold8(kept * got)
        put(r.part, 0, acc_s)
        put(r.part, 2, acc_q)
        put(r.part, 4, acc_fs)
        put(r.part, 5, acc_fq)
        if not carried:
            fetch()

    return body


def stage_third(d, fetched):
    def body(r):
        if fetched:
            early = fetching(r, 0, [(r.hbm_ex_own, r.hbm_ex_other, r.we_0)])
            late = fetching(r, 1, [(r.hbm_red_own, r.hbm_red_other, r.wred_1)], 1)
        tot = jnp.sum(r.sync[...], axis=0)
        r.tot[...] = tot
        inv_s, inv_f = invs(r)
        _, _, sg, sb = norm_of(r, tot, 0, "s1", inv_s)
        _, _, fg, fb = norm_of(r, tot, 4, "f2", inv_f)
        mask = r.mask[...]
        mask2 = wide(mask, d.cb)

        def frame(t, carry):
            at = at_frame(t, d.cells)
            v = r.s1[at, :] * sg + sb
            v = (v * sigm(v) * mask2).astype(BF)
            r.h1[at, :] = v
            put_windows(r.cols, at, v.astype(F32), d.side, False)
            v = r.f2[at, :] * fg + fb
            r.k2[at, :] = (v * sigm(v) * mask).astype(BF)
            return carry

        loop(d.frames, frame)
        wsp = r.wsp
        acc_s = acc_q = acc_fs = acc_fq = 0.0
        for a, n in spans(d.rows, d.step):
            got = dot(r.cols[a : a + n, :], wsp[...])
            r.s2[a : a + n, :] = got
            kept = (got.reshape(n // d.cells, d.cells, got.shape[1]) * mask2[None]).reshape(got.shape)
            acc_s = acc_s + fold8(kept)
            acc_q = acc_q + fold8(kept * got)
            got = dot(r.k2[a : a + n, :], r.w3[...])
            r.f3[a : a + n, :] = got
            acc_fs = acc_fs + fold8(got)
            acc_fq = acc_fq + fold8(got * got)
        put(r.part, 0, acc_s)
        put(r.part, 2, acc_q)
        put(r.part, 4, quarters(acc_fs, d.cf))
        put(r.part, 5, quarters(acc_fq, d.cf))
        if fetched:
            early()
            late()

    return body


def expand_slow(r, d, sg, sb, mask2):
    def frame(t, carry):
        at = at_frame(t, d.cells)
        v = r.s2[at, :] * sg + sb
        r.h2[at, :] = (v * sigm(v) * mask2).astype(BF)
        return carry

    loop(d.frames, frame)
    for c in range(0, d.cs, 256):
        acc_s = acc_q = 0.0
        for a, n in spans(d.rows, d.step):
            got = dot(r.h2[a : a + n, :], r.we[:, c : c + 256])
            r.s3[a : a + n, c : c + 256] = got
            acc_s = acc_s + fold8(got)
            acc_q = acc_q + fold8(got * got)
        put(r.part, c // LANES, acc_s)
        put(r.part, (d.cs + c) // LANES, acc_q)


def stage_fourth(d, last):
    def body(r):
        if not last:
            fetch = fetching(
                r,
                1,
                [
                    (r.hbm_sp_own, r.hbm_sp_other, r.wsp_1),
                    (r.hbm_ex_own, r.hbm_ex_other, r.we_1),
                ],
            )
        tot = jnp.sum(r.sync[...], axis=0)
        r.tot[...] = tot
        inv_s, inv_f = invs(r)
        _, _, sg, sb = norm_of(r, tot, 0, "s2", inv_s)
        fm, fr, fg, fb = norm_of(r, tot, 4, "f3", inv_f)
        mask = r.mask[...]
        mask2 = wide(mask, d.cb)
        expand_slow(r, d, sg, sb, mask2)
        if not last:
            clear_ends(r.ypad, d.cells)

        def frame(t, carry):
            at = at_frame(t, d.cells)
            up = at_frame(t, d.cells, d.cells)
            for q in range(d.quad):
                lane = slice(q * d.cf, (q + 1) * d.cf)
                f3 = r.f3[at, lane]
                z = r.xpad[up, lane].astype(F32) + (f3 * fg + fb)
                s = sigm(z)
                y = (z * s * mask).astype(BF)
                if last:
                    r.yout[t, q] = y
                    grad = r.cot[t, q].astype(F32) * mask * (s * (1.0 + z * (1.0 - s)))
                    r.dzf[at, lane] = grad
                    u = (f3 - fm) * fr
                    carry = (carry[0] + fold8(grad), carry[1] + fold8(grad * u))
                else:
                    r.ypad[up, lane] = y
            return carry

        zero = jnp.zeros((8, d.cf), F32)
        done = loop(d.frames, frame, (zero, zero))
        if last:
            put(r.part, 16, done[0])
            put(r.part, 17, done[1])
        else:
            first_mix(r, d, r.ypad, r.part, 16)
            fetch()

    return body


def fast_back3(r, d, gs, gg, tot_f3, tot_f2, row):
    _, inv_f = invs(r)
    mask = r.mask[...]
    mean, rs = moments(tot_f3, 4, "f3", inv_f)
    factor = rs * gain(r, "f3")
    gs, gg = gs * inv_f, gg * inv_f
    m2, r2, g2, b2 = norm_of(r, tot_f2, 4, "f2", inv_f)

    def frame(t, carry):
        at = at_frame(t, d.cells)
        for q in range(d.quad):
            lane = slice(q * d.cf, (q + 1) * d.cf)
            u = (r.f3[at, lane] - mean) * rs
            r.df3[at, lane] = (factor * (r.dzf[at, lane] - mask * (gs + u * gg))).astype(BF)
        return carry

    loop(d.frames, frame)
    acc_s = acc_q = 0.0
    for a, n in spans(d.rows, d.step):
        got = dot_t(r.df3[a : a + n, :], r.w3[...])
        f2 = r.f2[a : a + n, :]
        kept = (got.reshape(n // d.cells, d.cells, got.shape[1]) * mask[None]).reshape(got.shape)
        kept = kept * slope_of(f2 * g2 + b2)
        r.d2f[a : a + n, :] = kept
        acc_s = acc_s + fold8(kept)
        acc_q = acc_q + fold8(kept * ((f2 - m2) * r2))
    put(r.part, row, acc_s)
    put(r.part, row + 1, acc_q)


def fast_back2(r, d, gs, gg, tot_f2, tot_f1, f1_row, row):
    _, inv_f = invs(r)
    mask = r.mask[...]
    mean, rs = moments(tot_f2, 4, "f2", inv_f)
    factor = rs * gain(r, "f2")
    gs, gg = gs * inv_f, gg * inv_f
    m1, r1, g1, b1 = norm_of(r, tot_f1, f1_row, "f1", inv_f)

    def frame(t, carry):
        at = at_frame(t, d.cells)
        u = (r.f2[at, :] - mean) * rs
        v = (factor * (r.d2f[at, :] - mask * (gs + u * gg))).astype(BF)
        r.df2[at, :] = v
        put_windows(r.colf, at, v.astype(F32), d.side, True)
        return carry

    loop(d.frames, frame)
    acc_s = acc_q = 0.0
    wide_row = d.quad * d.fb
    for a, n in spans(d.rows, d.step):
        got = dot(r.colf[a : a + n, :], r.w2t[...])
        f1 = r.f1[a : a + n, :]
        kept = (got.reshape(n // d.cells, d.cells, got.shape[1]) * mask[None]).reshape(got.shape)
        kept = kept * slope_of(f1 * g1 + b1)
        r.d1f[a : a + n, :] = kept
        acc_s = acc_s + fold8(kept)
        acc_q = acc_q + fold8(kept * ((f1 - m1) * r1))
    put(r.part, row, acc_s)
    put(r.part, row + 1, acc_q)


def fast_back1(r, d, gs, gg, tot_f1, f1_row):
    _, inv_f = invs(r)
    mask = r.mask[...]
    mean, rs = moments(tot_f1, f1_row, "f1", inv_f)
    factor = rs * gain(r, "f1")
    gs, gg = gs * inv_f, gg * inv_f

    def frame(t, carry):
        at = at_frame(t, d.cells)
        u = (r.f1[at, :] - mean) * rs
        r.gpad[at_frame(t, d.cells, d.cells), d.cl :] = (
            factor * (r.d1f[at, :] - mask * (gs + u * gg))
        ).astype(BF)
        return carry

    loop(d.frames, frame)


def lateral_back(r, d, gs, gg, tot_lp, lp_row):
    inv_s, _ = invs(r)
    mask2 = wide(r.mask[...], d.cl)
    mean, rs = moments(tot_lp, lp_row, "lp", inv_s)
    factor = rs * gain(r, "lp")
    gs, gg = gs * inv_s, gg * inv_s

    def frame(t, carry):
        at = at_frame(t, d.cells)
        u = (r.lp[at, :] - mean) * rs
        r.gpad[at_frame(t, d.cells, d.cells), : d.cl] = (
            factor * (r.dl[at, :] - mask2 * (gs + u * gg))
        ).astype(BF)
        return carry

    loop(d.frames, frame)


def fast_input_grad(r, d, a, n):
    c = d.cf
    mid = dot_t(r.gpad[a + d.cells : a + d.cells + n, :], r.wa[2 * c : 6 * c, :])
    late = dot_t(r.gpad[a + 2 * d.cells : a + 2 * d.cells + n, :], r.wa[0 : 2 * c, :])
    early = dot_t(r.gpad[a : a + n, :], r.wa[6 * c : 7 * c, :])
    return [
        mid[:, :c] + early,
        mid[:, c : 2 * c],
        mid[:, 2 * c : 3 * c] + late[:, :c],
        mid[:, 3 * c :] + late[:, c:],
    ]


def slow_back3(r, d, gs, gg, tot_s3, tot_s2, row):
    inv_s, _ = invs(r)
    mask2 = wide(r.mask[...], d.cb)
    mean, rs = moments(tot_s3, 0, "s3", inv_s)
    factor = rs * gain(r, "s3")
    gs, gg = gs * inv_s, gg * inv_s
    m2, r2, g2, b2 = norm_of(r, tot_s2, 0, "s2", inv_s)

    def frame(t, carry):
        at = at_frame(t, d.cells)
        for c in range(0, d.cs, 256):
            lane = slice(c, c + 256)
            u = (r.s3[at, lane] - mean[:, lane]) * rs[:, lane]
            r.ds3[at, lane] = (
                factor[:, lane] * (r.dzs[at, lane] - mask2 * (gs[:, lane] + u * gg[:, lane]))
            ).astype(BF)
        return carry

    loop(d.frames, frame)
    acc_s = acc_q = 0.0
    for a, n in spans(d.rows, d.step):
        got = dot_t(r.ds3[a : a + n, :], r.we[...])
        s2 = r.s2[a : a + n, :]
        kept = (got.reshape(n // d.cells, d.cells, got.shape[1]) * mask2[None]).reshape(got.shape)
        kept = kept * slope_of(s2 * g2 + b2)
        r.d2[a : a + n, :] = kept
        acc_s = acc_s + fold8(kept)
        acc_q = acc_q + fold8(kept * ((s2 - m2) * r2))
    put(r.part, row, acc_s)
    put(r.part, row + 2, acc_q)


def slow_back2(r, d, gs, gg, tot_s2, tot_s1, row):
    inv_s, _ = invs(r)
    mask2 = wide(r.mask[...], d.cb)
    mean, rs = moments(tot_s2, 0, "s2", inv_s)
    factor = rs * gain(r, "s2")
    gs, gg = gs * inv_s, gg * inv_s
    m1, r1, g1, b1 = norm_of(r, tot_s1, 0, "s1", inv_s)

    def frame(t, carry):
        at = at_frame(t, d.cells)
        u = (r.s2[at, :] - mean) * rs
        v = (factor * (r.d2[at, :] - mask2 * (gs + u * gg))).astype(BF)
        r.ds2[at, :] = v
        put_windows(r.cols, at, v.astype(F32), d.side, True)
        return carry

    loop(d.frames, frame)
    acc_s = acc_q = 0.0
    for a, n in spans(d.rows, d.step):
        got = 0.0
        for k in range(9):
            lane = slice(k * d.cb, (k + 1) * d.cb)
            got = got + dot_t(r.cols[a : a + n, lane], r.wsp[lane, :])
        s1 = r.s1[a : a + n, :]
        kept = (got.reshape(n // d.cells, d.cells, got.shape[1]) * mask2[None]).reshape(got.shape)
        kept = kept * slope_of(s1 * g1 + b1)
        r.d1[a : a + n, :] = kept
        acc_s = acc_s + fold8(kept)
        acc_q = acc_q + fold8(kept * ((s1 - m1) * r1))
    put(r.part, row, acc_s)
    put(r.part, row + 2, acc_q)


def slow_back1(r, d, gs, gg, tot_s1, tot_lp, lp_row, row):
    inv_s, _ = invs(r)
    mask2 = wide(r.mask[...], d.cb)
    mean, rs = moments(tot_s1, 0, "s1", inv_s)
    factor = rs * gain(r, "s1")
    gs, gg = gs * inv_s, gg * inv_s
    ml, rl, gl, bl = norm_of(r, tot_lp, lp_row, "lp", inv_s)
    clear_ends(r.dpad, d.cells)

    def frame(t, carry):
        at = at_frame(t, d.cells)
        u = (r.s1[at, :] - mean) * rs
        r.dpad[at_frame(t, d.cells, d.cells), :] = (
            factor * (r.d1[at, :] - mask2 * (gs + u * gg))
        ).astype(BF)
        return carry

    loop(d.frames, frame)
    acc_s = acc_q = 0.0
    for a, n in spans(d.rows, d.step):
        got = slow_input_grad(r, d, a, n, d.cs, d.cs + d.cl)
        lp = r.lp[a : a + n, :]
        kept = (got.reshape(n // d.cells, d.cells, got.shape[1]) * mask2[None]).reshape(got.shape)
        kept = kept * slope_of(lp * gl + bl)
        r.dl[a : a + n, :] = kept
        acc_s = acc_s + fold8(kept)
        acc_q = acc_q + fold8(kept * ((lp - ml) * rl))
    put(r.part, row, acc_s)
    put(r.part, row + 2, acc_q)


def slow_input_grad(r, d, a, n, first, last):
    got = 0.0
    for k in range(3):
        b = a + (2 - k) * d.cells
        got = got + dot_t(r.dpad[b : b + n, :], r.wred[k, first:last, :])
    return got


def masked(x, mask, d):
    return (x.reshape(x.shape[0] // d.cells, d.cells, x.shape[1]) * mask[None]).reshape(x.shape)


def stage_e(d):
    def body(r):
        tot = jnp.sum(r.sync[...], axis=0)
        r.tot[...] = tot
        inv_s, _ = invs(r)
        mean, rs, sg, sb = norm_of(r, tot, 0, "s3", inv_s)
        mask2 = wide(r.mask[...], 256)

        def frame(t, carry):
            at = at_frame(t, d.cells)
            up = at_frame(t, d.cells, d.cells)
            sums = []
            for i, c in enumerate(range(0, d.cs, 256)):
                lane = slice(c, c + 256)
                s3 = r.s3[at, lane]
                z = r.spad[up, lane].astype(F32) + (s3 * sg[:, lane] + sb[:, lane])
                s = sigm(z)
                r.yout[t, :, lane] = (z * s * mask2).astype(BF)
                grad = r.cot[t, :, lane].astype(F32) * mask2 * (s * (1.0 + z * (1.0 - s)))
                r.dzs[at, lane] = grad
                u = (s3 - mean[:, lane]) * rs[:, lane]
                sums.append((carry[i][0] + fold8(grad), carry[i][1] + fold8(grad * u)))
            return tuple(sums)

        zero = jnp.zeros((8, 256), F32)
        done = loop(d.frames, frame, tuple((zero, zero) for c in range(0, d.cs, 256)))
        for i, c in enumerate(range(0, d.cs, 256)):
            put(r.part, c // LANES, done[i][0])
            put(r.part, (d.cs + c) // LANES, done[i][1])
        gs, gg = pair_of(tot, 16, "f3")
        fast_back3(r, d, gs, gg, r.tot_c[...], r.tot_b[...], 16)

    return body


def stage_f(d):
    def body(r):
        tot = jnp.sum(r.sync[...], axis=0)
        r.tot[...] = tot
        gs, gg = pair_of(tot, 0, "s3")
        slow_back3(r, d, gs, gg, r.tot_d[...], r.tot_c[...], 0)
        gs, gg = pair_of(tot, 16, "f2")
        fast_back2(r, d, gs, gg, r.tot_b[...], r.tot_a[...], 20, 4)

    return body


def stage_g(d):
    def body(r):
        tot = jnp.sum(r.sync[...], axis=0)
        r.tot[...] = tot
        gs, gg = pair_of(tot, 0, "s2")
        slow_back2(r, d, gs, gg, r.tot_c[...], r.tot_b[...], 0)

    return body


def stage_h(d):
    def body(r):
        tot = jnp.sum(r.sync[...], axis=0)
        r.tot[...] = tot
        inv_s, _ = invs(r)
        gs, gg = pair_of(tot, 0, "s1")
        slow_back1(r, d, gs, gg, r.tot_b[...], r.tot_a[...], 16, 16)
        mask2 = wide(r.mask[...], 256)
        r.par = r.par0
        mean, rs, sg, sb = norm_of(r, r.tot_a[...], 0, "s3", inv_s)
        for c in range(0, d.cs, 256):
            lane = slice(c, c + 256)
            acc_s = acc_q = 0.0
            for a, n in spans(d.rows, d.step):
                got = slow_input_grad(r, d, a, n, c, c + 256)
                got = masked(r.dzs[a : a + n, lane] + got, mask2, d).astype(BF).astype(F32)
                s3 = r.s3[a : a + n, lane]
                z = r.spad[a + d.cells : a + d.cells + n, lane].astype(F32) + (
                    s3 * sg[:, lane] + sb[:, lane]
                )
                grad = got * slope_of(z)
                r.dzs0[a : a + n, lane] = grad
                u = (s3 - mean[:, lane]) * rs[:, lane]
                acc_s = acc_s + fold8(grad)
                acc_q = acc_q + fold8(grad * u)
            put(r.part, c // LANES, acc_s)
            put(r.part, (d.cs + c) // LANES, acc_q)

    return body


def stage_i(d):
    def body(r):
        tot = jnp.sum(r.sync[...], axis=0)
        r.tot[...] = tot
        _, inv_f = invs(r)
        clear_ends(r.gpad, d.cells)
        gs, gg = pair_of(r.tot_f[...], 4, "f1")
        fast_back1(r, d, gs, gg, r.tot_a[...], 20)
        gs, gg = pair_of(tot, 16, "lp")
        lateral_back(r, d, gs, gg, r.tot_a[...], 16)
        r.par = r.par0
        mask = r.mask[...]
        mean, rs, fg, fb = norm_of(r, r.tot_c0[...], 4, "f3", inv_f)
        acc_s = acc_q = 0.0
        for a, n in spans(d.rows, d.step):
            pieces = fast_input_grad(r, d, a, n)
            for q in range(d.quad):
                lane = slice(q * d.cf, (q + 1) * d.cf)
                got = masked(r.dzf[a : a + n, lane] + pieces[q], mask, d).astype(BF).astype(F32)
                f3 = r.f3[a : a + n, lane]
                z = r.xpad[a + d.cells : a + d.cells + n, lane].astype(F32) + (f3 * fg + fb)
                grad = got * slope_of(z)
                r.dzf0[a : a + n, lane] = grad
                acc_s = acc_s + fold8(grad)
                acc_q = acc_q + fold8(grad * ((f3 - mean) * rs))
        put(r.part, 4, acc_s)
        put(r.part, 5, acc_q)
        gs, gg = pair_of(tot, 0, "s3")
        r.dzs = r.dzs0
        slow_back3(r, d, gs, gg, r.tot_a[...], r.tot_c0[...], 0)

    return body


def stage_j(d):
    def body(r):
        tot = jnp.sum(r.sync[...], axis=0)
        r.tot[...] = tot
        gs, gg = pair_of(tot, 0, "s2")
        slow_back2(r, d, gs, gg, r.tot_c[...], r.tot_b[...], 0)
        gs, gg = pair_of(tot, 4, "f3")
        fast_back3(r, d, gs, gg, r.tot_c[...], r.tot_b[...], 4)

    return body


def stage_k(d):
    def body(r):
        tot = jnp.sum(r.sync[...], axis=0)
        r.tot[...] = tot
        gs, gg = pair_of(tot, 0, "s1")
        slow_back1(r, d, gs, gg, r.tot_b[...], r.tot_a[...], 0, 0)
        gs, gg = pair_of(tot, 4, "f2")
        fast_back2(r, d, gs, gg, r.tot_b[...], r.tot_a[...], 4, 4)

    return body


def stage_slow_out(d):
    def body(r):
        mask2 = wide(r.mask[...], 256)
        for c in range(0, d.cs, 256):
            lane = slice(c, c + 256)
            for a, n in spans(d.rows, d.step):
                got = slow_input_grad(r, d, a, n, c, c + 256)
                got = masked(r.dzs[a : a + n, lane] + got, mask2, d)
                for t in range(n // d.cells):
                    at = (a // d.cells + t, slice(None), lane)
                    sort_out(r, got[t * d.cells : (t + 1) * d.cells, :], r.value[at], at)

    return body


def stage_l(d):
    def body(r):
        tot = jnp.sum(r.sync[...], axis=0)
        r.tot[...] = tot
        clear_ends(r.gpad, d.cells)
        gs, gg = pair_of(tot, 4, "f1")
        fast_back1(r, d, gs, gg, r.tot_a[...], 4)
        gs, gg = pair_of(tot, 0, "lp")
        lateral_back(r, d, gs, gg, r.tot_a[...], 0)
        mask = r.mask[...]
        for a, n in spans(d.rows, d.step):
            pieces = fast_input_grad(r, d, a, n)
            for q in range(d.quad):
                lane = slice(q * d.cf, (q + 1) * d.cf)
                got = masked(r.dzf[a : a + n, lane] + pieces[q], mask, d)
                for t in range(n // d.cells):
                    at = (a // d.cells + t, q)
                    sort_out(r, got[t * d.cells : (t + 1) * d.cells, :], r.value[at], at)

    return body


def small_block(r, row, value):
    for half in range(2):
        for i in range(2):
            at = 64 * half + 32 * i
            r.halves[half, row : row + 32, i * LANES : (i + 1) * LANES] = value[
                at : at + 32, :
            ].astype(BF)


def hand_over(r):
    r.keep[...] = r.halves[r.ids[0]]
    r.send[...] = r.halves[1 - r.ids[0]]


def grads_es(d):
    part = d.cb // 2

    def body(r):
        def frame(t, carry):
            at = at_frame(t, d.cells)
            put_windows(r.cols, at, r.ds2[at, :].astype(F32), d.side, True)
            put_windows(r.colf, at, r.df2[at, :].astype(F32), d.side, True)
            return carry

        loop(d.frames, frame)
        row = 0
        turned = r.h2[...].T
        for c in range(0, d.cs, 256):
            got = dot(turned, r.ds3[:, c : c + 256]).astype(BF)
            for half in range(2):
                r.halves[half, row : row + part, :] = got[half * part : (half + 1) * part, :]
            row += part
        turned = r.h1[...].T
        for k in range(9):
            got = dot(turned, r.cols[:, k * d.cb : (k + 1) * d.cb]).astype(BF)
            for half in range(2):
                r.halves[half, row : row + part, :] = got[half * part : (half + 1) * part, :]
            row += part
        r.g2[...] = t_dot(r.k1[...], r.colf[...])
        r.g3[...] = t_dot(r.k2[...], r.df3[...])
        where = lane_group((d.fb, LANES), d.fb)
        for i in range(3):
            total = jnp.zeros((d.fb, LANES), F32)
            for c in range(3):
                for q in range(d.quad):
                    tap = (3 * i + c) * LANES
                    piece = r.g2[q * d.fb : (q + 1) * d.fb, tap : tap + LANES]
                    if c != q:
                        piece = pltpu.roll(piece, ((c - q) * d.fb) % LANES, 1)
                    total = total + jnp.where(where == c, piece, 0.0)
            r.block[i * d.fb : (i + 1) * d.fb, :] = total
        total = jnp.zeros((d.fb, LANES), F32)
        for q in range(d.quad):
            total = total + r.g3[q * d.fb : (q + 1) * d.fb, q * d.cf : (q + 1) * d.cf]
        r.block[3 * d.fb :, :] = total
        small_block(r, row, r.block[...])
        hand_over(r)

    return body


def with_grads(stage_body, grads_body, names):
    def body(r):
        stage_body(r)
        for target, source in names.items():
            setattr(r, target, getattr(r, source))
        grads_body(r)

    return body


def grads_reduce(d):
    split = (d.cs + d.cl) // 2

    def body(r):
        for c in range(0, d.cs + d.cl, 256):
            if c < d.cs:
                source = r.spad[d.cells : d.cells + d.rows, c : c + 256]
            else:
                source = r.lapad[d.cells : d.cells + d.rows, c - d.cs : c - d.cs + 256]
            turned = source.T
            cut = min(max(split - c, 0), 256)
            for k in range(3):
                b = (2 - k) * d.cells
                got = dot(turned, r.dpad[b : b + d.rows, :]).astype(BF)
                if cut > 0:
                    row = k * split + c
                    r.halves[0, row : row + cut, :] = got[:cut, :]
                if cut < 256:
                    row = k * split + c + cut - split
                    r.halves[1, row : row + 256 - cut, :] = got[cut:, :]
        hand_over(r)

    return body


def grads_first(d):
    def body(r):
        c = d.cf
        grad = r.gpad[d.cells : d.cells + d.rows, :]
        r.ga[0 : 2 * c, :] = t_dot(r.xpad[0 : d.rows, 2 * c : 4 * c], grad)
        r.ga[2 * c : 6 * c, :] = t_dot(r.xpad[d.cells : d.cells + d.rows, :], grad)
        r.ga[6 * c :, :] = t_dot(r.xpad[2 * d.cells : 2 * d.cells + d.rows, 0:c], grad)
        row = 0
        for b in range(d.taps):
            for half in range(2):
                at = b * c + half * (c // 2)
                r.halves[half, row : row + c // 2, :] = r.ga[at : at + c // 2, : d.cl].astype(BF)
            row += c // 2
        where = lane_group((c, LANES), d.fb)
        total = jnp.zeros((c, LANES), F32)
        for k in range(3):
            for q in range(d.quad):
                at = (q + k + 1) * c
                piece = r.ga[at : at + c, d.cl :]
                if k != q:
                    piece = pltpu.roll(piece, ((k - q) * d.fb) % LANES, 1)
                total = total + jnp.where(where == k, piece, 0.0)
        small_block(r, row, total)
        hand_over(r)

    return body


def gather_pieces(r, count):
    row = 0
    for i in range(count):
        keep, got = getattr(r, "keep_%d" % i), getattr(r, "got_%d" % i)
        r.mine[row : row + keep.shape[0], :] = (
            keep[...].astype(F32) + got[...].astype(F32)
        ).astype(BF)
        row += keep.shape[0]
    if row < r.mine.shape[0]:
        r.mine[row:, :] = jnp.zeros((r.mine.shape[0] - row, r.mine.shape[1]), BF)


def split_near(count, turned=None):
    def body(r):
        gather_pieces(r, count)
        hand_shares(r, r.mine, r.ids[2 if turned is None else 4], turned)

    return body


def split_half(count, bit):
    def body(r):
        gather_pieces(r, count)
        halve(r, bit)

    return body


def hand_shares(r, source, place, turned=None):
    k = 0
    while hasattr(r, "to_%d" % k):
        target = getattr(r, "to_%d" % k)
        rows = target.shape[0]
        start = pl.multiple_of((place ^ (k if turned is None else turned[k])) * rows, 16)
        target[...] = source[pl.ds(start, rows), :]
        k += 1


def add_shares(r):
    total = r.from_0[...].astype(F32)
    k = 1
    while hasattr(r, "from_%d" % k):
        total = total + getattr(r, "from_%d" % k)[...].astype(F32)
        k += 1
    return total.astype(BF)


def sum_shares(r):
    r.out[...] = add_shares(r)


def sum_and_share(r):
    r.mine[...] = add_shares(r)
    hand_shares(r, r.mine, r.ids[3])


def collect(which):
    def body(r):
        rows = r.from_0.shape[0]
        k = 0
        while hasattr(r, "from_%d" % k):
            start = pl.multiple_of((r.ids[which] ^ k) * rows, 16)
            r.out[pl.ds(start, rows), :] = getattr(r, "from_%d" % k)[...]
            k += 1

    return body


def halve(r, bit):
    rows = r.keep.shape[0]
    mine = jnp.where((r.ids[1] & bit) > 0, 1, 0)
    r.keep[...] = r.mine[pl.ds(pl.multiple_of(mine * rows, 16), rows), :]
    r.send[...] = r.mine[pl.ds(pl.multiple_of((1 - mine) * rows, 16), rows), :]


def split_far(bit):
    def body(r):
        rows = r.early.shape[0]
        r.mine[0:rows, :] = r.early[...]
        r.mine[rows:, :] = add_shares(r)
        halve(r, bit)

    return body


def next_far(bit):
    def body(r):
        total = (r.own[...].astype(F32) + r.got[...].astype(F32)).astype(BF)
        if bit:
            r.mine[...] = total
            halve(r, bit)
        else:
            r.keep[...] = total

    return body


def join_far(bit):
    def body(r):
        rows = r.own.shape[0]
        mine = jnp.where((r.ids[1] & bit) > 0, 1, 0)
        r.out[pl.ds(pl.multiple_of(mine * rows, 16), rows), :] = r.own[...]
        r.out[pl.ds(pl.multiple_of((1 - mine) * rows, 16), rows), :] = r.got[...]

    return body


def join_last(bit):
    def body(r):
        rows = r.own.shape[0]
        mine = jnp.where((r.ids[1] & bit) > 0, 1, 0)
        r.all[pl.ds(pl.multiple_of(mine * rows, 16), rows), :] = r.own[...]
        r.all[pl.ds(pl.multiple_of((1 - mine) * rows, 16), rows), :] = r.got[...]
        cut = r.es.shape[0]
        r.es[...] = r.all[0:cut, :]
        r.red[...] = r.all[cut:, :]

    return body


def halve_parts(r, sizes, bit):
    mine = jnp.where((r.ids[1] & bit) > 0, 1, 0)
    start = done = 0
    for size in sizes:
        half = size // 2
        at = slice(done, done + half)
        r.keep[at, :] = r.mine[pl.ds(pl.multiple_of(start + mine * half, 16), half), :]
        r.send[at, :] = r.mine[pl.ds(pl.multiple_of(start + (1 - mine) * half, 16), half), :]
        start += size
        done += half


def join_parts(sizes, bit):
    def body(r):
        start = 0
        for i, size in enumerate(sizes):
            own, got = getattr(r, "own_%d" % i), getattr(r, "got_%d" % i)
            r.mine[start : start + size, :] = (own[...].astype(F32) + got[...].astype(F32)).astype(BF)
            start += size
        halve_parts(r, sizes, bit)

    return body


def next_parts(sizes, bit):
    def body(r):
        r.mine[...] = (r.own[...].astype(F32) + r.got[...].astype(F32)).astype(BF)
        halve_parts(r, sizes, bit)

    return body


def merge_far(bit):
    def body(r):
        rows = r.early.shape[0]
        r.mine[0:rows, :] = r.early[...]
        if hasattr(r, "own"):
            late = (r.own[...].astype(F32) + r.got[...].astype(F32)).astype(BF)
        else:
            late = r.late[...]
        r.mine[rows:, :] = late
        halve(r, bit)

    return body


def merge_shares(bit, count):
    def body(r):
        row = 0
        for name in ("early_", "late_"):
            total = getattr(r, name + "0")[...].astype(F32)
            for k in range(1, count):
                total = total + getattr(r, name + str(k))[...].astype(F32)
            r.mine[row : row + total.shape[0], :] = total.astype(BF)
            row += total.shape[0]
        halve(r, bit)

    return body


def part_far(bit):
    def body(r):
        rows = r.own.shape[0]
        mine = jnp.where((r.ids[1] & bit) > 0, 1, 0)
        r.all[pl.ds(pl.multiple_of(mine * rows, 16), rows), :] = r.own[...]
        r.all[pl.ds(pl.multiple_of((1 - mine) * rows, 16), rows), :] = r.got[...]
        cut = r.early.shape[0]
        r.early[...] = r.all[0:cut, :]
        r.late[...] = r.all[cut:, :]

    return body


def join_pair(bits):
    def body(r):
        for i, bit in enumerate(bits):
            own, got, out = (getattr(r, name + str(i)) for name in ("own_", "got_", "out_"))
            rows = own.shape[0]
            mine = jnp.where((r.ids[1] & bit) > 0, 1, 0)
            out[pl.ds(pl.multiple_of(mine * rows, 16), rows), :] = own[...]
            out[pl.ds(pl.multiple_of((1 - mine) * rows, 16), rows), :] = got[...]

    return body


def join_send(bit):
    def body(r):
        join_far(bit)(r)

        @pl.when(r.ids[0] == 0)
        def _():
            r.send[0 : r.second.shape[0], :] = r.second[...]

        @pl.when(r.ids[0] != 0)
        def _():
            r.send[0 : r.out.shape[0], :] = r.out[...]

    return body


def add_near(r):
    rows = r.got.shape[1]
    total = r.got[0].astype(F32)
    for i in range(1, r.got.shape[0]):
        total = total + r.got[i].astype(F32)
    r.out[0:rows, :] = total.astype(BF)
    r.out[rows:, :] = add_shares(r)


def add_up(r):
    total = jnp.zeros(r.got.shape[1:], F32)
    for i in range(r.got.shape[0]):
        total = total + r.got[i].astype(F32)
    total = total.astype(BF)
    if len(r.out.shape) == len(total.shape):
        r.out[...] = total
    else:
        for i in range(r.out.shape[0]):
            r.out[i] = total


def spread_out(r):
    for i in range(r.out.shape[0]):
        r.out[i] = r.got[...]


def store_all(r, todo):
    @pl.when(r.ids[0] == 0)
    def _():
        for out, done, step, first, at, _, _, lanes in todo:
            out[done : done + step, :] = first[at : at + step, lanes].astype(F32)

    @pl.when(r.ids[0] != 0)
    def _():
        for out, done, step, _, _, second, at, lanes in todo:
            out[done : done + step, :] = second[at : at + step, lanes].astype(F32)


def store_half(r, todo, spots, half, out, here_at, there_at, count, lanes=slice(None)):
    done = 0
    while done < count:
        step = count - done
        found = []
        for (kind, row), mine in ((here_at, half == 0), (there_at, half == 1)):
            own, got, piece, stride, offset = spots[kind]
            i, rest = divmod(row + done, piece)
            step = min(step, piece - rest)
            found.append((getattr(r, own if mine else got), i * stride + offset + rest))
        (first, at_0), (second, at_1) = found
        todo.append((out, done, step, first, at_0, second, at_1, lanes))
        done += step


def finish_reduce(d, spots):
    split = (d.cs + d.cl) // 2

    def body(r):
        r.mark[...] = jnp.zeros(r.mark.shape, F32)
        copies = []
        for k in range(3):
            todo = []
            for half in range(2):
                out = r.reduce.at[k, half * split : (half + 1) * split, :]
                store_half(r, todo, spots, half, out, ("r", k * split), ("red", k * split), split)
            store_all(r, todo)
            copies.append(
                pltpu.make_async_copy(r.reduce.at[k], r.hbm_reduce.at[0, k], r.sems.at[k])
            )
            copies[-1].start()
        for copy in copies:
            copy.wait()

    return body


def finish_rest(d, spots, rows_red):
    part = d.cb // 2
    side = d.cf // 2

    def body(r):
        row = 0
        todo = []
        for c in range(0, d.cs, 256):
            for half in range(2):
                out = r.expand.at[half * part : (half + 1) * part, c : c + 256]
                store_half(r, todo, spots, half, out, ("b", row), ("es", row), part)
            row += part
        store_all(r, todo)
        copies = [pltpu.make_async_copy(r.expand, r.hbm_expand.at[0], r.sems.at[0])]
        copies[-1].start()
        todo = []
        for k in range(9):
            for half in range(2):
                out = r.space.at[k, half * part : (half + 1) * part, :]
                store_half(r, todo, spots, half, out, ("b", row), ("es", row), part)
            row += part
        store_all(r, todo)
        copies.append(pltpu.make_async_copy(r.space, r.hbm_space.at[0], r.sems.at[1]))
        copies[-1].start()

        def small(here_at, there_at):
            todo = []
            for half in range(2):
                for i in range(2):
                    at = 64 * half + 32 * i
                    lanes = slice(i * LANES, (i + 1) * LANES)
                    store_half(
                        r, todo, spots, half, r.block.at[at : at + 32, :], here_at, there_at, 32, lanes
                    )
            store_all(r, todo)

        small(("b", row), ("es", row))
        for i in range(3):
            piece = r.block[i * d.fb : (i + 1) * d.fb, :]
            for c in range(3):
                moved = piece if c == 0 else pltpu.roll(piece, LANES - c * d.fb, 1)
                r.fspace[0, 3 * i + c] = moved[:, : d.fb]
        r.fexpand[0] = r.block[3 * d.fb :, :]
        row, row_1 = 0, rows_red
        todo = []
        for tap in range(d.taps):
            for half in range(2):
                out = r.lateral.at[0, tap, half * side : (half + 1) * side, :]
                store_half(r, todo, spots, half, out, ("f", row), ("red", row_1), side)
            row, row_1 = row + side, row_1 + side
        store_all(r, todo)
        small(("f", row), ("red", row_1))
        turned = r.block[...].T
        for k in range(3):
            r.freduce[0, k] = turned[k * d.fb : (k + 1) * d.fb, :]
        for copy in copies:
            copy.wait()

    return body


def norms_out(d, at):
    def body(r):
        made = []
        for layer in range(2):
            lines = []
            for which in (1, 0):
                pieces = []
                for key in ("s1", "s2", "s3", "f1", "f2", "f3", "lp"):
                    name, row = at[layer][key]
                    tot = getattr(r, name)[...]
                    count = SPAN[key][1]
                    if key in ("f1", "f2"):
                        tot = folded(tot, d.fb)
                    piece = lanes_of(tot, row + which * count, count)
                    pieces.append(piece[:, : d.fb] if key in ("f1", "f2") else piece)
                lines.append(jnp.concatenate(pieces, axis=1))
            made.append(lines)
        for i in range(2):
            r.keep[i : i + 1, :] = jnp.where(r.ids[0] == 0, made[0][i], made[1][i])
            r.send[i : i + 1, :] = jnp.where(r.ids[0] == 0, made[1][i], made[0][i])

    return body


def norms_add(r):
    total = r.keep[...] + r.got[...]
    r.gain[...] = total[0:1, :]
    r.shift[...] = total[1:2, :]


def on_device(
    edge_slow,
    edge_fast,
    slow_reduce,
    slow_spatial,
    slow_expand,
    fast_reduce,
    fast_spatial,
    fast_expand,
    lateral,
    norm_gain,
    norm_shift,
    present,
    crop_side,
):
    micro, _, frames, side, _, cs = edge_slow.shape[1:]
    cells = side * side
    fast_frames = edge_fast.shape[3]
    quad = fast_frames // frames
    d = SimpleNamespace(
        frames=frames,
        side=side,
        cells=cells,
        rows=frames * cells,
        step=min(512, frames * cells),
        quad=quad,
        cs=cs,
        cb=slow_expand.shape[1],
        cf=edge_fast.shape[-1],
        fb=fast_expand.shape[1],
        cl=lateral.shape[3],
    )
    d.taps = lateral.shape[1]
    d.micro = micro
    d.groups = lax.axis_size("dp")
    groups = d.groups
    rows, pads = d.rows, d.rows + 2 * cells
    swap = [(0, 1), (1, 0)]
    own_slow = edge_slow.reshape(micro, frames, cells, cs)
    own_fast = edge_fast.reshape(micro, frames, quad, cells, d.cf)

    def across(value, pairs=swap):
        return lax.ppermute(value, "pipe", pairs)

    inner = 1
    while 4 * inner * inner <= groups:
        inner *= 2
    outer = groups // inner
    group = lax.axis_index("dp")
    sect = lax.axis_index("pipe")
    shift_by = inner.bit_length() - 1
    turned = [
        sum(((i >> b) & 1) << (shift_by - 1 - b) for b in range(shift_by)) for i in range(inner)
    ]
    turned_place = jnp.int32(0)
    for b in range(shift_by):
        turned_place += (lax.shift_right_logical(group, jnp.int32(b)) & 1) << (shift_by - 1 - b)
    far_place = lax.shift_right_logical(group, jnp.int32(shift_by))
    ids = jnp.stack([sect, group, group & (inner - 1), far_place, turned_place]).astype(jnp.int32)
    meta = jnp.concatenate([ids, present.reshape(-1), crop_side.reshape(-1)])
    own_fast, lat_own, fr_own, ids = lax.optimization_barrier(
        (own_fast, lateral[0], jnp.swapaxes(fast_reduce[0], 1, 2), ids)
    )
    other_fast, lat_other, fr_other = across(own_fast), across(lat_own), across(fr_own)
    red_own, own_slow, fr_other, lat_other, other_fast, meta = lax.optimization_barrier(
        (slow_reduce[0], own_slow, fr_other, lat_other, other_fast, meta)
    )
    other_slow, red_other = across(own_slow), across(red_own)
    sems = pltpu.SemaphoreType.DMA

    def stage(*args, **others):
        return run(*args, groups=groups, **others)

    def exchange(part):
        return lax.all_to_all(part, "dp", 0, 0)

    slow_f = ((rows, cs), F32)
    mid_f = ((rows, d.cb), F32)
    fast_f = ((rows, quad * d.cf), F32)
    tiny_f = ((rows, quad * d.fb), F32)
    mid_b = ((rows, d.cb), BF)
    tiny_b = ((rows, quad * d.fb), BF)
    fast_b = ((rows, quad * d.cf), BF)
    small = ((8, LANES), F32)
    large = ((24, LANES), F32)
    xpad_s = ((pads, quad * d.cf), BF)
    spad_s = ((pads, cs), BF)
    mpad_s = ((pads, d.cb), BF)
    gpad_s = ((pads, d.cl + quad * d.fb), BF)
    cols_s = {"cols": ((rows, 9 * d.cb), BF)}
    colf_s = {"colf": ((rows, 9 * quad * d.fb), BF)}
    wa_s = (((quad + 3) * d.cf, d.cl + quad * d.fb), BF)

    out_fast = ((frames, quad, cells, d.cf), BF)
    out_slow = ((frames, cells, cs), BF)
    a0 = stage(
        stage_first(d),
        "stage_a0",
        dict(
            ids=meta,
            own=own_fast,
            other=other_fast,
            hbm_lat_own=lat_own,
            hbm_lat_other=lat_other,
            hbm_fr_own=fr_own,
            hbm_fr_other=fr_other,
        ),
        dict(
            mask=((cells, LANES), F32),
            inv=small,
            wa=wa_s,
            wa1=wa_s,
            xpad=xpad_s,
            cot=out_fast,
            lp=mid_f,
            f1=tiny_f,
            part=small,
        ),
        dict(
            lat_own=(lat_own.shape, BF),
            lat_other=(lat_own.shape, BF),
            fr_own=(fr_own.shape, BF),
            fr_other=(fr_own.shape, BF),
            loads=sems((6,)),
        ),
    )
    fs_own, fe_own, norm_gain, norm_shift, a0_inv = lax.optimization_barrier(
        (fast_spatial.reshape(9, d.fb, d.fb), fast_expand[0], norm_gain, norm_shift, a0.inv)
    )
    fs_other, fe_other = across(fs_own), across(fe_own)
    gain_other, shift_other = across(norm_gain), across(norm_shift)
    mask = a0.mask
    base = dict(mask=mask, inv=a0_inv)
    wa = (a0.wa, a0.wa1)
    rows_es = (cs // 256 + 9) * (d.cb // 2) + 32
    rows_red = 3 * (cs + d.cl) // 2
    rows_first = d.taps * (d.cf // 2) + 32

    def halves_of(body, name, rows_now, ins, scratch, hold):
        made = run(
            body,
            name,
            dict(ids=ids, **ins),
            dict(keep=((rows_now, 256), BF), send=((rows_now, 256), BF)),
            dict(scratch, halves=((2, rows_now, 256), BF)),
            hold=hold,
        )
        return made.keep, across(made.send)

    def halves_es(name, hold, **ins):
        scratch = dict(
            cols_s,
            **colf_s,
            g2=((quad * d.fb, 9 * quad * d.fb), F32),
            g3=((quad * d.fb, quad * d.cf), F32),
            block=((LANES, LANES), F32),
        )
        return halves_of(grads_es(d), "grads_es" + name, rows_es, ins, scratch, hold)

    def halves_red(name, hold, **ins):
        return halves_of(grads_reduce(d), "grads_red" + name, rows_red, ins, {}, hold)

    def halves_first(name, hold, **ins):
        scratch = dict(ga=(((quad + 3) * d.cf, d.cl + quad * d.fb), F32))
        return halves_of(grads_first(d), "grads_first" + name, rows_first, ins, scratch, hold)

    def padded(count):
        unit = 16 * groups
        return -(-count // unit) * unit

    es_all, red_all = padded(rows_es), padded(rows_red + rows_first)
    ga_s = (((quad + 3) * d.cf, d.cl + quad * d.fb), F32)

    def kept(count):
        return dict(keep=((count, 256), BF), send=((count, 256), BF))

    near_1 = (es_all + red_all) // inner

    def shares(count, rows_now):
        return {"to_%d" % k: ((rows_now, 256), BF) for k in range(count)}

    def sent_near(made):
        pairs = lambda k: [(i, i ^ k) for i in range(groups)]
        return {
            "from_%d" % k: made[k] if k == 0 else lax.ppermute(made[k], "dp", pairs(k))
            for k in range(inner)
        }

    bits = [inner << i for i in range(outer.bit_length() - 1)][::-1]
    near_bits = [1 << i for i in range(shift_by)]

    def over(value, bit):
        return lax.ppermute(value, "dp", [(i, i ^ bit) for i in range(groups)])

    def targets(made, count):
        return [getattr(made, "to_%d" % k) for k in range(count)]

    def pieces_of(*pieces):
        return {
            "%s_%d" % (key, i): value
            for i, piece in enumerate(pieces)
            for key, value in zip(("keep", "got"), piece)
        }

    arrived = (other_slow, red_other, fs_other, fe_other, gain_other, shift_other)
    part = run(gate, "gate", dict(part=a0.part), dict(out=(a0.part.shape, F32)), far_hold=arrived).out
    sync = exchange(part)
    sp_own, ex_own, sync = lax.optimization_barrier(
        (slow_spatial.reshape(9 * d.cb, d.cb), slow_expand[0], sync)
    )
    sp_other, ex_other = across(sp_own), across(ex_own)
    packed_2 = ((9 * quad * d.fb, quad * d.fb), BF)
    packed_3 = ((quad * d.fb, quad * d.cf), BF)
    norm_s = ((2 * SHIFT_ROW, LANES), F32)
    red_s = (red_own.shape, BF)
    slow_in = pack = stage(
        stage_slow_in(d),
        "stage_slow_in",
        dict(
            ids=ids,
            mask=mask,
            own=own_slow,
            other=other_slow,
            hbm_red_own=red_own,
            hbm_red_other=red_other,
            hbm_fs_own=fs_own,
            hbm_fs_other=fs_other,
            hbm_fe_own=fe_own,
            hbm_fe_other=fe_other,
            hbm_gain_own=norm_gain,
            hbm_gain_other=gain_other,
            hbm_shift_own=norm_shift,
            hbm_shift_other=shift_other,
        ),
        dict(
            spad=spad_s,
            cot=out_slow,
            y=mid_f,
            wred_0=red_s,
            w2_0=packed_2,
            w2_1=packed_2,
            w2t_0=packed_2,
            w2t_1=packed_2,
            w3_0=packed_3,
            w3_1=packed_3,
            par_0=norm_s,
            par_1=norm_s,
        ),
        dict(
            fs_own=(fs_own.shape, BF),
            fs_other=(fs_own.shape, BF),
            fe_own=(fe_own.shape, BF),
            fe_other=(fe_own.shape, BF),
            gain_own=(norm_gain.shape, F32),
            gain_other=(norm_gain.shape, F32),
            shift_own=(norm_gain.shape, F32),
            shift_other=(norm_gain.shape, F32),
            loads=sems((10,)),
            sems=sems((1,)),
        ),
        hold=(sync,),
    )
    w2, w2t = (pack.w2_0, pack.w2_1), (pack.w2t_0, pack.w2t_1)
    w3, par = (pack.w3_0, pack.w3_1), (pack.par_0, pack.par_1)

    def common(layer):
        return dict(base, par=par[layer])

    b0 = stage(
        stage_second(d, 0, False),
        "stage_b0",
        dict(
            common(0),
            sync=sync,
            lp=a0.lp,
            f1=a0.f1,
            y=slow_in.y,
            wred=slow_in.wred_0,
            w2=w2[0],
            ids=ids,
            hbm_sp_own=sp_own,
            hbm_sp_other=sp_other,
        ),
        dict(
            lapad=mpad_s,
            k1=tiny_b,
            s1=mid_f,
            f2=tiny_f,
            tot=small,
            wsp_0=(sp_own.shape, BF),
            part=small,
        ),
        dict(colf_s, sems=sems((1,))),
        far_hold=(ex_other,),
    )
    sync = exchange(b0.part)
    c0 = stage(
        stage_third(d, True),
        "stage_c0",
        dict(
            common(0),
            ids=ids,
            sync=sync,
            s1=b0.s1,
            f2=b0.f2,
            w3=w3[0],
            wsp=b0.wsp_0,
            hbm_red_own=red_own,
            hbm_red_other=red_other,
            hbm_ex_own=ex_own,
            hbm_ex_other=ex_other,
        ),
        dict(
            h1=mid_b,
            k2=tiny_b,
            s2=mid_f,
            f3=fast_f,
            tot=small,
            wred_1=red_s,
            we_0=(ex_own.shape, BF),
            part=small,
        ),
        dict(cols_s, sems=sems((2,))),
    )
    sync = exchange(c0.part)
    d0 = stage(
        stage_fourth(d, False),
        "stage_d0",
        dict(common(0), sync=sync, s2=c0.s2, f3=c0.f3, we=c0.we_0,
            ids=ids,
            hbm_sp_own=sp_own,
            hbm_sp_other=sp_other,
            hbm_ex_own=ex_own,
            hbm_ex_other=ex_other, xpad=a0.xpad, wa=wa[1]),
        dict(h2=mid_b, s3=slow_f, ypad=xpad_s, lp=mid_f, f1=tiny_f, tot=small, wsp_1=(sp_own.shape, BF), we_1=(ex_own.shape, BF), part=large),
        dict(sems=sems((2,))),
    )
    sync = exchange(d0.part)
    we, wsp = (c0.we_0, d0.we_1), (b0.wsp_0, d0.wsp_1)
    wred = (slow_in.wred_0, c0.wred_1)
    b1 = stage(
        stage_second(d, 16, True),
        "stage_b1",
        dict(
            base,
            par=par[1],
            par0=par[0],
            sync=sync,
            lp=d0.lp,
            f1=d0.f1,
            s3=d0.s3,
            xpad=slow_in.spad,
            wred=wred[1],
            w2=w2[1],
        ),
        dict(spad=spad_s, lapad=mpad_s, k1=tiny_b, s1=mid_f, f2=tiny_f, tot=large, part=small),
        colf_s,
    )
    sync = exchange(b1.part)
    c1 = stage(
        stage_third(d, False),
        "stage_c1",
        dict(common(1), sync=sync, s1=b1.s1, f2=b1.f2, wsp=wsp[1], w3=w3[1]),
        dict(h1=mid_b, k2=tiny_b, s2=mid_f, f3=fast_f, tot=small, part=small),
        cols_s,
    )
    sync = exchange(c1.part)
    d1 = stage(
        stage_fourth(d, True),
        "stage_d1",
        dict(
            common(1),
            sync=sync,
            s2=c1.s2,
            f3=c1.f3,
            we=we[1],
            xpad=d0.ypad,
            cot=a0.cot,
        ),
        dict(h2=mid_b, s3=slow_f, yout=out_fast, dzf=fast_f, tot=small, part=large),
    )
    sync = exchange(d1.part)
    e1 = stage(
        stage_e(d),
        "stage_e1",
        dict(
            common(1),
            sync=sync,
            s3=d1.s3,
            spad=b1.spad,
            cot=slow_in.cot,
            f3=c1.f3,
            dzf=d1.dzf,
            f2=b1.f2,
            w3=w3[1],
            tot_c=d1.tot,
            tot_b=c1.tot,
        ),
        dict(yout=out_slow, dzs=slow_f, df3=fast_b, d2f=tiny_f, tot=large, part=large),
    )
    sync = exchange(e1.part)
    f1 = stage(
        stage_f(d),
        "stage_f1",
        dict(
            common(1),
            sync=sync,
            s3=d1.s3,
            dzs=e1.dzs,
            s2=c1.s2,
            we=we[1],
            d2f=e1.d2f,
            f2=b1.f2,
            f1=d0.f1,
            w2t=w2t[1],
            tot_d=e1.tot,
            tot_c=d1.tot,
            tot_b=c1.tot,
            tot_a=b1.tot,
        ),
        dict(ds3=((rows, cs), BF), d2=mid_f, df2=tiny_b, d1f=tiny_f, tot=large, part=small),
        colf_s,
    )
    sync = exchange(f1.part)
    g1 = stage(
        stage_g(d),
        "stage_g1",
        dict(
            common(1), sync=sync, d2=f1.d2, s2=c1.s2, s1=b1.s1, wsp=wsp[1], tot_c=d1.tot, tot_b=c1.tot
        ),
        dict(ds2=mid_b, d1=mid_f, tot=small, part=small),
        cols_s,
    )
    sync = exchange(g1.part)
    es1 = halves_es(
        "1",
        (sync,),
        h2=d1.h2,
        k2=c1.k2,
        ds3=f1.ds3,
        df3=e1.df3,
        h1=c1.h1,
        k1=b1.k1,
        ds2=g1.ds2,
        df2=f1.df2,
    )
    h1 = stage(
        stage_h(d),
        "stage_h1",
        dict(
            base,
            par=par[1],
            par0=par[0],
            sync=sync,
            d1=g1.d1,
            s1=b1.s1,
            lp=d0.lp,
            wred=wred[1],
            dzs=e1.dzs,
            s3=d0.s3,
            spad=slow_in.spad,
            tot_b=c1.tot,
            tot_a=b1.tot,
        ),
        dict(dpad=mpad_s, dl=mid_f, dzs0=slow_f, tot=small, part=large),
        hold=(es1[0],),
    )
    sync = exchange(h1.part)
    red1 = halves_red("1", (sync,), spad=b1.spad, lapad=b1.lapad, dpad=h1.dpad)
    es_near = run(
        split_near(1),
        "es1_near",
        dict(ids=ids, **pieces_of(es1)),
        shares(inner, es_all // inner),
        dict(mine=((es_all, 256), BF)),
        hold=(sync,),
    )
    i0 = stage(
        stage_i(d),
        "stage_i0",
        dict(
            base,
            par=par[1],
            par0=par[0],
            sync=sync,
            lp=d0.lp,
            f1=d0.f1,
            d1f=f1.d1f,
            dl=h1.dl,
            wa=wa[1],
            dzf=d1.dzf,
            f3=c0.f3,
            xpad=a0.xpad,
            dzs0=h1.dzs0,
            s3=d0.s3,
            s2=c0.s2,
            we=we[0],
            tot_f=g1.tot,
            tot_a=b1.tot,
            tot_c0=d0.tot,
        ),
        dict(gpad=gpad_s, dzf0=fast_f, ds3=((rows, cs), BF), d2=mid_f, tot=large, part=small),
        hold=(red1[0], es_near.to_0),
    )
    sync = exchange(i0.part)
    es_shares = sent_near(targets(es_near, inner))
    first1 = halves_first("1", (sync, *list(es_shares.values())[1:]), xpad=d0.ypad, gpad=i0.gpad)
    red_near = run(
        split_near(2, turned),
        "red1_near",
        dict(ids=ids, **pieces_of(red1, first1)),
        shares(inner, red_all // inner),
        dict(mine=((red_all, 256), BF)),
        hold=(first1[0],),
    )
    j0 = stage(
        stage_j(d),
        "stage_j0",
        dict(
            common(0),
            sync=sync,
            d2=i0.d2,
            s2=c0.s2,
            s1=b0.s1,
            wsp=wsp[0],
            dzf=i0.dzf0,
            f3=c0.f3,
            f2=b0.f2,
            w3=w3[0],
            tot_c=d0.tot,
            tot_b=c0.tot,
        ),
        dict(ds2=mid_b, d1=mid_f, df3=fast_b, d2f=tiny_f, tot=small, part=small),
        cols_s,
        hold=(red_near.to_0,),
    )
    sync = exchange(j0.part)
    red_shares = sent_near(targets(red_near, inner))
    k0 = stage(
        with_grads(
            with_grads(stage_k(d), grads_reduce(d), {}),
            grads_es(d),
            dict(keep="keep_es", send="send_es", halves="halves_es"),
        ),
        "stage_k0",
        dict(
            common(0),
            ids=ids,
            spad=slow_in.spad,
            lapad=b0.lapad,
            h2=d0.h2,
            k2=c0.k2,
            ds3=i0.ds3,
            df3=j0.df3,
            h1=c0.h1,
            k1=b0.k1,
            ds2=j0.ds2,
            sync=sync,
            d1=j0.d1,
            s1=b0.s1,
            lp=a0.lp,
            wred=wred[0],
            d2f=j0.d2f,
            f2=b0.f2,
            f1=a0.f1,
            w2t=w2t[0],
            tot_b=c0.tot,
            tot_a=b0.tot,
        ),
        dict(
            kept(rows_red),
            keep_es=((rows_es, 256), BF),
            send_es=((rows_es, 256), BF),
            dpad=mpad_s,
            dl=mid_f,
            df2=tiny_b,
            d1f=tiny_f,
            tot=small,
            part=small,
        ),
        dict(
            colf_s,
            **cols_s,
            halves=((2, rows_red, 256), BF),
            halves_es=((2, rows_es, 256), BF),
            g2=((quad * d.fb, 9 * quad * d.fb), F32),
            g3=((quad * d.fb, quad * d.cf), F32),
            block=((LANES, LANES), F32),
        ),
        hold=list(red_shares.values())[1:],
    )
    red0, es0 = (k0.keep, across(k0.send)), (k0.keep_es, across(k0.send_es))
    sync = exchange(k0.part)

    order = [sync]

    def step(body, name, ins, outs, scratch=None, grant=16):
        key = name.rstrip("01")
        made = run(
            body,
            name,
            ins,
            outs,
            scratch,
            hold=(order[-1],),
            groups=groups,
            flops=int(WEIGHT * TIMES.get(key, 0.6)),
            grant=grant,
        )
        order.append(getattr(made, next(iter(outs))))
        return made

    def block(count):
        return ((count, 256), BF)

    b_all, r_all, f_all = padded(rows_es), padded(rows_red), padded(rows_first)
    b_near, r_near, f_near = b_all // inner, r_all // inner, f_all // inner
    es_near, red_near = es_all // inner, red_all // inner

    def down(name, made, bit, after):
        rows_now = made.keep.shape[0]
        extent = rows_now // 2 if after else rows_now
        outs = dict(keep=block(extent))
        if after:
            outs.update(send=block(extent))
        return step(
            next_far(after),
            "%s_down_%d" % (name, bit),
            dict(ids=ids, own=made.keep, got=over(made.send, bit)),
            outs,
            dict(mine=block(rows_now)),
        )

    def up(name, own, bit):
        return step(
            join_far(bit),
            "%s_up_%d" % (name, bit),
            dict(ids=ids, own=own, got=over(own, bit)),
            dict(out=block(2 * own.shape[0])),
        ).out

    def up_pair(name, first, second, bits):
        made = step(
            join_pair(bits),
            "%s_up_%d" % (name, bits[0]),
            dict(
                ids=ids,
                own_0=first,
                got_0=over(first, bits[0]),
                own_1=second,
                got_1=over(second, bits[1]),
            ),
            dict(out_0=block(2 * first.shape[0]), out_1=block(2 * second.shape[0])),
        )
        return made.out_0, made.out_1

    def halved(name, pieces, count, bit):
        return step(
            split_half(len(pieces), bit),
            name + "_split",
            dict(ids=ids, **pieces_of(*pieces)),
            dict(keep=block(count // 2), send=block(count // 2)),
            dict(mine=block(count)),
        )

    far_bits = bits[::-1]
    down_way, turned_way = list(near_bits), near_bits[::-1]

    def merge(name, count, **ins):
        return step(
            merge_far(far_bits[0]),
            name + "_merge",
            dict(ids=ids, **ins),
            dict(keep=block(count // 2), send=block(count // 2)),
            dict(mine=block(count)),
        )

    def apart(name, own, early, late):
        made = step(
            part_far(far_bits[0]),
            name + "_part",
            dict(ids=ids, own=own, got=over(own, far_bits[0])),
            dict(early=block(early), late=block(late)),
            dict(all=block(early + late)),
        )
        return made.early, made.late

    l1 = step(
        merge_shares(far_bits[0], inner),
        "l1_merge",
        dict(
            ids=ids,
            **{"early_%d" % k: es_shares["from_%d" % k] for k in range(inner)},
            **{"late_%d" % k: red_shares["from_%d" % k] for k in range(inner)},
        ),
        dict(keep=block((es_near + red_near) // 2), send=block((es_near + red_near) // 2)),
        dict(mine=block(es_near + red_near)),
    )
    r_made = halved("r", (red0,), r_all, down_way[0])
    b_made = halved("b", (es0,), b_all, turned_way[0])
    l0 = step(
        stage_l(d),
        "stage_l0",
        dict(
            common(0),
            sync=sync,
            lp=a0.lp,
            f1=a0.f1,
            d1f=k0.d1f,
            dl=k0.dl,
            wa=wa[0],
            dzf=i0.dzf0,
            tot_a=b0.tot,
            ids=ids,
            value=d1.yout,
        ),
        dict(gpad=gpad_s, keep_out=out_fast, send_out=out_fast, tot=small),
    )
    first0 = step(
        grads_first(d),
        "grads_first0",
        dict(ids=ids, xpad=a0.xpad, gpad=l0.gpad),
        kept(rows_first),
        dict(ga=ga_s, halves=((2, rows_first, 256), BF)),
    )
    first0 = (first0.keep, across(first0.send))
    for i, bit in enumerate(far_bits[:-1]):
        l1 = down("l1", l1, bit, far_bits[i + 1])
    slow_out = step(
        stage_slow_out(d),
        "stage_slow_out",
        dict(ids=ids, mask=mask, dpad=k0.dpad, wred=wred[0], dzs=h1.dzs0, value=e1.yout),
        dict(keep_out=out_slow, send_out=out_slow),
    )
    f_made = halved("f", (first0,), f_all, turned_way[0])
    r_made = down("r", r_made, down_way[0], (down_way + [0])[1])
    b_part, f_part = b_all // 2, f_all // 2
    bf_ins = dict(
        own_0=b_made.keep,
        got_0=over(b_made.send, turned_way[0]),
        own_1=f_made.keep,
        got_1=over(f_made.send, turned_way[0]),
    )
    bf_made = step(
        join_parts((b_part, f_part), (turned_way + [0])[1]),
        "bf_down",
        dict(ids=ids, **bf_ins),
        dict(keep=block((b_part + f_part) // 2), send=block((b_part + f_part) // 2)),
        dict(mine=block(b_part + f_part)),
    )
    for i, bit in enumerate(turned_way[1:-1]):
        b_part, f_part = b_part // 2, f_part // 2
        bf_made = step(
            next_parts((b_part, f_part), turned_way[i + 2]),
            "bf_down_%d" % bit,
            dict(ids=ids, own=bf_made.keep, got=over(bf_made.send, bit)),
            dict(keep=block((b_part + f_part) // 2), send=block((b_part + f_part) // 2)),
            dict(mine=block(b_part + f_part)),
        )
    l1 = down("l1", l1, far_bits[-1], 0).keep
    at_1 = dict(
        s1=("h1", 0), s2=("g1", 0), s3=("f1", 0), f1=("g1", 4), f2=("f1", 16), f3=("e1", 16), lp=("i0", 16)
    )
    at_0 = dict(
        s1=("k0", 0), s2=("j0", 0), s3=("i0", 0), f1=("l0", 4), f2=("k0", 4), f3=("j0", 4), lp=("l0", 0)
    )
    norms = step(
        norms_out(d, (at_0, at_1)),
        "norms_out",
        dict(
            ids=ids,
            e1=e1.tot,
            f1=f1.tot,
            g1=g1.tot,
            h1=h1.tot,
            i0=i0.tot,
            j0=j0.tot,
            k0=k0.tot,
            l0=l0.tot,
        ),
        dict(keep=((2, norm_gain.shape[1]), F32), send=((2, norm_gain.shape[1]), F32)),
    )
    for bit in far_bits[:0:-1]:
        l1 = up("l1", l1, bit)
    for i, bit in enumerate(down_way[1:]):
        r_made = down("r", r_made, bit, (down_way + [0])[i + 2])
    bf_near = b_near + f_near
    t = merge(
        "t",
        r_near + bf_near,
        early=r_made.keep,
        own=bf_made.keep,
        got=over(bf_made.send, turned_way[-1]),
    )
    def placed(name, made):
        whole = (micro,) + made.keep_out.shape
        return step(
            stage_place,
            "place_" + name,
            dict(ids=ids, keep=made.keep_out, got=across(made.send_out)),
            dict(mark=small, hbm_out=(whole, BF)),
            dict(both=(whole, BF), sems=sems((2,))),
        ).hbm_out

    placed_fast = placed("fast", l0)
    es1_all, red1_all = apart("l1", l1, es_near, red_near)
    for i in range(shift_by - 1):
        es1_all, red1_all = up_pair("l1", es1_all, red1_all, (down_way[i], turned_way[i]))
    for i, bit in enumerate(far_bits):
        t = down("t", t, bit, (far_bits + [0])[i + 1])
        if i == 0:
            placed_slow = placed("slow", slow_out)
    t = t.keep
    for bit in far_bits[:0:-1]:
        t = up("t", t, bit)
    r_up, bf_up = apart("t", t, r_near, bf_near)
    es1_all, red1_all = up_pair("l1", es1_all, red1_all, (down_way[-1], turned_way[-1]))
    for i in range(shift_by - 1):
        r_up, bf_up = up_pair("r_bf", r_up, bf_up, (turned_way[i], down_way[i]))
    norms = step(
        norms_add,
        "norms_add",
        dict(keep=norms.keep, got=across(norms.send)),
        dict(gain=(norm_gain.shape, F32), shift=(norm_shift.shape, F32)),
    )

    def last(name, own, second, bit):
        made = step(
            join_send(bit),
            name + "_last",
            dict(ids=ids, own=own, got=over(own, bit), second=second),
            dict(out=block(2 * own.shape[0]), send=block(max(2 * own.shape[0], second.shape[0]))),
        )
        return made, across(made.send)

    r_all_up, got_a = last("r", r_up, red1_all, turned_way[-1])
    b_all_up, got_b = last("bf", bf_up, es1_all, down_way[-1])
    spots = dict(
        r=("own_r", "got_a", r_all, r_all, 0),
        red=("own_red", "got_a", red_all, red_all, 0),
        b=("own_b", "got_b", b_near, bf_near, 0),
        f=("own_b", "got_b", f_near, bf_near, b_near),
        es=("own_es", "got_b", es_all, es_all, 0),
    )
    done_red = step(
        finish_reduce(d, spots),
        "finish_reduce",
        dict(ids=ids, own_r=r_all_up.out, own_red=red1_all, got_a=got_a),
        dict(mark=small, hbm_reduce=(slow_reduce.shape, F32)),
        dict(reduce=((3, cs + d.cl, d.cb), F32), sems=sems((3,))),
    )
    done = step(
        finish_rest(d, spots, rows_red),
        "finish_rest",
        dict(
            ids=ids,
            own_red=red1_all,
            got_a=got_a,
            own_b=b_all_up.out,
            own_es=es1_all,
            got_b=got_b,
        ),
        dict(
            fspace=((1, 9, d.fb, d.fb), F32),
            hbm_expand=(slow_expand.shape, F32),
            hbm_space=((1, 9, d.cb, d.cb), F32),
            fexpand=(fast_expand.shape, F32),
            lateral=(lateral.shape, F32),
            freduce=((1, 3, d.fb, d.cf), F32),
        ),
        dict(
            expand=((d.cb, cs), F32),
            space=((9, d.cb, d.cb), F32),
            block=((LANES, LANES), F32),
            sems=sems((2,)),
        ),
    )
    weights = (
        done_red.hbm_reduce,
        done.hbm_space.reshape(slow_spatial.shape),
        done.hbm_expand,
        jnp.swapaxes(done.freduce, 2, 3),
        done.fspace.reshape(fast_spatial.shape),
        done.fexpand,
        done.lateral,
    )

    return (
        placed_slow.reshape(edge_slow.shape),
        placed_fast.reshape(edge_fast.shape),
        *weights,
        norms.gain,
        norms.shift,
    )


def solution(mesh):
    edge = P("pipe", None, "dp", None, None, None, None)
    weights = (
        P("pipe", None, None, None),
        P("pipe", None, None, None, None),
        P("pipe", None, None),
        P("pipe", None, None, None),
        P("pipe", None, None, None, None),
        P("pipe", None, None),
        P("pipe", None, None, None),
    )
    norms = (P("pipe", None), P("pipe", None))
    return jax.shard_map(
        on_device,
        mesh=mesh,
        in_specs=(edge, edge, *weights, *norms, P(), P()),
        out_specs=(edge, edge, *weights, *norms),
        check_vma=False,
    )
```
